32 devices in a mesh: dp: 4 (over y, core), seq: 8 (over z, x).
Axes of the slice: x: 2, y: 2, z: 4, core: 2. Of those that a mesh axis runs over, the one named last changes fastest.
Arguments:
- inputs: bfloat16 [16384, 1024], P(('dp', 'seq')), may hold values from -6 to 6
- text_state: bfloat16 [8, 128, 1024], replicated, may hold values from -6 to 6
- text_segment: int32 [8, 128], replicated, may hold values from 0 to 3, never falling along the last dimension, each value on 1 to 64 neighbouring positions
- image_text: int32 [16], replicated, may hold values from 0 to 7
- image_segment: int32 [16], replicated, may hold values from 0 to 3
- self_gain: float32 [1024], replicated, may hold values from 0.5 to 1.5
- self_shift: float32 [1024], replicated, may hold values from -1.5 to 1.5
- qkv_weight: bfloat16 [1024, 3072], replicated, may hold values from -0.1875 to 0.1875
- self_weight: bfloat16 [1024, 1024], replicated, may hold values from -0.75 to 0.75
- cross_gain: float32 [1024], replicated, may hold values from 0.5 to 1.5
- cross_shift: float32 [1024], replicated, may hold values from -1.5 to 1.5
- query_weight: bfloat16 [1024, 1024], replicated, may hold values from -0.1875 to 0.1875
- text_weight: bfloat16 [1024, 2048], replicated, may hold values from -0.1875 to 0.1875
- cross_weight: bfloat16 [1024, 1024], replicated, may hold values from -0.75 to 0.75
- feed_gain: float32 [1024], replicated, may hold values from 0.5 to 1.5
- feed_shift: float32 [1024], replicated, may hold values from -1.5 to 1.5
- up_weight: bfloat16 [1024, 4096], replicated, may hold values from -0.1875 to 0.1875
- down_weight: bfloat16 [4096, 1024], replicated, may hold values from -0.09375 to 0.09375
- cotangent: bfloat16 [16384, 1024], P(('dp', 'seq')), may hold values from -6 to 6
Outputs:
- output: bfloat16 [16384, 1024], P(('dp', 'seq'))
- input_grad: float32 [16384, 1024], P(('dp', 'seq'))
- text_grad: float32 [8, 128, 1024], replicated
- self_gain_grad: float32 [1024], P('seq')
- self_shift_grad: float32 [1024], P('seq')
- qkv_weight_grad: float32 [1024, 3072], P('seq')
- self_weight_grad: float32 [1024, 1024], P('seq')
- cross_gain_grad: float32 [1024], P('seq')
- cross_shift_grad: float32 [1024], P('seq')
- query_weight_grad: float32 [1024, 1024], P('seq')
- text_weight_grad: float32 [1024, 2048], P('seq')
- cross_weight_grad: float32 [1024, 1024], P('seq')
- feed_gain_grad: float32 [1024], P('seq')
- feed_shift_grad: float32 [1024], P('seq')
- up_weight_grad: float32 [1024, 4096], P('seq')
- down_weight_grad: float32 [4096, 1024], P('seq')
The draws below stay inside these ranges and needn't reach their ends.
All inputs are finite; a program needn't handle non-finite values.
Results may differ from the reference program's by a relative error of at most 0.024.
Values may be sent and summed in bfloat16 or wider, within the bound.
No kernel may reach another device: no remote copies, remote signals or barrier semaphores. Data moves between devices by JAX's collectives and lax.ppermute only.
A program may use at most 320 MiB of HBM per device.

```python
import math
import jax
import jax.numpy as jnp
import numpy as np
from jax import lax

D = 1024
HEADS = 16
HEAD = 64
FF = 4096
TEXT_LEN = 128
TEXT_ROWS = 8
SEGS = 4
IMG_TOK = 1024
GROUP_TOK = 4096
IMG_GROUP = 4
IMAGES = 16
TOKENS = 16384
N_DP = 4


def with_ends(entries, rng, least, largest):
    spot = [jax.random.randint(jax.random.fold_in(rng, axis), (), 0, length) for axis, length in enumerate(entries.shape)]
    longest = entries.shape.index(max(entries.shape))
    neighbour = spot[:longest] + [(spot[longest] + 1) % entries.shape[longest]] + spot[longest + 1:]
    return entries.at[tuple(spot)].set(least).at[tuple(neighbour)].set(largest)


def level_of(rng, extent, pieces, least, largest):
    loudness, own = 1.0, jax.random.fold_in(rng, 6)
    for dim, shards_of in pieces:
        steps = jnp.exp(jax.random.uniform(jax.random.fold_in(own, dim), (shards_of,), jnp.float32, least / len(pieces), largest / len(pieces)))
        loudness = loudness * jnp.repeat(steps, extent[dim] // shards_of).reshape([-1 if axis == dim else 1 for axis in range(len(extent))])
    return loudness


def length_profile(amount, total, most, skew):
    portions = [(1 << 20) // math.isqrt(standing ** skew) + 1 for standing in range(2, amount + 1)]
    surplus, counts = total - most - (amount - 1), [1] * (amount - 1)
    while surplus > 0:
        candidates = [i for i in range(amount - 1) if counts[i] < most]
        whole, left = sum([portions[i] for i in candidates]), surplus
        for i in candidates:
            more = min(most - counts[i], max(1, left * portions[i] // whole), surplus)
            counts[i] = counts[i] + more
            surplus = surplus - more
    return np.array([most] + counts)


def uneven(own_key, count, total, most, lean):
    if count == 2:
        one = jax.random.randint(own_key, (), max(1, total - most), min(most, total - 1) + 1)
        return jnp.stack([one, total - one])
    tallies = jnp.asarray(length_profile(count, total, most, lean), jnp.int32)
    couples = (count - 1) // 2
    giver, sink = tallies[1:1 + 2 * couples:2], tallies[2:2 + 2 * couples:2]
    margin = jnp.minimum(giver - 1, most - sink)
    passed = jax.random.randint(jax.random.fold_in(own_key, 1), (couples,), 0, 1 << 20) % (margin + 1)
    tallies = tallies.at[1:1 + 2 * couples:2].set(giver - passed).at[2:2 + 2 * couples:2].set(sink + passed)
    return tallies[jax.random.permutation(jax.random.fold_in(own_key, 2), count)]


def noise(key, shape, scale, limit, pieces=(), kind=jnp.bfloat16):
    values = jax.random.normal(key, shape, jnp.float32) * scale
    if len(pieces) > 0:
        values = level_of(key, shape, pieces, -0.22, 0.18) * values
    return jnp.clip(values, min=-limit, max=limit).astype(kind)


def setup_inputs(seed: int = 0) -> dict:
    splits = jax.random.split(jax.random.key(seed), 20)
    return {
        "inputs": noise(splits[0], (TOKENS, D), 1.0, 6.0, ((0, 32),)),
        "text_state": noise(splits[1], (TEXT_ROWS, TEXT_LEN, D), 1.0, 6.0),
        "text_segment": jax.vmap(lambda own: jnp.searchsorted(jnp.cumsum(uneven(own, SEGS, TEXT_LEN, TEXT_LEN // 2, 0)), jnp.arange(TEXT_LEN), side="right"))(jax.random.split(splits[2], TEXT_ROWS)).reshape((TEXT_ROWS, TEXT_LEN)).astype(jnp.int32),
        "image_text": with_ends(jax.random.randint(splits[3], (IMAGES,), 0, TEXT_ROWS), jax.random.fold_in(splits[3], 1), 0, TEXT_ROWS - 1).astype(jnp.int32),
        "image_segment": with_ends(jax.random.randint(splits[4], (IMAGES,), 0, SEGS), jax.random.fold_in(splits[4], 1), 0, SEGS - 1).astype(jnp.int32),
        "self_gain": jnp.clip(1.0 + 0.1 * jax.random.normal(splits[5], (D,), jnp.float32), 0.5, 1.5),
        "self_shift": noise(splits[6], (D,), 0.3, 1.5, (), jnp.float32),
        "qkv_weight": noise(splits[7], (D, 3 * D), D ** -0.5, 0.1875),
        "self_weight": noise(splits[8], (D, D), HEAD ** -0.5, 0.75),
        "cross_gain": jnp.clip(1.0 + 0.1 * jax.random.normal(splits[9], (D,), jnp.float32), 0.5, 1.5),
        "cross_shift": noise(splits[10], (D,), 0.3, 1.5, (), jnp.float32),
        "query_weight": noise(splits[11], (D, D), D ** -0.5, 0.1875),
        "text_weight": noise(splits[12], (D, 2 * D), D ** -0.5, 0.1875),
        "cross_weight": noise(splits[13], (D, D), (D // 16) ** -0.5, 0.75),
        "feed_gain": jnp.clip(1.0 + 0.1 * jax.random.normal(splits[14], (D,), jnp.float32), 0.5, 1.5),
        "feed_shift": noise(splits[15], (D,), 0.3, 1.5, (), jnp.float32),
        "up_weight": noise(splits[16], (D, FF), D ** -0.5, 0.1875),
        "down_weight": noise(splits[17], (FF, D), FF ** -0.5, 0.09375),
        "cotangent": noise(splits[18], (TOKENS, D), 1.0, 6.0, ((0, 32),)),
    }


@jax.custom_vjp
def low(v):
    return lax.optimization_barrier(v.astype(jnp.bfloat16)).astype(jnp.float32)

@jax.custom_vjp
def low_back(v):
    return v

def low_keep(v):
    return (low(v), None)

def low_pass(kept, grad):
    return (grad,)

def back_keep(v):
    return (v, None)

def back_low(kept, grad):
    return (low(grad),)
low.defvjp(low_keep, low_pass)
low_back.defvjp(back_keep, back_low)
HIGH = lax.Precision.HIGHEST
NEGATIVE = -1e+30
EPSILON = 1e-05

def matmul(left, right):
    return jnp.dot(left, right, precision=HIGH, preferred_element_type=jnp.float32)

def layer_norm(values, gain, shift):
    average = lax.optimization_barrier(jnp.mean(values, axis=-1, keepdims=True))
    centered = values - average
    inverse = lax.rsqrt(lax.optimization_barrier(jnp.mean(centered * centered, axis=-1, keepdims=True)) + EPSILON)
    return centered * inverse * gain + shift

def reference(inputs, text_state, text_segment, image_text, image_segment, self_gain, self_shift, qkv_weight, self_weight, cross_gain, cross_shift, query_weight, text_weight, cross_weight, feed_gain, feed_shift, up_weight, down_weight, cotangent):
    score_scale = 1.0 / math.sqrt(HEAD)
    block_rows = math.gcd(GROUP_TOK, 512)
    block_count = GROUP_TOK // block_rows
    rows_table = image_text.reshape(N_DP, IMG_GROUP)
    segs_table = image_segment.reshape(N_DP, IMG_GROUP)
    text_keys = TEXT_ROWS * TEXT_LEN
    key_row = jnp.arange(text_keys, dtype=jnp.int32) // TEXT_LEN
    key_seg = text_segment.reshape(-1).astype(jnp.int32)
    positions = jnp.arange(GROUP_TOK, dtype=jnp.int32)
    image_slots = jnp.arange(IMG_GROUP, dtype=jnp.int32)
    image_of = positions // IMG_TOK

    def forward(inputs_f, text_f, gain_one, shift_one, w_qkv, w_self, gain_two, shift_two, w_query, w_text, w_cross, gain_three, shift_three, w_up, w_down):
        text_kv = low_back(low(matmul(text_f.reshape(text_keys, D), w_text)))
        text_k = text_kv[:, :D].reshape(text_keys, HEADS, HEAD)
        text_v = text_kv[:, D:].reshape(text_keys, HEADS, HEAD)

        def one_group(x_group, row_group, seg_group):
            onehot = (image_of[:, None] == image_slots[None, :]).astype(jnp.int32)
            tok_row = lax.optimization_barrier(jnp.sum(onehot * row_group[None, :], axis=1))
            tok_seg = lax.optimization_barrier(jnp.sum(onehot * seg_group[None, :], axis=1))
            act_one = low(layer_norm(x_group, gain_one, shift_one))
            qkv = low_back(low(matmul(act_one, w_qkv)))
            queries = qkv[:, :D].reshape(GROUP_TOK, HEADS, HEAD)
            key_heads = qkv[:, D:2 * D].reshape(GROUP_TOK, HEADS, HEAD)
            value_heads = qkv[:, 2 * D:].reshape(GROUP_TOK, HEADS, HEAD)

            def self_block(block_index):
                first = block_index * block_rows
                q_block = lax.dynamic_slice_in_dim(queries, first, block_rows, 0)
                q_pos = first + jnp.arange(block_rows, dtype=jnp.int32)
                q_img = q_pos // IMG_TOK
                scores = jnp.einsum('qhd,khd->hqk', q_block, key_heads, precision=HIGH) * score_scale
                allowed = (image_of[None, :] == q_img[:, None]) & (positions[None, :] <= q_pos[:, None])
                scores = low_back(jnp.where(allowed[None], scores, NEGATIVE))
                softmax_w = jax.nn.softmax(scores, axis=-1)
                return jnp.einsum('hqk,khd->qhd', low(softmax_w), value_heads, precision=HIGH)
            attended = lax.map(jax.checkpoint(self_block), jnp.arange(block_count, dtype=jnp.int32))
            attended = low_back(low(attended.reshape(GROUP_TOK, D)))
            mid_one = x_group + low_back(matmul(attended, w_self))
            act_two = low(layer_norm(mid_one, gain_two, shift_two))
            cross_q = low_back(low(matmul(act_two, w_query))).reshape(GROUP_TOK, HEADS, HEAD)

            def cross_block(block_index):
                first = block_index * block_rows
                q_block = lax.dynamic_slice_in_dim(cross_q, first, block_rows, 0)
                row_block = lax.dynamic_slice_in_dim(tok_row, first, block_rows, 0)
                seg_block = lax.dynamic_slice_in_dim(tok_seg, first, block_rows, 0)
                scores = jnp.einsum('qhd,khd->hqk', q_block, text_k, precision=HIGH) * score_scale
                allowed = (key_row[None, :] == row_block[:, None]) & (key_seg[None, :] == seg_block[:, None])
                scores = low_back(jnp.where(allowed[None], scores, NEGATIVE))
                softmax_w = jax.nn.softmax(scores, axis=-1)
                return jnp.einsum('hqk,khd->qhd', low(softmax_w), text_v, precision=HIGH)
            crossed = lax.map(jax.checkpoint(cross_block), jnp.arange(block_count, dtype=jnp.int32))
            crossed = low_back(low(crossed.reshape(GROUP_TOK, D)))
            mid_two = mid_one + low_back(matmul(crossed, w_cross))
            act_three = low(layer_norm(mid_two, gain_three, shift_three))
            hidden = low(jax.nn.gelu(low_back(matmul(act_three, w_up)), approximate=True))
            return mid_two + low_back(matmul(hidden, w_down))
        checked = jax.checkpoint(one_group)

        def scan_step(running, group_data):
            return (running, checked(*group_data))
        _, results = lax.scan(scan_step, None, (inputs_f.reshape(N_DP, GROUP_TOK, D), rows_table, segs_table))
        return results.reshape(N_DP * GROUP_TOK, D)
    primals = (inputs.astype(jnp.float32), text_state.astype(jnp.float32), self_gain.astype(jnp.float32), self_shift.astype(jnp.float32), qkv_weight.astype(jnp.float32), self_weight.astype(jnp.float32), cross_gain.astype(jnp.float32), cross_shift.astype(jnp.float32), query_weight.astype(jnp.float32), text_weight.astype(jnp.float32), cross_weight.astype(jnp.float32), feed_gain.astype(jnp.float32), feed_shift.astype(jnp.float32), up_weight.astype(jnp.float32), down_weight.astype(jnp.float32))
    result, pullback = jax.vjp(forward, *primals)
    grads = pullback(cotangent.astype(jnp.float32))
    return (result.astype(jnp.bfloat16), grads[0], grads[1], grads[2], grads[3], grads[4], grads[5], grads[6], grads[7], grads[8], grads[9], grads[10], grads[11], grads[12], grads[13], grads[14])
```

```python
import functools
import math

import jax
import jax.numpy as jnp
from jax import lax
from jax.experimental import pallas as pl
from jax.experimental.pallas import tpu as pltpu
from jax.sharding import PartitionSpec as P

D = 1024
HEADS = 16
HEAD = 64
FF = 4096
TEXT_LEN = 128
IMG_TOK = 1024
PAIR = 2 * HEAD
SCALE = 1.0 / math.sqrt(HEAD)

NEGATIVE = -1e30
EPSILON = 1e-05
BF = jnp.bfloat16
F32 = jnp.float32
NN = (((1,), (0,)), ((), ()))
NT = (((1,), (1,)), ((), ()))
TN = (((0,), (0,)), ((), ()))
VMEM_LIMIT = 56 * 1024 * 1024


def mm(a, b, dims=NN):
    return lax.dot_general(a, b, dims, preferred_element_type=F32)


def normed(values):
    average = jnp.mean(values, axis=-1, keepdims=True)
    centered = values - average
    inverse = lax.rsqrt(jnp.mean(centered * centered, axis=-1, keepdims=True) + EPSILON)
    return centered * inverse, inverse


def norm_back(normal, inverse, gain, upstream):
    w = upstream * gain
    along = jnp.mean(w * normal, axis=-1, keepdims=True)
    return inverse * (w - jnp.mean(w, axis=-1, keepdims=True) - normal * along)


def head_lanes(h):
    lane = lax.broadcasted_iota(jnp.int32, (1, PAIR), 1)
    return (lane >= h * HEAD) & (lane < (h + 1) * HEAD)


def only_head(block, h):
    return jnp.where(head_lanes(h), block, jnp.zeros_like(block))


def params(grid_dims=1):
    return pltpu.CompilerParams(
        dimension_semantics=("arbitrary",) * grid_dims, vmem_limit_bytes=VMEM_LIMIT
    )


def cost(flops, moved):
    return pl.CostEstimate(flops=int(flops), bytes_accessed=int(moved), transcendentals=0)


def whole(shape):
    zeros = (0,) * len(shape)
    return pl.BlockSpec(shape, lambda *_: zeros)


def shape_of(shape, dtype):
    return jax.ShapeDtypeStruct(shape, dtype)


def norm_project(x, gain, shift, weight, first_col, name):
    rows, width = x.shape
    cols = weight.shape[1] - first_col
    bn = 512

    def kernel(x_ref, gain_ref, shift_ref, w_ref, act_ref, out_ref):
        @pl.when(pl.program_id(0) == 0)
        def _():
            normal, _ = normed(x_ref[...].astype(F32))
            act_ref[...] = (normal * gain_ref[...] + shift_ref[...]).astype(BF)

        out_ref[...] = mm(act_ref[...], w_ref[...]).astype(BF)

    return pl.pallas_call(
        kernel,
        grid=(cols // bn,),
        in_specs=[
            whole((rows, width)),
            whole((1, width)),
            whole((1, width)),
            pl.BlockSpec((width, bn), lambda j: (0, first_col // bn + j)),
        ],
        out_specs=[whole((rows, width)), pl.BlockSpec((rows, bn), lambda j: (0, j))],
        out_shape=[shape_of((rows, width), BF), shape_of((rows, cols), BF)],
        compiler_params=params(),
        cost_estimate=cost(2 * rows * width * cols, 2 * width * cols + 4 * rows * width),
        name=name,
    )(x, gain, shift, weight)


def causal_forward(qkv):
    rows = qkv.shape[0]
    half = rows // 2
    pairs = D // PAIR

    def kernel(q_ref, k_ref, v_ref, out_ref, log_ref):
        for first in (0, half):
            keys = first + half
            q = q_ref[first:keys, :] * SCALE
            k = k_ref[:keys, :]
            v = v_ref[:keys, :]
            at_q = first + lax.broadcasted_iota(jnp.int32, (half, keys), 0)
            at_k = lax.broadcasted_iota(jnp.int32, (half, keys), 1)
            total = jnp.zeros((half, PAIR), F32)
            logs = jnp.zeros((half, PAIR), F32)
            for h in (0, 1):
                s = mm(q, only_head(k, h), NT)
                s = jnp.where(at_q >= at_k, s, NEGATIVE)
                top = jnp.max(s, axis=1, keepdims=True)
                p = jnp.exp(s - top)
                part = jnp.sum(p, axis=1, keepdims=True)
                total = total + mm(p.astype(BF), only_head(v, h)) * (1.0 / part)
                logs = jnp.where(head_lanes(h), top + jnp.log(part), logs)
            out_ref[first:keys, :] = total
            log_ref[first:keys, :] = logs

    block = (rows, PAIR)
    return pl.pallas_call(
        kernel,
        grid=(pairs,),
        in_specs=[
            pl.BlockSpec(block, lambda p: (0, p)),
            pl.BlockSpec(block, lambda p: (0, pairs + p)),
            pl.BlockSpec(block, lambda p: (0, 2 * pairs + p)),
        ],
        out_specs=[pl.BlockSpec(block, lambda p: (0, p))] * 2,
        out_shape=[shape_of((rows, D), F32)] * 2,
        compiler_params=params(),
        cost_estimate=cost(8 * rows * rows * D, 14 * rows * D),
        name="causal_forward",
    )(qkv, qkv, qkv)


def earlier_forward(odd, qkv, pairs_before, own_out, own_log):
    rows = qkv.shape[0]
    half = rows // 2
    pairs = D // PAIR

    def kernel(odd_ref, q_ref, k_ref, v_ref, own_ref, log_ref, out_ref, new_log_ref):
        @pl.when(odd_ref[0] == 0)
        def _():
            out_ref[...] = own_ref[...].astype(BF)
            new_log_ref[...] = log_ref[...]

        @pl.when(odd_ref[0] != 0)
        def _():
            for first in (0, half):
                span = slice(first, first + half)
                q = q_ref[span, :] * SCALE
                total = own_ref[span, :]
                logs = log_ref[span, :]
                result = jnp.zeros_like(total)
                new_logs = logs
                for h in (0, 1):
                    s = mm(q, only_head(k_ref[...], h), NT)
                    old = logs[:, h * HEAD : h * HEAD + 1]
                    top = jnp.maximum(old, jnp.max(s, axis=1, keepdims=True))
                    p = jnp.exp(s - top)
                    share = jnp.exp(old - top)
                    part = share + jnp.sum(p, axis=1, keepdims=True)
                    mixed = mm(p.astype(BF), only_head(v_ref[...], h))
                    mixed = mixed + only_head(total, h) * share
                    result = result + mixed * (1.0 / part)
                    new_logs = jnp.where(head_lanes(h), top + jnp.log(part), new_logs)
                out_ref[span, :] = result.astype(BF)
                new_log_ref[span, :] = new_logs

    block = (rows, PAIR)
    first = pl.BlockSpec(block, lambda p, odd: (0, p))
    second = pl.BlockSpec(block, lambda p, odd: (0, pairs + p))
    return pl.pallas_call(
        kernel,
        grid_spec=pltpu.PrefetchScalarGridSpec(
            num_scalar_prefetch=1,
            grid=(pairs,),
            in_specs=[first, first, second, first, first],
            out_specs=[first, first],
        ),
        out_shape=[shape_of((rows, D), BF), shape_of((rows, D), F32)],
        compiler_params=params(),
        cost_estimate=cost(8 * rows * rows * D, 18 * rows * D),
        name="earlier_forward",
    )(odd, qkv, pairs_before, pairs_before, own_out, own_log)


def cross_weights(keys, queries, bias):
    s = mm(keys, queries, NT) + bias
    p = jnp.exp(s - jnp.max(s, axis=0, keepdims=True))
    return p * (1.0 / jnp.sum(p, axis=0, keepdims=True))


def middle_forward(attended, x, self_w, query_w, cross_w, gains, text_kv, bias):
    rows = x.shape[0]
    tile = rows // 2

    def kernel(
        at_ref, x_ref, sw_ref, qw_ref, cw_ref, gains_ref, kv_ref, bias_ref,
        mid1_ref, act2_ref, cq_ref, crossed_ref, mid2_ref, act3_ref,
    ):
        mid1 = x_ref[...].astype(F32) + mm(at_ref[...], sw_ref[...])
        mid1_ref[...] = mid1
        normal, _ = normed(mid1)
        act2 = (normal * gains_ref[0:1, :] + gains_ref[1:2, :]).astype(BF)
        act2_ref[...] = act2
        cq_ref[...] = mm(act2, qw_ref[...]).astype(BF)
        bias_col = bias_ref[:, 0:1]
        for p in range(D // PAIR):
            span = slice(p * PAIR, (p + 1) * PAIR)
            q = cq_ref[:, span] * SCALE
            k = kv_ref[:, span]
            v = kv_ref[:, D + p * PAIR : D + (p + 1) * PAIR]
            total = jnp.zeros((tile, PAIR), F32)
            for h in (0, 1):
                w = cross_weights(only_head(k, h), q, bias_col)
                total = total + mm(w.astype(BF), only_head(v, h), TN)
            crossed_ref[:, span] = total.astype(BF)
        mid2 = mid1 + mm(crossed_ref[...], cw_ref[...])
        mid2_ref[...] = mid2
        normal, _ = normed(mid2)
        act3_ref[...] = (normal * gains_ref[2:3, :] + gains_ref[3:4, :]).astype(BF)

    row_block = pl.BlockSpec((tile, D), lambda i: (i, 0))
    square = whole((D, D))
    return pl.pallas_call(
        kernel,
        grid=(rows // tile,),
        in_specs=[
            row_block, row_block, square, square, square,
            whole(gains.shape), whole(text_kv.shape), whole(bias.shape),
        ],
        out_specs=[row_block] * 6,
        out_shape=[
            shape_of((rows, D), t) for t in (F32, BF, BF, BF, F32, BF)
        ],
        compiler_params=params(),
        cost_estimate=cost(8 * rows * D * D, 6 * D * D + 20 * rows * D),
        name="middle_forward",
    )(attended, x, self_w, query_w, cross_w, gains, text_kv, bias)


def feed_half(which, act3, grad3, up, down, shards, before):
    rows = act3.shape[0]
    bw = FF // (2 * shards)
    root = math.sqrt(2.0 / math.pi)

    def kernel(which_ref, a_ref, g_ref, up_ref, down_ref, *rest):
        if before is None:
            y_ref, dh_ref, da_ref = rest
        else:
            before_ref, y_ref, dh_ref, da_ref = rest
        h = mm(a_ref[...], up_ref[...])
        sq = h * h
        t = jnp.tanh(h * (root + (root * 0.044715) * sq))
        y_ref[...] = (0.5 * h * (1.0 + t)).astype(BF)
        slope = 0.5 * (1.0 + t) + (0.5 * h) * (1.0 - t * t) * (root + (3 * root * 0.044715) * sq)
        dy = mm(g_ref[...], down_ref[...], NT)
        dh = (dy * slope).astype(BF)
        dh_ref[...] = dh
        part = mm(dh, up_ref[...], NT)

        @pl.when(pl.program_id(0) == 0)
        def _():
            if before is None:
                da_ref[...] = part
            else:
                da_ref[...] = before_ref[...] + part

        @pl.when(pl.program_id(0) != 0)
        def _():
            da_ref[...] += part

    token = whole((rows, D))
    in_specs = [
        token,
        token,
        pl.BlockSpec((D, bw), lambda s, which: (0, 2 * s + which[0])),
        pl.BlockSpec((bw, D), lambda s, which: (2 * s + which[0], 0)),
    ]
    operands = [which, act3, grad3, up, down]
    if before is not None:
        in_specs.append(token)
        operands.append(before)
    return pl.pallas_call(
        kernel,
        grid_spec=pltpu.PrefetchScalarGridSpec(
            num_scalar_prefetch=1,
            grid=(shards,),
            in_specs=in_specs,
            out_specs=[pl.BlockSpec((rows, bw), lambda s, which: (0, s))] * 2 + [token],
        ),
        out_shape=[
            shape_of((rows, FF // 2), BF),
            shape_of((rows, FF // 2), BF),
            shape_of((rows, D), F32),
        ],
        compiler_params=params(),
        cost_estimate=cost(3 * rows * D * FF, 2 * D * FF + 8 * rows * D),
        name="feed_half",
    )(*operands)


def feed_output(own, mid2, hidden_own, hidden_other, down, shards):
    rows = mid2.shape[0]
    bw = FF // (2 * shards)

    def kernel(own_ref, mid_ref, a_ref, b_ref, da_ref, db_ref, out_ref, acc_ref):
        s = pl.program_id(0)
        part = mm(a_ref[...], da_ref[...]) + mm(b_ref[...], db_ref[...])

        @pl.when(s == 0)
        def _():
            acc_ref[...] = mid_ref[...] + part

        @pl.when(s != 0)
        def _():
            acc_ref[...] += part

        @pl.when(s == shards - 1)
        def _():
            out_ref[...] = acc_ref[...].astype(BF)

    token = whole((rows, D))
    hid = pl.BlockSpec((rows, bw), lambda s, own: (0, s))
    return pl.pallas_call(
        kernel,
        grid_spec=pltpu.PrefetchScalarGridSpec(
            num_scalar_prefetch=1,
            grid=(shards,),
            in_specs=[
                token,
                hid,
                hid,
                pl.BlockSpec((bw, D), lambda s, own: (2 * s + own[0], 0)),
                pl.BlockSpec((bw, D), lambda s, own: (2 * s + 1 - own[0], 0)),
            ],
            out_specs=token,
            scratch_shapes=[pltpu.VMEM((rows, D), F32)],
        ),
        out_shape=shape_of((rows, D), BF),
        compiler_params=params(),
        cost_estimate=cost(2 * rows * D * FF, 2 * D * FF + 14 * rows * D),
        name="feed_output",
    )(own, mid2, hidden_own, hidden_other, down, down)


def middle_backward(d_act3, mid2, upstream, mid1, cq, text_kv, bias, cross_w, query_w, self_w, gains):
    rows = mid2.shape[0]
    tile = rows // 2
    steps = rows // tile

    def kernel(
        da3_ref, mid2_ref, g_ref, mid1_ref, cq_ref, kv_ref, bias_ref, cw_ref, qw_ref, sw_ref, gains_ref,
        g2_ref, dcq_ref, dmid1_ref, g1_ref, dat_ref, dkv_ref, dgains_ref, kv_acc,
    ):
        i = pl.program_id(0)

        @pl.when(i == 0)
        def _():
            kv_acc[...] = jnp.zeros_like(kv_acc)
            dgains_ref[...] = jnp.zeros_like(dgains_ref)

        up3 = da3_ref[...]
        normal, inverse = normed(mid2_ref[...])
        dgains_ref[2:3, :] += jnp.sum(up3 * normal, axis=0, keepdims=True)
        dgains_ref[3:4, :] += jnp.sum(up3, axis=0, keepdims=True)
        dmid2 = g_ref[...].astype(F32) + norm_back(normal, inverse, gains_ref[2:3, :], up3)
        g2 = dmid2.astype(BF)
        g2_ref[...] = g2
        dat_ref[...] = mm(g2, cw_ref[...], NT).astype(BF)
        bias_col = bias_ref[:, 0:1]
        for p in range(D // PAIR):
            span = slice(p * PAIR, (p + 1) * PAIR)
            vspan = slice(D + p * PAIR, D + (p + 1) * PAIR)
            q = cq_ref[:, span] * SCALE
            dc = dat_ref[:, span]
            k = kv_ref[:, span]
            v = kv_ref[:, vspan]
            dq = jnp.zeros((tile, PAIR), F32)
            dk = jnp.zeros((TEXT_LEN, PAIR), F32)
            dv = jnp.zeros((TEXT_LEN, PAIR), F32)
            for h in (0, 1):
                kh = only_head(k, h)
                w = cross_weights(kh, q, bias_col)
                dw = mm(only_head(v, h), dc, NT)
                ds = (w * (dw - jnp.sum(w * dw, axis=0, keepdims=True))).astype(BF)
                dq = dq + mm(ds, kh, TN)
                dk = dk + mm(ds, only_head(q, h))
                dv = dv + mm(w.astype(BF), only_head(dc, h))
            dcq_ref[:, span] = (dq * SCALE).astype(BF)
            kv_acc[:, span] += dk
            kv_acc[:, vspan] += dv
        up2 = mm(dcq_ref[...], qw_ref[...], NT)
        normal, inverse = normed(mid1_ref[...])
        dgains_ref[0:1, :] += jnp.sum(up2 * normal, axis=0, keepdims=True)
        dgains_ref[1:2, :] += jnp.sum(up2, axis=0, keepdims=True)
        dmid1 = dmid2 + norm_back(normal, inverse, gains_ref[0:1, :], up2)
        dmid1_ref[...] = dmid1
        g1 = dmid1.astype(BF)
        g1_ref[...] = g1
        dat_ref[...] = mm(g1, sw_ref[...], NT).astype(BF)

        @pl.when(i == steps - 1)
        def _():
            dkv_ref[...] = kv_acc[...].astype(BF)

    row_block = pl.BlockSpec((tile, D), lambda i: (i, 0))
    square = whole((D, D))
    return pl.pallas_call(
        kernel,
        grid=(steps,),
        in_specs=[
            row_block, row_block, row_block, row_block, row_block,
            whole(text_kv.shape), whole(bias.shape), square, square, square, whole(gains.shape),
        ],
        out_specs=[row_block] * 5 + [whole(text_kv.shape), whole((8, D))],
        out_shape=[shape_of((rows, D), t) for t in (BF, BF, F32, BF, BF)]
        + [shape_of(text_kv.shape, BF), shape_of((8, D), F32)],
        scratch_shapes=[pltpu.VMEM(text_kv.shape, F32)],
        compiler_params=params(),
        cost_estimate=cost(10 * rows * D * D, 6 * D * D + 24 * rows * D),
        name="middle_backward",
    )(d_act3, mid2, upstream, mid1, cq, text_kv, bias, cross_w, query_w, self_w, gains)


def deltas_of(d_out, out):
    prod = d_out.astype(F32) * out.astype(F32)
    high = prod.astype(BF)
    low = (prod - high.astype(F32)).astype(BF)
    row = lax.broadcasted_iota(jnp.int32, (8, PAIR), 0)
    lane = lax.broadcasted_iota(jnp.int32, (8, PAIR), 1)
    pick = jnp.where(lane // HEAD == row, 1.0, 0.0).astype(BF)
    return mm(pick, high, NT) + mm(pick, low, NT)


def key_block_back(k, v, q, d_out, log_row, delta_row, h, masked_from=None):
    kh = only_head(k, h)
    s = mm(kh, q, NT)
    p = jnp.exp(s - log_row)
    if masked_from is not None:
        at_k = lax.broadcasted_iota(jnp.int32, s.shape, 0)
        at_q = lax.broadcasted_iota(jnp.int32, s.shape, 1) + masked_from
        p = jnp.where(at_q >= at_k, p, 0.0)
    dp = mm(only_head(v, h), d_out, NT)
    ds = (p * (dp - delta_row)).astype(BF)
    dv = mm(p.astype(BF), only_head(d_out, h))
    dk = mm(ds, only_head(q, h))
    dq = mm(ds, kh, TN)
    return dq, dk, dv


def earlier_backward(scalars, qkv, pairs_before, d_out, out, logs):
    rows = qkv.shape[0]
    half = rows // 2
    pairs = D // PAIR
    count = pairs // 2

    def kernel(sc_ref, q_ref, k_ref, v_ref, do_ref, out_ref, log_ref, dq_ref, dkv_ref):
        @pl.when(sc_ref[0] == 0)
        def _():
            dq_ref[...] = jnp.zeros_like(dq_ref)
            dkv_ref[...] = jnp.zeros_like(dkv_ref)

        @pl.when(sc_ref[0] != 0)
        def _():
            q = q_ref[...] * SCALE
            d_o = do_ref[...]
            deltas = deltas_of(d_o, out_ref[...])
            dq_total = jnp.zeros((rows, PAIR), F32)
            for first in (0, half):
                span = slice(first, first + half)
                dk_total = jnp.zeros((half, PAIR), F32)
                dv_total = jnp.zeros((half, PAIR), F32)
                for h in (0, 1):
                    dq, dk, dv = key_block_back(
                        k_ref[span, :], v_ref[span, :], q, d_o,
                        log_ref[0, h : h + 1, :], deltas[h : h + 1, :], h,
                    )
                    dq_total = dq_total + dq
                    dk_total = dk_total + dk
                    dv_total = dv_total + dv
                dkv_ref[0, span, :] = dk_total.astype(BF)
                dkv_ref[1, span, :] = dv_total.astype(BF)
            dq_ref[...] = dq_total

    block = (rows, PAIR)

    def at(offset):
        return pl.BlockSpec(block, lambda p, sc: (0, offset + sc[1] * count + p))

    return pl.pallas_call(
        kernel,
        grid_spec=pltpu.PrefetchScalarGridSpec(
            num_scalar_prefetch=1,
            grid=(count,),
            in_specs=[
                at(0),
                at(0),
                at(pairs),
                at(0),
                at(0),
                pl.BlockSpec((1, 2, rows), lambda p, sc: (sc[1] * count + p, 0, 0)),
            ],
            out_specs=[
                pl.BlockSpec(block, lambda p, sc: (0, p)),
                pl.BlockSpec((2, rows, PAIR), lambda p, sc: (0, 0, p)),
            ],
        ),
        out_shape=[shape_of((rows, D // 2), F32), shape_of((2, rows, D // 2), BF)],
        compiler_params=params(),
        cost_estimate=cost(10 * rows * rows * D, 10 * rows * D),
        name="earlier_backward",
    )(scalars, qkv, pairs_before, pairs_before, d_out, out, logs)


def causal_backward(scalars, qkv, d_out, out, logs, dq_before):
    rows = qkv.shape[0]
    half = rows // 2
    pairs = D // PAIR
    count = pairs // 2

    def kernel(sc_ref, q_ref, k_ref, v_ref, do_ref, out_ref, log_ref, before_ref, grads_ref):
        q = q_ref[...] * SCALE
        d_o = do_ref[...]
        deltas = deltas_of(d_o, out_ref[...])
        dq_late = before_ref[half:, :]
        dq_early = before_ref[:half, :]
        for first in (0, half):
            span = slice(first, first + half)
            dk_total = jnp.zeros((half, PAIR), F32)
            dv_total = jnp.zeros((half, PAIR), F32)
            for h in (0, 1):
                dq, dk, dv = key_block_back(
                    k_ref[span, :], v_ref[span, :], q[first:], d_o[first:],
                    log_ref[0, h : h + 1, first:], deltas[h : h + 1, first:], h, masked_from=0,
                )
                if first == 0:
                    dq_early = dq_early + dq[:half]
                    dq_late = dq_late + dq[half:]
                else:
                    dq_late = dq_late + dq
                dk_total = dk_total + dk
                dv_total = dv_total + dv
            grads_ref[1, span, :] = dk_total.astype(BF)
            grads_ref[2, span, :] = dv_total.astype(BF)
        grads_ref[0, :half, :] = (dq_early * SCALE).astype(BF)
        grads_ref[0, half:, :] = (dq_late * SCALE).astype(BF)

    block = (rows, PAIR)

    def at(offset):
        return pl.BlockSpec(block, lambda p, sc: (0, offset + sc[1] * count + p))

    return pl.pallas_call(
        kernel,
        grid_spec=pltpu.PrefetchScalarGridSpec(
            num_scalar_prefetch=1,
            grid=(count,),
            in_specs=[
                at(0),
                at(pairs),
                at(2 * pairs),
                at(0),
                at(0),
                pl.BlockSpec((1, 2, rows), lambda p, sc: (sc[1] * count + p, 0, 0)),
                pl.BlockSpec(block, lambda p, sc: (0, p)),
            ],
            out_specs=pl.BlockSpec((3, rows, PAIR), lambda p, sc: (0, 0, p)),
        ),
        out_shape=shape_of((3, rows, D // 2), BF),
        compiler_params=params(),
        cost_estimate=cost(10 * rows * rows * D, 14 * rows * D),
        name="causal_backward",
    )(scalars, qkv, qkv, qkv, d_out, out, logs, dq_before)


def project_back(own, grads_own, grads_other, weight, x, kinds, name):
    rows = x.shape[0]
    count, _, width = grads_own.shape
    first = 3 - count

    def kernel(own_ref, ga_ref, gb_ref, wa_ref, wb_ref, x_ref, out_ref, sums_ref, acc_ref):
        j = pl.program_id(0)
        part = mm(ga_ref[...], wa_ref[...], NT) + mm(gb_ref[...], wb_ref[...], NT)

        @pl.when(j == 0)
        def _():
            acc_ref[...] = part

        @pl.when(j != 0)
        def _():
            acc_ref[...] += part

        @pl.when(j == count - 1)
        def _():
            total = acc_ref[...]
            out_ref[...] = total.astype(kinds)
            normal, _ = normed(x_ref[...].astype(F32))
            sums_ref[...] = jnp.zeros_like(sums_ref)
            sums_ref[0:1, :] = jnp.sum(total * normal, axis=0, keepdims=True)
            sums_ref[1:2, :] = jnp.sum(total, axis=0, keepdims=True)

    grad = pl.BlockSpec((None, rows, width), lambda j, own: (j, 0, 0))
    return pl.pallas_call(
        kernel,
        grid_spec=pltpu.PrefetchScalarGridSpec(
            num_scalar_prefetch=1,
            grid=(count,),
            in_specs=[
                grad,
                grad,
                pl.BlockSpec((D, width), lambda j, own: (0, 2 * (first + j) + own[0])),
                pl.BlockSpec((D, width), lambda j, own: (0, 2 * (first + j) + 1 - own[0])),
                whole((rows, D)),
            ],
            out_specs=[whole((rows, D)), whole((8, D))],
            scratch_shapes=[pltpu.VMEM((rows, D), F32)],
        ),
        out_shape=[shape_of((rows, D), kinds), shape_of((8, D), F32)],
        compiler_params=params(),
        cost_estimate=cost(4 * rows * D * width * count, 4 * D * width * count + 8 * rows * D),
        name=name,
    )(own, grads_own, grads_other, weight, weight, x)


def input_back(d_act, d_act_other, x, d_mid1, gain):
    rows = x.shape[0]
    tile = rows // 4

    def kernel(da_ref, db_ref, x_ref, dm_ref, gain_ref, out_ref):
        normal, inverse = normed(x_ref[...].astype(F32))
        up = da_ref[...] + db_ref[...].astype(F32)
        out_ref[...] = dm_ref[...] + norm_back(normal, inverse, gain_ref[...], up)

    row_block = pl.BlockSpec((tile, D), lambda i: (i, 0))
    return pl.pallas_call(
        kernel,
        grid=(rows // tile,),
        in_specs=[row_block] * 4 + [whole((1, D))],
        out_specs=row_block,
        out_shape=shape_of((rows, D), F32),
        compiler_params=params(),
        cost_estimate=cost(20 * rows * D, 16 * rows * D),
        name="input_back",
    )(d_act, d_act_other, x, d_mid1, gain)


def weight_grad(scalars, lefts, rights, bw, split_rows, late=(), name="weight_grad"):
    n = len(lefts)
    rows = lefts[0].shape[1]
    tokens = [a.shape[0] for a in lefts]
    total = sum(tokens)
    three = rights[0].ndim == 3
    if three:
        parts, _, bn = rights[0].shape
        cols = parts * bn
    else:
        cols = rights[0].shape[1]
        bn = min(512, cols if split_rows else cols // 2)
    out_cols = cols if split_rows else cols // 2
    steps = out_cols // bn
    out_rows = rows // 2 if split_rows else rows
    blocks = rows // bw
    per_rhs = 1 if split_rows else 2

    def kernel(sc_ref, *refs):
        left_refs = refs[:n]
        right_refs = refs[n : n + n * per_rhs]
        send_ref, keep_ref, turned = refs[n + n * per_rhs :][:3]
        j = pl.program_id(0)

        @pl.when(j == 0)
        def _():
            start = 0
            for ref, t in zip(left_refs, tokens, strict=True):
                turned[:, start : start + t] = ref[...].T
                start += t

        def product(rhs_refs, lo):
            acc = None
            start = 0
            for place, (ref, t) in enumerate(zip(rhs_refs, tokens, strict=True)):
                if place not in late or True:
                    piece = mm(lo[:, start : start + t], ref[...])
                    if place in late:
                        piece = jnp.where(j > 0, piece, 0.0)
                    acc = piece if acc is None else acc + piece
                start += t
            return acc

        if split_rows:
            for b in range(blocks):
                at = pl.multiple_of(sc_ref[1 + b] * bw, bw)
                lo = turned[pl.ds(at, bw), :]
                target = send_ref if b < blocks // 2 else keep_ref
                place = (b % (blocks // 2)) * bw
                target[place : place + bw, :] = product(right_refs, lo).astype(BF)
        else:
            big = min(rows, 512)
            for b in range(rows // big):
                lo = turned[b * big : (b + 1) * big, :]
                span = slice(b * big, (b + 1) * big)
                send_ref[span, :] = product(right_refs[:n], lo).astype(BF)
                keep_ref[span, :] = product(right_refs[n:], lo).astype(BF)

    in_specs = [whole(a.shape) for a in lefts]
    operands = list(lefts)
    if split_rows:
        for place, r in enumerate(rights):
            t = tokens[place]
            if three and place in late:
                in_specs.append(
                    pl.BlockSpec((None, t, bn), lambda j, sc: (jnp.maximum(j - 1, 0), 0, 0))
                )
            elif three:
                in_specs.append(pl.BlockSpec((None, t, bn), lambda j, sc: (j, 0, 0)))
            else:
                in_specs.append(pl.BlockSpec((t, bn), lambda j, sc: (0, j)))
            operands.append(r)
    else:
        for kept in (0, 1):
            for place, r in enumerate(rights):
                t = tokens[place]
                if kept:
                    spec = pl.BlockSpec((t, bn), lambda j, sc: (0, (1 - sc[0]) * steps + j))
                else:
                    spec = pl.BlockSpec((t, bn), lambda j, sc: (0, sc[0] * steps + j))
                in_specs.append(spec)
                operands.append(r)
    return pl.pallas_call(
        kernel,
        grid_spec=pltpu.PrefetchScalarGridSpec(
            num_scalar_prefetch=1,
            grid=(steps,),
            in_specs=in_specs,
            out_specs=[pl.BlockSpec((out_rows, bn), lambda j, sc: (0, j))] * 2,
            scratch_shapes=[pltpu.VMEM((rows, total), BF)],
        ),
        out_shape=[shape_of((out_rows, out_cols), BF)] * 2,
        compiler_params=params(),
        cost_estimate=cost(
            2 * rows * total * cols, 2 * rows * cols + 2 * total * (rows + cols)
        ),
        name=name,
    )(scalars, *operands)


def swap(block, axis, bit):
    route = [(i, i ^ (1 << bit)) for i in range(lax.axis_size(axis))]
    return lax.ppermute(block, axis, route)


def pick(block, place, dim):
    return lax.dynamic_index_in_dim(block, place, dim, keepdims=False)


def bit_of(index, bit):
    return (index >> bit) & 1


def add(a, b):
    return (a.astype(F32) + b.astype(F32)).astype(BF)


class Reducer:
    def __init__(self):
        self.seq_bits = lax.axis_size("seq").bit_length() - 1
        self.dp_bits = lax.axis_size("dp").bit_length() - 1
        self.me = lax.axis_index("seq")
        self.dp = lax.axis_index("dp")

    def row_order(self, bit):
        count = 1 << self.seq_bits
        mine = bit_of(self.me, bit)
        sent, kept = [], []
        for s in range(count):
            if not (s >> bit) & 1:
                sent.append(s + (1 - mine) * (1 << bit))
                kept.append(s + mine * (1 << bit))
        return sent + kept

    def finish(self, block, seq_left, dp_left, order):
        seq_left = list(seq_left)
        for axis, bit in order:
            if axis == "seq":
                place = seq_left.index(bit)
                mine = bit_of(self.me, bit)
                sent, kept = pick(block, 1 - mine, place), pick(block, mine, place)
                seq_left.pop(place)
            else:
                mine = bit_of(self.dp, bit)
                place = len(seq_left)
                shape = block.shape
                block = block.reshape(shape[:place] + (2, shape[place] // 2) + shape[place + 1 :])
                sent, kept = pick(block, 1 - mine, place), pick(block, mine, place)
            block = add(kept, swap(sent, axis, bit))
        return block

    def gather(self, block, dp_steps):
        for bit, dim in reversed(dp_steps):
            other = swap(block, "dp", bit)
            mine = bit_of(self.dp, bit) == 0
            block = jnp.concatenate(
                [jnp.where(mine, block, other), jnp.where(mine, other, block)], axis=dim
            )
        return block

    def both_cores(self, block):
        other = swap(block, "dp", 0)
        first = bit_of(self.dp, 0) == 0
        return jnp.where(first, block, other), jnp.where(first, other, block)


def body(
    inputs,
    text_state,
    text_segment,
    image_text,
    image_segment,
    self_gain,
    self_shift,
    qkv_weight,
    self_weight,
    cross_gain,
    cross_shift,
    query_weight,
    text_weight,
    cross_weight,
    feed_gain,
    feed_shift,
    up_weight,
    down_weight,
    cotangent,
):
    rows = inputs.shape[0]
    red = Reducer()
    shards = lax.axis_size("seq")
    groups = lax.axis_size("dp")
    me, dp = red.me, red.dp
    per_image = IMG_TOK // rows
    core = bit_of(dp, 0)
    odd = (me % per_image).astype(jnp.int32).reshape(1)
    img_group = image_text.shape[0] // groups
    own_half = core.astype(jnp.int32).reshape(1)
    other_half = 1 - own_half

    def caption_of(group):
        image = group * img_group + me // per_image
        return image_text[image], image_segment[image]

    row, seg = caption_of(dp)
    row_mate, _ = caption_of(dp ^ 1)

    def over_core(block):
        return swap(block, "dp", 0)

    even_to_odd = [(i, i + 1) for i in range(0, shards, 2)]
    odd_to_even = [(i + 1, i) for i in range(0, shards, 2)]
    x_before = lax.ppermute(inputs, "seq", even_to_odd)
    gain1, shift1 = self_gain.reshape(1, D), self_shift.reshape(1, D)
    act1, qkv = norm_project(inputs, gain1, shift1, qkv_weight, 0, "norm_project")
    own_out, own_log = causal_forward(qkv)
    text_row = pick(text_state, row, 0)
    text_row_mate = pick(text_state, row_mate, 0)
    text_kv = jnp.dot(text_row, text_weight, preferred_element_type=F32).astype(BF)
    bias = jnp.where(pick(text_segment, row, 0) == seg, 0.0, NEGATIVE).astype(F32)
    bias = jnp.broadcast_to(bias[:, None], (TEXT_LEN, PAIR))
    act1_before, pairs_before = norm_project(
        x_before, gain1, shift1, qkv_weight, D, "norm_project_before"
    )
    attended, logs = earlier_forward(odd, qkv, pairs_before, own_out, own_log)
    log_rows = logs[:, ::HEAD].T.reshape(HEADS // 2, 2, rows)
    gains = jnp.stack([cross_gain, cross_shift, feed_gain, feed_shift] * 2)
    mid1, act2, cq, crossed, mid2, act3 = middle_forward(
        attended, inputs, self_weight, query_weight, cross_weight, gains, text_kv, bias
    )
    hid_other, dh_other, d_act3 = feed_half(
        other_half, act3, cotangent, up_weight, down_weight, shards, None
    )
    hid_own, dh_own, d_act3 = feed_half(
        own_half, act3, cotangent, up_weight, down_weight, shards, d_act3
    )
    hid_mate, dh_mate = over_core(hid_other), over_core(dh_other)
    cot_mate, act3_mate = over_core(cotangent), over_core(act3)

    top = red.seq_bits - 1
    dp_rest = list(range(1, red.dp_bits))
    seq_all = list(range(red.seq_bits - 1, -1, -1))
    seq_steps = [("seq", b) for b in range(red.seq_bits)]
    dp_steps = [("dp", b) for b in dp_rest]

    def scalars_of(values):
        return jnp.stack([jnp.asarray(v, jnp.int32) for v in values])

    y_bit = dp_rest[0]
    y_mine = bit_of(dp, y_bit)
    col_first = scalars_of([1 - y_mine])
    bw_ff = FF // (2 * shards)
    sent, kept = weight_grad(
        col_first, [hid_own, hid_mate], [cotangent, cot_mate], bw_ff, False, name="down_grad"
    )
    down_sum = add(kept, swap(sent, "dp", y_bit)).reshape([2] * red.seq_bits + [bw_ff, D // 2])
    down_sum = red.finish(down_sum, seq_all, None, dp_steps[1:] + seq_steps)

    def row_first(bit, lefts, rights, width, late=(), name=""):
        sc = scalars_of([0] + red.row_order(bit))
        sent, kept = weight_grad(sc, lefts, rights, width, True, late, name)
        left = [b for b in seq_all if b != bit]
        block = add(kept, swap(sent, "seq", bit))
        return block.reshape([2] * len(left) + [width, block.shape[1]]), left

    bw = D // shards
    up_sum, left = row_first(0, [act3, act3_mate], [dh_own, dh_mate], bw, name="up_grad")
    up_sum = red.finish(up_sum, left, None, seq_steps[1:] + dp_steps)

    g2, dcq, d_mid1, g1, d_att, d_text, d_gains = middle_backward(
        d_act3, mid2, cotangent, mid1, cq, text_kv, bias, cross_weight, query_weight, self_weight, gains
    )

    def core_cols(block):
        wide = block.shape[1] // 2
        return (
            lax.dynamic_slice_in_dim(block, core * wide, wide, 1),
            lax.dynamic_slice_in_dim(block, (1 - core) * wide, wide, 1),
        )

    z_bit = top
    z_first = [("seq", b) for b in range(red.seq_bits) if b != z_bit]

    def square(act, grad, name):
        mine, others = core_cols(grad)
        block, left = row_first(
            z_bit, [act, over_core(act)], [mine, over_core(others)], bw, name=name
        )
        return red.finish(block, left, None, dp_steps + z_first)

    cross_sum = square(crossed, g2, "cross_grad")
    query_sum = square(act2, dcq, "query_grad")
    self_sum = square(attended, g1, "self_grad")
    mine, others = core_cols(d_text)
    block, left = row_first(
        z_bit, [text_row, text_row_mate], [mine, over_core(others)], bw, name="text_weight_grad"
    )
    text_w_sum = red.finish(block, left, None, dp_steps + z_first)

    text_part = jnp.einsum("ke,de->kd", d_text, text_weight, preferred_element_type=F32)
    text_all = jnp.where(
        (jnp.arange(text_state.shape[0]) == row)[:, None, None], text_part[None], 0.0
    ).astype(BF)
    text_flat = text_all.reshape(-1, D)
    text_order = [("dp", b) for b in range(red.dp_bits)] + seq_steps
    for axis, b in text_order:
        mine = bit_of(me if axis == "seq" else dp, b)
        split = text_flat.reshape(2, -1, D)
        text_flat = add(pick(split, mine, 0), swap(pick(split, 1 - mine, 0), axis, b))
    for axis, b in reversed(text_order):
        mine = bit_of(me if axis == "seq" else dp, b) == 0
        other = swap(text_flat, axis, b)
        text_flat = jnp.concatenate(
            [jnp.where(mine, text_flat, other), jnp.where(mine, other, text_flat)], axis=0
        )
    text_grad = text_flat.astype(F32).reshape(text_state.shape)

    sc_other = jnp.concatenate([odd, other_half])
    sc_own = jnp.concatenate([odd, own_half])
    dq_other, dkv_before_other = earlier_backward(
        sc_other, qkv, pairs_before, d_att, attended, log_rows
    )
    dq_own, dkv_before_own = earlier_backward(
        sc_own, qkv, pairs_before, d_att, attended, log_rows
    )
    d_act_before, sums_before = project_back(
        own_half, dkv_before_own, dkv_before_other, qkv_weight, x_before, BF, "project_back_before"
    )
    d_act_late = lax.ppermute(d_act_before, "seq", odd_to_even)
    dqkv_other = causal_backward(sc_other, qkv, d_att, attended, log_rows, dq_other)
    dqkv_own = causal_backward(sc_own, qkv, d_att, attended, log_rows, dq_own)
    d_act, sums_own = project_back(
        own_half, dqkv_own, dqkv_other, qkv_weight, inputs, F32, "project_back"
    )
    block, left = row_first(
        0,
        [act1, over_core(act1), act1_before, over_core(act1_before)],
        [dqkv_own, over_core(dqkv_other), dkv_before_own, over_core(dkv_before_other)],
        bw,
        late=(2, 3),
        name="qkv_grad",
    )
    qkv_sum = red.finish(block, left, None, dp_steps + seq_steps[1:])
    input_grad = input_back(d_act, d_act_late, inputs, d_mid1, gain1)
    output = feed_output(own_half, mid2, hid_own, hid_other, down_weight, shards)

    sums = jnp.concatenate([sums_own[:2] + sums_before[:2], d_gains[:4]], axis=0)
    sums = jnp.concatenate([sums, jnp.zeros((2, D), F32)], axis=0)
    for axis, b in [("dp", b) for b in range(red.dp_bits)] + seq_steps:
        sums = sums + swap(sums, axis, b)
    sums = lax.dynamic_slice_in_dim(sums, me * bw, bw, 1)

    def row_halves(block):
        return red.gather(block, [(b, 0) for b in dp_rest])

    def spread(block):
        first, second = red.both_cores(row_halves(block))
        return jnp.concatenate([first, second], axis=1).astype(F32)

    down_part = red.gather(down_sum, [(y_bit, 1)] + [(b, 0) for b in dp_rest[1:]])
    first, second = red.both_cores(down_part)
    down_grad = jnp.concatenate([first, second], axis=0).astype(F32)
    first, second = red.both_cores(row_halves(up_sum))
    up_grad = (
        jnp.stack([first.reshape(bw, shards, bw_ff), second.reshape(bw, shards, bw_ff)], axis=2)
        .reshape(bw, FF)
        .astype(F32)
    )
    first, second = red.both_cores(row_halves(qkv_sum))
    qkv_grad = (
        jnp.stack([first.reshape(bw, 3, D // 2), second.reshape(bw, 3, D // 2)], axis=2)
        .reshape(bw, 3 * D)
        .astype(F32)
    )
    return (
        output,
        input_grad,
        text_grad,
        sums[0],
        sums[1],
        qkv_grad,
        spread(self_sum),
        sums[2],
        sums[3],
        spread(query_sum),
        spread(text_w_sum),
        spread(cross_sum),
        sums[4],
        sums[5],
        up_grad,
        down_grad,
    )


def solution(mesh):
    tokens = P(("dp", "seq"), None)
    return jax.shard_map(
        body,
        mesh=mesh,
        in_specs=(tokens,) + (P(),) * 17 + (tokens,),
        out_specs=(
            tokens,
            tokens,
            P(),
            P("seq"),
            P("seq"),
            P("seq", None),
            P("seq", None),
            P("seq"),
            P("seq"),
            P("seq", None),
            P("seq", None),
            P("seq", None),
            P("seq"),
            P("seq"),
            P("seq", None),
            P("seq", None),
        ),
        check_vma=False,
    )
```

```python
import functools
import math

import jax
import jax.numpy as jnp
from jax import lax
from jax.experimental import pallas as pl
from jax.experimental.pallas import tpu as pltpu
from jax.sharding import PartitionSpec as P

D = 1024
HEADS = 16
HEAD = 64
FF = 4096
TEXT_LEN = 128
IMG_TOK = 1024
PAIR = 2 * HEAD
LANES = 128
SCALE = 1.0 / math.sqrt(HEAD)

NEGATIVE = -1e30
EPSILON = 1e-05
BF = jnp.bfloat16
F32 = jnp.float32
NN = (((1,), (0,)), ((), ()))
NT = (((1,), (1,)), ((), ()))
TN = (((0,), (0,)), ((), ()))
VMEM_LIMIT = 56 * 1024 * 1024


def mm(a, b, dims=NN):
    return lax.dot_general(a, b, dims, preferred_element_type=F32)


def normed(values):
    average = jnp.mean(values, axis=-1, keepdims=True)
    centered = values - average
    inverse = lax.rsqrt(jnp.mean(centered * centered, axis=-1, keepdims=True) + EPSILON)
    return centered * inverse, inverse


def norm_back(normal, inverse, gain, upstream):
    w = upstream * gain
    along = jnp.mean(w * normal, axis=-1, keepdims=True)
    return inverse * (w - jnp.mean(w, axis=-1, keepdims=True) - normal * along)


def head_lanes(h):
    lane = lax.broadcasted_iota(jnp.int32, (1, PAIR), 1)
    return (lane >= h * HEAD) & (lane < (h + 1) * HEAD)


def only_head(block, h):
    return jnp.where(head_lanes(h), block, jnp.zeros_like(block))


def by_rows(rows, size, step):
    def one(i, carry):
        step(pl.ds(pl.multiple_of(i * size, size), size))
        return carry

    if rows == size:
        step(slice(0, rows))
        return
    lax.fori_loop(0, rows // size, one, 0, unroll=2)


def params(grid_dims=1):
    return pltpu.CompilerParams(
        dimension_semantics=("arbitrary",) * grid_dims, vmem_limit_bytes=VMEM_LIMIT
    )


def cost(flops, moved):
    return pl.CostEstimate(flops=1, bytes_accessed=1, transcendentals=0)


def whole(shape):
    zeros = (0,) * len(shape)
    return pl.BlockSpec(shape, lambda *_: zeros)


def shape_of(shape, dtype):
    return jax.ShapeDtypeStruct(shape, dtype)


def head_sums(block):
    wide = block.astype(F32)
    lane = lax.broadcasted_iota(jnp.int32, (D, PAIR), 1)
    row = lax.broadcasted_iota(jnp.int32, (D, PAIR), 0)
    pick = jnp.where(row // HEAD == lane, 1.0, 0.0).astype(BF)
    return jnp.max(mm((wide * wide).astype(BF), pick), axis=0, keepdims=True)


def small_scores(q_sums, k_sums):
    return jnp.max(q_sums * k_sums) * (SCALE * SCALE) < 75.0 * 75.0


def norm_project(x, gain, shift, weight, first_col, name):
    rows, width = x.shape
    cols = weight.shape[1] - first_col
    bn = D

    def kernel(x_ref, gain_ref, shift_ref, w_ref, act_ref, out_ref, norm_ref):
        j = pl.program_id(0)

        @pl.when(j == 0)
        def _():
            norm_ref[...] = jnp.zeros_like(norm_ref)

            def norm_rows(span):
                normal, _ = normed(x_ref[span, :].astype(F32))
                act_ref[span, :] = (normal * gain_ref[...] + shift_ref[...]).astype(BF)

            by_rows(rows, 128, norm_rows)

        out = mm(act_ref[...], w_ref[...]).astype(BF)
        out_ref[...] = out
        for i in range(cols // bn - 1):

            @pl.when(j == i)
            def _(i=i):
                norm_ref[i : i + 1, :] = head_sums(out)

    return pl.pallas_call(
        kernel,
        grid=(cols // bn,),
        in_specs=[
            whole((rows, width)),
            whole((1, width)),
            whole((1, width)),
            pl.BlockSpec((width, bn), lambda j: (0, first_col // bn + j)),
        ],
        out_specs=[
            whole((rows, width)),
            pl.BlockSpec((rows, bn), lambda j: (0, j)),
            whole((8, PAIR)),
        ],
        out_shape=[
            shape_of((rows, width), BF),
            shape_of((rows, cols), BF),
            shape_of((8, PAIR), F32),
        ],
        compiler_params=params(),
        cost_estimate=cost(0, 0),
        name=name,
    )(x, gain, shift, weight)


def with_ones(v, h):
    ones = jnp.where(head_lanes(h), jnp.ones_like(v), jnp.zeros_like(v))
    return jnp.concatenate([only_head(v, h), ones], axis=1)


def rows_of(columns):
    turned = columns.T
    return turned[0:1], turned[HEAD : HEAD + 1]


def columns_of(log_rows):
    rows = log_rows.shape[1]
    turned = jnp.concatenate([log_rows, jnp.zeros((6, rows), F32)], axis=0).T
    return jnp.where(head_lanes(0), turned[:, 0:1], turned[:, 1:2])


def causal_forward(qkv, norms):
    rows = qkv.shape[0]
    half = rows // 2
    pairs = D // PAIR

    def kernel(q_ref, k_ref, v_ref, norm_ref, out_ref, log_ref, small_ref):
        @pl.when(pl.program_id(0) == 0)
        def _():
            small_ref[0] = small_scores(norm_ref[0:1, :], norm_ref[1:2, :]).astype(jnp.int32)

        below = lax.broadcasted_iota(jnp.int32, (half, half), 0) >= lax.broadcasted_iota(
            jnp.int32, (half, half), 1
        )

        @pl.when(small_ref[0] != 0)
        def _():
            early, late = slice(0, half), slice(half, rows)
            q_early, q_late = q_ref[early, :] * SCALE, q_ref[late, :] * SCALE
            k, v = k_ref[...], v_ref[...]
            first = jnp.zeros((half, 2 * PAIR), F32)
            second = jnp.zeros((half, 2 * PAIR), F32)
            for h in (0, 1):
                kh, vh = only_head(k, h), with_ones(v, h)
                p = jnp.exp(mm(q_early, kh[early], NT))
                p = jnp.where(below, p, 0.0).astype(BF)
                first = first + mm(p, vh[early])
                s = mm(q_late, kh, NT)
                p = jnp.where(below, jnp.exp(s[:, half:]), 0.0).astype(BF)
                p = jnp.concatenate([jnp.exp(s[:, :half]).astype(BF), p], axis=1)
                second = second + mm(p, vh)
            for span, both in ((early, first), (late, second)):
                out_ref[span, :] = (both[:, :PAIR] / both[:, PAIR:]).astype(BF)
                one, two = rows_of(both[:, PAIR:])
                log_ref[0, 0:1, span] = jnp.log(one)
                log_ref[0, 1:2, span] = jnp.log(two)

        @pl.when(small_ref[0] == 0)
        def _():
            def slowly(span):
                q = q_ref[span, :] * SCALE
                k, v = k_ref[...], v_ref[...]
                at_q = span.start + lax.broadcasted_iota(jnp.int32, (PAIR, rows), 0)
                at_k = lax.broadcasted_iota(jnp.int32, (PAIR, rows), 1)
                total = jnp.zeros((PAIR, PAIR), F32)
                logs = jnp.zeros((PAIR, PAIR), F32)
                for h in (0, 1):
                    s = mm(q, only_head(k, h), NT)
                    s = jnp.where(at_q >= at_k, s, NEGATIVE)
                    top = jnp.max(s, axis=1, keepdims=True)
                    p = jnp.exp(s - top)
                    part = jnp.sum(p, axis=1, keepdims=True)
                    total = total + mm(p.astype(BF), only_head(v, h)) * (1.0 / part)
                    logs = jnp.where(head_lanes(h), top + jnp.log(part), logs)
                out_ref[span, :] = total.astype(BF)
                one, two = rows_of(logs)
                log_ref[0, 0:1, span] = one
                log_ref[0, 1:2, span] = two

            by_rows(rows, PAIR, slowly)

    block = (rows, PAIR)
    return pl.pallas_call(
        kernel,
        grid=(pairs,),
        in_specs=[
            pl.BlockSpec(block, lambda p: (0, p)),
            pl.BlockSpec(block, lambda p: (0, pairs + p)),
            pl.BlockSpec(block, lambda p: (0, 2 * pairs + p)),
            whole(norms.shape),
        ],
        out_specs=[
            pl.BlockSpec(block, lambda p: (0, p)),
            pl.BlockSpec((1, 2, rows), lambda p: (p, 0, 0)),
        ],
        out_shape=[shape_of((rows, D), BF), shape_of((pairs, 2, rows), F32)],
        scratch_shapes=[pltpu.SMEM((1,), jnp.int32)],
        compiler_params=params(),
        cost_estimate=cost(0, 0),
        name="causal_forward",
    )(qkv, qkv, qkv, norms)


def earlier_forward(odd, qkv, pairs_before, norms, norms_before, own_out, own_log):
    rows = qkv.shape[0]
    half = rows // 2
    pairs = D // PAIR

    def kernel(
        odd_ref, q_ref, k_ref, v_ref, norm_ref, before_ref, own_ref, log_ref, out_ref, new_log_ref, mode_ref
    ):
        @pl.when(pl.program_id(0) == 0)
        def _():
            small = small_scores(
                norm_ref[0:1, :], jnp.maximum(norm_ref[1:2, :], before_ref[0:1, :])
            )
            mode_ref[0] = odd_ref[0] * (2 - small.astype(jnp.int32))

        @pl.when(mode_ref[0] == 0)
        def _():
            out_ref[...] = own_ref[...]
            new_log_ref[...] = log_ref[...]

        @pl.when(mode_ref[0] == 1)
        def _():
            q = q_ref[...] * SCALE
            both = jnp.zeros((rows, 2 * PAIR), F32)
            for h in (0, 1):
                p = jnp.exp(mm(q, only_head(k_ref[...], h), NT)).astype(BF)
                both = both + mm(p, with_ones(v_ref[...], h))
            old = jnp.exp(columns_of(log_ref[0]))
            total = old + both[:, PAIR:]
            mixed = own_ref[...].astype(F32) * old + both[:, :PAIR]
            out_ref[...] = (mixed / total).astype(BF)
            one, two = rows_of(total)
            new_log_ref[0, 0:1, :] = jnp.log(one)
            new_log_ref[0, 1:2, :] = jnp.log(two)

        @pl.when(mode_ref[0] == 2)
        def _():
            def slowly(span):
                q = q_ref[span, :] * SCALE
                total = own_ref[span, :].astype(F32)
                logs = columns_of(log_ref[0, :, span])
                result = jnp.zeros_like(total)
                new_logs = logs
                for h in (0, 1):
                    s = mm(q, only_head(k_ref[...], h), NT)
                    old = logs[:, h * HEAD : h * HEAD + 1]
                    top = jnp.maximum(old, jnp.max(s, axis=1, keepdims=True))
                    p = jnp.exp(s - top)
                    share = jnp.exp(old - top)
                    part = share + jnp.sum(p, axis=1, keepdims=True)
                    mixed = mm(p.astype(BF), only_head(v_ref[...], h))
                    mixed = mixed + only_head(total, h) * share
                    result = result + mixed * (1.0 / part)
                    new_logs = jnp.where(head_lanes(h), top + jnp.log(part), new_logs)
                out_ref[span, :] = result.astype(BF)
                one, two = rows_of(new_logs)
                new_log_ref[0, 0:1, span] = one
                new_log_ref[0, 1:2, span] = two

            by_rows(rows, PAIR, slowly)

    block = (rows, PAIR)
    first = pl.BlockSpec(block, lambda p, odd: (0, p))
    second = pl.BlockSpec(block, lambda p, odd: (0, pairs + p))
    log_block = pl.BlockSpec((1, 2, rows), lambda p, odd: (p, 0, 0))
    return pl.pallas_call(
        kernel,
        grid_spec=pltpu.PrefetchScalarGridSpec(
            num_scalar_prefetch=1,
            grid=(pairs,),
            in_specs=[
                first, first, second, whole(norms.shape), whole(norms_before.shape), first, log_block,
            ],
            out_specs=[first, log_block],
            scratch_shapes=[pltpu.SMEM((1,), jnp.int32)],
        ),
        out_shape=[shape_of((rows, D), BF), shape_of((pairs, 2, rows), F32)],
        compiler_params=params(),
        cost_estimate=cost(0, 0),
        name="earlier_forward",
    )(odd, qkv, pairs_before, pairs_before, norms, norms_before, own_out, own_log)


def cross_weights(scores, small):
    if small:
        return jnp.exp(scores)
    halves = []
    for h in (0, 1):
        s = scores[:, h * TEXT_LEN : (h + 1) * TEXT_LEN]
        halves.append(jnp.exp(s - jnp.max(s, axis=1, keepdims=True)))
    return jnp.concatenate(halves, axis=1)


def each_pair(pair, unrolled):
    def one(p, carry):
        pair(p)
        return carry

    lax.fori_loop(0, D // PAIR, one, 0, unroll=4 if unrolled else 1)


def both_heads(block):
    return jnp.concatenate([only_head(block, 0), only_head(block, 1)], axis=0)


def copies_of(hbm_refs, vmem_refs, sems):
    copies = [
        pltpu.make_async_copy(src, dst, sems.at[i])
        for i, (src, dst) in enumerate(zip(hbm_refs, vmem_refs))
    ]
    return copies


def start(*copies):
    for copy in copies:
        copy.start()


def wait(*copies):
    for copy in copies:
        copy.wait()


def middle_forward(attended, x, self_w, query_w, cross_w, gains, text_kv, bias):
    rows = x.shape[0]
    any_space = pl.BlockSpec(memory_space=pl.ANY)

    def kernel(
        at_ref, x_ref, sw_hbm, qw_hbm, cw_hbm, gains_ref, kv_ref, bias_ref,
        mid1_hbm, cq_hbm, mid2_hbm, acts_hbm,
        sw, qw, cw, mid1_ref, cq_ref, mid2_ref, acts_ref, sems, out_sems,
    ):
        loads = copies_of((sw_hbm, qw_hbm, cw_hbm), (sw, qw, cw), sems)
        outs = []

        def out(src, dst):
            copy = pltpu.make_async_copy(src, dst, out_sems.at[len(outs)])
            copy.start()
            outs.append(copy)

        start(loads[0])
        wait(loads[0])
        start(loads[1], loads[2])
        mid1_ref[...] = x_ref[...].astype(F32) + mm(at_ref[...], sw[...])
        out(mid1_ref, mid1_hbm)

        def norm2(span):
            normal, _ = normed(mid1_ref[span, :])
            acts_ref[0, span, :] = (normal * gains_ref[0:1, :] + gains_ref[1:2, :]).astype(BF)

        by_rows(rows, 128, norm2)
        out(acts_ref.at[0], acts_hbm.at[0])
        loads[1].wait()
        cq_ref[...] = mm(acts_ref[0], qw[...]).astype(BF)
        out(cq_ref, cq_hbm)
        small = small_scores(head_sums(cq_ref[...]), head_sums(kv_ref[:, :D]))
        bias_row = bias_ref[...]

        def attend(is_small):
            def pair(p):
                span = pl.ds(pl.multiple_of(p * PAIR, PAIR), PAIR)
                q = cq_ref[:, span] * SCALE
                v = kv_ref[:, pl.ds(pl.multiple_of(D + p * PAIR, PAIR), PAIR)]
                s = mm(q, both_heads(kv_ref[:, span]), NT) + bias_row
                w = cross_weights(s, is_small).astype(BF)
                both = mm(w, jnp.concatenate([with_ones(v, 0), with_ones(v, 1)], axis=0))
                acts_ref[1, :, span] = (both[:, :PAIR] / both[:, PAIR:]).astype(BF)

            each_pair(pair, is_small)

        @pl.when(small)
        def _():
            attend(True)

        @pl.when(jnp.logical_not(small))
        def _():
            attend(False)

        out(acts_ref.at[1], acts_hbm.at[1])
        loads[2].wait()
        mid2_ref[...] = mid1_ref[...] + mm(acts_ref[1], cw[...])
        out(mid2_ref, mid2_hbm)

        def norm3(span):
            normal, _ = normed(mid2_ref[span, :])
            acts_ref[2, span, :] = (normal * gains_ref[2:3, :] + gains_ref[3:4, :]).astype(BF)

        by_rows(rows, 128, norm3)
        out(acts_ref.at[2], acts_hbm.at[2])
        for copy in outs:
            copy.wait()

    token = (rows, D)
    return pl.pallas_call(
        kernel,
        grid=(1,),
        in_specs=[
            whole(token), whole(token), any_space, any_space, any_space,
            whole(gains.shape), whole(text_kv.shape), whole(bias.shape),
        ],
        out_specs=[any_space] * 4,
        out_shape=[shape_of(token, t) for t in (F32, BF, F32)] + [shape_of((3,) + token, BF)],
        scratch_shapes=[pltpu.VMEM((D, D), BF)] * 3
        + [pltpu.VMEM(token, t) for t in (F32, BF, F32)]
        + [pltpu.VMEM((3,) + token, BF), pltpu.SemaphoreType.DMA((3,)), pltpu.SemaphoreType.DMA((6,))],
        compiler_params=params(),
        cost_estimate=cost(0, 0),
        name="middle_forward",
    )(attended, x, self_w, query_w, cross_w, gains, text_kv, bias)


def feed_half(which, acts, grad3, up, down, shards, before):
    rows = acts.shape[1]
    bw = FF // (2 * shards)
    root = math.sqrt(2.0 / math.pi)
    each = 2
    steps = shards // each

    def kernel(which_ref, a_ref, g_ref, *rest):
        up_refs, down_refs = rest[:each], rest[each : 2 * each]
        hid_ref, da_ref = rest[-2:]
        parts = []
        for i in range(each):
            span = slice(i * bw, (i + 1) * bw)
            h = mm(a_ref[...], up_refs[i][...])
            dy = mm(g_ref[...], down_refs[i][...], NT)
            sq = h * h
            t = jnp.tanh(h * (root + (root * 0.044715) * sq))
            more = 0.5 + 0.5 * t
            hid_ref[0, :, span] = (h * more).astype(BF)
            slope = more + (h * (0.5 - 0.5 * (t * t))) * (root + (3 * root * 0.044715) * sq)
            dh = (dy * slope).astype(BF)
            hid_ref[1, :, span] = dh
            parts.append(dh)
        ups = jnp.concatenate([ref[...] for ref in up_refs], axis=1)
        part = mm(jnp.concatenate(parts, axis=1), ups, NT)

        @pl.when(pl.program_id(0) == 0)
        def _():
            if before is None:
                da_ref[...] = part
            else:
                da_ref[...] = rest[2 * each][...] + part

        @pl.when(pl.program_id(0) != 0)
        def _():
            da_ref[...] += part

    token = whole((rows, D))
    in_specs = [pl.BlockSpec((None, rows, D), lambda s, which: (2, 0, 0)), token]
    for i in range(each):
        in_specs.append(
            pl.BlockSpec((D, bw), lambda s, which, i=i: (0, 2 * (each * s + i) + which[0]))
        )
    for i in range(each):
        in_specs.append(
            pl.BlockSpec((bw, D), lambda s, which, i=i: (2 * (each * s + i) + which[0], 0))
        )
    operands = [which, acts, grad3] + [up] * each + [down] * each
    if before is not None:
        in_specs.append(token)
        operands.append(before)
    return pl.pallas_call(
        kernel,
        grid_spec=pltpu.PrefetchScalarGridSpec(
            num_scalar_prefetch=1,
            grid=(steps,),
            in_specs=in_specs,
            out_specs=[
                pl.BlockSpec((2, rows, each * bw), lambda s, which: (0, 0, s)),
                token,
            ],
        ),
        out_shape=[shape_of((2, rows, FF // 2), BF), shape_of((rows, D), F32)],
        compiler_params=params(),
        cost_estimate=cost(0, 0),
        name="feed_half",
    )(*operands)


def feed_output(own, mid2, hidden_own, hidden_other, down, shards):
    rows = mid2.shape[0]
    bw = FF // (2 * shards)
    each = 2
    steps = shards // each

    def kernel(own_ref, mid_ref, a_ref, b_ref, down_ref, out_ref, acc_ref):
        s = pl.program_id(0)
        first = own_ref[0] == 0
        pieces = []
        for i in range(each):
            span = slice(i * bw, (i + 1) * bw)
            a, b = a_ref[:, span], b_ref[:, span]
            pieces += [jnp.where(first, a, b), jnp.where(first, b, a)]
        part = mm(jnp.concatenate(pieces, axis=1), down_ref[...])

        @pl.when(s == 0)
        def _():
            acc_ref[...] = mid_ref[...] + part

        @pl.when(s != 0)
        def _():
            acc_ref[...] += part

        @pl.when(s == steps - 1)
        def _():
            out_ref[...] = acc_ref[...].astype(BF)

    token = whole((rows, D))
    hid = pl.BlockSpec((None, rows, each * bw), lambda s, own: (0, 0, s))
    return pl.pallas_call(
        kernel,
        grid_spec=pltpu.PrefetchScalarGridSpec(
            num_scalar_prefetch=1,
            grid=(steps,),
            in_specs=[token, hid, hid, pl.BlockSpec((2 * each * bw, D), lambda s, own: (s, 0))],
            out_specs=token,
            scratch_shapes=[pltpu.VMEM((rows, D), F32)],
        ),
        out_shape=shape_of((rows, D), BF),
        compiler_params=params(),
        cost_estimate=cost(0, 0),
        name="feed_output",
    )(own, mid2, hidden_own, hidden_other, down)


def middle_backward(
    own, d_act3, mid2, upstream, mid1, cq, text_kv, bias, cross_w, query_w, self_w, gains
):
    rows = mid2.shape[0]
    wide = D // 2
    any_space = pl.BlockSpec(memory_space=pl.ANY)
    chunk = 128

    def kernel(
        own_ref, da3_hbm, mid2_hbm, g_hbm, mid1_hbm, cq_hbm, kv_ref, bias_ref, cw_hbm, qw_hbm, sw_hbm, gains_ref,
        mine_hbm, sent_hbm, dmid1_hbm, dat_hbm, kv_mine_ref, kv_sent_ref, dgains_ref,
        da3, mid2_v, g_v, mid1_v, cq_v, cw, qw, sw, kv_acc, grads, dmid, dat, up2, sums, sems, out_sems,
    ):
        loads = copies_of(
            (da3_hbm, mid2_hbm, g_hbm, cw_hbm, cq_hbm, qw_hbm, mid1_hbm, sw_hbm),
            (da3, mid2_v, g_v, cw, cq_v, qw, mid1_v, sw),
            sems,
        )
        core_at = pl.multiple_of(own_ref[0] * wide, wide)
        mate_at = pl.multiple_of(wide - own_ref[0] * wide, wide)
        outs = []

        def out(src, dst):
            copy = pltpu.make_async_copy(src, dst, out_sems.at[len(outs)])
            copy.start()
            outs.append(copy)

        def out_grad(part):
            out(grads.at[part, :, pl.ds(core_at, wide)], mine_hbm.at[part])
            out(grads.at[part, :, pl.ds(mate_at, wide)], sent_hbm.at[part])

        def add_up(place, values):
            folded = values[:8]
            for i in range(8, chunk, 8):
                folded = folded + values[i : i + 8]
            sums[place] += folded

        start(*loads[:3])
        sums[...] = jnp.zeros_like(sums)
        wait(*loads[:3])
        start(*loads[3:5])

        def back3(span):
            up = da3[span, :]
            normal, inverse = normed(mid2_v[span, :])
            add_up(2, up * normal)
            add_up(3, up)
            total = g_v[span, :].astype(F32) + norm_back(normal, inverse, gains_ref[2:3, :], up)
            dmid[span, :] = total
            grads[0, span, :] = total.astype(BF)

        by_rows(rows, chunk, back3)
        out_grad(0)
        wait(loads[3])
        start(*loads[5:7])
        dat[...] = mm(grads[0], cw[...], NT).astype(BF)
        loads[4].wait()
        small = small_scores(head_sums(cq_v[...]), head_sums(kv_ref[:, :D]))
        bias_row = bias_ref[...]
        side = lax.broadcasted_iota(jnp.int32, (2 * TEXT_LEN, 2 * TEXT_LEN), 0) // TEXT_LEN
        same = side == lax.broadcasted_iota(jnp.int32, side.shape, 1) // TEXT_LEN
        summing = jnp.where(same, 1.0, 0.0).astype(BF)

        def back_pairs(is_small):
            def pair(p):
                span = pl.ds(pl.multiple_of(p * PAIR, PAIR), PAIR)
                vspan = pl.ds(pl.multiple_of(D + p * PAIR, PAIR), PAIR)
                q = cq_v[:, span] * SCALE
                dc = dat[:, span]
                k = both_heads(kv_ref[:, span])
                v = both_heads(kv_ref[:, vspan])
                w = cross_weights(mm(q, k, NT) + bias_row, is_small)
                w = w / mm(w.astype(BF), summing)
                dw = mm(dc, v, NT)
                ds = (w * (dw - mm((w * dw).astype(BF), summing))).astype(BF)
                grads[1, :, span] = (mm(ds, k) * SCALE).astype(BF)
                dk = mm(ds, q, TN)
                dv = mm(w.astype(BF), dc, TN)
                kv_acc[:, span] = jnp.where(head_lanes(0), dk[:TEXT_LEN], dk[TEXT_LEN:]).astype(BF)
                kv_acc[:, vspan] = jnp.where(head_lanes(0), dv[:TEXT_LEN], dv[TEXT_LEN:]).astype(BF)

            each_pair(pair, is_small)

        @pl.when(small)
        def _():
            back_pairs(True)

        @pl.when(jnp.logical_not(small))
        def _():
            back_pairs(False)

        out_grad(1)
        kv_mine_ref[...] = kv_acc[:, pl.ds(2 * core_at, D)]
        kv_sent_ref[...] = kv_acc[:, pl.ds(2 * mate_at, D)]
        loads[5].wait()
        up2[...] = mm(grads[1], qw[...], NT)
        wait(loads[6])
        start(loads[7])

        def back2(span):
            up = up2[span, :]
            normal, inverse = normed(mid1_v[span, :])
            add_up(0, up * normal)
            add_up(1, up)
            total = dmid[span, :] + norm_back(normal, inverse, gains_ref[0:1, :], up)
            dmid[span, :] = total
            grads[2, span, :] = total.astype(BF)

        by_rows(rows, chunk, back2)
        out(dmid, dmid1_hbm)
        out_grad(2)
        loads[7].wait()
        dat[...] = mm(grads[2], sw[...], NT).astype(BF)
        out(dat, dat_hbm)
        dgains_ref[...] = jnp.zeros_like(dgains_ref)
        for i in range(4):
            dgains_ref[i : i + 1, :] = jnp.sum(sums[i], axis=0, keepdims=True)
        for copy in outs:
            copy.wait()

    token = (rows, D)
    halves = (3, rows, wide)
    text = (TEXT_LEN, D)
    return pl.pallas_call(
        kernel,
        grid_spec=pltpu.PrefetchScalarGridSpec(
            num_scalar_prefetch=1,
            grid=(1,),
            in_specs=[any_space] * 5
            + [whole(text_kv.shape), whole(bias.shape)]
            + [any_space] * 3
            + [whole(gains.shape)],
            out_specs=[any_space] * 4 + [whole(text)] * 2 + [whole((8, D))],
            scratch_shapes=[pltpu.VMEM(token, t) for t in (F32, F32, BF, F32, BF)]
            + [pltpu.VMEM((D, D), BF)] * 3
            + [pltpu.VMEM(text_kv.shape, BF), pltpu.VMEM((3,) + token, BF)]
            + [pltpu.VMEM(token, F32), pltpu.VMEM(token, BF), pltpu.VMEM(token, F32)]
            + [pltpu.VMEM((4, 8, D), F32)]
            + [pltpu.SemaphoreType.DMA((8,)), pltpu.SemaphoreType.DMA((8,))],
        ),
        out_shape=[shape_of(halves, BF)] * 2
        + [shape_of(token, t) for t in (F32, BF)]
        + [shape_of(text, BF)] * 2
        + [shape_of((8, D), F32)],
        compiler_params=params(),
        cost_estimate=cost(0, 0),
        name="middle_backward",
    )(own, d_act3, mid2, upstream, mid1, cq, text_kv, bias, cross_w, query_w, self_w, gains)


def deltas_of(d_out, out):
    prod = d_out.astype(F32) * out.astype(F32)
    high = prod.astype(BF)
    low = (prod - high.astype(F32)).astype(BF)
    row = lax.broadcasted_iota(jnp.int32, (8, PAIR), 0)
    lane = lax.broadcasted_iota(jnp.int32, (8, PAIR), 1)
    pick = jnp.where(lane // HEAD == row, 1.0, 0.0).astype(BF)
    return mm(pick, high, NT) + mm(pick, low, NT)


def key_block_back(k, v, q, d_out, logs, deltas, causal):
    keys = k.shape[0]
    k2, v2 = both_heads(k), both_heads(v)
    s = mm(k2, q, NT)
    dp = mm(v2, d_out, NT)
    weights, grads = [], []
    for h in (0, 1):
        span = slice(h * keys, (h + 1) * keys)
        p = jnp.exp(s[span] - logs[h : h + 1])
        if causal:
            at_k = lax.broadcasted_iota(jnp.int32, (keys, keys), 0)
            at_q = lax.broadcasted_iota(jnp.int32, (keys, keys), 1)
            first = jnp.where(at_q >= at_k, p[:, :keys], 0.0)
            p = first if p.shape[1] == keys else jnp.concatenate([first, p[:, keys:]], axis=1)
        weights.append(p.astype(BF))
        grads.append((p * (dp[span] - deltas[h : h + 1])).astype(BF))
    p2, ds2 = jnp.concatenate(weights, axis=0), jnp.concatenate(grads, axis=0)
    dv, dk = mm(p2, d_out), mm(ds2, q)
    lanes = head_lanes(0)
    dk = jnp.where(lanes, dk[:keys], dk[keys:]).astype(BF)
    dv = jnp.where(lanes, dv[:keys], dv[keys:]).astype(BF)
    return mm(ds2, k2, TN), dk, dv


def attention_backward(scalars, qkv, pairs_before, d_out, out, logs):
    rows = qkv.shape[0]
    half = rows // 2
    pairs = D // PAIR
    count = pairs // 2

    def kernel(
        sc_ref, q_ref, k_ref, v_ref, kb_ref, vb_ref, do_ref, out_ref, log_ref, grads_ref, dq_ref
    ):
        q = q_ref[...] * SCALE
        d_o = do_ref[...]
        deltas = deltas_of(d_o, out_ref[...])
        log_rows = log_ref[0]

        @pl.when(sc_ref[0] == 0)
        def _():
            dq_ref[...] = jnp.zeros_like(dq_ref)
            grads_ref[3:] = jnp.zeros((2, rows, PAIR), BF)

        @pl.when(sc_ref[0] != 0)
        def _():
            for first in (0, half):
                span = slice(first, first + half)
                dq, dk, dv = key_block_back(
                    kb_ref[span, :], vb_ref[span, :], q, d_o, log_rows, deltas, False
                )
                if first == 0:
                    dq_ref[...] = dq
                else:
                    dq_ref[...] += dq
                grads_ref[3, span, :] = dk
                grads_ref[4, span, :] = dv

        for first in (0, half):
            span = slice(first, first + half)
            dq, dk, dv = key_block_back(
                k_ref[span, :], v_ref[span, :], q[first:], d_o[first:],
                log_rows[:, first:], deltas[:, first:], True,
            )
            dq_ref[first:, :] += dq
            grads_ref[1, span, :] = dk
            grads_ref[2, span, :] = dv
        grads_ref[0] = (dq_ref[...] * SCALE).astype(BF)

    block = (rows, PAIR)

    def at(offset):
        return pl.BlockSpec(block, lambda p, sc: (0, offset + sc[1] * count + p))

    return pl.pallas_call(
        kernel,
        grid_spec=pltpu.PrefetchScalarGridSpec(
            num_scalar_prefetch=1,
            grid=(count,),
            in_specs=[
                at(0), at(pairs), at(2 * pairs), at(0), at(pairs), at(0), at(0),
                pl.BlockSpec((1, 2, rows), lambda p, sc: (sc[1] * count + p, 0, 0)),
            ],
            out_specs=pl.BlockSpec((5, rows, PAIR), lambda p, sc: (0, 0, p)),
            scratch_shapes=[pltpu.VMEM(block, F32)],
        ),
        out_shape=shape_of((5, rows, D // 2), BF),
        compiler_params=params(),
        cost_estimate=cost(0, 0),
        name="attention_backward",
    )(scalars, qkv, qkv, qkv, pairs_before, pairs_before, d_out, out, logs)


def project_back(own, grads_own, grads_other, parts, weight, x, name):
    rows = x.shape[0]
    base, count = parts
    width = grads_own.shape[2]
    first = 3 - count
    chunk = 128

    def kernel(own_ref, ga_ref, gb_ref, wa_ref, wb_ref, x_ref, out_ref, sums_ref, acc_ref, part_sums):
        j = pl.program_id(0)
        grad = jnp.concatenate([ga_ref[...], gb_ref[...]], axis=1)
        part = mm(grad, jnp.concatenate([wa_ref[...], wb_ref[...]], axis=1), NT)

        @pl.when(j == 0)
        def _():
            acc_ref[...] = part

        @pl.when(j != 0)
        def _():
            acc_ref[...] += part

        @pl.when(j == count - 1)
        def _():
            part_sums[...] = jnp.zeros_like(part_sums)

            def finish(span):
                total = acc_ref[span, :]
                normal, _ = normed(x_ref[span, :].astype(F32))
                for place, values in ((0, total * normal), (1, total)):
                    folded = values[:8]
                    for i in range(8, chunk, 8):
                        folded = folded + values[i : i + 8]
                    part_sums[place] += folded
                out_ref[span, :] = total.astype(BF)

            by_rows(rows, chunk, finish)
            sums_ref[...] = jnp.zeros_like(sums_ref)
            for i in (0, 1):
                sums_ref[i : i + 1, :] = jnp.sum(part_sums[i], axis=0, keepdims=True)

    grad = pl.BlockSpec((None, rows, width), lambda j, own: (base + j, 0, 0))
    return pl.pallas_call(
        kernel,
        grid_spec=pltpu.PrefetchScalarGridSpec(
            num_scalar_prefetch=1,
            grid=(count,),
            in_specs=[
                grad,
                grad,
                pl.BlockSpec((D, width), lambda j, own: (0, 2 * (first + j) + own[0])),
                pl.BlockSpec((D, width), lambda j, own: (0, 2 * (first + j) + 1 - own[0])),
                whole((rows, D)),
            ],
            out_specs=[whole((rows, D)), whole((8, D))],
            scratch_shapes=[pltpu.VMEM((rows, D), F32), pltpu.VMEM((2, 8, D), F32)],
        ),
        out_shape=[shape_of((rows, D), BF), shape_of((8, D), F32)],
        compiler_params=params(),
        cost_estimate=cost(0, 0),
        name=name,
    )(own, grads_own, grads_other, weight, weight, x)


def input_back(d_act, d_act_other, x, d_mid1, gain):
    rows = x.shape[0]
    tile = rows // 4

    def kernel(da_ref, db_ref, x_ref, dm_ref, gain_ref, out_ref):
        normal, inverse = normed(x_ref[...].astype(F32))
        up = da_ref[...].astype(F32) + db_ref[...].astype(F32)
        out_ref[...] = dm_ref[...] + norm_back(normal, inverse, gain_ref[...], up)

    row_block = pl.BlockSpec((tile, D), lambda i: (i, 0))
    return pl.pallas_call(
        kernel,
        grid=(rows // tile,),
        in_specs=[row_block] * 4 + [whole((1, D))],
        out_specs=row_block,
        out_shape=shape_of((rows, D), F32),
        compiler_params=params(),
        cost_estimate=cost(0, 0),
        name="input_back",
    )(d_act, d_act_other, x, d_mid1, gain)


def part_of(operand):
    if isinstance(operand, tuple):
        array, part = operand
        return array, array.shape[1:], lambda *at: (part,) + at
    return operand, operand.shape, None


def spec_of(operand, block, place):
    _, _, lead = part_of(operand)
    if lead is None:
        return pl.BlockSpec(block, place)
    return pl.BlockSpec((None,) + block, lambda *at: lead(*place(*at)))


def joined(refs):
    blocks = [ref[...] for ref in refs]
    return blocks[0] if len(blocks) == 1 else jnp.concatenate(blocks, axis=0)


def put_strips(ref, values, first=0):
    for c in range(values.shape[1] // LANES):
        ref[first + c] = values[:, c * LANES : (c + 1) * LANES]


def row_grad(scalars, lefts, rights, name):
    n = len(lefts)
    left_shapes = [part_of(a)[1] for a in lefts]
    right_shapes = [part_of(a)[1] for a in rights]
    rows = left_shapes[0][1]
    wide = right_shapes[0][1] // 2
    tile = 512
    strips = wide // LANES

    def kernel(sc_ref, *refs):
        left = joined(refs[:n])
        put_strips(refs[-2], mm(left, joined(refs[n : 2 * n]), TN).astype(BF))
        put_strips(refs[-1], mm(left, joined(refs[2 * n : 3 * n]), TN).astype(BF))

    operands = [part_of(a)[0] for a in lefts]
    in_specs = [
        spec_of(a, (shape[0], tile), lambda j, sc: (0, j)) for a, shape in zip(lefts, left_shapes)
    ]
    for place in (lambda j, sc: (0, sc[0]), lambda j, sc: (0, 1 - sc[0])):
        for a, shape in zip(rights, right_shapes):
            in_specs.append(spec_of(a, (shape[0], wide), place))
            operands.append(part_of(a)[0])
    return pl.pallas_call(
        kernel,
        grid_spec=pltpu.PrefetchScalarGridSpec(
            num_scalar_prefetch=1,
            grid=(rows // tile,),
            in_specs=in_specs,
            out_specs=[pl.BlockSpec((strips, tile, LANES), lambda j, sc: (0, j, 0))] * 2,
        ),
        out_shape=[shape_of((strips, rows, LANES), BF)] * 2,
        compiler_params=params(),
        cost_estimate=cost(0, 0),
        name=name,
    )(scalars, *operands)


def column_grad(scalars, lefts, rights, bw, name):
    n = len(lefts)
    left_shapes = [part_of(a)[1] for a in lefts]
    right_shapes = [part_of(a)[1] for a in rights]
    rows = left_shapes[0][1]
    cols = right_shapes[0][1]
    bn = 512
    blocks = rows // bw
    strips = bn // LANES

    def kernel(sc_ref, *refs):
        send_ref, keep_ref, product = refs[-3:]
        product[...] = mm(joined(refs[:n]), joined(refs[n : 2 * n]), TN).astype(BF)
        for i in range(blocks):
            block = product[pl.ds(pl.multiple_of(sc_ref[1 + i] * bw, bw), bw), :]
            target = send_ref if i < blocks // 2 else keep_ref
            place = (i % (blocks // 2)) * bw
            for c in range(strips):
                target[c, place : place + bw, :] = block[:, c * LANES : (c + 1) * LANES]

    operands = [part_of(a)[0] for a in lefts] + [part_of(a)[0] for a in rights]
    in_specs = [spec_of(a, shape, lambda j, sc: (0, 0)) for a, shape in zip(lefts, left_shapes)]
    in_specs += [spec_of(a, (shape[0], bn), lambda j, sc: (0, j)) for a, shape in zip(rights, right_shapes)]
    return pl.pallas_call(
        kernel,
        grid_spec=pltpu.PrefetchScalarGridSpec(
            num_scalar_prefetch=1,
            grid=(cols // bn,),
            in_specs=in_specs,
            out_specs=[pl.BlockSpec((strips, rows // 2, LANES), lambda j, sc: (j, 0, 0))] * 2,
            scratch_shapes=[pltpu.VMEM((rows, bn), BF)],
        ),
        out_shape=[shape_of((cols // LANES, rows // 2, LANES), BF)] * 2,
        compiler_params=params(),
        cost_estimate=cost(0, 0),
        name=name,
    )(scalars, *operands)


def block_grads(scalars, bw, lefts, rights, blocks, name, text=None):
    count = len(blocks)
    width = 512
    part = width // 2
    row_blocks = D // bw
    in_specs, operands = [], []
    for a, lead in lefts:
        if lead is None:
            in_specs.append(whole(a.shape))
        else:
            in_specs.append(pl.BlockSpec((None,) + a.shape[1:], lambda j, sc, lead=lead: (lead, 0, 0)))
        operands.append(a)
    for a, place in rights:
        if a.ndim == 3:
            in_specs.append(
                pl.BlockSpec((None, a.shape[1], width), lambda j, sc, place=place: (place(j), 0, 0))
            )
        else:
            in_specs.append(pl.BlockSpec((a.shape[0], width), lambda j, sc, place=place: (0, place(j))))
        operands.append(a)
    n, m = len(lefts), len(rights)
    if text is not None:
        for a in text[:4]:
            in_specs.append(whole(a.shape))
            operands.append(a)
        wide = text[0].shape[1]
        for at in (0, 1):
            in_specs.append(
                pl.BlockSpec((D // 2, wide), lambda j, sc, at=at: (sc[1 + row_blocks], at))
            )
            operands.append(text[4])
        count += 1
    inputs_count = len(operands)

    def kernel(sc_ref, *refs):
        left_refs, right_refs = refs[:n], refs[n : n + m]
        sent_a, kept_a, sent_b, kept_b, product = refs[inputs_count:]
        j = pl.program_id(0)

        if text is not None:
            text_refs = refs[n + m : inputs_count]

            @pl.when(j == count - 1)
            def _():
                product[...] = jnp.zeros_like(product)
                core = sc_ref[1 + row_blocks]
                for i in (0, 1):
                    mine, others = text_refs[2 * i][...], text_refs[2 * i + 1][...]
                    low = jnp.where(core == 0, mine, others)
                    high = jnp.where(core == 0, others, mine)
                    term = mm(low, text_refs[4][...], NT) + mm(high, text_refs[5][...], NT)
                    at = pl.multiple_of(sc_ref[2 + row_blocks + i] * TEXT_LEN, TEXT_LEN)
                    span = pl.ds(at, TEXT_LEN)
                    product[span, :] = add(product[span, :], term)

        for at, (left_places, right_places) in enumerate(blocks):

            @pl.when(j == at)
            def _(left_places=left_places, right_places=right_places):
                left = joined([left_refs[i] for i in left_places])
                right = joined([right_refs[i] for i in right_places])
                product[...] = mm(left, right, TN).astype(BF)

        eighth = part // 2
        sent_a[0] = product[:, pl.ds(pl.multiple_of(sc_ref[0] * eighth, eighth), eighth)]
        kept_a[0] = product[:, pl.ds(pl.multiple_of(eighth - sc_ref[0] * eighth, eighth), eighth)]
        for i in range(row_blocks):
            rows = product[pl.ds(pl.multiple_of(sc_ref[1 + i] * bw, bw), bw), part:]
            target = sent_b if i < row_blocks // 2 else kept_b
            place = (i % (row_blocks // 2)) * bw
            for c in (0, 1):
                target[c, place : place + bw, :] = rows[:, c * LANES : (c + 1) * LANES]

    a_block, b_block = (1, D, LANES), (2, D // 2, LANES)
    return pl.pallas_call(
        kernel,
        grid_spec=pltpu.PrefetchScalarGridSpec(
            num_scalar_prefetch=1,
            grid=(count,),
            in_specs=in_specs,
            out_specs=[
                pl.BlockSpec(a_block, lambda j, sc: (j, 0, 0)),
                pl.BlockSpec(a_block, lambda j, sc: (j, 0, 0)),
                pl.BlockSpec(b_block, lambda j, sc: (j, 0, 0)),
                pl.BlockSpec(b_block, lambda j, sc: (j, 0, 0)),
            ],
            scratch_shapes=[pltpu.VMEM((D, width), BF)],
        ),
        out_shape=[
            shape_of((count, D, LANES), BF),
            shape_of((count, D, LANES), BF),
            shape_of((2 * count, D // 2, LANES), BF),
            shape_of((2 * count, D // 2, LANES), BF),
        ],
        compiler_params=params(),
        cost_estimate=cost(0, 0),
        name=name,
    )(scalars, *operands)


def swap(block, axis, bit):
    route = [(i, i ^ (1 << bit)) for i in range(lax.axis_size(axis))]
    return lax.ppermute(block, axis, route)


def pick(block, place, dim):
    return lax.dynamic_index_in_dim(block, place, dim, keepdims=False)


def bit_of(index, bit):
    return (index >> bit) & 1


def add(a, b):
    return (a.astype(F32) + b.astype(F32)).astype(BF)


class Order:
    def __init__(self):
        self.token = None

    def then(self, *values):
        if self.token is not None:
            values = lax.optimization_barrier(values + (self.token,))[:-1]
        return values if len(values) > 1 else values[0]

    def mark(self, value):
        self.token = value
        return value


def exchange(block, axis, mask):
    route = [(i, i ^ mask) for i in range(lax.axis_size(axis))]
    return lax.ppermute(block, axis, route)


def flat(block):
    return block.reshape(-1, LANES)


def rows_at(first, count):
    return pl.ds(pl.multiple_of(first, 16) if not isinstance(first, int) else first, count)


def repeat(count, step):
    def one(i, carry):
        step(i)
        return carry

    lax.fori_loop(0, count, one, 0)


def sum_stage(order, name, scalars, inputs, outputs, work):
    n = len(inputs)

    def kernel(sc_ref, *refs):
        work(sc_ref, refs[:n], refs[n:])

    outs = pl.pallas_call(
        kernel,
        grid_spec=pltpu.PrefetchScalarGridSpec(
            num_scalar_prefetch=1,
            grid=(1,),
            in_specs=[whole(a.shape) for a in inputs],
            out_specs=[whole((rows, LANES)) for rows in outputs],
        ),
        out_shape=[shape_of((rows, LANES), BF) for rows in outputs],
        compiler_params=params(),
        cost_estimate=cost(0, 0),
        name=name,
    )(scalars, *inputs)
    order.mark(outs[0])
    return outs


class Streams:
    def __init__(self, a_strips, a_rows, b_strips, b_rows, left):
        self.a_strips, self.a_rows, self.b_strips, self.b_rows = a_strips, a_rows, b_strips, b_rows // 2
        self.left = left
        self.a_half = a_strips * left * a_rows
        self.b_half = b_strips * left * (b_rows // 2)
        self.a_first, self.b_first = 2 * self.a_half, 2 * self.b_half
        self.piece = (self.a_half + self.b_half) // left

    def second(self, kept, came, sent, keep, mine, a):
        rows = self.a_rows if a else self.b_rows
        strips = self.a_strips if a else self.b_strips

        def step(i):
            for out, side in ((sent, 1 - mine), (keep, mine)):
                first = i * 2 * rows + side * rows
                out[rows_at(i * rows, rows), :] = (
                    kept[rows_at(first, rows), :] + came[rows_at(first, rows), :]
                )

        repeat(strips * self.left, step)

    def third(self, kept_a, came_a, kept_b, came_b, sent, keep, place):
        a_rows, b_rows, left = self.a_rows, self.b_rows, self.left
        mine = place & 1
        for j in range(left // 2):
            for out, side in ((sent, 1 - mine), (keep, mine)):
                block = 2 * j + side
                base = j * self.piece

                def a_step(i, out=out, block=block, base=base):
                    first = (i * left + block) * a_rows
                    out[rows_at(base + i * a_rows, a_rows), :] = (
                        kept_a[rows_at(first, a_rows), :] + came_a[rows_at(first, a_rows), :]
                    )

                def b_step(i, out=out, block=block, base=base):
                    first = (i * left + block) * b_rows
                    at = base + self.a_strips * a_rows + i * b_rows
                    out[rows_at(at, b_rows), :] = (
                        kept_b[rows_at(first, b_rows), :] + came_b[rows_at(first, b_rows), :]
                    )

                repeat(self.a_strips, a_step)
                repeat(self.b_strips, b_step)


def add_rows(a, b, a_at, out, out_at, count):
    chunk = math.gcd(count, 256)

    def step(i):
        span = rows_at(a_at + i * chunk, chunk)
        out[rows_at(out_at + i * chunk, chunk), :] = a[span, :] + b[span, :]

    repeat(count // chunk, step)


def total_over_rest(pieces):
    for bit in range(2, lax.axis_size("dp").bit_length() - 1):
        pieces = [add(piece, swap(piece, "dp", bit)) for piece in pieces]
    return pieces


class Spread:
    def __init__(self, order, piece):
        self.order, self.piece = order, piece
        self.y = swap(piece, "dp", 1)
        self.core = swap(piece, "dp", 0)

    def forward(self):
        self.y = self.order.then(self.y)
        self.both = swap(self.y, "dp", 0)

    def finish(self, rows, shapes, write, name, rider=0):
        pieces = self.order.then(self.piece, self.core, self.y, self.both)
        out_shapes = list(shapes) + ([(rider, LANES)] if rider else [])

        def kernel(sc_ref, *refs):
            outs = refs[4:]
            for at in range(4):
                for k in range(4):

                    @pl.when(sc_ref[0] == at ^ k)
                    def _(at=at, k=k):
                        write(outs, refs[k], at & 1, at >> 1)

            if rider:
                total = refs[0][rows:, :].astype(F32)
                for ref in refs[1:4]:
                    total = total + ref[rows:, :].astype(F32)
                outs[-1][...] = total

        scalars = (lax.axis_index("dp") & 3).astype(jnp.int32).reshape(1)
        outs = pl.pallas_call(
            kernel,
            grid_spec=pltpu.PrefetchScalarGridSpec(
                num_scalar_prefetch=1,
                grid=(1,),
                in_specs=[whole(self.piece.shape)] * 4,
                out_specs=[whole(shape) for shape in out_shapes],
            ),
            out_shape=[shape_of(shape, F32) for shape in out_shapes],
            compiler_params=params(),
            cost_estimate=cost(0, 0),
            name=name,
        )(scalars, *pieces)
        self.order.mark(outs[0])
        return outs

    def finish_text(self, rows, bw):
        pieces = self.order.then(self.piece, self.core, self.y, self.both)
        shards = lax.axis_size("seq")
        half = bw // 2

        def kernel(sc_ref, *refs):
            out_ref = refs[4]

            def one(i, carry):
                place = i ^ sc_ref[0]
                seq_at = (place & 1) * (shards // 2) + (place >> 1)
                at = pl.multiple_of(seq_at * rows, rows)
                first = pl.multiple_of(i * bw, bw)
                for core in (0, 1):
                    for y in (0, 1):
                        for k in range(4):

                            @pl.when(sc_ref[1] == (2 * y + core) ^ k)
                            def _(ref=refs[k], core=core, y=y):
                                col = core * (D // 2) + y * LANES
                                out_ref[pl.ds(first, bw), col : col + LANES] = ref[
                                    pl.ds(at, bw), :
                                ].astype(F32)
                                for c in (0, 1):
                                    col = core * (D // 2) + 256 + c * LANES
                                    out_ref[pl.ds(first + y * half, half), col : col + LANES] = ref[
                                        rows_at(at + bw + c * half, half), :
                                    ].astype(F32)

                return carry

            lax.fori_loop(0, shards, one, 0)

        scalars = jnp.stack([lax.axis_index("seq"), lax.axis_index("dp") & 3]).astype(jnp.int32)
        return pl.pallas_call(
            kernel,
            grid_spec=pltpu.PrefetchScalarGridSpec(
                num_scalar_prefetch=1,
                grid=(1,),
                in_specs=[whole(self.piece.shape)] * 4,
                out_specs=whole((shards * bw, D)),
            ),
            out_shape=shape_of((shards * bw, D), F32),
            compiler_params=params(),
            cost_estimate=cost(0, 0),
            name="text_finish",
        )(scalars, *pieces)


def row_order(bit):
    mine = bit_of(lax.axis_index("seq"), bit)
    low = [s for s in range(lax.axis_size("seq")) if not (s >> bit) & 1]
    sent = [s + (1 - mine) * (1 << bit) for s in low]
    kept = [s + mine * (1 << bit) for s in low]
    return jnp.stack([jnp.asarray(v, jnp.int32) for v in [0] + sent + kept])


def body(
    inputs,
    text_state,
    text_segment,
    image_text,
    image_segment,
    self_gain,
    self_shift,
    qkv_weight,
    self_weight,
    cross_gain,
    cross_shift,
    query_weight,
    text_weight,
    cross_weight,
    feed_gain,
    feed_shift,
    up_weight,
    down_weight,
    cotangent,
):
    rows = inputs.shape[0]
    shards = lax.axis_size("seq")
    groups = lax.axis_size("dp")
    me, dp = lax.axis_index("seq"), lax.axis_index("dp")
    per_image = IMG_TOK // rows
    core = bit_of(dp, 0)
    odd = (me % per_image).astype(jnp.int32).reshape(1)
    img_group = image_text.shape[0] // groups
    own_half = core.astype(jnp.int32).reshape(1)
    other_half = 1 - own_half
    order = Order()

    def caption_of(group):
        image = group * img_group + me // per_image
        return image_text[image], image_segment[image]

    row, seg = caption_of(dp)
    row_mate, _ = caption_of(dp ^ 1)

    def over_core(block):
        return swap(block, "dp", 0)

    seq_bits = shards.bit_length() - 1
    dp_bits = groups.bit_length() - 1
    spread_steps = [("seq", b) for b in reversed(range(seq_bits))] + [("dp", 1), ("dp", 0)]
    bw = D // shards
    bw_ff = FF // (2 * shards)
    order_x = row_order(0)
    y_first = (1 - bit_of(dp, 1)).astype(jnp.int32).reshape(1)
    order_xy = jnp.concatenate([y_first, order_x[1:]])

    even_to_odd = [(i, i + 1) for i in range(0, shards, 2)]
    odd_to_even = [(i + 1, i) for i in range(0, shards, 2)]
    x_before = lax.ppermute(inputs, "seq", even_to_odd)
    cot_mate = over_core(cotangent)
    gain1, shift1 = self_gain.reshape(1, D), self_shift.reshape(1, D)
    act1, qkv, norms = norm_project(inputs, gain1, shift1, qkv_weight, 0, "norm_project")
    act1_mate = over_core(act1)
    order.mark(qkv)
    text_row, text_row_mate = order.then(pick(text_state, row, 0), pick(text_state, row_mate, 0))
    text_kv = jnp.dot(text_row, text_weight, preferred_element_type=F32).astype(BF)
    bias = jnp.where(pick(text_segment, row, 0) == seg, 0.0, NEGATIVE).astype(F32)
    bias_row = jnp.tile(bias[None, :], (1, 2))
    order.mark((text_kv, bias_row))
    qkv = order.then(qkv)
    own_out, own_log = causal_forward(qkv, norms)
    order.mark(own_out)
    x_before, act1_mate, cot_mate = order.then(x_before, act1_mate, cot_mate)
    act1_before, pairs_before, norms_before = norm_project(
        x_before, gain1, shift1, qkv_weight, D, "norm_project_before"
    )
    before_mate = over_core(act1_before)
    attended, log_rows = earlier_forward(
        odd, qkv, pairs_before, norms, norms_before, own_out, own_log
    )
    order.mark(attended)
    before_mate, attended = order.then(before_mate, attended)
    attended_mate = over_core(attended)
    gains = jnp.stack([cross_gain, cross_shift, feed_gain, feed_shift] * 2)
    mid1, cq, mid2, acts = middle_forward(
        attended, inputs, self_weight, query_weight, cross_weight, gains, text_kv, bias_row
    )
    order.mark(mid1)
    attended_mate, acts = order.then(attended_mate, acts)
    acts_mate = over_core(acts)
    hid_other, d_act3 = feed_half(
        other_half, acts, cotangent, up_weight, down_weight, shards, None
    )
    order.mark(d_act3)
    d_act3, acts_mate, hid_other = order.then(d_act3, acts_mate, hid_other)
    hid_mate = over_core(hid_other)
    hid_own, d_act3 = feed_half(
        own_half, acts, cotangent, up_weight, down_weight, shards, d_act3
    )
    order.mark(d_act3)
    hid_mate = order.then(hid_mate)

    left = shards // 2
    feed = Streams(D // 2 // LANES, bw_ff, FF // 2 // LANES, bw, left)
    mids = Streams(6, bw, 12, bw, left)
    qkvs = Streams(3, bw, 6, bw, left)
    x_bit, y_bit = bit_of(me, 0), bit_of(dp, 1)
    places = jnp.stack([x_bit, y_bit, me >> 1]).astype(jnp.int32)
    others = range(1, left)

    sent, feed_a = row_grad(
        y_first, [(hid_own, 0), (hid_mate, 0)], [cotangent, cot_mate], "down_grad"
    )
    order.mark(sent)
    feed_a = flat(feed_a)
    came_fa = swap(flat(sent), "dp", 1)
    acts_late = order.then(acts)
    sent, feed_b = column_grad(
        order_x, [(acts_late, 2), (acts_mate, 2)], [(hid_own, 1), (hid_mate, 1)], bw, "up_grad"
    )
    order.mark(sent)
    feed_b = flat(feed_b)
    came_fb = swap(flat(sent), "seq", 0)

    d_act3 = order.then(d_act3)
    g_mine, g_sent, d_mid1, d_att, text_mine, text_sent, d_gains = middle_backward(
        own_half, d_act3, mid2, cotangent, mid1, cq, text_kv, bias_row, cross_weight, query_weight,
        self_weight, gains,
    )
    order.mark(d_mid1)
    g_mate = over_core(g_sent)
    text_both = order.mark(jnp.concatenate([text_sent, text_mine], axis=0))
    text_both = over_core(text_both)
    g_mine, g_mate, text_both = order.then(g_mine, g_mate, text_both)
    text_mate, text_mate_other = text_both[:TEXT_LEN], text_both[TEXT_LEN:]
    lefts = [(acts, 1), (acts_mate, 1), (acts, 0), (acts_mate, 0), (attended, None), (attended_mate, None)]
    lefts += [(text_row, None), (text_row_mate, None)]
    rights = [(g_mine, lambda j: jnp.minimum(j, 2)), (g_mate, lambda j: jnp.minimum(j, 2))]
    rights += [(text_mine, lambda j: jnp.clip(j - 3, 0, 1)), (text_mate, lambda j: jnp.clip(j - 3, 0, 1))]
    blocks = [((0, 1), (0, 1)), ((2, 3), (0, 1)), ((4, 5), (0, 1)), ((6, 7), (2, 3)), ((6, 7), (2, 3))]
    mid_scalars = jnp.concatenate([order_xy, jnp.stack([core, row, row_mate]).astype(jnp.int32)])
    sent_a, mid_a, sent_b, mid_b = block_grads(
        mid_scalars, bw, lefts, rights, blocks, "middle_grads",
        text=(text_mine, text_sent, text_mate, text_mate_other, text_weight),
    )
    order.mark(mid_a)
    mid_sent_a, mid_sent_b = flat(sent_a), flat(sent_b)
    mid_a, mid_b = flat(mid_a), flat(mid_b)

    def second(streams, name, kept_a, came_a, kept_b, came_b):
        def work(sc, ins, outs):
            streams.second(ins[0], ins[1], outs[0], outs[2], sc[0], True)
            streams.second(ins[2], ins[3], outs[1], outs[3], sc[1], False)

        inputs = order.then(kept_a, came_a, kept_b, came_b)
        sent_x, sent_y, kept_a, kept_b = sum_stage(
            order, name, places, inputs, [streams.a_half, streams.b_half] * 2, work
        )
        return kept_a, swap(sent_x, "seq", 0), kept_b, swap(sent_y, "dp", 1)

    def third(streams, name, kept_a, came_a, kept_b, came_b, rider=0):
        def work(sc, ins, outs):
            streams.third(ins[0], ins[1], ins[2], ins[3], outs[0], outs[1], sc[2])
            if rider:
                count = left // 2 * streams.piece
                span = slice(streams.a_half, streams.a_half + rider)
                for out in outs:
                    out[count : count + rider, :] = ins[0][span, :] + ins[1][span, :]

        inputs = order.then(kept_a, came_a, kept_b, came_b)
        out_rows = left // 2 * streams.piece + rider
        sent, kept = sum_stage(order, name, places, inputs, [out_rows] * 2, work)
        return kept, swap(sent, "seq", 1)

    def further(streams, name, kept, came, rider=0):
        blocks = left // 2
        for bit in range(1, left.bit_length() - 1):
            half = blocks // 2 * streams.piece

            def work(sc, ins, outs, bit=bit, half=half):
                mine = (sc[2] >> bit) & 1
                for i in range(half // streams.piece):
                    for out, side in ((outs[0], 1 - mine), (outs[1], mine)):
                        add_rows(
                            ins[0], ins[1], (2 * i + side) * streams.piece, out, i * streams.piece, streams.piece
                        )
                if rider:
                    for out in outs:
                        out[half : half + rider, :] = ins[0][2 * half :, :] + ins[1][2 * half :, :]

            inputs = order.then(kept, came)
            sent, kept = sum_stage(order, name, places, inputs, [half + rider] * 2, work)
            came = swap(sent, "seq", bit + 1)
            blocks //= 2
        return kept, came

    def fourth(streams, name, kept, came, rider=0):
        def work(sc, ins, outs):
            add_rows(ins[0], ins[1], 0, outs[0], 0, streams.piece + rider)

        inputs = order.then(kept, came)
        (total,) = sum_stage(order, name, places, inputs, [streams.piece + rider], work)
        return total_over_rest([total])[0]

    feed_streams = second(feed, "feed_second", feed_a, came_fa, feed_b, came_fb)

    sc_other = jnp.concatenate([odd, other_half])
    sc_own = jnp.concatenate([odd, own_half])
    d_att = order.then(d_att)
    att_other = attention_backward(sc_other, qkv, pairs_before, d_att, attended, log_rows)
    order.mark(att_other)
    feed_left = third(feed, "feed_third", *feed_streams)
    att_other, mid_sent_a, mid_sent_b = order.then(att_other, mid_sent_a, mid_sent_b)
    att_mate = over_core(att_other)
    came_ma, came_mb = swap(mid_sent_a, "dp", 1), swap(mid_sent_b, "seq", 0)
    d_att = order.then(d_att)
    att_own = attention_backward(sc_own, qkv, pairs_before, d_att, attended, log_rows)
    order.mark(att_own)
    att_own = order.then(att_own)
    d_act_before, sums_before = project_back(
        own_half, att_own, att_other, (3, 2), qkv_weight, x_before, "project_back_before"
    )
    order.mark(d_act_before)
    att_mate = order.then(att_mate)
    feed_left = further(feed, "feed_further", *feed_left)
    mid_streams = second(mids, "mid_second", mid_a, came_ma, mid_b, came_mb)

    act1_late = order.then(act1)
    lefts = [(act1_late, None), (act1_mate, None), (act1_before, None), (before_mate, None)]
    rights = [(att_own, lambda j: j), (att_mate, lambda j: j)]
    rights += [(att_own, lambda j: 3 + jnp.maximum(j - 1, 0))]
    rights += [(att_mate, lambda j: 3 + jnp.maximum(j - 1, 0))]
    blocks = [((0, 1), (0, 1))] + [((0, 1, 2, 3), (0, 1, 2, 3))] * 2
    sent_a, qkv_a, sent_b, qkv_b = block_grads(order_xy, bw, lefts, rights, blocks, "qkv_grads")
    order.mark(qkv_a)
    came_qa, came_qb = swap(flat(sent_a), "dp", 1), swap(flat(sent_b), "seq", 0)
    att_own = order.then(att_own)
    d_act, sums_own = project_back(
        own_half, att_own, att_other, (0, 3), qkv_weight, inputs, "project_back"
    )
    order.mark(d_act)
    rider = jnp.concatenate([sums_own[:2] + sums_before[:2], d_gains[:4]], axis=0).astype(BF)
    rider = flat(rider)
    rides = rider.shape[0]
    mid_left = third(mids, "mid_third", *mid_streams)

    inputs_q = order.then(flat(qkv_a), came_qa, flat(qkv_b), came_qb, rider)

    def work_q(sc, ins, outs):
        qkvs.second(ins[0], ins[1], outs[0], outs[2], sc[0], True)
        qkvs.second(ins[2], ins[3], outs[1], outs[3], sc[1], False)
        for out in (outs[0], outs[2]):
            out[qkvs.a_half : qkvs.a_half + rides, :] = ins[4][...]

    sent_x, sent_y, qkv_a, qkv_b = sum_stage(
        order, "qkv_second", places, inputs_q,
        [qkvs.a_half + rides, qkvs.b_half] * 2, work_q,
    )
    came_qa, came_qb = swap(sent_x, "seq", 0), swap(sent_y, "dp", 1)
    feed_piece = fourth(feed, "feed_fourth", *feed_left)
    mid2_late = order.then(mid2)
    output = feed_output(own_half, mid2_late, hid_own, hid_other, down_weight, shards)
    order.mark(output)
    mid_left = further(mids, "mid_further", *mid_left)
    qkv_left = third(qkvs, "qkv_third", qkv_a, came_qa, qkv_b, came_qb, rides)
    d_act_before = order.then(d_act_before)
    d_act_late = lax.ppermute(d_act_before, "seq", odd_to_even)
    feed_piece = order.then(feed_piece)
    feed_all = Spread(order, feed_piece)
    mid_piece = fourth(mids, "mid_fourth", *mid_left)
    qkv_left = further(qkvs, "qkv_further", *qkv_left, rides)

    text_rows = 2 * bw
    text_piece = jnp.concatenate(
        [mid_piece[5 * bw : 6 * bw], mid_piece[11 * bw : 12 * bw]], axis=0
    )
    order.mark(text_piece)
    feed_all.forward()
    text_pieces = [text_piece] + [exchange(text_piece, "seq", 2 * k) for k in others]
    d_act, d_act_late = order.then(d_act, d_act_late)
    input_grad = input_back(d_act, d_act_late, inputs, d_mid1, gain1)
    order.mark(input_grad)

    def join(name, pieces):
        def work(sc, ins, outs):
            for i, ref in enumerate(ins):
                count = ref.shape[0]
                outs[0][i * count : (i + 1) * count, :] = ref[...]

        inputs = order.then(*pieces)
        return sum_stage(order, name, places, inputs, [len(pieces) * pieces[0].shape[0]], work)[0]

    text_block = join("text_join", text_pieces)
    came_text = swap(text_block, "seq", 0)
    qkv_piece = fourth(qkvs, "qkv_fourth", *qkv_left, rides)
    qkv_all = Spread(order, qkv_piece)
    mid_piece = order.then(mid_piece)
    mid_all = Spread(order, mid_piece)
    text_block = join("text_join", [text_block, came_text])
    text_all = Spread(order, text_block)

    b_rows = bw // 2

    def write_feed(outs, ref, at_core, y):
        at = 0
        strips = D // 2 // LANES
        for c in range(strips):
            col = y * (D // 2) + c * LANES
            outs[0][at_core * bw_ff : (at_core + 1) * bw_ff, col : col + LANES] = ref[
                at + c * bw_ff : at + (c + 1) * bw_ff, :
            ].astype(F32)
        at = at + strips * bw_ff
        per = bw_ff // LANES
        for c in range(FF // 2 // LANES):
            s, inside = divmod(c, per)
            col = (2 * s + at_core) * bw_ff + inside * LANES
            outs[1][y * b_rows : (y + 1) * b_rows, col : col + LANES] = ref[
                at + c * b_rows : at + (c + 1) * b_rows, :
            ].astype(F32)

    def writer(targets):
        count = len(targets)

        def write(outs, ref, at_core, y):
            for j, where in enumerate(targets):
                if where is None:
                    continue
                out, first = where
                col = first[at_core]
                outs[out][:, col + y * LANES : col + (y + 1) * LANES] = ref[
                    j * bw : (j + 1) * bw, :
                ].astype(F32)
                for half in (0, 1):
                    row_at = count * bw + (2 * j + half) * b_rows
                    to = col + 256 + half * LANES
                    outs[out][y * b_rows : (y + 1) * b_rows, to : to + LANES] = ref[
                        row_at : row_at + b_rows, :
                    ].astype(F32)

        return write

    down_grad, up_grad = feed_all.finish(
        feed.piece, [(2 * bw_ff, D), (bw, FF)], write_feed, "feed_finish"
    )
    qkv_all.forward()
    mid_all.forward()
    text_all.forward()
    targets = [(0, (0, 512)), (1, (0, 512)), (2, (0, 512)), (3, (0, 1024)), (3, (512, 1536)), None]
    cross_grad, query_grad, self_grad, text_weight_grad = mid_all.finish(
        mids.piece, [(bw, D), (bw, D), (bw, D), (bw, 2 * D)], writer(targets), "mids_finish"
    )
    targets = [(0, (0, 512)), (0, (1024, 1536)), (0, (2048, 2560))]
    qkv_grad, sums = qkv_all.finish(
        qkvs.piece, [(bw, 3 * D)], writer(targets), "qkv_finish", rider=rides
    )
    text_grad = text_all.finish_text(text_rows, bw)
    sums = lax.dynamic_slice_in_dim(sums.reshape(6, D), me * bw, bw, 1)
    return (
        output,
        input_grad,
        text_grad.reshape(text_state.shape),
        sums[0],
        sums[1],
        qkv_grad,
        self_grad,
        sums[2],
        sums[3],
        query_grad,
        text_weight_grad,
        cross_grad,
        sums[4],
        sums[5],
        up_grad,
        down_grad,
    )


def solution(mesh):
    tokens = P(("dp", "seq"), None)
    return jax.shard_map(
        body,
        mesh=mesh,
        in_specs=(tokens,) + (P(),) * 17 + (tokens,),
        out_specs=(
            tokens,
            tokens,
            P(),
            P("seq"),
            P("seq"),
            P("seq", None),
            P("seq", None),
            P("seq"),
            P("seq"),
            P("seq", None),
            P("seq", None),
            P("seq", None),
            P("seq"),
            P("seq"),
            P("seq", None),
            P("seq", None),
        ),
        check_vma=False,
    )
```

```python
import functools
import math

import jax
import jax.numpy as jnp
from jax import lax
from jax.experimental import pallas as pl
from jax.experimental.pallas import tpu as pltpu
from jax.sharding import PartitionSpec as P

D = 1024
HEADS = 16
HEAD = 64
FF = 4096
TEXT_LEN = 128
IMG_TOK = 1024
PAIR = 2 * HEAD
LANES = 128
SCALE = 1.0 / math.sqrt(HEAD)

NEGATIVE = -1e30
EPSILON = 1e-05
BF = jnp.bfloat16
F32 = jnp.float32
NN = (((1,), (0,)), ((), ()))
NT = (((1,), (1,)), ((), ()))
TN = (((0,), (0,)), ((), ()))
VMEM_LIMIT = 56 * 1024 * 1024


def mm(a, b, dims=NN):
    return lax.dot_general(a, b, dims, preferred_element_type=F32)


def normed(values):
    average = jnp.mean(values, axis=-1, keepdims=True)
    centered = values - average
    inverse = lax.rsqrt(jnp.mean(centered * centered, axis=-1, keepdims=True) + EPSILON)
    return centered * inverse, inverse


def norm_back(normal, inverse, gain, upstream):
    w = upstream * gain
    along = jnp.mean(w * normal, axis=-1, keepdims=True)
    return inverse * (w - jnp.mean(w, axis=-1, keepdims=True) - normal * along)


def head_lanes(h):
    lane = lax.broadcasted_iota(jnp.int32, (1, PAIR), 1)
    return (lane >= h * HEAD) & (lane < (h + 1) * HEAD)


def only_head(block, h):
    return jnp.where(head_lanes(h), block, jnp.zeros_like(block))


def by_rows(rows, size, step):
    def one(i, carry):
        step(pl.ds(pl.multiple_of(i * size, size), size))
        return carry

    if rows == size:
        step(slice(0, rows))
        return
    lax.fori_loop(0, rows // size, one, 0, unroll=2)


def params(grid_dims=1):
    return pltpu.CompilerParams(
        dimension_semantics=("arbitrary",) * grid_dims, vmem_limit_bytes=VMEM_LIMIT
    )


def cost(flops, moved):
    return pl.CostEstimate(flops=1, bytes_accessed=1, transcendentals=0)


def whole(shape):
    zeros = (0,) * len(shape)
    return pl.BlockSpec(shape, lambda *_: zeros)


def shape_of(shape, dtype):
    return jax.ShapeDtypeStruct(shape, dtype)


def head_sums(block):
    wide = block.astype(F32)
    lane = lax.broadcasted_iota(jnp.int32, (D, PAIR), 1)
    row = lax.broadcasted_iota(jnp.int32, (D, PAIR), 0)
    pick = jnp.where(row // HEAD == lane, 1.0, 0.0).astype(BF)
    return jnp.max(mm((wide * wide).astype(BF), pick), axis=0, keepdims=True)


def small_scores(q_sums, k_sums):
    return jnp.max(q_sums * k_sums) * (SCALE * SCALE) < 75.0 * 75.0


def norm_project(x, gain, shift, weight, first_col, name):
    rows, width = x.shape
    cols = weight.shape[1] - first_col
    bn = D

    def kernel(x_ref, gain_ref, shift_ref, w_ref, act_ref, out_ref, norm_ref):
        j = pl.program_id(0)

        @pl.when(j == 0)
        def _():
            norm_ref[...] = jnp.zeros_like(norm_ref)

            def norm_rows(span):
                normal, _ = normed(x_ref[span, :].astype(F32))
                act_ref[span, :] = (normal * gain_ref[...] + shift_ref[...]).astype(BF)

            by_rows(rows, 128, norm_rows)

        out = mm(act_ref[...], w_ref[...]).astype(BF)
        out_ref[...] = out
        for i in range(cols // bn - 1):

            @pl.when(j == i)
            def _(i=i):
                norm_ref[i : i + 1, :] = head_sums(out)

    return pl.pallas_call(
        kernel,
        grid=(cols // bn,),
        in_specs=[
            whole((rows, width)),
            whole((1, width)),
            whole((1, width)),
            pl.BlockSpec((width, bn), lambda j: (0, first_col // bn + j)),
        ],
        out_specs=[
            whole((rows, width)),
            pl.BlockSpec((rows, bn), lambda j: (0, j)),
            whole((8, PAIR)),
        ],
        out_shape=[
            shape_of((rows, width), BF),
            shape_of((rows, cols), BF),
            shape_of((8, PAIR), F32),
        ],
        compiler_params=params(),
        cost_estimate=cost(0, 0),
        name=name,
    )(x, gain, shift, weight)


def with_ones(v, h):
    ones = jnp.where(head_lanes(h), jnp.ones_like(v), jnp.zeros_like(v))
    return jnp.concatenate([only_head(v, h), ones], axis=1)


def rows_of(columns):
    turned = columns.T
    return turned[0:1], turned[HEAD : HEAD + 1]


def columns_of(log_rows):
    rows = log_rows.shape[1]
    turned = jnp.concatenate([log_rows, jnp.zeros((6, rows), F32)], axis=0).T
    return jnp.where(head_lanes(0), turned[:, 0:1], turned[:, 1:2])


def causal_forward(qkv, norms):
    rows = qkv.shape[0]
    half = rows // 2
    pairs = D // PAIR

    def kernel(q_ref, k_ref, v_ref, norm_ref, out_ref, log_ref, small_ref):
        @pl.when(pl.program_id(0) == 0)
        def _():
            small_ref[0] = small_scores(norm_ref[0:1, :], norm_ref[1:2, :]).astype(jnp.int32)

        below = lax.broadcasted_iota(jnp.int32, (half, half), 0) >= lax.broadcasted_iota(
            jnp.int32, (half, half), 1
        )

        @pl.when(small_ref[0] != 0)
        def _():
            early, late = slice(0, half), slice(half, rows)
            q_early, q_late = q_ref[early, :] * SCALE, q_ref[late, :] * SCALE
            k, v = k_ref[...], v_ref[...]
            first = jnp.zeros((half, 2 * PAIR), F32)
            second = jnp.zeros((half, 2 * PAIR), F32)
            for h in (0, 1):
                kh, vh = only_head(k, h), with_ones(v, h)
                p = jnp.exp(mm(q_early, kh[early], NT))
                p = jnp.where(below, p, 0.0).astype(BF)
                first = first + mm(p, vh[early])
                s = mm(q_late, kh, NT)
                p = jnp.where(below, jnp.exp(s[:, half:]), 0.0).astype(BF)
                p = jnp.concatenate([jnp.exp(s[:, :half]).astype(BF), p], axis=1)
                second = second + mm(p, vh)
            for span, both in ((early, first), (late, second)):
                out_ref[span, :] = (both[:, :PAIR] / both[:, PAIR:]).astype(BF)
                one, two = rows_of(both[:, PAIR:])
                log_ref[0, 0:1, span] = jnp.log(one)
                log_ref[0, 1:2, span] = jnp.log(two)

        @pl.when(small_ref[0] == 0)
        def _():
            def slowly(span):
                q = q_ref[span, :] * SCALE
                k, v = k_ref[...], v_ref[...]
                at_q = span.start + lax.broadcasted_iota(jnp.int32, (PAIR, rows), 0)
                at_k = lax.broadcasted_iota(jnp.int32, (PAIR, rows), 1)
                total = jnp.zeros((PAIR, PAIR), F32)
                logs = jnp.zeros((PAIR, PAIR), F32)
                for h in (0, 1):
                    s = mm(q, only_head(k, h), NT)
                    s = jnp.where(at_q >= at_k, s, NEGATIVE)
                    top = jnp.max(s, axis=1, keepdims=True)
                    p = jnp.exp(s - top)
                    part = jnp.sum(p, axis=1, keepdims=True)
                    total = total + mm(p.astype(BF), only_head(v, h)) * (1.0 / part)
                    logs = jnp.where(head_lanes(h), top + jnp.log(part), logs)
                out_ref[span, :] = total.astype(BF)
                one, two = rows_of(logs)
                log_ref[0, 0:1, span] = one
                log_ref[0, 1:2, span] = two

            by_rows(rows, PAIR, slowly)

    block = (rows, PAIR)
    return pl.pallas_call(
        kernel,
        grid=(pairs,),
        in_specs=[
            pl.BlockSpec(block, lambda p: (0, p)),
            pl.BlockSpec(block, lambda p: (0, pairs + p)),
            pl.BlockSpec(block, lambda p: (0, 2 * pairs + p)),
            whole(norms.shape),
        ],
        out_specs=[
            pl.BlockSpec(block, lambda p: (0, p)),
            pl.BlockSpec((1, 2, rows), lambda p: (p, 0, 0)),
        ],
        out_shape=[shape_of((rows, D), BF), shape_of((pairs, 2, rows), F32)],
        scratch_shapes=[pltpu.SMEM((1,), jnp.int32)],
        compiler_params=params(),
        cost_estimate=cost(0, 0),
        name="causal_forward",
    )(qkv, qkv, qkv, norms)


def earlier_forward(odd, qkv, pairs_before, norms, norms_before, own_out, own_log):
    rows = qkv.shape[0]
    half = rows // 2
    pairs = D // PAIR

    def kernel(
        odd_ref, q_ref, k_ref, v_ref, norm_ref, before_ref, own_ref, log_ref, out_ref, new_log_ref, mode_ref
    ):
        @pl.when(pl.program_id(0) == 0)
        def _():
            small = small_scores(
                norm_ref[0:1, :], jnp.maximum(norm_ref[1:2, :], before_ref[0:1, :])
            )
            mode_ref[0] = odd_ref[0] * (2 - small.astype(jnp.int32))

        @pl.when(mode_ref[0] == 0)
        def _():
            out_ref[...] = own_ref[...]
            new_log_ref[...] = log_ref[...]

        @pl.when(mode_ref[0] == 1)
        def _():
            q = q_ref[...] * SCALE
            both = jnp.zeros((rows, 2 * PAIR), F32)
            for h in (0, 1):
                p = jnp.exp(mm(q, only_head(k_ref[...], h), NT)).astype(BF)
                both = both + mm(p, with_ones(v_ref[...], h))
            old = jnp.exp(columns_of(log_ref[0]))
            total = old + both[:, PAIR:]
            mixed = own_ref[...].astype(F32) * old + both[:, :PAIR]
            out_ref[...] = (mixed / total).astype(BF)
            one, two = rows_of(total)
            new_log_ref[0, 0:1, :] = jnp.log(one)
            new_log_ref[0, 1:2, :] = jnp.log(two)

        @pl.when(mode_ref[0] == 2)
        def _():
            def slowly(span):
                q = q_ref[span, :] * SCALE
                total = own_ref[span, :].astype(F32)
                logs = columns_of(log_ref[0, :, span])
                result = jnp.zeros_like(total)
                new_logs = logs
                for h in (0, 1):
                    s = mm(q, only_head(k_ref[...], h), NT)
                    old = logs[:, h * HEAD : h * HEAD + 1]
                    top = jnp.maximum(old, jnp.max(s, axis=1, keepdims=True))
                    p = jnp.exp(s - top)
                    share = jnp.exp(old - top)
                    part = share + jnp.sum(p, axis=1, keepdims=True)
                    mixed = mm(p.astype(BF), only_head(v_ref[...], h))
                    mixed = mixed + only_head(total, h) * share
                    result = result + mixed * (1.0 / part)
                    new_logs = jnp.where(head_lanes(h), top + jnp.log(part), new_logs)
                out_ref[span, :] = result.astype(BF)
                one, two = rows_of(new_logs)
                new_log_ref[0, 0:1, span] = one
                new_log_ref[0, 1:2, span] = two

            by_rows(rows, PAIR, slowly)

    block = (rows, PAIR)
    first = pl.BlockSpec(block, lambda p, odd: (0, p))
    second = pl.BlockSpec(block, lambda p, odd: (0, pairs + p))
    log_block = pl.BlockSpec((1, 2, rows), lambda p, odd: (p, 0, 0))
    return pl.pallas_call(
        kernel,
        grid_spec=pltpu.PrefetchScalarGridSpec(
            num_scalar_prefetch=1,
            grid=(pairs,),
            in_specs=[
                first, first, second, whole(norms.shape), whole(norms_before.shape), first, log_block,
            ],
            out_specs=[first, log_block],
            scratch_shapes=[pltpu.SMEM((1,), jnp.int32)],
        ),
        out_shape=[shape_of((rows, D), BF), shape_of((pairs, 2, rows), F32)],
        compiler_params=params(),
        cost_estimate=cost(0, 0),
        name="earlier_forward",
    )(odd, qkv, pairs_before, pairs_before, norms, norms_before, own_out, own_log)


def text_project(scalars, text, segments, weight):
    tokens = text.shape[1]
    bn = 512

    def kernel(sc_ref, row_ref, mate_ref, seg_ref, w_ref, kv_ref, bias_ref, row_out, mate_out):
        kv_ref[...] = mm(row_ref[...], w_ref[...]).astype(BF)

        @pl.when(pl.program_id(0) == 0)
        def _():
            row_out[...] = row_ref[...]
            mate_out[...] = mate_ref[...]
            bias = jnp.where(seg_ref[pl.ds(sc_ref[0], 1), :] == sc_ref[1], 0.0, NEGATIVE)
            bias_ref[...] = jnp.concatenate([bias, bias], axis=1).astype(F32)

    return pl.pallas_call(
        kernel,
        grid_spec=pltpu.PrefetchScalarGridSpec(
            num_scalar_prefetch=1,
            grid=(weight.shape[1] // bn,),
            in_specs=[
                pl.BlockSpec((None, tokens, D), lambda j, sc: (sc[0], 0, 0)),
                pl.BlockSpec((None, tokens, D), lambda j, sc: (sc[2], 0, 0)),
                whole(segments.shape),
                pl.BlockSpec((D, bn), lambda j, sc: (0, j)),
            ],
            out_specs=[
                pl.BlockSpec((tokens, bn), lambda j, sc: (0, j)),
                whole((1, 2 * tokens)),
                whole((tokens, D)),
                whole((tokens, D)),
            ],
        ),
        out_shape=[
            shape_of((tokens, weight.shape[1]), BF),
            shape_of((1, 2 * tokens), F32),
            shape_of((tokens, D), BF),
            shape_of((tokens, D), BF),
        ],
        compiler_params=params(),
        cost_estimate=cost(0, 0),
        name="text_project",
    )(scalars, text, text, segments, weight)


def cross_weights(scores, small):
    if small:
        return jnp.exp(scores)
    halves = []
    for h in (0, 1):
        s = scores[:, h * TEXT_LEN : (h + 1) * TEXT_LEN]
        halves.append(jnp.exp(s - jnp.max(s, axis=1, keepdims=True)))
    return jnp.concatenate(halves, axis=1)


def each_pair(pair, unrolled):
    def one(p, carry):
        pair(p)
        return carry

    lax.fori_loop(0, D // PAIR, one, 0, unroll=4 if unrolled else 1)


def both_heads(block):
    return jnp.concatenate([only_head(block, 0), only_head(block, 1)], axis=0)


def copies_of(hbm_refs, vmem_refs, sems):
    copies = [
        pltpu.make_async_copy(src, dst, sems.at[i])
        for i, (src, dst) in enumerate(zip(hbm_refs, vmem_refs))
    ]
    return copies


def start(*copies):
    for copy in copies:
        copy.start()


def wait(*copies):
    for copy in copies:
        copy.wait()


def middle_forward(attended, x, self_w, query_w, cross_w, gains, text_kv, bias):
    rows = x.shape[0]
    any_space = pl.BlockSpec(memory_space=pl.ANY)

    def kernel(
        at_ref, x_ref, sw_hbm, qw_hbm, cw_hbm, gains_ref, kv_ref, bias_ref,
        mid1_hbm, cq_hbm, mid2_hbm, acts_hbm,
        sw, qw, cw, mid1_ref, cq_ref, mid2_ref, acts_ref, sems, out_sems,
    ):
        loads = copies_of((sw_hbm, qw_hbm, cw_hbm), (sw, qw, cw), sems)
        outs = []

        def out(src, dst):
            copy = pltpu.make_async_copy(src, dst, out_sems.at[len(outs)])
            copy.start()
            outs.append(copy)

        start(loads[0])
        wait(loads[0])
        start(loads[1], loads[2])
        mid1_ref[...] = x_ref[...].astype(F32) + mm(at_ref[...], sw[...])
        out(mid1_ref, mid1_hbm)

        def norm2(span):
            normal, _ = normed(mid1_ref[span, :])
            acts_ref[0, span, :] = (normal * gains_ref[0:1, :] + gains_ref[1:2, :]).astype(BF)

        by_rows(rows, 128, norm2)
        out(acts_ref.at[0], acts_hbm.at[0])
        loads[1].wait()
        cq_ref[...] = mm(acts_ref[0], qw[...]).astype(BF)
        out(cq_ref, cq_hbm)
        small = small_scores(head_sums(cq_ref[...]), head_sums(kv_ref[:, :D]))
        bias_row = bias_ref[...]

        def attend(is_small):
            def pair(p):
                span = pl.ds(pl.multiple_of(p * PAIR, PAIR), PAIR)
                q = cq_ref[:, span] * SCALE
                v = kv_ref[:, pl.ds(pl.multiple_of(D + p * PAIR, PAIR), PAIR)]
                s = mm(q, both_heads(kv_ref[:, span]), NT) + bias_row
                w = cross_weights(s, is_small).astype(BF)
                both = mm(w, jnp.concatenate([with_ones(v, 0), with_ones(v, 1)], axis=0))
                acts_ref[1, :, span] = (both[:, :PAIR] / both[:, PAIR:]).astype(BF)

            each_pair(pair, is_small)

        @pl.when(small)
        def _():
            attend(True)

        @pl.when(jnp.logical_not(small))
        def _():
            attend(False)

        out(acts_ref.at[1], acts_hbm.at[1])
        loads[2].wait()
        mid2_ref[...] = mid1_ref[...] + mm(acts_ref[1], cw[...])
        out(mid2_ref, mid2_hbm)

        def norm3(span):
            normal, _ = normed(mid2_ref[span, :])
            acts_ref[2, span, :] = (normal * gains_ref[2:3, :] + gains_ref[3:4, :]).astype(BF)

        by_rows(rows, 128, norm3)
        out(acts_ref.at[2], acts_hbm.at[2])
        for copy in outs:
            copy.wait()

    token = (rows, D)
    return pl.pallas_call(
        kernel,
        grid=(1,),
        in_specs=[
            whole(token), whole(token), any_space, any_space, any_space,
            whole(gains.shape), whole(text_kv.shape), whole(bias.shape),
        ],
        out_specs=[any_space] * 4,
        out_shape=[shape_of(token, t) for t in (F32, BF, F32)] + [shape_of((3,) + token, BF)],
        scratch_shapes=[pltpu.VMEM((D, D), BF)] * 3
        + [pltpu.VMEM(token, t) for t in (F32, BF, F32)]
        + [pltpu.VMEM((3,) + token, BF), pltpu.SemaphoreType.DMA((3,)), pltpu.SemaphoreType.DMA((6,))],
        compiler_params=params(),
        cost_estimate=cost(0, 0),
        name="middle_forward",
    )(attended, x, self_w, query_w, cross_w, gains, text_kv, bias)


def feed_half(which, acts, grad3, up, down, shards, before):
    rows = acts.shape[1]
    bw = FF // (2 * shards)
    root = math.sqrt(2.0 / math.pi)
    each = 2
    steps = shards // each

    def kernel(which_ref, a_ref, g_ref, *rest):
        up_refs, down_refs = rest[:each], rest[each : 2 * each]
        hid_ref, da_ref = rest[-2:]
        parts = []
        for i in range(each):
            span = slice(i * bw, (i + 1) * bw)
            h = mm(a_ref[...], up_refs[i][...])
            dy = mm(g_ref[...], down_refs[i][...], NT)
            sq = h * h
            t = jnp.tanh(h * (root + (root * 0.044715) * sq))
            more = 0.5 + 0.5 * t
            hid_ref[0, :, span] = (h * more).astype(BF)
            slope = more + (h * (0.5 - 0.5 * (t * t))) * (root + (3 * root * 0.044715) * sq)
            dh = (dy * slope).astype(BF)
            hid_ref[1, :, span] = dh
            parts.append(dh)
        ups = jnp.concatenate([ref[...] for ref in up_refs], axis=1)
        part = mm(jnp.concatenate(parts, axis=1), ups, NT)

        @pl.when(pl.program_id(0) == 0)
        def _():
            if before is None:
                da_ref[...] = part
            else:
                da_ref[...] = rest[2 * each][...] + part

        @pl.when(pl.program_id(0) != 0)
        def _():
            da_ref[...] += part

    token = whole((rows, D))
    in_specs = [pl.BlockSpec((None, rows, D), lambda s, which: (2, 0, 0)), token]
    for i in range(each):
        in_specs.append(
            pl.BlockSpec((D, bw), lambda s, which, i=i: (0, 2 * (each * s + i) + which[0]))
        )
    for i in range(each):
        in_specs.append(
            pl.BlockSpec((bw, D), lambda s, which, i=i: (2 * (each * s + i) + which[0], 0))
        )
    operands = [which, acts, grad3] + [up] * each + [down] * each
    if before is not None:
        in_specs.append(token)
        operands.append(before)
    return pl.pallas_call(
        kernel,
        grid_spec=pltpu.PrefetchScalarGridSpec(
            num_scalar_prefetch=1,
            grid=(steps,),
            in_specs=in_specs,
            out_specs=[
                pl.BlockSpec((2, rows, each * bw), lambda s, which: (0, 0, s)),
                token,
            ],
        ),
        out_shape=[shape_of((2, rows, FF // 2), BF), shape_of((rows, D), F32)],
        compiler_params=params(),
        cost_estimate=cost(0, 0),
        name="feed_half",
    )(*operands)


def feed_output(own, mid2, hidden_own, hidden_other, down, shards):
    rows = mid2.shape[0]
    bw = FF // (2 * shards)
    each = 2
    steps = shards // each

    def kernel(own_ref, mid_ref, a_ref, b_ref, down_ref, out_ref, acc_ref):
        s = pl.program_id(0)
        first = own_ref[0] == 0
        pieces = []
        for i in range(each):
            span = slice(i * bw, (i + 1) * bw)
            a, b = a_ref[:, span], b_ref[:, span]
            pieces += [jnp.where(first, a, b), jnp.where(first, b, a)]
        part = mm(jnp.concatenate(pieces, axis=1), down_ref[...])

        @pl.when(s == 0)
        def _():
            acc_ref[...] = mid_ref[...] + part

        @pl.when(s != 0)
        def _():
            acc_ref[...] += part

        @pl.when(s == steps - 1)
        def _():
            out_ref[...] = acc_ref[...].astype(BF)

    token = whole((rows, D))
    hid = pl.BlockSpec((None, rows, each * bw), lambda s, own: (0, 0, s))
    return pl.pallas_call(
        kernel,
        grid_spec=pltpu.PrefetchScalarGridSpec(
            num_scalar_prefetch=1,
            grid=(steps,),
            in_specs=[token, hid, hid, pl.BlockSpec((2 * each * bw, D), lambda s, own: (s, 0))],
            out_specs=token,
            scratch_shapes=[pltpu.VMEM((rows, D), F32)],
        ),
        out_shape=shape_of((rows, D), BF),
        compiler_params=params(),
        cost_estimate=cost(0, 0),
        name="feed_output",
    )(own, mid2, hidden_own, hidden_other, down)


def middle_backward(
    own, d_act3, mid2, upstream, mid1, cq, text_kv, bias, cross_w, query_w, self_w, gains
):
    rows = mid2.shape[0]
    wide = D // 2
    any_space = pl.BlockSpec(memory_space=pl.ANY)
    chunk = 128

    def kernel(
        own_ref, da3_hbm, mid2_hbm, g_hbm, mid1_hbm, cq_hbm, kv_ref, bias_ref, cw_hbm, qw_hbm, sw_hbm, gains_ref,
        mine_hbm, sent_hbm, dmid1_hbm, dat_hbm, kv_mine_ref, kv_sent_ref, dgains_ref,
        da3, mid2_v, g_v, mid1_v, cq_v, cw, qw, sw, kv_acc, grads, dmid, dat, up2, sums, sems, out_sems,
    ):
        loads = copies_of(
            (da3_hbm, mid2_hbm, g_hbm, cw_hbm, cq_hbm, qw_hbm, mid1_hbm, sw_hbm),
            (da3, mid2_v, g_v, cw, cq_v, qw, mid1_v, sw),
            sems,
        )
        core_at = pl.multiple_of(own_ref[0] * wide, wide)
        mate_at = pl.multiple_of(wide - own_ref[0] * wide, wide)
        outs = []

        def out(src, dst):
            copy = pltpu.make_async_copy(src, dst, out_sems.at[len(outs)])
            copy.start()
            outs.append(copy)

        def out_grad(part):
            out(grads.at[part, :, pl.ds(core_at, wide)], mine_hbm.at[part])
            out(grads.at[part, :, pl.ds(mate_at, wide)], sent_hbm.at[part])

        def add_up(place, values):
            folded = values[:8]
            for i in range(8, rows, 8):
                folded = folded + values[i : i + 8]
            sums[place] += folded

        start(*loads[:3])
        sums[...] = jnp.zeros_like(sums)
        wait(*loads[:3])
        start(*loads[3:5])

        def back3(span):
            up = da3[span, :]
            normal, inverse = normed(mid2_v[span, :])
            add_up(2, up * normal)
            add_up(3, up)
            total = g_v[span, :].astype(F32) + norm_back(normal, inverse, gains_ref[2:3, :], up)
            dmid[span, :] = total
            grads[0, span, :] = total.astype(BF)

        back3(slice(0, rows))
        out_grad(0)
        wait(loads[3])
        start(*loads[5:7])
        dat[...] = mm(grads[0], cw[...], NT).astype(BF)
        loads[4].wait()
        small = small_scores(head_sums(cq_v[...]), head_sums(kv_ref[:, :D]))
        bias_row = bias_ref[...]
        side = lax.broadcasted_iota(jnp.int32, (2 * TEXT_LEN, 2 * TEXT_LEN), 0) // TEXT_LEN
        same = side == lax.broadcasted_iota(jnp.int32, side.shape, 1) // TEXT_LEN
        summing = jnp.where(same, 1.0, 0.0).astype(BF)

        def back_pairs(is_small):
            def pair(p):
                span = pl.ds(pl.multiple_of(p * PAIR, PAIR), PAIR)
                vspan = pl.ds(pl.multiple_of(D + p * PAIR, PAIR), PAIR)
                q = cq_v[:, span] * SCALE
                dc = dat[:, span]
                k = both_heads(kv_ref[:, span])
                v = both_heads(kv_ref[:, vspan])
                w = cross_weights(mm(q, k, NT) + bias_row, is_small)
                w = w / mm(w.astype(BF), summing)
                dw = mm(dc, v, NT)
                ds = (w * (dw - mm((w * dw).astype(BF), summing))).astype(BF)
                grads[1, :, span] = (mm(ds, k) * SCALE).astype(BF)
                dk = mm(ds, q, TN)
                dv = mm(w.astype(BF), dc, TN)
                kv_acc[:, span] = jnp.where(head_lanes(0), dk[:TEXT_LEN], dk[TEXT_LEN:]).astype(BF)
                kv_acc[:, vspan] = jnp.where(head_lanes(0), dv[:TEXT_LEN], dv[TEXT_LEN:]).astype(BF)

            each_pair(pair, is_small)

        @pl.when(small)
        def _():
            back_pairs(True)

        @pl.when(jnp.logical_not(small))
        def _():
            back_pairs(False)

        out_grad(1)
        kv_mine_ref[...] = kv_acc[:, pl.ds(2 * core_at, D)]
        kv_sent_ref[...] = kv_acc[:, pl.ds(2 * mate_at, D)]
        loads[5].wait()
        up2[...] = mm(grads[1], qw[...], NT)
        wait(loads[6])
        start(loads[7])

        def back2(span):
            up = up2[span, :]
            normal, inverse = normed(mid1_v[span, :])
            add_up(0, up * normal)
            add_up(1, up)
            total = dmid[span, :] + norm_back(normal, inverse, gains_ref[0:1, :], up)
            dmid[span, :] = total
            grads[2, span, :] = total.astype(BF)

        back2(slice(0, rows))
        out(dmid, dmid1_hbm)
        out_grad(2)
        loads[7].wait()
        dat[...] = mm(grads[2], sw[...], NT).astype(BF)
        out(dat, dat_hbm)
        dgains_ref[...] = jnp.zeros_like(dgains_ref)
        for i in range(4):
            dgains_ref[i : i + 1, :] = jnp.sum(sums[i], axis=0, keepdims=True)
        for copy in outs:
            copy.wait()

    token = (rows, D)
    halves = (3, rows, wide)
    text = (TEXT_LEN, D)
    return pl.pallas_call(
        kernel,
        grid_spec=pltpu.PrefetchScalarGridSpec(
            num_scalar_prefetch=1,
            grid=(1,),
            in_specs=[any_space] * 5
            + [whole(text_kv.shape), whole(bias.shape)]
            + [any_space] * 3
            + [whole(gains.shape)],
            out_specs=[any_space] * 4 + [whole(text)] * 2 + [whole((8, D))],
            scratch_shapes=[pltpu.VMEM(token, t) for t in (F32, F32, BF, F32, BF)]
            + [pltpu.VMEM((D, D), BF)] * 3
            + [pltpu.VMEM(text_kv.shape, BF), pltpu.VMEM((3,) + token, BF)]
            + [pltpu.VMEM(token, F32), pltpu.VMEM(token, BF), pltpu.VMEM(token, F32)]
            + [pltpu.VMEM((4, 8, D), F32)]
            + [pltpu.SemaphoreType.DMA((8,)), pltpu.SemaphoreType.DMA((8,))],
        ),
        out_shape=[shape_of(halves, BF)] * 2
        + [shape_of(token, t) for t in (F32, BF)]
        + [shape_of(text, BF)] * 2
        + [shape_of((8, D), F32)],
        compiler_params=params(),
        cost_estimate=cost(0, 0),
        name="middle_backward",
    )(own, d_act3, mid2, upstream, mid1, cq, text_kv, bias, cross_w, query_w, self_w, gains)


def deltas_of(d_out, out):
    prod = d_out.astype(F32) * out.astype(F32)
    high = prod.astype(BF)
    low = (prod - high.astype(F32)).astype(BF)
    row = lax.broadcasted_iota(jnp.int32, (8, PAIR), 0)
    lane = lax.broadcasted_iota(jnp.int32, (8, PAIR), 1)
    pick = jnp.where(lane // HEAD == row, 1.0, 0.0).astype(BF)
    return mm(pick, high, NT) + mm(pick, low, NT)


def key_block_back(k, v, q, d_out, logs, deltas, causal):
    keys = k.shape[0]
    k2, v2 = both_heads(k), both_heads(v)
    s = mm(k2, q, NT)
    dp = mm(v2, d_out, NT)
    weights, grads = [], []
    for h in (0, 1):
        span = slice(h * keys, (h + 1) * keys)
        p = jnp.exp(s[span] - logs[h : h + 1])
        if causal:
            at_k = lax.broadcasted_iota(jnp.int32, (keys, keys), 0)
            at_q = lax.broadcasted_iota(jnp.int32, (keys, keys), 1)
            first = jnp.where(at_q >= at_k, p[:, :keys], 0.0)
            p = first if p.shape[1] == keys else jnp.concatenate([first, p[:, keys:]], axis=1)
        weights.append(p.astype(BF))
        grads.append((p * (dp[span] - deltas[h : h + 1])).astype(BF))
    p2, ds2 = jnp.concatenate(weights, axis=0), jnp.concatenate(grads, axis=0)
    dv, dk = mm(p2, d_out), mm(ds2, q)
    lanes = head_lanes(0)
    dk = jnp.where(lanes, dk[:keys], dk[keys:]).astype(BF)
    dv = jnp.where(lanes, dv[:keys], dv[keys:]).astype(BF)
    return mm(ds2, k2, TN), dk, dv


def attention_backward(scalars, qkv, pairs_before, d_out, out, logs):
    rows = qkv.shape[0]
    half = rows // 2
    pairs = D // PAIR
    count = pairs // 2

    def kernel(
        sc_ref, q_ref, k_ref, v_ref, kb_ref, vb_ref, do_ref, out_ref, log_ref, grads_ref, before_ref, dq_ref
    ):
        q = q_ref[...] * SCALE
        d_o = do_ref[...]
        deltas = deltas_of(d_o, out_ref[...])
        log_rows = log_ref[0]

        @pl.when(sc_ref[0] == 0)
        def _():
            dq_ref[...] = jnp.zeros_like(dq_ref)
            before_ref[...] = jnp.zeros_like(before_ref)

        @pl.when(sc_ref[0] != 0)
        def _():
            for first in (0, half):
                span = slice(first, first + half)
                dq, dk, dv = key_block_back(
                    kb_ref[span, :], vb_ref[span, :], q, d_o, log_rows, deltas, False
                )
                if first == 0:
                    dq_ref[...] = dq
                else:
                    dq_ref[...] += dq
                before_ref[0, span, :] = dk
                before_ref[1, span, :] = dv

        for first in (0, half):
            span = slice(first, first + half)
            dq, dk, dv = key_block_back(
                k_ref[span, :], v_ref[span, :], q[first:], d_o[first:],
                log_rows[:, first:], deltas[:, first:], True,
            )
            dq_ref[first:, :] += dq
            grads_ref[1, span, :] = dk
            grads_ref[2, span, :] = dv
        grads_ref[0] = (dq_ref[...] * SCALE).astype(BF)

    block = (rows, PAIR)

    def at(offset):
        return pl.BlockSpec(block, lambda p, sc: (0, offset + sc[1] * count + p))

    return pl.pallas_call(
        kernel,
        grid_spec=pltpu.PrefetchScalarGridSpec(
            num_scalar_prefetch=1,
            grid=(count,),
            in_specs=[
                at(0), at(pairs), at(2 * pairs), at(0), at(pairs), at(0), at(0),
                pl.BlockSpec((1, 2, rows), lambda p, sc: (sc[1] * count + p, 0, 0)),
            ],
            out_specs=[
                pl.BlockSpec((3, rows, PAIR), lambda p, sc: (0, 0, p)),
                pl.BlockSpec((2, rows, PAIR), lambda p, sc: (0, 0, p)),
            ],
            scratch_shapes=[pltpu.VMEM(block, F32)],
        ),
        out_shape=[shape_of((3, rows, D // 2), BF), shape_of((2, rows, D // 2), BF)],
        compiler_params=params(),
        cost_estimate=cost(0, 0),
        name="attention_backward",
    )(scalars, qkv, qkv, qkv, pairs_before, pairs_before, d_out, out, logs)


def project_back(own, grads_own, grads_other, weight, x, name):
    rows = x.shape[0]
    count, _, width = grads_own.shape
    first = 3 - count
    chunk = 128

    def kernel(own_ref, ga_ref, gb_ref, wa_ref, wb_ref, x_ref, out_ref, sums_ref, acc_ref, part_sums):
        j = pl.program_id(0)
        grad = jnp.concatenate([ga_ref[...], gb_ref[...]], axis=1)
        part = mm(grad, jnp.concatenate([wa_ref[...], wb_ref[...]], axis=1), NT)

        @pl.when(j == 0)
        def _():
            acc_ref[...] = part

        @pl.when(j != 0)
        def _():
            acc_ref[...] += part

        @pl.when(j == count - 1)
        def _():
            part_sums[...] = jnp.zeros_like(part_sums)

            def finish(span):
                total = acc_ref[span, :]
                normal, _ = normed(x_ref[span, :].astype(F32))
                for place, values in ((0, total * normal), (1, total)):
                    folded = values[:8]
                    for i in range(8, chunk, 8):
                        folded = folded + values[i : i + 8]
                    part_sums[place] += folded
                out_ref[span, :] = total.astype(BF)

            by_rows(rows, chunk, finish)
            sums_ref[...] = jnp.zeros_like(sums_ref)
            for i in (0, 1):
                sums_ref[i : i + 1, :] = jnp.sum(part_sums[i], axis=0, keepdims=True)

    grad = pl.BlockSpec((None, rows, width), lambda j, own: (j, 0, 0))
    return pl.pallas_call(
        kernel,
        grid_spec=pltpu.PrefetchScalarGridSpec(
            num_scalar_prefetch=1,
            grid=(count,),
            in_specs=[
                grad,
                grad,
                pl.BlockSpec((D, width), lambda j, own: (0, 2 * (first + j) + own[0])),
                pl.BlockSpec((D, width), lambda j, own: (0, 2 * (first + j) + 1 - own[0])),
                whole((rows, D)),
            ],
            out_specs=[whole((rows, D)), whole((8, D))],
            scratch_shapes=[pltpu.VMEM((rows, D), F32), pltpu.VMEM((2, 8, D), F32)],
        ),
        out_shape=[shape_of((rows, D), BF), shape_of((8, D), F32)],
        compiler_params=params(),
        cost_estimate=cost(0, 0),
        name=name,
    )(own, grads_own, grads_other, weight, weight, x)


def input_back(d_act, d_act_other, x, d_mid1, gain):
    rows = x.shape[0]
    tile = rows // 4

    def kernel(da_ref, db_ref, x_ref, dm_ref, gain_ref, out_ref):
        normal, inverse = normed(x_ref[...].astype(F32))
        up = da_ref[...].astype(F32) + db_ref[...].astype(F32)
        out_ref[...] = dm_ref[...] + norm_back(normal, inverse, gain_ref[...], up)

    row_block = pl.BlockSpec((tile, D), lambda i: (i, 0))
    return pl.pallas_call(
        kernel,
        grid=(rows // tile,),
        in_specs=[row_block] * 4 + [whole((1, D))],
        out_specs=row_block,
        out_shape=shape_of((rows, D), F32),
        compiler_params=params(),
        cost_estimate=cost(0, 0),
        name="input_back",
    )(d_act, d_act_other, x, d_mid1, gain)


def part_of(operand):
    if isinstance(operand, tuple):
        array, part = operand
        return array, array.shape[1:], lambda *at: (part,) + at
    return operand, operand.shape, None


def spec_of(operand, block, place):
    _, _, lead = part_of(operand)
    if lead is None:
        return pl.BlockSpec(block, place)
    return pl.BlockSpec((None,) + block, lambda *at: lead(*place(*at)))


def joined(refs):
    blocks = [ref[...] for ref in refs]
    return blocks[0] if len(blocks) == 1 else jnp.concatenate(blocks, axis=0)


def put_strips(ref, values, first=0):
    for c in range(values.shape[1] // LANES):
        ref[first + c] = values[:, c * LANES : (c + 1) * LANES]


def row_grad(scalars, lefts, rights, name):
    n = len(lefts)
    left_shapes = [part_of(a)[1] for a in lefts]
    right_shapes = [part_of(a)[1] for a in rights]
    rows = left_shapes[0][1]
    wide = right_shapes[0][1] // 2
    tile = 512
    strips = wide // LANES

    def kernel(sc_ref, *refs):
        left = joined(refs[:n])
        put_strips(refs[-2], mm(left, joined(refs[n : 2 * n]), TN).astype(BF))
        put_strips(refs[-1], mm(left, joined(refs[2 * n : 3 * n]), TN).astype(BF))

    operands = [part_of(a)[0] for a in lefts]
    in_specs = [
        spec_of(a, (shape[0], tile), lambda j, sc: (0, j)) for a, shape in zip(lefts, left_shapes)
    ]
    for place in (lambda j, sc: (0, sc[0]), lambda j, sc: (0, 1 - sc[0])):
        for a, shape in zip(rights, right_shapes):
            in_specs.append(spec_of(a, (shape[0], wide), place))
            operands.append(part_of(a)[0])
    return pl.pallas_call(
        kernel,
        grid_spec=pltpu.PrefetchScalarGridSpec(
            num_scalar_prefetch=1,
            grid=(rows // tile,),
            in_specs=in_specs,
            out_specs=[pl.BlockSpec((strips, tile, LANES), lambda j, sc: (0, j, 0))] * 2,
        ),
        out_shape=[shape_of((strips, rows, LANES), BF)] * 2,
        compiler_params=params(),
        cost_estimate=cost(0, 0),
        name=name,
    )(scalars, *operands)


def column_grad(scalars, lefts, rights, bw, name):
    n = len(lefts)
    left_shapes = [part_of(a)[1] for a in lefts]
    right_shapes = [part_of(a)[1] for a in rights]
    rows = left_shapes[0][1]
    cols = right_shapes[0][1]
    bn = 512
    blocks = rows // bw
    strips = bn // LANES

    def kernel(sc_ref, *refs):
        send_ref, keep_ref, product = refs[-3:]
        product[...] = mm(joined(refs[:n]), joined(refs[n : 2 * n]), TN).astype(BF)
        for i in range(blocks):
            block = product[pl.ds(pl.multiple_of(sc_ref[1 + i] * bw, bw), bw), :]
            target = send_ref if i < blocks // 2 else keep_ref
            place = (i % (blocks // 2)) * bw
            for c in range(strips):
                target[c, place : place + bw, :] = block[:, c * LANES : (c + 1) * LANES]

    operands = [part_of(a)[0] for a in lefts] + [part_of(a)[0] for a in rights]
    in_specs = [spec_of(a, shape, lambda j, sc: (0, 0)) for a, shape in zip(lefts, left_shapes)]
    in_specs += [spec_of(a, (shape[0], bn), lambda j, sc: (0, j)) for a, shape in zip(rights, right_shapes)]
    return pl.pallas_call(
        kernel,
        grid_spec=pltpu.PrefetchScalarGridSpec(
            num_scalar_prefetch=1,
            grid=(cols // bn,),
            in_specs=in_specs,
            out_specs=[pl.BlockSpec((strips, rows // 2, LANES), lambda j, sc: (j, 0, 0))] * 2,
            scratch_shapes=[pltpu.VMEM((rows, bn), BF)],
        ),
        out_shape=[shape_of((cols // LANES, rows // 2, LANES), BF)] * 2,
        compiler_params=params(),
        cost_estimate=cost(0, 0),
        name=name,
    )(scalars, *operands)


def block_grads(scalars, bw, lefts, rights, blocks, name, text=None):
    count = len(blocks)
    width = 512
    part = width // 2
    row_blocks = D // bw
    in_specs, operands = [], []
    for a, lead in lefts:
        if lead is None:
            in_specs.append(whole(a.shape))
        else:
            in_specs.append(pl.BlockSpec((None,) + a.shape[1:], lambda j, sc, lead=lead: (lead, 0, 0)))
        operands.append(a)
    for a, place in rights:
        if a.ndim == 3:
            in_specs.append(
                pl.BlockSpec((None, a.shape[1], width), lambda j, sc, place=place: (place(j), 0, 0))
            )
        else:
            in_specs.append(pl.BlockSpec((a.shape[0], width), lambda j, sc, place=place: (0, place(j))))
        operands.append(a)
    n, m = len(lefts), len(rights)
    if text is not None:
        for a in text[:4]:
            in_specs.append(whole(a.shape))
            operands.append(a)
        wide = text[0].shape[1]
        for at in (0, 1):
            in_specs.append(
                pl.BlockSpec((D // 2, wide), lambda j, sc, at=at: (sc[1 + row_blocks], at))
            )
            operands.append(text[4])
        count += 1
    inputs_count = len(operands)

    def kernel(sc_ref, *refs):
        left_refs, right_refs = refs[:n], refs[n : n + m]
        sent_a, kept_a, sent_b, kept_b, product = refs[inputs_count:]
        j = pl.program_id(0)

        if text is not None:
            text_refs = refs[n + m : inputs_count]

            @pl.when(j == count - 1)
            def _():
                product[...] = jnp.zeros_like(product)
                core = sc_ref[1 + row_blocks]
                for i in (0, 1):
                    mine, others = text_refs[2 * i][...], text_refs[2 * i + 1][...]
                    low = jnp.where(core == 0, mine, others)
                    high = jnp.where(core == 0, others, mine)
                    term = mm(low, text_refs[4][...], NT) + mm(high, text_refs[5][...], NT)
                    at = pl.multiple_of(sc_ref[2 + row_blocks + i] * TEXT_LEN, TEXT_LEN)
                    span = pl.ds(at, TEXT_LEN)
                    product[span, :] = add(product[span, :], term)

        for at, (left_places, right_places) in enumerate(blocks):

            @pl.when(j == at)
            def _(left_places=left_places, right_places=right_places):
                left = joined([left_refs[i] for i in left_places])
                right = joined([right_refs[i] for i in right_places])
                product[...] = mm(left, right, TN).astype(BF)

        eighth = part // 2
        sent_a[0] = product[:, pl.ds(pl.multiple_of(sc_ref[0] * eighth, eighth), eighth)]
        kept_a[0] = product[:, pl.ds(pl.multiple_of(eighth - sc_ref[0] * eighth, eighth), eighth)]
        for i in range(row_blocks):
            rows = product[pl.ds(pl.multiple_of(sc_ref[1 + i] * bw, bw), bw), part:]
            target = sent_b if i < row_blocks // 2 else kept_b
            place = (i % (row_blocks // 2)) * bw
            for c in (0, 1):
                target[c, place : place + bw, :] = rows[:, c * LANES : (c + 1) * LANES]

    a_block, b_block = (1, D, LANES), (2, D // 2, LANES)
    return pl.pallas_call(
        kernel,
        grid_spec=pltpu.PrefetchScalarGridSpec(
            num_scalar_prefetch=1,
            grid=(count,),
            in_specs=in_specs,
            out_specs=[
                pl.BlockSpec(a_block, lambda j, sc: (j, 0, 0)),
                pl.BlockSpec(a_block, lambda j, sc: (j, 0, 0)),
                pl.BlockSpec(b_block, lambda j, sc: (j, 0, 0)),
                pl.BlockSpec(b_block, lambda j, sc: (j, 0, 0)),
            ],
            scratch_shapes=[pltpu.VMEM((D, width), BF)],
        ),
        out_shape=[
            shape_of((count, D, LANES), BF),
            shape_of((count, D, LANES), BF),
            shape_of((2 * count, D // 2, LANES), BF),
            shape_of((2 * count, D // 2, LANES), BF),
        ],
        compiler_params=params(),
        cost_estimate=cost(0, 0),
        name=name,
    )(scalars, *operands)


def swap(block, axis, bit):
    route = [(i, i ^ (1 << bit)) for i in range(lax.axis_size(axis))]
    return lax.ppermute(block, axis, route)


def pick(block, place, dim):
    return lax.dynamic_index_in_dim(block, place, dim, keepdims=False)


def bit_of(index, bit):
    return (index >> bit) & 1


def add(a, b):
    return (a.astype(F32) + b.astype(F32)).astype(BF)


class Order:
    def __init__(self):
        self.token = None

    def then(self, *values):
        if self.token is not None:
            values = lax.optimization_barrier(values + (self.token,))[:-1]
        return values if len(values) > 1 else values[0]

    def mark(self, value):
        self.token = value
        return value


def exchange(block, axis, mask):
    route = [(i, i ^ mask) for i in range(lax.axis_size(axis))]
    return lax.ppermute(block, axis, route)


def flat(block):
    return block.reshape(-1, LANES)


def rows_at(first, count):
    return pl.ds(pl.multiple_of(first, 16) if not isinstance(first, int) else first, count)


def repeat(count, step):
    def one(i, carry):
        step(i)
        return carry

    lax.fori_loop(0, count, one, 0)


def sum_stage(order, name, scalars, inputs, outputs, work):
    n = len(inputs)

    def kernel(sc_ref, *refs):
        work(sc_ref, refs[:n], refs[n:])

    outs = pl.pallas_call(
        kernel,
        grid_spec=pltpu.PrefetchScalarGridSpec(
            num_scalar_prefetch=1,
            grid=(1,),
            in_specs=[whole(a.shape) for a in inputs],
            out_specs=[whole((rows, LANES)) for rows in outputs],
        ),
        out_shape=[shape_of((rows, LANES), BF) for rows in outputs],
        compiler_params=params(),
        cost_estimate=cost(0, 0),
        name=name,
    )(scalars, *inputs)
    order.mark(outs[0])
    return outs


class Streams:
    def __init__(self, a_strips, a_rows, b_strips, b_rows, left):
        self.a_strips, self.a_rows, self.b_strips, self.b_rows = a_strips, a_rows, b_strips, b_rows // 2
        self.left = left
        self.a_half = a_strips * left * a_rows
        self.b_half = b_strips * left * (b_rows // 2)
        self.a_first, self.b_first = 2 * self.a_half, 2 * self.b_half
        self.piece = (self.a_half + self.b_half) // left

    def by_place(self, kept, came, sent, sent_at, keep, mine, a):
        rows = 2 * (self.a_rows if a else self.b_rows)
        strips = self.a_strips if a else self.b_strips

        def step(i):
            for out, at, side in ((sent, sent_at, 1 - mine), (keep, 0, mine)):
                first = (2 * i + side) * rows
                out[rows_at(at + i * rows, rows), :] = (
                    kept[rows_at(first, rows), :] + came[rows_at(first, rows), :]
                )

        repeat(strips * self.left // 2, step)

    def second(self, kept, came, sent, keep, mine, a, came_at=0):
        rows = self.a_rows if a else self.b_rows
        strips = self.a_strips if a else self.b_strips

        def step(i):
            for out, side in ((sent, 1 - mine), (keep, mine)):
                first = i * 2 * rows + side * rows
                out[rows_at(i * rows, rows), :] = (
                    kept[rows_at(first, rows), :] + came[rows_at(came_at + first, rows), :]
                )

        repeat(strips * self.left, step)

    def third(self, kept_a, came_a, kept_b, came_b, sent, keep, place):
        a_rows, b_rows, left = self.a_rows, self.b_rows, self.left
        mine = place & 1
        for j in range(left // 2):
            for out, side in ((sent, 1 - mine), (keep, mine)):
                block = 2 * j + side
                base = j * self.piece

                def a_step(i, out=out, block=block, base=base):
                    first = (i * left + block) * a_rows
                    out[rows_at(base + i * a_rows, a_rows), :] = (
                        kept_a[rows_at(first, a_rows), :] + came_a[rows_at(first, a_rows), :]
                    )

                def b_step(i, out=out, block=block, base=base):
                    first = (i * left + block) * b_rows
                    at = base + self.a_strips * a_rows + i * b_rows
                    out[rows_at(at, b_rows), :] = (
                        kept_b[rows_at(first, b_rows), :] + came_b[rows_at(first, b_rows), :]
                    )

                repeat(self.a_strips, a_step)
                repeat(self.b_strips, b_step)


def add_rows(a, b, a_at, out, out_at, count):
    chunk = math.gcd(count, 256)

    def step(i):
        span = rows_at(a_at + i * chunk, chunk)
        out[rows_at(out_at + i * chunk, chunk), :] = a[span, :] + b[span, :]

    repeat(count // chunk, step)


def total_over_rest(pieces):
    for bit in range(2, lax.axis_size("dp").bit_length() - 1):
        pieces = [add(piece, swap(piece, "dp", bit)) for piece in pieces]
    return pieces


class Spread:
    def __init__(self, order, piece):
        self.order, self.piece = order, piece
        self.y = swap(order.then(piece), "dp", 1)

    def forward(self):
        self.piece, self.y = self.order.then(self.piece, self.y)
        self.core = swap(self.piece, "dp", 0)
        self.both = swap(self.y, "dp", 0)

    def finish(self, rows, shapes, write, name, rider=0):
        pieces = self.order.then(self.piece, self.core, self.y, self.both)
        out_shapes = list(shapes) + ([(rider, LANES)] if rider else [])

        def kernel(sc_ref, *refs):
            outs = refs[4:]
            for at in range(4):
                for k in range(4):

                    @pl.when(sc_ref[0] == at ^ k)
                    def _(at=at, k=k):
                        write(outs, refs[k], at & 1, at >> 1)

            if rider:
                total = refs[0][rows:, :].astype(F32)
                for ref in refs[1:4]:
                    total = total + ref[rows:, :].astype(F32)
                outs[-1][...] = total

        scalars = (lax.axis_index("dp") & 3).astype(jnp.int32).reshape(1)
        outs = pl.pallas_call(
            kernel,
            grid_spec=pltpu.PrefetchScalarGridSpec(
                num_scalar_prefetch=1,
                grid=(1,),
                in_specs=[whole(self.piece.shape)] * 4,
                out_specs=[whole(shape) for shape in out_shapes],
            ),
            out_shape=[shape_of(shape, F32) for shape in out_shapes],
            compiler_params=params(),
            cost_estimate=cost(0, 0),
            name=name,
        )(scalars, *pieces)
        self.order.mark(outs[0])
        return outs

    def finish_text(self, rows, bw):
        pieces = self.order.then(self.piece, self.core, self.y, self.both)
        shards = lax.axis_size("seq")
        half = bw // 2

        def kernel(sc_ref, *refs):
            out_ref = refs[4]

            def one(i, carry):
                place = i ^ sc_ref[0]
                seq_at = (place & 1) * (shards // 2) + (place >> 1)
                at = pl.multiple_of(seq_at * rows, rows)
                first = pl.multiple_of(i * bw, bw)
                for core in (0, 1):
                    for y in (0, 1):
                        for k in range(4):

                            @pl.when(sc_ref[1] == (2 * y + core) ^ k)
                            def _(ref=refs[k], core=core, y=y):
                                col = core * (D // 2) + y * LANES
                                out_ref[pl.ds(first, bw), col : col + LANES] = ref[
                                    pl.ds(at, bw), :
                                ].astype(F32)
                                for c in (0, 1):
                                    col = core * (D // 2) + 256 + c * LANES
                                    out_ref[pl.ds(first + y * half, half), col : col + LANES] = ref[
                                        rows_at(at + bw + c * half, half), :
                                    ].astype(F32)

                return carry

            lax.fori_loop(0, shards, one, 0)

        scalars = jnp.stack([lax.axis_index("seq"), lax.axis_index("dp") & 3]).astype(jnp.int32)
        return pl.pallas_call(
            kernel,
            grid_spec=pltpu.PrefetchScalarGridSpec(
                num_scalar_prefetch=1,
                grid=(1,),
                in_specs=[whole(self.piece.shape)] * 4,
                out_specs=whole((shards * bw, D)),
            ),
            out_shape=shape_of((shards * bw, D), F32),
            compiler_params=params(),
            cost_estimate=cost(0, 0),
            name="text_finish",
        )(scalars, *pieces)


def row_order(bit):
    mine = bit_of(lax.axis_index("seq"), bit)
    low = [s for s in range(lax.axis_size("seq")) if not (s >> bit) & 1]
    sent = [s + (1 - mine) * (1 << bit) for s in low]
    kept = [s + mine * (1 << bit) for s in low]
    return jnp.stack([jnp.asarray(v, jnp.int32) for v in [0] + sent + kept])


def body(
    inputs,
    text_state,
    text_segment,
    image_text,
    image_segment,
    self_gain,
    self_shift,
    qkv_weight,
    self_weight,
    cross_gain,
    cross_shift,
    query_weight,
    text_weight,
    cross_weight,
    feed_gain,
    feed_shift,
    up_weight,
    down_weight,
    cotangent,
):
    rows = inputs.shape[0]
    shards = lax.axis_size("seq")
    groups = lax.axis_size("dp")
    me, dp = lax.axis_index("seq"), lax.axis_index("dp")
    per_image = IMG_TOK // rows
    core = bit_of(dp, 0)
    odd = (me % per_image).astype(jnp.int32).reshape(1)
    img_group = image_text.shape[0] // groups
    own_half = core.astype(jnp.int32).reshape(1)
    other_half = 1 - own_half
    order = Order()

    def caption_of(group):
        image = group * img_group + me // per_image
        return image_text[image], image_segment[image]

    row, seg = caption_of(dp)
    row_mate, _ = caption_of(dp ^ 1)

    def over_core(block):
        return swap(block, "dp", 0)

    seq_bits = shards.bit_length() - 1
    dp_bits = groups.bit_length() - 1
    spread_steps = [("seq", b) for b in reversed(range(seq_bits))] + [("dp", 1), ("dp", 0)]
    bw = D // shards
    bw_ff = FF // (2 * shards)
    order_x = row_order(0)
    y_first = (1 - bit_of(dp, 1)).astype(jnp.int32).reshape(1)
    order_xy = jnp.concatenate([y_first, order_x[1:]])

    even_to_odd = [(i, i + 1) for i in range(0, shards, 2)]
    odd_to_even = [(i + 1, i) for i in range(0, shards, 2)]
    x_before = lax.ppermute(inputs, "seq", even_to_odd)
    cot_mate = over_core(cotangent)
    gain1, shift1 = self_gain.reshape(1, D), self_shift.reshape(1, D)
    act1, qkv, norms = norm_project(inputs, gain1, shift1, qkv_weight, 0, "norm_project")
    act1_mate = over_core(act1)
    own_out, own_log = causal_forward(qkv, norms)
    order.mark(own_out)
    text_scalars = order.then(jnp.stack([row, seg, row_mate]).astype(jnp.int32))
    text_kv, bias_row, text_row, text_row_mate = text_project(
        text_scalars, text_state, text_segment, text_weight
    )
    order.mark(text_kv)
    x_before, act1_mate, cot_mate = order.then(x_before, act1_mate, cot_mate)
    act1_before, pairs_before, norms_before = norm_project(
        x_before, gain1, shift1, qkv_weight, D, "norm_project_before"
    )
    before_mate = over_core(act1_before)
    attended, log_rows = earlier_forward(
        odd, qkv, pairs_before, norms, norms_before, own_out, own_log
    )
    order.mark(attended)
    before_mate, attended = order.then(before_mate, attended)
    attended_mate = over_core(attended)
    gains = jnp.stack([cross_gain, cross_shift, feed_gain, feed_shift] * 2)
    mid1, cq, mid2, acts = middle_forward(
        attended, inputs, self_weight, query_weight, cross_weight, gains, text_kv, bias_row
    )
    order.mark(mid1)
    attended_mate, acts = order.then(attended_mate, acts)
    acts_mate = over_core(acts)
    hid_other, d_act3 = feed_half(
        other_half, acts, cotangent, up_weight, down_weight, shards, None
    )
    order.mark(d_act3)
    d_act3, acts_mate, hid_other = order.then(d_act3, acts_mate, hid_other)
    hid_mate = over_core(hid_other)
    hid_own, d_act3 = feed_half(
        own_half, acts, cotangent, up_weight, down_weight, shards, d_act3
    )
    order.mark(d_act3)
    hid_mate = order.then(hid_mate)

    left = shards // 2
    feed = Streams(D // 2 // LANES, bw_ff, FF // 2 // LANES, bw, left)
    feed_later = Streams(D // 2 // LANES, bw_ff, FF // 2 // LANES, bw, left // 2)
    mids = Streams(6, bw, 12, bw, left)
    qkvs = Streams(3, bw, 6, bw, left)
    x_bit, y_bit = bit_of(me, 0), bit_of(dp, 1)
    places = jnp.stack([x_bit, y_bit, me >> 1]).astype(jnp.int32)
    others = range(1, left)

    sent, feed_a = row_grad(
        y_first, [(hid_own, 0), (hid_mate, 0)], [cotangent, cot_mate], "down_grad"
    )
    order.mark(sent)
    feed_a = flat(feed_a)
    came_fa = swap(flat(sent), "dp", 1)
    acts_late = order.then(acts)
    sent, feed_b = column_grad(
        order_x, [(acts_late, 2), (acts_mate, 2)], [(hid_own, 1), (hid_mate, 1)], bw, "up_grad"
    )
    order.mark(sent)
    feed_b = flat(feed_b)
    came_fb = swap(flat(sent), "seq", 0)

    d_act3 = order.then(d_act3)
    g_mine, g_sent, d_mid1, d_att, text_mine, text_sent, d_gains = middle_backward(
        own_half, d_act3, mid2, cotangent, mid1, cq, text_kv, bias_row, cross_weight, query_weight,
        self_weight, gains,
    )
    order.mark(d_mid1)
    g_mate = over_core(g_sent)
    text_both = order.mark(jnp.concatenate([text_sent, text_mine], axis=0))
    text_both = over_core(text_both)
    g_mine, g_mate, text_both = order.then(g_mine, g_mate, text_both)
    text_mate, text_mate_other = text_both[:TEXT_LEN], text_both[TEXT_LEN:]
    lefts = [(acts, 1), (acts_mate, 1), (acts, 0), (acts_mate, 0), (attended, None), (attended_mate, None)]
    lefts += [(text_row, None), (text_row_mate, None)]
    rights = [(g_mine, lambda j: jnp.minimum(j, 2)), (g_mate, lambda j: jnp.minimum(j, 2))]
    rights += [(text_mine, lambda j: jnp.clip(j - 3, 0, 1)), (text_mate, lambda j: jnp.clip(j - 3, 0, 1))]
    blocks = [((0, 1), (0, 1)), ((2, 3), (0, 1)), ((4, 5), (0, 1)), ((6, 7), (2, 3)), ((6, 7), (2, 3))]
    mid_scalars = jnp.concatenate([order_xy, jnp.stack([core, row, row_mate]).astype(jnp.int32)])
    sent_a, mid_a, sent_b, mid_b = block_grads(
        mid_scalars, bw, lefts, rights, blocks, "middle_grads",
        text=(text_mine, text_sent, text_mate, text_mate_other, text_weight),
    )
    order.mark(mid_a)
    mid_sent_a, mid_sent_b = flat(sent_a), flat(sent_b)
    mid_a, mid_b = flat(mid_a), flat(mid_b)

    def second(streams, name, kept_a, came_a, kept_b, came_b=None):
        def work(sc, ins, outs):
            b_at = 0 if came_b is not None else 2 * streams.a_half
            streams.second(ins[0], ins[1], outs[0], outs[2], sc[0], True)
            streams.second(ins[2], ins[-1] if b_at == 0 else ins[1], outs[1], outs[3], sc[1], False, b_at)

        inputs = order.then(kept_a, came_a, kept_b, *([] if came_b is None else [came_b]))
        sent_x, sent_y, kept_a, kept_b = sum_stage(
            order, name, places, inputs, [streams.a_half, streams.b_half] * 2, work
        )
        return kept_a, sent_x, kept_b, sent_y

    def third(streams, name, kept_a, came_a, kept_b, came_b, rider=0, skip=0):
        def work(sc, ins, outs):
            streams.third(ins[0], ins[1], ins[2], ins[3], outs[0], outs[1], sc[2] >> skip)
            if rider:
                count = streams.left // 2 * streams.piece
                span = slice(streams.a_half, streams.a_half + rider)
                for out in outs:
                    out[count : count + rider, :] = ins[0][span, :] + ins[1][span, :]

        inputs = order.then(kept_a, came_a, kept_b, came_b)
        out_rows = streams.left // 2 * streams.piece + rider
        sent, kept = sum_stage(order, name, places, inputs, [out_rows] * 2, work)
        return kept, swap(sent, "seq", 1 + skip)

    def further(streams, name, kept, came, rider=0, skip=0):
        blocks = streams.left // 2
        for bit in range(1, streams.left.bit_length() - 1):
            half = blocks // 2 * streams.piece

            def work(sc, ins, outs, bit=bit, half=half):
                mine = (sc[2] >> (bit + skip)) & 1
                for i in range(half // streams.piece):
                    for out, side in ((outs[0], 1 - mine), (outs[1], mine)):
                        add_rows(
                            ins[0], ins[1], (2 * i + side) * streams.piece, out, i * streams.piece, streams.piece
                        )
                if rider:
                    for out in outs:
                        out[half : half + rider, :] = ins[0][2 * half :, :] + ins[1][2 * half :, :]

            inputs = order.then(kept, came)
            sent, kept = sum_stage(order, name, places, inputs, [half + rider] * 2, work)
            came = swap(sent, "seq", bit + 1 + skip)
            blocks //= 2
        return kept, came

    def fourth(streams, name, kept, came, rider=0):
        def work(sc, ins, outs):
            add_rows(ins[0], ins[1], 0, outs[0], 0, streams.piece + rider)

        inputs = order.then(kept, came)
        (total,) = sum_stage(order, name, places, inputs, [streams.piece + rider], work)
        return total_over_rest([total])[0]

    mid2_late = order.then(mid2)
    output = feed_output(own_half, mid2_late, hid_own, hid_other, down_weight, shards)
    order.mark(output)

    mid_sent_a, mid_sent_b, came_fa, came_fb = order.then(mid_sent_a, mid_sent_b, came_fa, came_fb)
    came_ma, came_mb = swap(mid_sent_a, "dp", 1), swap(mid_sent_b, "seq", 0)
    inputs_f = order.then(feed_a, came_fa, feed_b, came_fb)

    def work_f(sc, ins, outs):
        mine = sc[2] & 1
        feed.by_place(ins[0], ins[1], outs[0], 0, outs[1], mine, True)
        feed.by_place(ins[2], ins[3], outs[0], feed.a_half, outs[2], mine, False)

    feed_sent, feed_a, feed_b = sum_stage(
        order, "feed_second", places, inputs_f, [feed.a_half + feed.b_half, feed.a_half, feed.b_half], work_f
    )
    came_f = swap(feed_sent, "seq", 1)

    sc_other = jnp.concatenate([odd, other_half])
    sc_own = jnp.concatenate([odd, own_half])
    d_att = order.then(d_att)
    att_other, before_other = attention_backward(
        sc_other, qkv, pairs_before, d_att, attended, log_rows
    )
    order.mark(att_other)
    att_mate, before_mate_grads = over_core(att_other), over_core(before_other)
    d_att = order.then(d_att)
    att_own, before_own = attention_backward(sc_own, qkv, pairs_before, d_att, attended, log_rows)
    order.mark(att_own)
    mid_a, mid_sent_x, mid_b, mid_sent_y = second(mids, "mid_second", mid_a, came_ma, mid_b, came_mb)
    came_ma, came_mb = swap(mid_sent_x, "seq", 0), swap(mid_sent_y, "dp", 1)

    act1_late, att_mate, before_mate_grads = order.then(act1, att_mate, before_mate_grads)
    lefts = [(act1_late, None), (act1_mate, None), (act1_before, None), (before_mate, None)]
    rights = [(att_own, lambda j: j), (att_mate, lambda j: j)]
    rights += [(before_own, lambda j: jnp.maximum(j - 1, 0))]
    rights += [(before_mate_grads, lambda j: jnp.maximum(j - 1, 0))]
    blocks = [((0, 1), (0, 1))] + [((0, 1, 2, 3), (0, 1, 2, 3))] * 2
    sent_a, qkv_a, sent_b, qkv_b = block_grads(order_xy, bw, lefts, rights, blocks, "qkv_grads")
    order.mark(qkv_a)
    came_qa, came_qb = swap(flat(sent_a), "dp", 1), swap(flat(sent_b), "seq", 0)
    before_own = order.then(before_own)
    d_act_before, sums_before = project_back(
        own_half, before_own, before_other, qkv_weight, x_before, "project_back_before"
    )
    order.mark(d_act_before)
    mid_left = third(mids, "mid_third", mid_a, came_ma, mid_b, came_mb)
    feed_a, feed_sent_x, feed_b, feed_sent_y = second(feed_later, "feed_third", feed_a, came_f, feed_b)
    came_fa, came_fb = swap(feed_sent_x, "seq", 0), swap(feed_sent_y, "dp", 1)
    att_own = order.then(att_own)
    d_act, sums_own = project_back(own_half, att_own, att_other, qkv_weight, inputs, "project_back")
    order.mark(d_act)
    rider = jnp.concatenate([sums_own[:2] + sums_before[:2], d_gains[:4]], axis=0).astype(BF)
    rider = flat(rider)
    rides = rider.shape[0]

    inputs_q = order.then(flat(qkv_a), came_qa, flat(qkv_b), came_qb, rider)

    def work_q(sc, ins, outs):
        qkvs.second(ins[0], ins[1], outs[0], outs[2], sc[0], True)
        qkvs.second(ins[2], ins[3], outs[1], outs[3], sc[1], False)
        for out in (outs[0], outs[2]):
            out[qkvs.a_half : qkvs.a_half + rides, :] = ins[4][...]

    sent_x, sent_y, qkv_a, qkv_b = sum_stage(
        order, "qkv_second", places, inputs_q,
        [qkvs.a_half + rides, qkvs.b_half] * 2, work_q,
    )
    came_qa, came_qb = swap(sent_x, "seq", 0), swap(sent_y, "dp", 1)
    mid_left = further(mids, "mid_further", *mid_left)
    feed_left = third(feed_later, "feed_join", feed_a, came_fa, feed_b, came_fb, skip=1)
    feed_left = further(feed_later, "feed_further", *feed_left, skip=1)
    qkv_left = third(qkvs, "qkv_third", qkv_a, came_qa, qkv_b, came_qb, rides)
    mid_piece = fourth(mids, "mid_fourth", *mid_left)

    text_rows = 2 * bw
    text_piece = jnp.concatenate(
        [mid_piece[5 * bw : 6 * bw], mid_piece[11 * bw : 12 * bw]], axis=0
    )
    order.mark(text_piece)
    text_pieces = [text_piece] + [exchange(text_piece, "seq", 2 * k) for k in others]

    def join(name, pieces):
        def work(sc, ins, outs):
            for i, ref in enumerate(ins):
                count = ref.shape[0]
                outs[0][i * count : (i + 1) * count, :] = ref[...]

        inputs = order.then(*pieces)
        return sum_stage(order, name, places, inputs, [len(pieces) * pieces[0].shape[0]], work)[0]

    qkv_left = further(qkvs, "qkv_further", *qkv_left, rides)
    feed_piece = fourth(feed_later, "feed_fourth", *feed_left)
    text_block = join("text_join", text_pieces)
    came_text = swap(text_block, "seq", 0)
    mid_all = Spread(order, mid_piece)
    qkv_piece = fourth(qkvs, "qkv_fourth", *qkv_left, rides)
    qkv_all = Spread(order, qkv_piece)
    d_act_before = order.then(d_act_before)
    d_act_late = lax.ppermute(d_act_before, "seq", odd_to_even)
    text_block = join("text_join", [text_block, came_text])
    text_all = Spread(order, text_block)
    mid_all.forward()
    feed_all = Spread(order, feed_piece)
    qkv_all.forward()

    b_rows = bw // 2

    def write_feed(outs, ref, at_core, y):
        at = 0
        strips = D // 2 // LANES
        for c in range(strips):
            col = y * (D // 2) + c * LANES
            outs[0][at_core * bw_ff : (at_core + 1) * bw_ff, col : col + LANES] = ref[
                at + c * bw_ff : at + (c + 1) * bw_ff, :
            ].astype(F32)
        at = at + strips * bw_ff
        per = bw_ff // LANES
        for c in range(FF // 2 // LANES):
            s, inside = divmod(c, per)
            col = (2 * s + at_core) * bw_ff + inside * LANES
            outs[1][y * b_rows : (y + 1) * b_rows, col : col + LANES] = ref[
                at + c * b_rows : at + (c + 1) * b_rows, :
            ].astype(F32)

    def writer(targets):
        count = len(targets)

        def write(outs, ref, at_core, y):
            for j, where in enumerate(targets):
                if where is None:
                    continue
                out, first = where
                col = first[at_core]
                outs[out][:, col + y * LANES : col + (y + 1) * LANES] = ref[
                    j * bw : (j + 1) * bw, :
                ].astype(F32)
                for half in (0, 1):
                    row_at = count * bw + (2 * j + half) * b_rows
                    to = col + 256 + half * LANES
                    outs[out][y * b_rows : (y + 1) * b_rows, to : to + LANES] = ref[
                        row_at : row_at + b_rows, :
                    ].astype(F32)

        return write

    targets = [(0, (0, 512)), (1, (0, 512)), (2, (0, 512)), (3, (0, 1024)), (3, (512, 1536)), None]
    cross_grad, query_grad, self_grad, text_weight_grad = mid_all.finish(
        mids.piece, [(bw, D), (bw, D), (bw, D), (bw, 2 * D)], writer(targets), "mids_finish"
    )
    text_all.forward()
    targets = [(0, (0, 512)), (0, (1024, 1536)), (0, (2048, 2560))]
    qkv_grad, sums = qkv_all.finish(
        qkvs.piece, [(bw, 3 * D)], writer(targets), "qkv_finish", rider=rides
    )
    feed_all.forward()
    d_act, d_act_late = order.then(d_act, d_act_late)
    input_grad = input_back(d_act, d_act_late, inputs, d_mid1, gain1)
    order.mark(input_grad)
    text_grad = text_all.finish_text(text_rows, bw)
    order.mark(text_grad)
    down_grad, up_grad = feed_all.finish(
        feed.piece, [(2 * bw_ff, D), (bw, FF)], write_feed, "feed_finish"
    )
    sums = lax.dynamic_slice_in_dim(sums.reshape(6, D), me * bw, bw, 1)
    return (
        output,
        input_grad,
        text_grad.reshape(text_state.shape),
        sums[0],
        sums[1],
        qkv_grad,
        self_grad,
        sums[2],
        sums[3],
        query_grad,
        text_weight_grad,
        cross_grad,
        sums[4],
        sums[5],
        up_grad,
        down_grad,
    )


def solution(mesh):
    tokens = P(("dp", "seq"), None)
    return jax.shard_map(
        body,
        mesh=mesh,
        in_specs=(tokens,) + (P(),) * 17 + (tokens,),
        out_specs=(
            tokens,
            tokens,
            P(),
            P("seq"),
            P("seq"),
            P("seq", None),
            P("seq", None),
            P("seq"),
            P("seq"),
            P("seq", None),
            P("seq", None),
            P("seq", None),
            P("seq"),
            P("seq"),
            P("seq", None),
            P("seq", None),
        ),
        check_vma=False,
    )
```

```python
import functools
import math

import jax
import jax.numpy as jnp
from jax import lax
from jax.experimental import pallas as pl
from jax.experimental.pallas import tpu as pltpu
from jax.sharding import PartitionSpec as P

D = 1024
HEADS = 16
HEAD = 64
FF = 4096
TEXT_LEN = 128
IMG_TOK = 1024
PAIR = 2 * HEAD
LANES = 128
SCALE = 1.0 / math.sqrt(HEAD)

NEGATIVE = -1e30
EPSILON = 1e-05
BF = jnp.bfloat16
F32 = jnp.float32
NN = (((1,), (0,)), ((), ()))
NT = (((1,), (1,)), ((), ()))
TN = (((0,), (0,)), ((), ()))
VMEM_LIMIT = 65000 * 1024
ODD, CORE, OTHER, X, Y, NOT_Y, PLACE, QUARTER, ME, ROW, SEG, ROW_MATE = range(12)


def mm(a, b, dims=NN):
    return lax.dot_general(a, b, dims, preferred_element_type=F32)


def normed(values):
    average = jnp.mean(values, axis=-1, keepdims=True)
    centered = values - average
    inverse = lax.rsqrt(jnp.mean(centered * centered, axis=-1, keepdims=True) + EPSILON)
    return centered * inverse, inverse


def norm_back(normal, inverse, gain, upstream):
    w = upstream * gain
    along = jnp.mean(w * normal, axis=-1, keepdims=True)
    return inverse * (w - jnp.mean(w, axis=-1, keepdims=True) - normal * along)


def head_lanes(h):
    lane = lax.broadcasted_iota(jnp.int32, (1, PAIR), 1)
    return (lane >= h * HEAD) & (lane < (h + 1) * HEAD)


def only_head(block, h):
    return jnp.where(head_lanes(h), block, jnp.zeros_like(block))


def by_rows(rows, size, step):
    def one(i, carry):
        step(pl.ds(pl.multiple_of(i * size, size), size))
        return carry

    if rows == size:
        step(slice(0, rows))
        return
    lax.fori_loop(0, rows // size, one, 0, unroll=2)


def params(grid_dims=1):
    return pltpu.CompilerParams(
        dimension_semantics=("arbitrary",) * grid_dims, vmem_limit_bytes=VMEM_LIMIT
    )


def cost(flops, moved):
    return pl.CostEstimate(flops=1, bytes_accessed=1, transcendentals=0)


def number(ref, which):
    packed = ref[0]
    if which == ODD:
        return packed & 1
    if which == CORE:
        return (packed >> 1) & 1
    if which == OTHER:
        return 1 - ((packed >> 1) & 1)
    if which == Y:
        return (packed >> 2) & 1
    if which == NOT_Y:
        return 1 - ((packed >> 2) & 1)
    if which == QUARTER:
        return (packed >> 1) & 3
    if which == ME:
        return packed >> 3
    if which == X:
        return (packed >> 3) & 1
    if which == PLACE:
        return packed >> 4
    return (packed >> {ROW: 0, SEG: 8, ROW_MATE: 16}[which]) & 255


def row_block(ref, i, blocks):
    x = number(ref, X)
    half = blocks // 2
    return 2 * i + 1 - x if i < half else 2 * (i - half) + x


def whole(shape):
    zeros = (0,) * len(shape)
    return pl.BlockSpec(shape, lambda *_: zeros)


def shape_of(shape, dtype):
    return jax.ShapeDtypeStruct(shape, dtype)


def head_sums(block):
    wide = block.astype(F32)
    lane = lax.broadcasted_iota(jnp.int32, (D, PAIR), 1)
    row = lax.broadcasted_iota(jnp.int32, (D, PAIR), 0)
    pick = jnp.where(row // HEAD == lane, 1.0, 0.0).astype(BF)
    return jnp.max(mm((wide * wide).astype(BF), pick), axis=0, keepdims=True)


def small_scores(q_sums, k_sums):
    return jnp.max(q_sums * k_sums) * (SCALE * SCALE) < 75.0 * 75.0


def norm_project(x, gain, shift, weight, first_col, name):
    rows, width = x.shape
    cols = weight.shape[1] - first_col
    bn = D

    def kernel(x_ref, gain_ref, shift_ref, w_ref, act_ref, out_ref, norm_ref):
        j = pl.program_id(0)

        @pl.when(j == 0)
        def _():
            norm_ref[...] = jnp.zeros_like(norm_ref)

            def norm_rows(span):
                normal, _ = normed(x_ref[span, :].astype(F32))
                act_ref[span, :] = (normal * gain_ref[...] + shift_ref[...]).astype(BF)

            by_rows(rows, 128, norm_rows)

        out = mm(act_ref[...], w_ref[...]).astype(BF)
        out_ref[...] = out
        for i in range(cols // bn - 1):

            @pl.when(j == i)
            def _(i=i):
                norm_ref[i : i + 1, :] = head_sums(out)

    return pl.pallas_call(
        kernel,
        grid=(cols // bn,),
        in_specs=[
            whole((rows, width)),
            whole((1, width)),
            whole((1, width)),
            pl.BlockSpec((width, bn), lambda j: (0, first_col // bn + j)),
        ],
        out_specs=[
            whole((rows, width)),
            pl.BlockSpec((rows, bn), lambda j: (0, j)),
            whole((8, PAIR)),
        ],
        out_shape=[
            shape_of((rows, width), BF),
            shape_of((rows, cols), BF),
            shape_of((8, PAIR), F32),
        ],
        compiler_params=params(),
        cost_estimate=cost(0, 0),
        name=name,
    )(x, gain, shift, weight)


def with_ones(v, h):
    ones = jnp.where(head_lanes(h), jnp.ones_like(v), jnp.zeros_like(v))
    return jnp.concatenate([only_head(v, h), ones], axis=1)


def rows_of(columns):
    turned = columns.T
    return turned[0:1], turned[HEAD : HEAD + 1]


def columns_of(log_rows):
    rows = log_rows.shape[1]
    turned = jnp.concatenate([log_rows, jnp.zeros((6, rows), F32)], axis=0).T
    return jnp.where(head_lanes(0), turned[:, 0:1], turned[:, 1:2])


def causal_forward(qkv, norms):
    rows = qkv.shape[0]
    half = rows // 2
    pairs = D // PAIR

    def kernel(q_ref, k_ref, v_ref, norm_ref, out_ref, log_ref, small_ref):
        @pl.when(pl.program_id(0) == 0)
        def _():
            small_ref[0] = small_scores(norm_ref[0:1, :], norm_ref[1:2, :]).astype(jnp.int32)

        below = lax.broadcasted_iota(jnp.int32, (half, half), 0) >= lax.broadcasted_iota(
            jnp.int32, (half, half), 1
        )

        @pl.when(small_ref[0] != 0)
        def _():
            early, late = slice(0, half), slice(half, rows)
            q_early, q_late = q_ref[early, :] * SCALE, q_ref[late, :] * SCALE
            k, v = k_ref[...], v_ref[...]
            first = jnp.zeros((half, 2 * PAIR), F32)
            second = jnp.zeros((half, 2 * PAIR), F32)
            for h in (0, 1):
                kh, vh = only_head(k, h), with_ones(v, h)
                p = jnp.exp(mm(q_early, kh[early], NT))
                p = jnp.where(below, p, 0.0).astype(BF)
                first = first + mm(p, vh[early])
                s = mm(q_late, kh, NT)
                p = jnp.where(below, jnp.exp(s[:, half:]), 0.0).astype(BF)
                p = jnp.concatenate([jnp.exp(s[:, :half]).astype(BF), p], axis=1)
                second = second + mm(p, vh)
            for span, both in ((early, first), (late, second)):
                out_ref[span, :] = (both[:, :PAIR] / both[:, PAIR:]).astype(BF)
                one, two = rows_of(both[:, PAIR:])
                log_ref[0, 0:1, span] = jnp.log(one)
                log_ref[0, 1:2, span] = jnp.log(two)

        @pl.when(small_ref[0] == 0)
        def _():
            def slowly(span):
                q = q_ref[span, :] * SCALE
                k, v = k_ref[...], v_ref[...]
                at_q = span.start + lax.broadcasted_iota(jnp.int32, (PAIR, rows), 0)
                at_k = lax.broadcasted_iota(jnp.int32, (PAIR, rows), 1)
                total = jnp.zeros((PAIR, PAIR), F32)
                logs = jnp.zeros((PAIR, PAIR), F32)
                for h in (0, 1):
                    s = mm(q, only_head(k, h), NT)
                    s = jnp.where(at_q >= at_k, s, NEGATIVE)
                    top = jnp.max(s, axis=1, keepdims=True)
                    p = jnp.exp(s - top)
                    part = jnp.sum(p, axis=1, keepdims=True)
                    total = total + mm(p.astype(BF), only_head(v, h)) * (1.0 / part)
                    logs = jnp.where(head_lanes(h), top + jnp.log(part), logs)
                out_ref[span, :] = total.astype(BF)
                one, two = rows_of(logs)
                log_ref[0, 0:1, span] = one
                log_ref[0, 1:2, span] = two

            by_rows(rows, PAIR, slowly)

    block = (rows, PAIR)
    return pl.pallas_call(
        kernel,
        grid=(pairs,),
        in_specs=[
            pl.BlockSpec(block, lambda p: (0, p)),
            pl.BlockSpec(block, lambda p: (0, pairs + p)),
            pl.BlockSpec(block, lambda p: (0, 2 * pairs + p)),
            whole(norms.shape),
        ],
        out_specs=[
            pl.BlockSpec(block, lambda p: (0, p)),
            pl.BlockSpec((1, 2, rows), lambda p: (p, 0, 0)),
        ],
        out_shape=[shape_of((rows, D), BF), shape_of((pairs, 2, rows), F32)],
        scratch_shapes=[pltpu.SMEM((1,), jnp.int32)],
        compiler_params=params(),
        cost_estimate=cost(0, 0),
        name="causal_forward",
    )(qkv, qkv, qkv, norms)


def earlier_forward(odd, qkv, pairs_before, norms, norms_before, own_out, own_log):
    rows = qkv.shape[0]
    half = rows // 2
    pairs = D // PAIR

    def kernel(
        odd_ref, q_ref, k_ref, v_ref, norm_ref, before_ref, own_ref, log_ref, out_ref, new_log_ref, mode_ref
    ):
        @pl.when(pl.program_id(0) == 0)
        def _():
            small = small_scores(
                norm_ref[0:1, :], jnp.maximum(norm_ref[1:2, :], before_ref[0:1, :])
            )
            mode_ref[0] = number(odd_ref, ODD) * (2 - small.astype(jnp.int32))

        @pl.when(mode_ref[0] == 0)
        def _():
            out_ref[...] = own_ref[...]
            new_log_ref[...] = log_ref[...]

        @pl.when(mode_ref[0] == 1)
        def _():
            q = q_ref[...] * SCALE
            both = jnp.zeros((rows, 2 * PAIR), F32)
            for h in (0, 1):
                p = jnp.exp(mm(q, only_head(k_ref[...], h), NT)).astype(BF)
                both = both + mm(p, with_ones(v_ref[...], h))
            old = jnp.exp(columns_of(log_ref[0]))
            total = old + both[:, PAIR:]
            mixed = own_ref[...].astype(F32) * old + both[:, :PAIR]
            out_ref[...] = (mixed / total).astype(BF)
            one, two = rows_of(total)
            new_log_ref[0, 0:1, :] = jnp.log(one)
            new_log_ref[0, 1:2, :] = jnp.log(two)

        @pl.when(mode_ref[0] == 2)
        def _():
            def slowly(span):
                q = q_ref[span, :] * SCALE
                total = own_ref[span, :].astype(F32)
                logs = columns_of(log_ref[0, :, span])
                result = jnp.zeros_like(total)
                new_logs = logs
                for h in (0, 1):
                    s = mm(q, only_head(k_ref[...], h), NT)
                    old = logs[:, h * HEAD : h * HEAD + 1]
                    top = jnp.maximum(old, jnp.max(s, axis=1, keepdims=True))
                    p = jnp.exp(s - top)
                    share = jnp.exp(old - top)
                    part = share + jnp.sum(p, axis=1, keepdims=True)
                    mixed = mm(p.astype(BF), only_head(v_ref[...], h))
                    mixed = mixed + only_head(total, h) * share
                    result = result + mixed * (1.0 / part)
                    new_logs = jnp.where(head_lanes(h), top + jnp.log(part), new_logs)
                out_ref[span, :] = result.astype(BF)
                one, two = rows_of(new_logs)
                new_log_ref[0, 0:1, span] = one
                new_log_ref[0, 1:2, span] = two

            by_rows(rows, PAIR, slowly)

    block = (rows, PAIR)
    first = pl.BlockSpec(block, lambda p, odd: (0, p))
    second = pl.BlockSpec(block, lambda p, odd: (0, pairs + p))
    log_block = pl.BlockSpec((1, 2, rows), lambda p, odd: (p, 0, 0))
    return pl.pallas_call(
        kernel,
        grid_spec=pltpu.PrefetchScalarGridSpec(
            num_scalar_prefetch=1,
            grid=(pairs,),
            in_specs=[
                first, first, second, whole(norms.shape), whole(norms_before.shape), first, log_block,
            ],
            out_specs=[first, log_block],
            scratch_shapes=[pltpu.SMEM((1,), jnp.int32)],
        ),
        out_shape=[shape_of((rows, D), BF), shape_of((pairs, 2, rows), F32)],
        compiler_params=params(),
        cost_estimate=cost(0, 0),
        name="earlier_forward",
    )(odd, qkv, pairs_before, pairs_before, norms, norms_before, own_out, own_log)


def text_project(scalars, text, segments, weight):
    tokens = text.shape[1]
    bn = 512

    def kernel(sc_ref, row_ref, mate_ref, seg_ref, w_ref, kv_ref, bias_ref, row_out, mate_out):
        kv_ref[...] = mm(row_ref[...], w_ref[...]).astype(BF)

        @pl.when(pl.program_id(0) == 0)
        def _():
            row_out[...] = row_ref[...]
            mate_out[...] = mate_ref[...]
            bias = jnp.where(seg_ref[pl.ds(number(sc_ref, ROW), 1), :] == number(sc_ref, SEG), 0.0, NEGATIVE)
            bias_ref[...] = jnp.concatenate([bias, bias], axis=1).astype(F32)

    return pl.pallas_call(
        kernel,
        grid_spec=pltpu.PrefetchScalarGridSpec(
            num_scalar_prefetch=1,
            grid=(weight.shape[1] // bn,),
            in_specs=[
                pl.BlockSpec((None, tokens, D), lambda j, sc: (number(sc, ROW), 0, 0)),
                pl.BlockSpec((None, tokens, D), lambda j, sc: (number(sc, ROW_MATE), 0, 0)),
                whole(segments.shape),
                pl.BlockSpec((D, bn), lambda j, sc: (0, j)),
            ],
            out_specs=[
                pl.BlockSpec((tokens, bn), lambda j, sc: (0, j)),
                whole((1, 2 * tokens)),
                whole((tokens, D)),
                whole((tokens, D)),
            ],
        ),
        out_shape=[
            shape_of((tokens, weight.shape[1]), BF),
            shape_of((1, 2 * tokens), F32),
            shape_of((tokens, D), BF),
            shape_of((tokens, D), BF),
        ],
        compiler_params=params(),
        cost_estimate=cost(0, 0),
        name="text_project",
    )(scalars, text, text, segments, weight)


def cross_weights(scores, small):
    if small:
        return jnp.exp(scores)
    halves = []
    for h in (0, 1):
        s = scores[:, h * TEXT_LEN : (h + 1) * TEXT_LEN]
        halves.append(jnp.exp(s - jnp.max(s, axis=1, keepdims=True)))
    return jnp.concatenate(halves, axis=1)


def each_pair(pair, unrolled):
    def one(p, carry):
        pair(p)
        return carry

    lax.fori_loop(0, D // PAIR, one, 0, unroll=4 if unrolled else 1)


def both_heads(block):
    return jnp.concatenate([only_head(block, 0), only_head(block, 1)], axis=0)


def copies_of(hbm_refs, vmem_refs, sems):
    copies = [
        pltpu.make_async_copy(src, dst, sems.at[i])
        for i, (src, dst) in enumerate(zip(hbm_refs, vmem_refs))
    ]
    return copies


def start(*copies):
    for copy in copies:
        copy.start()


def wait(*copies):
    for copy in copies:
        copy.wait()


def middle_forward(attended, x, self_w, query_w, cross_w, gains, text_kv, bias):
    rows = x.shape[0]
    any_space = pl.BlockSpec(memory_space=pl.ANY)

    def kernel(
        at_ref, x_ref, sw_hbm, qw_hbm, cw_hbm, gains_ref, kv_ref, bias_ref,
        mid1_hbm, cq_hbm, mid2_hbm, acts_hbm,
        sw, qw, cw, mid1_ref, cq_ref, mid2_ref, acts_ref, sems, out_sems,
    ):
        loads = copies_of((sw_hbm, qw_hbm, cw_hbm), (sw, qw, cw), sems)
        outs = []

        def out(src, dst):
            copy = pltpu.make_async_copy(src, dst, out_sems.at[len(outs)])
            copy.start()
            outs.append(copy)

        start(loads[0])
        wait(loads[0])
        start(loads[1], loads[2])
        mid1_ref[...] = x_ref[...].astype(F32) + mm(at_ref[...], sw[...])
        out(mid1_ref, mid1_hbm)

        def norm2(span):
            normal, _ = normed(mid1_ref[span, :])
            acts_ref[0, span, :] = (normal * gains_ref[0:1, :] + gains_ref[1:2, :]).astype(BF)

        by_rows(rows, 128, norm2)
        out(acts_ref.at[0], acts_hbm.at[0])
        loads[1].wait()
        cq_ref[...] = mm(acts_ref[0], qw[...]).astype(BF)
        out(cq_ref, cq_hbm)
        small = small_scores(head_sums(cq_ref[...]), head_sums(kv_ref[:, :D]))
        bias_row = bias_ref[...]

        def attend(is_small):
            def pair(p):
                span = pl.ds(pl.multiple_of(p * PAIR, PAIR), PAIR)
                q = cq_ref[:, span] * SCALE
                v = kv_ref[:, pl.ds(pl.multiple_of(D + p * PAIR, PAIR), PAIR)]
                s = mm(q, both_heads(kv_ref[:, span]), NT) + bias_row
                w = cross_weights(s, is_small).astype(BF)
                both = mm(w, jnp.concatenate([with_ones(v, 0), with_ones(v, 1)], axis=0))
                acts_ref[1, :, span] = (both[:, :PAIR] / both[:, PAIR:]).astype(BF)

            each_pair(pair, is_small)

        @pl.when(small)
        def _():
            attend(True)

        @pl.when(jnp.logical_not(small))
        def _():
            attend(False)

        out(acts_ref.at[1], acts_hbm.at[1])
        loads[2].wait()
        mid2_ref[...] = mid1_ref[...] + mm(acts_ref[1], cw[...])
        out(mid2_ref, mid2_hbm)

        def norm3(span):
            normal, _ = normed(mid2_ref[span, :])
            acts_ref[2, span, :] = (normal * gains_ref[2:3, :] + gains_ref[3:4, :]).astype(BF)

        by_rows(rows, 128, norm3)
        out(acts_ref.at[2], acts_hbm.at[2])
        for copy in outs:
            copy.wait()

    token = (rows, D)
    return pl.pallas_call(
        kernel,
        grid=(1,),
        in_specs=[
            whole(token), whole(token), any_space, any_space, any_space,
            whole(gains.shape), whole(text_kv.shape), whole(bias.shape),
        ],
        out_specs=[any_space] * 4,
        out_shape=[shape_of(token, t) for t in (F32, BF, F32)] + [shape_of((3,) + token, BF)],
        scratch_shapes=[pltpu.VMEM((D, D), BF)] * 3
        + [pltpu.VMEM(token, t) for t in (F32, BF, F32)]
        + [pltpu.VMEM((3,) + token, BF), pltpu.SemaphoreType.DMA((3,)), pltpu.SemaphoreType.DMA((6,))],
        compiler_params=params(),
        cost_estimate=cost(0, 0),
        name="middle_forward",
    )(attended, x, self_w, query_w, cross_w, gains, text_kv, bias)


def feed_half(which, half, acts, grad3, up, down, shards, before):
    rows = acts.shape[1]
    bw = FF // (2 * shards)
    root = math.sqrt(2.0 / math.pi)
    each = 2
    steps = shards // each

    def kernel(which_ref, a_ref, g_ref, *rest):
        up_refs, down_refs = rest[:each], rest[each : 2 * each]
        hid_ref, da_ref = rest[-2:]
        parts = []
        for i in range(each):
            span = slice(i * bw, (i + 1) * bw)
            h = mm(a_ref[...], up_refs[i][...])
            dy = mm(g_ref[...], down_refs[i][...], NT)
            sq = h * h
            t = jnp.tanh(h * (root + (root * 0.044715) * sq))
            more = 0.5 + 0.5 * t
            hid_ref[0, :, span] = (h * more).astype(BF)
            slope = more + (h * (0.5 - 0.5 * (t * t))) * (root + (3 * root * 0.044715) * sq)
            dh = (dy * slope).astype(BF)
            hid_ref[1, :, span] = dh
            parts.append(dh)
        ups = jnp.concatenate([ref[...] for ref in up_refs], axis=1)
        part = mm(jnp.concatenate(parts, axis=1), ups, NT)

        @pl.when(pl.program_id(0) == 0)
        def _():
            if before is None:
                da_ref[...] = part
            else:
                da_ref[...] = rest[2 * each][...] + part

        @pl.when(pl.program_id(0) != 0)
        def _():
            da_ref[...] += part

    token = whole((rows, D))
    in_specs = [pl.BlockSpec((None, rows, D), lambda s, which: (2, 0, 0)), token]
    for i in range(each):
        in_specs.append(
            pl.BlockSpec((D, bw), lambda s, which, i=i: (0, 2 * (each * s + i) + number(which, half)))
        )
    for i in range(each):
        in_specs.append(
            pl.BlockSpec((bw, D), lambda s, which, i=i: (2 * (each * s + i) + number(which, half), 0))
        )
    operands = [which, acts, grad3] + [up] * each + [down] * each
    if before is not None:
        in_specs.append(token)
        operands.append(before)
    return pl.pallas_call(
        kernel,
        grid_spec=pltpu.PrefetchScalarGridSpec(
            num_scalar_prefetch=1,
            grid=(steps,),
            in_specs=in_specs,
            out_specs=[
                pl.BlockSpec((2, rows, each * bw), lambda s, which: (0, 0, s)),
                token,
            ],
        ),
        out_shape=[shape_of((2, rows, FF // 2), BF), shape_of((rows, D), F32)],
        compiler_params=params(),
        cost_estimate=cost(0, 0),
        name="feed_half",
    )(*operands)


def feed_output(own, mid2, hidden_own, hidden_other, down, shards):
    rows = mid2.shape[0]
    bw = FF // (2 * shards)
    each = 2
    steps = shards // each

    def kernel(own_ref, mid_ref, a_ref, b_ref, down_ref, out_ref, acc_ref):
        s = pl.program_id(0)
        first = number(own_ref, CORE) == 0
        pieces = []
        for i in range(each):
            span = slice(i * bw, (i + 1) * bw)
            a, b = a_ref[:, span], b_ref[:, span]
            pieces += [jnp.where(first, a, b), jnp.where(first, b, a)]
        part = mm(jnp.concatenate(pieces, axis=1), down_ref[...])

        @pl.when(s == 0)
        def _():
            acc_ref[...] = mid_ref[...] + part

        @pl.when(s != 0)
        def _():
            acc_ref[...] += part

        @pl.when(s == steps - 1)
        def _():
            out_ref[...] = acc_ref[...].astype(BF)

    token = whole((rows, D))
    hid = pl.BlockSpec((None, rows, each * bw), lambda s, own: (0, 0, s))
    return pl.pallas_call(
        kernel,
        grid_spec=pltpu.PrefetchScalarGridSpec(
            num_scalar_prefetch=1,
            grid=(steps,),
            in_specs=[token, hid, hid, pl.BlockSpec((2 * each * bw, D), lambda s, own: (s, 0))],
            out_specs=token,
            scratch_shapes=[pltpu.VMEM((rows, D), F32)],
        ),
        out_shape=shape_of((rows, D), BF),
        compiler_params=params(),
        cost_estimate=cost(0, 0),
        name="feed_output",
    )(own, mid2, hidden_own, hidden_other, down)


def middle_backward(
    own, d_act3, mid2, upstream, mid1, cq, text_kv, bias, cross_w, query_w, self_w, gains
):
    rows = mid2.shape[0]
    wide = D // 2
    any_space = pl.BlockSpec(memory_space=pl.ANY)
    chunk = 128

    def kernel(
        own_ref, da3_hbm, mid2_hbm, g_hbm, mid1_hbm, cq_hbm, kv_ref, bias_ref, cw_hbm, qw_hbm, sw_hbm, gains_ref,
        mine_hbm, sent_hbm, dmid1_hbm, dat_hbm, kv_ref_out, dgains_ref,
        da3, mid2_v, g_v, mid1_v, cq_v, cw, qw, sw, kv_acc, grads, dmid, dat, up2, sums, sems, out_sems,
    ):
        loads = copies_of(
            (da3_hbm, mid2_hbm, g_hbm, cw_hbm, cq_hbm, qw_hbm, mid1_hbm, sw_hbm),
            (da3, mid2_v, g_v, cw, cq_v, qw, mid1_v, sw),
            sems,
        )
        core_at = pl.multiple_of(number(own_ref, CORE) * wide, wide)
        mate_at = pl.multiple_of(number(own_ref, OTHER) * wide, wide)
        outs = []

        def out(src, dst):
            copy = pltpu.make_async_copy(src, dst, out_sems.at[len(outs)])
            copy.start()
            outs.append(copy)

        def out_grad(part):
            out(grads.at[part, :, pl.ds(core_at, wide)], mine_hbm.at[part])
            out(grads.at[part, :, pl.ds(mate_at, wide)], sent_hbm.at[part])

        def add_up(place, values):
            folded = values[:8]
            for i in range(8, rows, 8):
                folded = folded + values[i : i + 8]
            sums[place] += folded

        start(*loads[:3])
        sums[...] = jnp.zeros_like(sums)
        wait(*loads[:3])
        start(*loads[3:5])

        def back3(span):
            up = da3[span, :]
            normal, inverse = normed(mid2_v[span, :])
            add_up(2, up * normal)
            add_up(3, up)
            total = g_v[span, :].astype(F32) + norm_back(normal, inverse, gains_ref[2:3, :], up)
            dmid[span, :] = total
            grads[0, span, :] = total.astype(BF)

        back3(slice(0, rows))
        out_grad(0)
        wait(loads[3])
        start(*loads[5:7])
        dat[...] = mm(grads[0], cw[...], NT).astype(BF)
        loads[4].wait()
        small = small_scores(head_sums(cq_v[...]), head_sums(kv_ref[:, :D]))
        bias_row = bias_ref[...]
        side = lax.broadcasted_iota(jnp.int32, (2 * TEXT_LEN, 2 * TEXT_LEN), 0) // TEXT_LEN
        same = side == lax.broadcasted_iota(jnp.int32, side.shape, 1) // TEXT_LEN
        summing = jnp.where(same, 1.0, 0.0).astype(BF)

        def back_pairs(is_small):
            def pair(p):
                span = pl.ds(pl.multiple_of(p * PAIR, PAIR), PAIR)
                vspan = pl.ds(pl.multiple_of(D + p * PAIR, PAIR), PAIR)
                q = cq_v[:, span] * SCALE
                dc = dat[:, span]
                k = both_heads(kv_ref[:, span])
                v = both_heads(kv_ref[:, vspan])
                w = cross_weights(mm(q, k, NT) + bias_row, is_small)
                w = w / mm(w.astype(BF), summing)
                dw = mm(dc, v, NT)
                ds = (w * (dw - mm((w * dw).astype(BF), summing))).astype(BF)
                grads[1, :, span] = (mm(ds, k) * SCALE).astype(BF)
                dk = mm(ds, q, TN)
                dv = mm(w.astype(BF), dc, TN)
                kv_acc[:, span] = jnp.where(head_lanes(0), dk[:TEXT_LEN], dk[TEXT_LEN:]).astype(BF)
                kv_acc[:, vspan] = jnp.where(head_lanes(0), dv[:TEXT_LEN], dv[TEXT_LEN:]).astype(BF)

            each_pair(pair, is_small)

        @pl.when(small)
        def _():
            back_pairs(True)

        @pl.when(jnp.logical_not(small))
        def _():
            back_pairs(False)

        out_grad(1)
        kv_ref_out[0] = kv_acc[:, pl.ds(2 * core_at, D)]
        kv_ref_out[1] = kv_acc[:, pl.ds(2 * mate_at, D)]
        loads[5].wait()
        up2[...] = mm(grads[1], qw[...], NT)
        wait(loads[6])
        start(loads[7])

        def back2(span):
            up = up2[span, :]
            normal, inverse = normed(mid1_v[span, :])
            add_up(0, up * normal)
            add_up(1, up)
            total = dmid[span, :] + norm_back(normal, inverse, gains_ref[0:1, :], up)
            dmid[span, :] = total
            grads[2, span, :] = total.astype(BF)

        back2(slice(0, rows))
        out(dmid, dmid1_hbm)
        out_grad(2)
        loads[7].wait()
        dat[...] = mm(grads[2], sw[...], NT).astype(BF)
        out(dat, dat_hbm)
        dgains_ref[...] = jnp.zeros_like(dgains_ref)
        for i in range(4):
            dgains_ref[i : i + 1, :] = jnp.sum(sums[i], axis=0, keepdims=True)
        for copy in outs:
            copy.wait()

    token = (rows, D)
    halves = (3, rows, wide)
    text = (2, TEXT_LEN, D)
    return pl.pallas_call(
        kernel,
        grid_spec=pltpu.PrefetchScalarGridSpec(
            num_scalar_prefetch=1,
            grid=(1,),
            in_specs=[any_space] * 5
            + [whole(text_kv.shape), whole(bias.shape)]
            + [any_space] * 3
            + [whole(gains.shape)],
            out_specs=[any_space] * 4 + [whole(text), whole((8, D))],
            scratch_shapes=[pltpu.VMEM(token, t) for t in (F32, F32, BF, F32, BF)]
            + [pltpu.VMEM((D, D), BF)] * 3
            + [pltpu.VMEM(text_kv.shape, BF), pltpu.VMEM((3,) + token, BF)]
            + [pltpu.VMEM(token, F32), pltpu.VMEM(token, BF), pltpu.VMEM(token, F32)]
            + [pltpu.VMEM((4, 8, D), F32)]
            + [pltpu.SemaphoreType.DMA((8,)), pltpu.SemaphoreType.DMA((8,))],
        ),
        out_shape=[shape_of(halves, BF)] * 2
        + [shape_of(token, t) for t in (F32, BF)]
        + [shape_of(text, BF)]
        + [shape_of((8, D), F32)],
        compiler_params=params(),
        cost_estimate=cost(0, 0),
        name="middle_backward",
    )(own, d_act3, mid2, upstream, mid1, cq, text_kv, bias, cross_w, query_w, self_w, gains)


def deltas_of(d_out, out):
    prod = d_out.astype(F32) * out.astype(F32)
    high = prod.astype(BF)
    low = (prod - high.astype(F32)).astype(BF)
    row = lax.broadcasted_iota(jnp.int32, (8, PAIR), 0)
    lane = lax.broadcasted_iota(jnp.int32, (8, PAIR), 1)
    pick = jnp.where(lane // HEAD == row, 1.0, 0.0).astype(BF)
    return mm(pick, high, NT) + mm(pick, low, NT)


def key_block_back(k, v, q, d_out, logs, deltas, causal):
    keys = k.shape[0]
    k2, v2 = both_heads(k), both_heads(v)
    s = mm(k2, q, NT)
    dp = mm(v2, d_out, NT)
    weights, grads = [], []
    for h in (0, 1):
        span = slice(h * keys, (h + 1) * keys)
        p = jnp.exp(s[span] - logs[h : h + 1])
        if causal:
            at_k = lax.broadcasted_iota(jnp.int32, (keys, keys), 0)
            at_q = lax.broadcasted_iota(jnp.int32, (keys, keys), 1)
            first = jnp.where(at_q >= at_k, p[:, :keys], 0.0)
            p = first if p.shape[1] == keys else jnp.concatenate([first, p[:, keys:]], axis=1)
        weights.append(p.astype(BF))
        grads.append((p * (dp[span] - deltas[h : h + 1])).astype(BF))
    p2, ds2 = jnp.concatenate(weights, axis=0), jnp.concatenate(grads, axis=0)
    dv, dk = mm(p2, d_out), mm(ds2, q)
    lanes = head_lanes(0)
    dk = jnp.where(lanes, dk[:keys], dk[keys:]).astype(BF)
    dv = jnp.where(lanes, dv[:keys], dv[keys:]).astype(BF)
    return mm(ds2, k2, TN), dk, dv


def attention_backward(scalars, side, qkv, pairs_before, d_out, out, logs):
    rows = qkv.shape[0]
    half = rows // 2
    pairs = D // PAIR
    count = pairs // 2

    def kernel(
        sc_ref, q_ref, k_ref, v_ref, kb_ref, vb_ref, do_ref, out_ref, log_ref, grads_ref, before_ref, dq_ref
    ):
        q = q_ref[...] * SCALE
        d_o = do_ref[...]
        deltas = deltas_of(d_o, out_ref[...])
        log_rows = log_ref[0]

        @pl.when(number(sc_ref, ODD) == 0)
        def _():
            dq_ref[...] = jnp.zeros_like(dq_ref)
            before_ref[...] = jnp.zeros_like(before_ref)

        @pl.when(number(sc_ref, ODD) != 0)
        def _():
            for first in (0, half):
                span = slice(first, first + half)
                dq, dk, dv = key_block_back(
                    kb_ref[span, :], vb_ref[span, :], q, d_o, log_rows, deltas, False
                )
                if first == 0:
                    dq_ref[...] = dq
                else:
                    dq_ref[...] += dq
                before_ref[0, span, :] = dk
                before_ref[1, span, :] = dv

        for first in (0, half):
            span = slice(first, first + half)
            dq, dk, dv = key_block_back(
                k_ref[span, :], v_ref[span, :], q[first:], d_o[first:],
                log_rows[:, first:], deltas[:, first:], True,
            )
            dq_ref[first:, :] += dq
            grads_ref[1, span, :] = dk
            grads_ref[2, span, :] = dv
        grads_ref[0] = (dq_ref[...] * SCALE).astype(BF)

    block = (rows, PAIR)

    def at(offset):
        return pl.BlockSpec(block, lambda p, sc: (0, offset + number(sc, side) * count + p))

    return pl.pallas_call(
        kernel,
        grid_spec=pltpu.PrefetchScalarGridSpec(
            num_scalar_prefetch=1,
            grid=(count,),
            in_specs=[
                at(0), at(pairs), at(2 * pairs), at(0), at(pairs), at(0), at(0),
                pl.BlockSpec((1, 2, rows), lambda p, sc: (number(sc, side) * count + p, 0, 0)),
            ],
            out_specs=[
                pl.BlockSpec((3, rows, PAIR), lambda p, sc: (0, 0, p)),
                pl.BlockSpec((2, rows, PAIR), lambda p, sc: (0, 0, p)),
            ],
            scratch_shapes=[pltpu.VMEM(block, F32)],
        ),
        out_shape=[shape_of((3, rows, D // 2), BF), shape_of((2, rows, D // 2), BF)],
        compiler_params=params(),
        cost_estimate=cost(0, 0),
        name="attention_backward",
    )(scalars, qkv, qkv, qkv, pairs_before, pairs_before, d_out, out, logs)


def project_back(own, grads_own, grads_other, weight, x, name, before=None, others=None):
    rows = x.shape[0]
    count, _, width = grads_own.shape
    first = 3 - count
    chunk = 128

    def kernel(own_ref, ga_ref, gb_ref, wa_ref, wb_ref, x_ref, *refs):
        out_ref, sums_ref, acc_ref, part_sums = refs[-4:]
        j = pl.program_id(0)
        grad = jnp.concatenate([ga_ref[...], gb_ref[...]], axis=1)
        part = mm(grad, jnp.concatenate([wa_ref[...], wb_ref[...]], axis=1), NT)

        @pl.when(j == 0)
        def _():
            acc_ref[...] = part

        @pl.when(j != 0)
        def _():
            acc_ref[...] += part

        @pl.when(j == count - 1)
        def _():
            part_sums[...] = jnp.zeros_like(part_sums)

            def finish(span):
                total = acc_ref[span, :]
                normal, _ = normed(x_ref[span, :].astype(F32))
                for place, values in ((0, total * normal), (1, total)):
                    folded = values[:8]
                    for i in range(8, chunk, 8):
                        folded = folded + values[i : i + 8]
                    part_sums[place] += folded
                out_ref[span, :] = total.astype(BF)

            by_rows(rows, chunk, finish)
            rows_of_sums = [jnp.sum(part_sums[i], axis=0, keepdims=True) for i in (0, 1)]
            if before is None:
                sums_ref[...] = jnp.zeros_like(sums_ref)
                for i in (0, 1):
                    sums_ref[i : i + 1, :] = rows_of_sums[i]
            else:
                all_rows = [rows_of_sums[i] + refs[0][i : i + 1, :] for i in (0, 1)]
                all_rows += [refs[1][i : i + 1, :] for i in range(4)]
                strips = [
                    row[:, c * LANES : (c + 1) * LANES] for row in all_rows for c in range(D // LANES)
                ]
                sums_ref[...] = jnp.concatenate(strips, axis=0).astype(BF)

    grad = pl.BlockSpec((None, rows, width), lambda j, own: (j, 0, 0))
    more = [] if before is None else [before, others]
    sums_shape = shape_of((8, D), F32) if before is None else shape_of((6 * D // LANES, LANES), BF)
    return pl.pallas_call(
        kernel,
        grid_spec=pltpu.PrefetchScalarGridSpec(
            num_scalar_prefetch=1,
            grid=(count,),
            in_specs=[
                grad,
                grad,
                pl.BlockSpec((D, width), lambda j, own: (0, 2 * (first + j) + number(own, CORE))),
                pl.BlockSpec((D, width), lambda j, own: (0, 2 * (first + j) + 1 - number(own, CORE))),
                whole((rows, D)),
            ]
            + [whole(a.shape) for a in more],
            out_specs=[whole((rows, D)), whole(sums_shape.shape)],
            scratch_shapes=[pltpu.VMEM((rows, D), F32), pltpu.VMEM((2, 8, D), F32)],
        ),
        out_shape=[shape_of((rows, D), BF), sums_shape],
        compiler_params=params(),
        cost_estimate=cost(0, 0),
        name=name,
    )(own, grads_own, grads_other, weight, weight, x, *more)


def input_back(d_act, d_act_other, x, d_mid1, gain):
    rows = x.shape[0]
    tile = rows // 4

    def kernel(da_ref, db_ref, x_ref, dm_ref, gain_ref, out_ref):
        normal, inverse = normed(x_ref[...].astype(F32))
        up = da_ref[...].astype(F32) + db_ref[...].astype(F32)
        out_ref[...] = dm_ref[...] + norm_back(normal, inverse, gain_ref[...], up)

    row_block = pl.BlockSpec((tile, D), lambda i: (i, 0))
    return pl.pallas_call(
        kernel,
        grid=(rows // tile,),
        in_specs=[row_block] * 4 + [whole((1, D))],
        out_specs=row_block,
        out_shape=shape_of((rows, D), F32),
        compiler_params=params(),
        cost_estimate=cost(0, 0),
        name="input_back",
    )(d_act, d_act_other, x, d_mid1, gain)


def part_of(operand):
    if isinstance(operand, tuple):
        array, part = operand
        return array, array.shape[1:], lambda *at: (part,) + at
    return operand, operand.shape, None


def spec_of(operand, block, place):
    _, _, lead = part_of(operand)
    if lead is None:
        return pl.BlockSpec(block, place)
    return pl.BlockSpec((None,) + block, lambda *at: lead(*place(*at)))


def joined(refs):
    blocks = [ref[...] for ref in refs]
    return blocks[0] if len(blocks) == 1 else jnp.concatenate(blocks, axis=0)


def put_strips(ref, values, first=0):
    for c in range(values.shape[1] // LANES):
        ref[first + c] = values[:, c * LANES : (c + 1) * LANES]


def row_grad(scalars, lefts, rights, name):
    n = len(lefts)
    left_shapes = [part_of(a)[1] for a in lefts]
    right_shapes = [part_of(a)[1] for a in rights]
    rows = left_shapes[0][1]
    wide = right_shapes[0][1] // 2
    tile = 512
    strips = wide // LANES

    def kernel(sc_ref, *refs):
        left = joined(refs[:n])
        put_strips(refs[-2], mm(left, joined(refs[n : 2 * n]), TN).astype(BF))
        put_strips(refs[-1], mm(left, joined(refs[2 * n : 3 * n]), TN).astype(BF))

    operands = [part_of(a)[0] for a in lefts]
    in_specs = [
        spec_of(a, (shape[0], tile), lambda j, sc: (0, j)) for a, shape in zip(lefts, left_shapes)
    ]
    for place in (lambda j, sc: (0, number(sc, NOT_Y)), lambda j, sc: (0, number(sc, Y))):
        for a, shape in zip(rights, right_shapes):
            in_specs.append(spec_of(a, (shape[0], wide), place))
            operands.append(part_of(a)[0])
    return pl.pallas_call(
        kernel,
        grid_spec=pltpu.PrefetchScalarGridSpec(
            num_scalar_prefetch=1,
            grid=(rows // tile,),
            in_specs=in_specs,
            out_specs=[pl.BlockSpec((strips, tile, LANES), lambda j, sc: (0, j, 0))] * 2,
        ),
        out_shape=[shape_of((strips, rows, LANES), BF)] * 2,
        compiler_params=params(),
        cost_estimate=cost(0, 0),
        name=name,
    )(scalars, *operands)


def column_grad(scalars, lefts, rights, bw, name):
    n = len(lefts)
    left_shapes = [part_of(a)[1] for a in lefts]
    right_shapes = [part_of(a)[1] for a in rights]
    rows = left_shapes[0][1]
    cols = right_shapes[0][1]
    bn = 512
    blocks = rows // bw
    strips = bn // LANES

    def kernel(sc_ref, *refs):
        send_ref, keep_ref, product = refs[-3:]
        product[...] = mm(joined(refs[:n]), joined(refs[n : 2 * n]), TN).astype(BF)
        for i in range(blocks):
            block = product[pl.ds(pl.multiple_of(row_block(sc_ref, i, blocks) * bw, bw), bw), :]
            target = send_ref if i < blocks // 2 else keep_ref
            place = (i % (blocks // 2)) * bw
            for c in range(strips):
                target[c, place : place + bw, :] = block[:, c * LANES : (c + 1) * LANES]

    operands = [part_of(a)[0] for a in lefts] + [part_of(a)[0] for a in rights]
    in_specs = [spec_of(a, shape, lambda j, sc: (0, 0)) for a, shape in zip(lefts, left_shapes)]
    in_specs += [spec_of(a, (shape[0], bn), lambda j, sc: (0, j)) for a, shape in zip(rights, right_shapes)]
    return pl.pallas_call(
        kernel,
        grid_spec=pltpu.PrefetchScalarGridSpec(
            num_scalar_prefetch=1,
            grid=(cols // bn,),
            in_specs=in_specs,
            out_specs=[pl.BlockSpec((strips, rows // 2, LANES), lambda j, sc: (j, 0, 0))] * 2,
            scratch_shapes=[pltpu.VMEM((rows, bn), BF)],
        ),
        out_shape=[shape_of((cols // LANES, rows // 2, LANES), BF)] * 2,
        compiler_params=params(),
        cost_estimate=cost(0, 0),
        name=name,
    )(scalars, *operands)


def block_grads(scalars, bw, lefts, rights, blocks, name, text=None, captions=None):
    count = len(blocks)
    width = 512
    part = width // 2
    row_blocks = D // bw
    in_specs, operands = [], []
    for a, lead in lefts:
        if lead is None:
            in_specs.append(whole(a.shape))
        else:
            in_specs.append(pl.BlockSpec((None,) + a.shape[1:], lambda j, sc, *_, lead=lead: (lead, 0, 0)))
        operands.append(a)
    for a, place in rights:
        if isinstance(a, tuple):
            a, lead = a
            in_specs.append(
                pl.BlockSpec(
                    (None, a.shape[1], width), lambda j, sc, *_, place=place, lead=lead: (lead, 0, place(j))
                )
            )
        elif a.ndim == 3:
            in_specs.append(
                pl.BlockSpec((None, a.shape[1], width), lambda j, sc, *_, place=place: (place(j), 0, 0))
            )
        else:
            in_specs.append(pl.BlockSpec((a.shape[0], width), lambda j, sc, *_, place=place: (0, place(j))))
        operands.append(a)
    n, m = len(lefts), len(rights)
    if text is not None:
        for a, leads in ((text[0], (0, 1)), (text[1], (1, 0))):
            for lead in leads:
                in_specs.append(pl.BlockSpec((None,) + a.shape[1:], lambda j, sc, *_, lead=lead: (lead, 0, 0)))
                operands.append(a)
        wide = text[0].shape[2]
        for at in (0, 1):
            in_specs.append(
                pl.BlockSpec((D // 2, wide), lambda j, sc, *_, at=at: (number(sc, CORE), at))
            )
            operands.append(text[2])
        count += 1
    inputs_count = len(operands)

    prefetched = [scalars] if captions is None else [scalars, captions]

    def kernel(sc_ref, *refs):
        if captions is not None:
            captions_ref, refs = refs[0], refs[1:]
        left_refs, right_refs = refs[:n], refs[n : n + m]
        sent_a, kept_a, sent_b, kept_b, product = refs[inputs_count:]
        j = pl.program_id(0)

        if text is not None:
            text_refs = refs[n + m : inputs_count]

            @pl.when(j == count - 1)
            def _():
                product[...] = jnp.zeros_like(product)
                core = number(sc_ref, CORE)
                for i in (0, 1):
                    mine, others = text_refs[2 * i][...], text_refs[2 * i + 1][...]
                    low = jnp.where(core == 0, mine, others)
                    high = jnp.where(core == 0, others, mine)
                    term = mm(low, text_refs[4][...], NT) + mm(high, text_refs[5][...], NT)
                    at = pl.multiple_of(number(captions_ref, (ROW, ROW_MATE)[i]) * TEXT_LEN, TEXT_LEN)
                    span = pl.ds(at, TEXT_LEN)
                    product[span, :] = add(product[span, :], term)

        for at, (left_places, right_places) in enumerate(blocks):

            @pl.when(j == at)
            def _(left_places=left_places, right_places=right_places):
                left = joined([left_refs[i] for i in left_places])
                right = joined([right_refs[i] for i in right_places])
                product[...] = mm(left, right, TN).astype(BF)

        eighth = part // 2
        sent_a[0] = product[:, pl.ds(pl.multiple_of(number(sc_ref, NOT_Y) * eighth, eighth), eighth)]
        kept_a[0] = product[:, pl.ds(pl.multiple_of(number(sc_ref, Y) * eighth, eighth), eighth)]
        for i in range(row_blocks):
            rows = product[pl.ds(pl.multiple_of(row_block(sc_ref, i, row_blocks) * bw, bw), bw), part:]
            target = sent_b if i < row_blocks // 2 else kept_b
            place = (i % (row_blocks // 2)) * bw
            for c in (0, 1):
                target[c, place : place + bw, :] = rows[:, c * LANES : (c + 1) * LANES]

    a_block, b_block = (1, D, LANES), (2, D // 2, LANES)
    return pl.pallas_call(
        kernel,
        grid_spec=pltpu.PrefetchScalarGridSpec(
            num_scalar_prefetch=len(prefetched),
            grid=(count,),
            in_specs=in_specs,
            out_specs=[
                pl.BlockSpec(a_block, lambda j, sc, *_: (j, 0, 0)),
                pl.BlockSpec(a_block, lambda j, sc, *_: (j, 0, 0)),
                pl.BlockSpec(b_block, lambda j, sc, *_: (j, 0, 0)),
                pl.BlockSpec(b_block, lambda j, sc, *_: (j, 0, 0)),
            ],
            scratch_shapes=[pltpu.VMEM((D, width), BF)],
        ),
        out_shape=[
            shape_of((count, D, LANES), BF),
            shape_of((count, D, LANES), BF),
            shape_of((2 * count, D // 2, LANES), BF),
            shape_of((2 * count, D // 2, LANES), BF),
        ],
        compiler_params=params(),
        cost_estimate=cost(0, 0),
        name=name,
    )(*prefetched, *operands)


def swap(block, axis, bit):
    route = [(i, i ^ (1 << bit)) for i in range(lax.axis_size(axis))]
    return lax.ppermute(block, axis, route)


def pick(block, place, dim):
    return lax.dynamic_index_in_dim(block, place, dim, keepdims=False)


def bit_of(index, bit):
    return (index >> bit) & 1


def add(a, b):
    return (a.astype(F32) + b.astype(F32)).astype(BF)


class Order:
    def __init__(self):
        self.token = None

    def then(self, *values):
        if self.token is not None:
            values = lax.optimization_barrier(values + (self.token,))[:-1]
        return values if len(values) > 1 else values[0]

    def mark(self, value):
        self.token = value
        return value


def exchange(block, axis, mask):
    route = [(i, i ^ mask) for i in range(lax.axis_size(axis))]
    return lax.ppermute(block, axis, route)


def flat(block):
    return block.reshape(-1, LANES)


def rows_at(first, count):
    return pl.ds(pl.multiple_of(first, 16) if not isinstance(first, int) else first, count)


def repeat(count, step):
    def one(i, carry):
        step(i)
        return carry

    lax.fori_loop(0, count, one, 0)


def sum_stage(order, name, scalars, inputs, outputs, work):
    n = len(inputs)

    def kernel(sc_ref, *refs):
        work(sc_ref, refs[:n], refs[n:])

    outs = pl.pallas_call(
        kernel,
        grid_spec=pltpu.PrefetchScalarGridSpec(
            num_scalar_prefetch=1,
            grid=(1,),
            in_specs=[whole(a.shape) for a in inputs],
            out_specs=[whole((rows, LANES)) for rows in outputs],
        ),
        out_shape=[shape_of((rows, LANES), BF) for rows in outputs],
        compiler_params=params(),
        cost_estimate=cost(0, 0),
        name=name,
    )(scalars, *inputs)
    order.mark(outs[0])
    return outs


class Streams:
    def __init__(self, a_strips, a_rows, b_strips, b_rows, left):
        self.a_strips, self.a_rows, self.b_strips, self.b_rows = a_strips, a_rows, b_strips, b_rows // 2
        self.left = left
        self.a_half = a_strips * left * a_rows
        self.b_half = b_strips * left * (b_rows // 2)
        self.a_first, self.b_first = 2 * self.a_half, 2 * self.b_half
        self.piece = (self.a_half + self.b_half) // left

    def by_place(self, kept, came, sent, sent_at, keep, mine, a):
        rows = 2 * (self.a_rows if a else self.b_rows)
        strips = self.a_strips if a else self.b_strips

        def step(i):
            for out, at, side in ((sent, sent_at, 1 - mine), (keep, 0, mine)):
                first = (2 * i + side) * rows
                out[rows_at(at + i * rows, rows), :] = (
                    kept[rows_at(first, rows), :] + came[rows_at(first, rows), :]
                )

        repeat(strips * self.left // 2, step)

    def second(self, kept, came, sent, keep, mine, a, came_at=0):
        rows = self.a_rows if a else self.b_rows
        strips = self.a_strips if a else self.b_strips

        def step(i):
            for out, side in ((sent, 1 - mine), (keep, mine)):
                first = i * 2 * rows + side * rows
                out[rows_at(i * rows, rows), :] = (
                    kept[rows_at(first, rows), :] + came[rows_at(came_at + first, rows), :]
                )

        repeat(strips * self.left, step)

    def third(self, kept_a, came_a, kept_b, came_b, sent, keep, place):
        a_rows, b_rows, left = self.a_rows, self.b_rows, self.left
        mine = place & 1
        for j in range(left // 2):
            for out, side in ((sent, 1 - mine), (keep, mine)):
                block = 2 * j + side
                base = j * self.piece

                def a_step(i, out=out, block=block, base=base):
                    first = (i * left + block) * a_rows
                    out[rows_at(base + i * a_rows, a_rows), :] = (
                        kept_a[rows_at(first, a_rows), :] + came_a[rows_at(first, a_rows), :]
                    )

                def b_step(i, out=out, block=block, base=base):
                    first = (i * left + block) * b_rows
                    at = base + self.a_strips * a_rows + i * b_rows
                    out[rows_at(at, b_rows), :] = (
                        kept_b[rows_at(first, b_rows), :] + came_b[rows_at(first, b_rows), :]
                    )

                repeat(self.a_strips, a_step)
                repeat(self.b_strips, b_step)


def add_rows(a, b, a_at, out, out_at, count):
    chunk = math.gcd(count, 256)

    def step(i):
        span = rows_at(a_at + i * chunk, chunk)
        out[rows_at(out_at + i * chunk, chunk), :] = a[span, :] + b[span, :]

    repeat(count // chunk, step)


def total_over_rest(pieces):
    for bit in range(2, lax.axis_size("dp").bit_length() - 1):
        pieces = [add(piece, swap(piece, "dp", bit)) for piece in pieces]
    return pieces


class Spread:
    def __init__(self, order, scalars, piece):
        self.order, self.scalars, self.piece = order, scalars, piece
        self.y = swap(order.then(piece), "dp", 1)

    def forward(self):
        self.piece, self.y = self.order.then(self.piece, self.y)
        self.core = swap(self.piece, "dp", 0)
        self.both = swap(self.y, "dp", 0)

    def finish(self, rows, shapes, write, name, rider=0):
        pieces = self.order.then(self.piece, self.core, self.y, self.both)
        out_shapes = list(shapes) + ([(rider, LANES)] if rider else [])

        def kernel(sc_ref, *refs):
            outs = refs[4:]
            for at in range(4):
                for k in range(4):

                    @pl.when(number(sc_ref, QUARTER) == at ^ k)
                    def _(at=at, k=k):
                        write(outs, refs[k], at & 1, at >> 1)

            if rider:
                total = refs[0][rows:, :].astype(F32)
                for ref in refs[1:4]:
                    total = total + ref[rows:, :].astype(F32)
                outs[-1][...] = total

        outs = pl.pallas_call(
            kernel,
            grid_spec=pltpu.PrefetchScalarGridSpec(
                num_scalar_prefetch=1,
                grid=(1,),
                in_specs=[whole(self.piece.shape)] * 4,
                out_specs=[whole(shape) for shape in out_shapes],
            ),
            out_shape=[shape_of(shape, F32) for shape in out_shapes],
            compiler_params=params(),
            cost_estimate=cost(0, 0),
            name=name,
        )(self.scalars, *pieces)
        self.order.mark(outs[0])
        return outs

    def finish_text(self, rows, bw):
        pieces = self.order.then(self.piece, self.core, self.y, self.both)
        shards = lax.axis_size("seq")
        half = bw // 2

        def kernel(sc_ref, *refs):
            out_ref = refs[4]

            def one(i, carry):
                place = i ^ number(sc_ref, ME)
                seq_at = (place & 1) * (shards // 2) + (place >> 1)
                at = pl.multiple_of(seq_at * rows, rows)
                first = pl.multiple_of(i * bw, bw)
                for core in (0, 1):
                    for y in (0, 1):
                        for k in range(4):

                            @pl.when(number(sc_ref, QUARTER) == (2 * y + core) ^ k)
                            def _(ref=refs[k], core=core, y=y):
                                col = core * (D // 2) + y * LANES
                                out_ref[pl.ds(first, bw), col : col + LANES] = ref[
                                    pl.ds(at, bw), :
                                ].astype(F32)
                                for c in (0, 1):
                                    col = core * (D // 2) + 256 + c * LANES
                                    out_ref[pl.ds(first + y * half, half), col : col + LANES] = ref[
                                        rows_at(at + bw + c * half, half), :
                                    ].astype(F32)

                return carry

            lax.fori_loop(0, shards, one, 0)

        return pl.pallas_call(
            kernel,
            grid_spec=pltpu.PrefetchScalarGridSpec(
                num_scalar_prefetch=1,
                grid=(1,),
                in_specs=[whole(self.piece.shape)] * 4,
                out_specs=whole((shards * bw, D)),
            ),
            out_shape=shape_of((shards * bw, D), F32),
            compiler_params=params(),
            cost_estimate=cost(0, 0),
            name="text_finish",
        )(self.scalars, *pieces)


def numbers_of(per_image):
    me, dp = lax.axis_index("seq"), lax.axis_index("dp")
    packed = (me % per_image) | ((dp & 3) << 1) | (me << 3)
    return packed.astype(jnp.int32).reshape(1)


def captions_of(image_text, image_segment, per_image):
    me, dp = lax.axis_index("seq"), lax.axis_index("dp")
    images = image_text.shape[0] // lax.axis_size("dp")
    image = images * dp + me // per_image
    image_mate = images * (dp ^ 1) + me // per_image
    packed = image_text[image] | (image_segment[image] << 8) | (image_text[image_mate] << 16)
    return packed.astype(jnp.int32).reshape(1)


def body(
    inputs,
    text_state,
    text_segment,
    image_text,
    image_segment,
    self_gain,
    self_shift,
    qkv_weight,
    self_weight,
    cross_gain,
    cross_shift,
    query_weight,
    text_weight,
    cross_weight,
    feed_gain,
    feed_shift,
    up_weight,
    down_weight,
    cotangent,
):
    rows = inputs.shape[0]
    shards = lax.axis_size("seq")
    groups = lax.axis_size("dp")
    me, dp = lax.axis_index("seq"), lax.axis_index("dp")
    per_image = IMG_TOK // rows
    order = Order()
    scalars = numbers_of(per_image)
    captions = captions_of(image_text, image_segment, per_image)

    def over_core(block):
        return swap(block, "dp", 0)

    seq_bits = shards.bit_length() - 1
    dp_bits = groups.bit_length() - 1
    spread_steps = [("seq", b) for b in reversed(range(seq_bits))] + [("dp", 1), ("dp", 0)]
    bw = D // shards
    bw_ff = FF // (2 * shards)

    even_to_odd = [(i, i + 1) for i in range(0, shards, 2)]
    odd_to_even = [(i + 1, i) for i in range(0, shards, 2)]
    x_before = lax.ppermute(inputs, "seq", even_to_odd)
    cot_mate = over_core(cotangent)
    gain1, shift1 = self_gain.reshape(1, D), self_shift.reshape(1, D)
    act1, qkv, norms = norm_project(inputs, gain1, shift1, qkv_weight, 0, "norm_project")
    act1_mate = over_core(act1)
    own_out, own_log = causal_forward(qkv, norms)
    order.mark(own_out)
    text_state = order.then(text_state)
    text_kv, bias_row, text_row, text_row_mate = text_project(
        captions, text_state, text_segment, text_weight
    )
    order.mark(text_kv)
    x_before, act1_mate, cot_mate = order.then(x_before, act1_mate, cot_mate)
    act1_before, pairs_before, norms_before = norm_project(
        x_before, gain1, shift1, qkv_weight, D, "norm_project_before"
    )
    before_mate = over_core(act1_before)
    attended, log_rows = earlier_forward(
        scalars, qkv, pairs_before, norms, norms_before, own_out, own_log
    )
    order.mark(attended)
    before_mate, attended = order.then(before_mate, attended)
    attended_mate = over_core(attended)
    gains = jnp.stack([cross_gain, cross_shift, feed_gain, feed_shift] * 2)
    mid1, cq, mid2, acts = middle_forward(
        attended, inputs, self_weight, query_weight, cross_weight, gains, text_kv, bias_row
    )
    order.mark(mid1)
    attended_mate, acts = order.then(attended_mate, acts)
    acts_mate = over_core(acts)
    hid_other, d_act3 = feed_half(
        scalars, OTHER, acts, cotangent, up_weight, down_weight, shards, None
    )
    order.mark(d_act3)
    d_act3, acts_mate, hid_other = order.then(d_act3, acts_mate, hid_other)
    hid_mate = over_core(hid_other)
    hid_own, d_act3 = feed_half(
        scalars, CORE, acts, cotangent, up_weight, down_weight, shards, d_act3
    )
    order.mark(d_act3)
    hid_mate = order.then(hid_mate)

    left = shards // 2
    feed = Streams(D // 2 // LANES, bw_ff, FF // 2 // LANES, bw, left)
    feed_later = Streams(D // 2 // LANES, bw_ff, FF // 2 // LANES, bw, left // 2)
    mids = Streams(6, bw, 12, bw, left)
    qkvs = Streams(3, bw, 6, bw, left)
    others = range(1, left)

    sent, feed_a = row_grad(
        scalars, [(hid_own, 0), (hid_mate, 0)], [cotangent, cot_mate], "down_grad"
    )
    order.mark(sent)
    feed_a = flat(feed_a)
    came_fa = swap(flat(sent), "dp", 1)
    acts_late = order.then(acts)
    sent, feed_b = column_grad(
        scalars, [(acts_late, 2), (acts_mate, 2)], [(hid_own, 1), (hid_mate, 1)], bw, "up_grad"
    )
    order.mark(sent)
    feed_b = flat(feed_b)
    came_fb = swap(flat(sent), "seq", 0)

    d_act3 = order.then(d_act3)
    g_mine, g_sent, d_mid1, d_att, text_grads, d_gains = middle_backward(
        scalars, d_act3, mid2, cotangent, mid1, cq, text_kv, bias_row, cross_weight, query_weight,
        self_weight, gains,
    )
    order.mark(d_mid1)
    g_mate = over_core(g_sent)
    text_mate = over_core(text_grads)
    g_mine, g_mate, text_mate = order.then(g_mine, g_mate, text_mate)
    lefts = [(acts, 1), (acts_mate, 1), (acts, 0), (acts_mate, 0), (attended, None), (attended_mate, None)]
    lefts += [(text_row, None), (text_row_mate, None)]
    rights = [(g_mine, lambda j: jnp.minimum(j, 2)), (g_mate, lambda j: jnp.minimum(j, 2))]
    rights += [((text_grads, 0), lambda j: jnp.clip(j - 3, 0, 1))]
    rights += [((text_mate, 1), lambda j: jnp.clip(j - 3, 0, 1))]
    blocks = [((0, 1), (0, 1)), ((2, 3), (0, 1)), ((4, 5), (0, 1)), ((6, 7), (2, 3)), ((6, 7), (2, 3))]
    sent_a, mid_a, sent_b, mid_b = block_grads(
        scalars, bw, lefts, rights, blocks, "middle_grads",
        text=(text_grads, text_mate, text_weight), captions=captions,
    )
    order.mark(mid_a)
    mid_sent_a, mid_sent_b = flat(sent_a), flat(sent_b)
    mid_a, mid_b = flat(mid_a), flat(mid_b)

    def second(streams, name, kept_a, came_a, kept_b, came_b=None):
        def work(sc, ins, outs):
            b_at = 0 if came_b is not None else 2 * streams.a_half
            streams.second(ins[0], ins[1], outs[0], outs[2], number(sc, X), True)
            streams.second(ins[2], ins[-1] if b_at == 0 else ins[1], outs[1], outs[3], number(sc, Y), False, b_at)

        inputs = order.then(kept_a, came_a, kept_b, *([] if came_b is None else [came_b]))
        sent_x, sent_y, kept_a, kept_b = sum_stage(
            order, name, scalars, inputs, [streams.a_half, streams.b_half] * 2, work
        )
        return kept_a, sent_x, kept_b, sent_y

    def third(streams, name, kept_a, came_a, kept_b, came_b, rider=0, skip=0, late=False):
        def work(sc, ins, outs):
            streams.third(ins[0], ins[1], ins[2], ins[3], outs[0], outs[1], number(sc, PLACE) >> skip)
            if rider:
                count = streams.left // 2 * streams.piece
                span = slice(streams.a_half, streams.a_half + rider)
                for out in outs:
                    out[count : count + rider, :] = ins[0][span, :] + ins[1][span, :]

        inputs = order.then(kept_a, came_a, kept_b, came_b)
        out_rows = streams.left // 2 * streams.piece + rider
        sent, kept = sum_stage(order, name, scalars, inputs, [out_rows] * 2, work)
        return kept, (lambda: swap(order.then(sent), "seq", 1 + skip)) if late else swap(sent, "seq", 1 + skip)

    def further(streams, name, kept, came, rider=0, skip=0):
        blocks = streams.left // 2
        for bit in range(1, streams.left.bit_length() - 1):
            half = blocks // 2 * streams.piece

            def work(sc, ins, outs, bit=bit, half=half):
                mine = (number(sc, PLACE) >> (bit + skip)) & 1
                for i in range(half // streams.piece):
                    for out, side in ((outs[0], 1 - mine), (outs[1], mine)):
                        add_rows(
                            ins[0], ins[1], (2 * i + side) * streams.piece, out, i * streams.piece, streams.piece
                        )
                if rider:
                    for out in outs:
                        out[half : half + rider, :] = ins[0][2 * half :, :] + ins[1][2 * half :, :]

            inputs = order.then(kept, came)
            sent, kept = sum_stage(order, name, scalars, inputs, [half + rider] * 2, work)
            came = swap(sent, "seq", bit + 1 + skip)
            blocks //= 2
        return kept, came

    def fourth(streams, name, kept, came, rider=0):
        def work(sc, ins, outs):
            add_rows(ins[0], ins[1], 0, outs[0], 0, streams.piece + rider)

        inputs = order.then(kept, came)
        (total,) = sum_stage(order, name, scalars, inputs, [streams.piece + rider], work)
        return total_over_rest([total])[0]

    mid2_late = order.then(mid2)
    output = feed_output(scalars, mid2_late, hid_own, hid_other, down_weight, shards)
    order.mark(output)

    mid_sent_a, mid_sent_b, came_fa, came_fb = order.then(mid_sent_a, mid_sent_b, came_fa, came_fb)
    came_ma, came_mb = swap(mid_sent_a, "dp", 1), swap(mid_sent_b, "seq", 0)
    inputs_f = order.then(feed_a, came_fa, feed_b, came_fb)

    def work_f(sc, ins, outs):
        mine = number(sc, PLACE) & 1
        feed.by_place(ins[0], ins[1], outs[0], 0, outs[1], mine, True)
        feed.by_place(ins[2], ins[3], outs[0], feed.a_half, outs[2], mine, False)

    feed_sent, feed_a, feed_b = sum_stage(
        order, "feed_second", scalars, inputs_f, [feed.a_half + feed.b_half, feed.a_half, feed.b_half], work_f
    )
    came_f = swap(feed_sent, "seq", 1)

    d_att = order.then(d_att)
    att_other, before_other = attention_backward(
        scalars, OTHER, qkv, pairs_before, d_att, attended, log_rows
    )
    order.mark(att_other)
    att_mate, before_mate_grads = over_core(att_other), over_core(before_other)
    d_att = order.then(d_att)
    att_own, before_own = attention_backward(scalars, CORE, qkv, pairs_before, d_att, attended, log_rows)
    order.mark(att_own)
    mid_a, mid_sent_x, mid_b, mid_sent_y = second(mids, "mid_second", mid_a, came_ma, mid_b, came_mb)
    came_ma, came_mb = swap(mid_sent_x, "seq", 0), swap(mid_sent_y, "dp", 1)

    act1_late, att_mate, before_mate_grads = order.then(act1, att_mate, before_mate_grads)
    lefts = [(act1_late, None), (act1_mate, None), (act1_before, None), (before_mate, None)]
    rights = [(att_own, lambda j: j), (att_mate, lambda j: j)]
    rights += [(before_own, lambda j: jnp.maximum(j - 1, 0))]
    rights += [(before_mate_grads, lambda j: jnp.maximum(j - 1, 0))]
    blocks = [((0, 1), (0, 1))] + [((0, 1, 2, 3), (0, 1, 2, 3))] * 2
    sent_a, qkv_a, sent_b, qkv_b = block_grads(scalars, bw, lefts, rights, blocks, "qkv_grads")
    order.mark(qkv_a)
    came_qa, came_qb = swap(flat(sent_a), "dp", 1), swap(flat(sent_b), "seq", 0)
    before_own = order.then(before_own)
    d_act_before, sums_before = project_back(
        scalars, before_own, before_other, qkv_weight, x_before, "project_back_before"
    )
    order.mark(d_act_before)
    mid_left = third(mids, "mid_third", mid_a, came_ma, mid_b, came_mb)
    feed_a, feed_sent_x, feed_b, feed_sent_y = second(feed_later, "feed_third", feed_a, came_f, feed_b)
    came_fa, came_fb = swap(feed_sent_x, "seq", 0), swap(feed_sent_y, "dp", 1)
    att_own = order.then(att_own)
    d_act, rider = project_back(
        scalars, att_own, att_other, qkv_weight, inputs, "project_back", sums_before, d_gains
    )
    order.mark(d_act)
    rides = rider.shape[0]

    inputs_q = order.then(flat(qkv_a), came_qa, flat(qkv_b), came_qb, rider)

    def work_q(sc, ins, outs):
        qkvs.second(ins[0], ins[1], outs[0], outs[2], number(sc, X), True)
        qkvs.second(ins[2], ins[3], outs[1], outs[3], number(sc, Y), False)
        for out in (outs[0], outs[2]):
            out[qkvs.a_half : qkvs.a_half + rides, :] = ins[4][...]

    sent_x, sent_y, qkv_a, qkv_b = sum_stage(
        order, "qkv_second", scalars, inputs_q,
        [qkvs.a_half + rides, qkvs.b_half] * 2, work_q,
    )
    came_qa, came_qb = swap(sent_x, "seq", 0), swap(sent_y, "dp", 1)
    mid_left = further(mids, "mid_further", *mid_left)
    feed_kept, feed_start = third(
        feed_later, "feed_join", feed_a, came_fa, feed_b, came_fb, skip=1, late=True
    )
    qkv_left = third(qkvs, "qkv_third", qkv_a, came_qa, qkv_b, came_qb, rides)
    d_act_before = order.then(d_act_before)
    d_act_late = lax.ppermute(d_act_before, "seq", odd_to_even)
    mid_piece = fourth(mids, "mid_fourth", *mid_left)

    text_rows = 2 * bw
    text_piece = jnp.concatenate(
        [mid_piece[5 * bw : 6 * bw], mid_piece[11 * bw : 12 * bw]], axis=0
    )
    order.mark(text_piece)
    text_pieces = [text_piece] + [exchange(text_piece, "seq", 2 * k) for k in others]

    def join(name, pieces):
        def work(sc, ins, outs):
            for i, ref in enumerate(ins):
                count = ref.shape[0]
                outs[0][i * count : (i + 1) * count, :] = ref[...]

        inputs = order.then(*pieces)
        return sum_stage(order, name, scalars, inputs, [len(pieces) * pieces[0].shape[0]], work)[0]

    qkv_left = further(qkvs, "qkv_further", *qkv_left, rides)
    text_block = join("text_join", text_pieces)
    came_text = swap(text_block, "seq", 0)
    mid_all = Spread(order, scalars, mid_piece)
    d_act, d_act_late = order.then(d_act, d_act_late)
    input_grad = input_back(d_act, d_act_late, inputs, d_mid1, gain1)
    order.mark(input_grad)
    qkv_piece = fourth(qkvs, "qkv_fourth", *qkv_left, rides)
    qkv_all = Spread(order, scalars, qkv_piece)
    feed_left = (feed_kept, feed_start())
    text_block = join("text_join", [text_block, came_text])
    text_all = Spread(order, scalars, text_block)
    mid_all.forward()

    b_rows = bw // 2

    def write_feed(outs, ref, at_core, y):
        at = 0
        strips = D // 2 // LANES
        for c in range(strips):
            col = y * (D // 2) + c * LANES
            outs[0][at_core * bw_ff : (at_core + 1) * bw_ff, col : col + LANES] = ref[
                at + c * bw_ff : at + (c + 1) * bw_ff, :
            ].astype(F32)
        at = at + strips * bw_ff
        per = bw_ff // LANES
        for c in range(FF // 2 // LANES):
            s, inside = divmod(c, per)
            col = (2 * s + at_core) * bw_ff + inside * LANES
            outs[1][y * b_rows : (y + 1) * b_rows, col : col + LANES] = ref[
                at + c * b_rows : at + (c + 1) * b_rows, :
            ].astype(F32)

    def writer(targets):
        count = len(targets)

        def write(outs, ref, at_core, y):
            for j, where in enumerate(targets):
                if where is None:
                    continue
                out, first = where
                col = first[at_core]
                outs[out][:, col + y * LANES : col + (y + 1) * LANES] = ref[
                    j * bw : (j + 1) * bw, :
                ].astype(F32)
                for half in (0, 1):
                    row_at = count * bw + (2 * j + half) * b_rows
                    to = col + 256 + half * LANES
                    outs[out][y * b_rows : (y + 1) * b_rows, to : to + LANES] = ref[
                        row_at : row_at + b_rows, :
                    ].astype(F32)

        return write

    targets = [(0, (0, 512)), (1, (0, 512)), (2, (0, 512)), (3, (0, 1024)), (3, (512, 1536)), None]
    cross_grad, query_grad, self_grad, text_weight_grad = mid_all.finish(
        mids.piece, [(bw, D), (bw, D), (bw, D), (bw, 2 * D)], writer(targets), "mids_finish"
    )
    qkv_all.forward()
    text_all.forward()
    targets = [(0, (0, 512)), (0, (1024, 1536)), (0, (2048, 2560))]
    qkv_grad, sums = qkv_all.finish(
        qkvs.piece, [(bw, 3 * D)], writer(targets), "qkv_finish", rider=rides
    )
    feed_left = further(feed_later, "feed_further", *feed_left, skip=1)
    feed_piece = fourth(feed_later, "feed_fourth", *feed_left)
    feed_all = Spread(order, scalars, feed_piece)
    text_grad = text_all.finish_text(text_rows, bw)
    order.mark(text_grad)
    feed_all.forward()
    down_grad, up_grad = feed_all.finish(
        feed.piece, [(2 * bw_ff, D), (bw, FF)], write_feed, "feed_finish"
    )
    sums = lax.dynamic_slice_in_dim(sums.reshape(6, D), me * bw, bw, 1)
    return (
        output,
        input_grad,
        text_grad.reshape(text_state.shape),
        sums[0],
        sums[1],
        qkv_grad,
        self_grad,
        sums[2],
        sums[3],
        query_grad,
        text_weight_grad,
        cross_grad,
        sums[4],
        sums[5],
        up_grad,
        down_grad,
    )


def solution(mesh):
    tokens = P(("dp", "seq"), None)
    return jax.shard_map(
        body,
        mesh=mesh,
        in_specs=(tokens,) + (P(),) * 17 + (tokens,),
        out_specs=(
            tokens,
            tokens,
            P(),
            P("seq"),
            P("seq"),
            P("seq", None),
            P("seq", None),
            P("seq"),
            P("seq"),
            P("seq", None),
            P("seq", None),
            P("seq", None),
            P("seq"),
            P("seq"),
            P("seq", None),
            P("seq", None),
        ),
        check_vma=False,
    )
```

```python
import functools
import math

import jax
import jax.numpy as jnp
from jax import lax
from jax.experimental import pallas as pl
from jax.experimental.pallas import tpu as pltpu
from jax.sharding import PartitionSpec as P

D = 1024
HEADS = 16
HEAD = 64
FF = 4096
TEXT_LEN = 128
IMG_TOK = 1024
PAIR = 2 * HEAD
LANES = 128
SCALE = 1.0 / math.sqrt(HEAD)

NEGATIVE = -1e30
EPSILON = 1e-05
BF = jnp.bfloat16
F32 = jnp.float32
NN = (((1,), (0,)), ((), ()))
NT = (((1,), (1,)), ((), ()))
TN = (((0,), (0,)), ((), ()))
VMEM_LIMIT = 65000 * 1024
ODD, CORE, OTHER, X, Y, NOT_Y, PLACE, QUARTER, ME, GROUP = range(10)


def mm(a, b, dims=NN):
    return lax.dot_general(a, b, dims, preferred_element_type=F32)


def normed(values):
    average = jnp.mean(values, axis=-1, keepdims=True)
    centered = values - average
    inverse = lax.rsqrt(jnp.mean(centered * centered, axis=-1, keepdims=True) + EPSILON)
    return centered * inverse, inverse


def norm_back(normal, inverse, gain, upstream):
    w = upstream * gain
    along = jnp.mean(w * normal, axis=-1, keepdims=True)
    return inverse * (w - jnp.mean(w, axis=-1, keepdims=True) - normal * along)


def head_lanes(h):
    lane = lax.broadcasted_iota(jnp.int32, (1, PAIR), 1)
    return (lane >= h * HEAD) & (lane < (h + 1) * HEAD)


def only_head(block, h):
    return jnp.where(head_lanes(h), block, jnp.zeros_like(block))


def by_rows(rows, size, step):
    def one(i, carry):
        step(pl.ds(pl.multiple_of(i * size, size), size))
        return carry

    if rows == size:
        step(slice(0, rows))
        return
    lax.fori_loop(0, rows // size, one, 0, unroll=2)


def params(grid_dims=1):
    return pltpu.CompilerParams(
        dimension_semantics=("arbitrary",) * grid_dims, vmem_limit_bytes=VMEM_LIMIT
    )


def cost(flops, moved):
    return pl.CostEstimate(flops=1, bytes_accessed=1, transcendentals=0)


def number(ref, which):
    packed = ref[0]
    if which == ODD:
        return packed & 1
    if which == CORE:
        return (packed >> 1) & 1
    if which == OTHER:
        return 1 - ((packed >> 1) & 1)
    if which == Y:
        return (packed >> 2) & 1
    if which == NOT_Y:
        return 1 - ((packed >> 2) & 1)
    if which == QUARTER:
        return (packed >> 1) & 3
    if which == ME:
        return (packed >> 3) & 4095
    if which == GROUP:
        return ((packed >> 1) & 3) | ((packed >> 15) << 2)
    if which == X:
        return (packed >> 3) & 1
    return (packed >> 4) & 2047


def image_entry(scalars_ref, table_ref, per_image, groups, other=0):
    group = number(scalars_ref, GROUP) ^ other
    return table_ref[table_ref.shape[0] // groups * group + number(scalars_ref, ME) // per_image]


def row_block(ref, i, blocks):
    x = number(ref, X)
    half = blocks // 2
    return 2 * i + 1 - x if i < half else 2 * (i - half) + x


def whole(shape):
    zeros = (0,) * len(shape)
    return pl.BlockSpec(shape, lambda *_: zeros)


def shape_of(shape, dtype):
    return jax.ShapeDtypeStruct(shape, dtype)


def head_sums(block):
    wide = block.astype(F32)
    lane = lax.broadcasted_iota(jnp.int32, (D, PAIR), 1)
    row = lax.broadcasted_iota(jnp.int32, (D, PAIR), 0)
    pick = jnp.where(row // HEAD == lane, 1.0, 0.0).astype(BF)
    return jnp.max(mm((wide * wide).astype(BF), pick), axis=0, keepdims=True)


def small_scores(q_sums, k_sums):
    return jnp.max(q_sums * k_sums) * (SCALE * SCALE) < 75.0 * 75.0


def norm_project(x, gain, shift, weight, first_col, name):
    rows, width = x.shape
    cols = weight.shape[1] - first_col
    bn = D

    def kernel(x_ref, gain_ref, shift_ref, w_ref, act_ref, out_ref, norm_ref):
        j = pl.program_id(0)

        @pl.when(j == 0)
        def _():
            norm_ref[...] = jnp.zeros_like(norm_ref)

            def norm_rows(span):
                normal, _ = normed(x_ref[span, :].astype(F32))
                act_ref[span, :] = (normal * gain_ref[...] + shift_ref[...]).astype(BF)

            by_rows(rows, 128, norm_rows)

        out = mm(act_ref[...], w_ref[...]).astype(BF)
        out_ref[...] = out
        for i in range(cols // bn - 1):

            @pl.when(j == i)
            def _(i=i):
                norm_ref[i : i + 1, :] = head_sums(out)

    return pl.pallas_call(
        kernel,
        grid=(cols // bn,),
        in_specs=[
            whole((rows, width)),
            whole((1, width)),
            whole((1, width)),
            pl.BlockSpec((width, bn), lambda j: (0, first_col // bn + j)),
        ],
        out_specs=[
            whole((rows, width)),
            pl.BlockSpec((rows, bn), lambda j: (0, j)),
            whole((8, PAIR)),
        ],
        out_shape=[
            shape_of((rows, width), BF),
            shape_of((rows, cols), BF),
            shape_of((8, PAIR), F32),
        ],
        compiler_params=params(),
        cost_estimate=cost(0, 0),
        name=name,
    )(x, gain, shift, weight)


def with_ones(v, h):
    ones = jnp.where(head_lanes(h), jnp.ones_like(v), jnp.zeros_like(v))
    return jnp.concatenate([only_head(v, h), ones], axis=1)


def rows_of(columns):
    turned = columns.T
    return turned[0:1], turned[HEAD : HEAD + 1]


def columns_of(log_rows):
    rows = log_rows.shape[1]
    turned = jnp.concatenate([log_rows, jnp.zeros((6, rows), F32)], axis=0).T
    return jnp.where(head_lanes(0), turned[:, 0:1], turned[:, 1:2])


def causal_forward(qkv, norms):
    rows = qkv.shape[0]
    half = rows // 2
    pairs = D // PAIR

    def kernel(q_ref, k_ref, v_ref, norm_ref, out_ref, log_ref, small_ref):
        @pl.when(pl.program_id(0) == 0)
        def _():
            small_ref[0] = small_scores(norm_ref[0:1, :], norm_ref[1:2, :]).astype(jnp.int32)

        below = lax.broadcasted_iota(jnp.int32, (half, half), 0) >= lax.broadcasted_iota(
            jnp.int32, (half, half), 1
        )

        @pl.when(small_ref[0] != 0)
        def _():
            early, late = slice(0, half), slice(half, rows)
            q_early, q_late = q_ref[early, :] * SCALE, q_ref[late, :] * SCALE
            k, v = k_ref[...], v_ref[...]
            values = [with_ones(v, h) for h in (0, 1)]
            p = jnp.exp(mm(q_early, both_heads(k[early]), NT))
            p = jnp.concatenate(
                [jnp.where(below, p[:, :half], 0.0).astype(BF), jnp.where(below, p[:, half:], 0.0).astype(BF)], axis=1
            )
            first = mm(p, jnp.concatenate([values[0][early], values[1][early]], axis=0))
            p = jnp.exp(mm(q_late, both_heads(k), NT))
            parts = [p[:, i * half : (i + 1) * half] for i in range(4)]
            parts = [parts[0], jnp.where(below, parts[1], 0.0), parts[2], jnp.where(below, parts[3], 0.0)]
            p = jnp.concatenate([part.astype(BF) for part in parts], axis=1)
            second = mm(p, jnp.concatenate(values, axis=0))
            for span, both in ((early, first), (late, second)):
                out_ref[span, :] = (both[:, :PAIR] / both[:, PAIR:]).astype(BF)
                one, two = rows_of(both[:, PAIR:])
                log_ref[0, 0:1, span] = jnp.log(one)
                log_ref[0, 1:2, span] = jnp.log(two)

        @pl.when(small_ref[0] == 0)
        def _():
            def slowly(span):
                q = q_ref[span, :] * SCALE
                k, v = k_ref[...], v_ref[...]
                at_q = span.start + lax.broadcasted_iota(jnp.int32, (PAIR, rows), 0)
                at_k = lax.broadcasted_iota(jnp.int32, (PAIR, rows), 1)
                total = jnp.zeros((PAIR, PAIR), F32)
                logs = jnp.zeros((PAIR, PAIR), F32)
                for h in (0, 1):
                    s = mm(q, only_head(k, h), NT)
                    s = jnp.where(at_q >= at_k, s, NEGATIVE)
                    top = jnp.max(s, axis=1, keepdims=True)
                    p = jnp.exp(s - top)
                    part = jnp.sum(p, axis=1, keepdims=True)
                    total = total + mm(p.astype(BF), only_head(v, h)) * (1.0 / part)
                    logs = jnp.where(head_lanes(h), top + jnp.log(part), logs)
                out_ref[span, :] = total.astype(BF)
                one, two = rows_of(logs)
                log_ref[0, 0:1, span] = one
                log_ref[0, 1:2, span] = two

            by_rows(rows, PAIR, slowly)

    block = (rows, PAIR)
    return pl.pallas_call(
        kernel,
        grid=(pairs,),
        in_specs=[
            pl.BlockSpec(block, lambda p: (0, p)),
            pl.BlockSpec(block, lambda p: (0, pairs + p)),
            pl.BlockSpec(block, lambda p: (0, 2 * pairs + p)),
            whole(norms.shape),
        ],
        out_specs=[
            pl.BlockSpec(block, lambda p: (0, p)),
            pl.BlockSpec((1, 2, rows), lambda p: (p, 0, 0)),
        ],
        out_shape=[shape_of((rows, D), BF), shape_of((pairs, 2, rows), F32)],
        scratch_shapes=[pltpu.SMEM((1,), jnp.int32)],
        compiler_params=params(),
        cost_estimate=cost(0, 0),
        name="causal_forward",
    )(qkv, qkv, qkv, norms)


def earlier_forward(odd, qkv, pairs_before, norms, norms_before, own_out, own_log):
    rows = qkv.shape[0]
    half = rows // 2
    pairs = D // PAIR

    def kernel(
        odd_ref, q_ref, k_ref, v_ref, norm_ref, before_ref, own_ref, log_ref, out_ref, new_log_ref, mode_ref
    ):
        @pl.when(pl.program_id(0) == 0)
        def _():
            small = small_scores(
                norm_ref[0:1, :], jnp.maximum(norm_ref[1:2, :], before_ref[0:1, :])
            )
            mode_ref[0] = number(odd_ref, ODD) * (2 - small.astype(jnp.int32))

        @pl.when(mode_ref[0] == 0)
        def _():
            out_ref[...] = own_ref[...]
            new_log_ref[...] = log_ref[...]

        @pl.when(mode_ref[0] == 1)
        def _():
            keys = both_heads(k_ref[...])
            values = jnp.concatenate([with_ones(v_ref[...], h) for h in (0, 1)], axis=0)
            old = jnp.exp(columns_of(log_ref[0]))
            for first in range(0, rows, 128):
                span = slice(first, first + 128)
                p = jnp.exp(mm(q_ref[span, :] * SCALE, keys, NT)).astype(BF)
                both = mm(p, values)
                total = old[span] + both[:, PAIR:]
                mixed = own_ref[span, :].astype(F32) * old[span] + both[:, :PAIR]
                out_ref[span, :] = (mixed / total).astype(BF)
                one, two = rows_of(total)
                new_log_ref[0, 0:1, span] = jnp.log(one)
                new_log_ref[0, 1:2, span] = jnp.log(two)

        @pl.when(mode_ref[0] == 2)
        def _():
            def slowly(span):
                q = q_ref[span, :] * SCALE
                total = own_ref[span, :].astype(F32)
                logs = columns_of(log_ref[0, :, span])
                result = jnp.zeros_like(total)
                new_logs = logs
                for h in (0, 1):
                    s = mm(q, only_head(k_ref[...], h), NT)
                    old = logs[:, h * HEAD : h * HEAD + 1]
                    top = jnp.maximum(old, jnp.max(s, axis=1, keepdims=True))
                    p = jnp.exp(s - top)
                    share = jnp.exp(old - top)
                    part = share + jnp.sum(p, axis=1, keepdims=True)
                    mixed = mm(p.astype(BF), only_head(v_ref[...], h))
                    mixed = mixed + only_head(total, h) * share
                    result = result + mixed * (1.0 / part)
                    new_logs = jnp.where(head_lanes(h), top + jnp.log(part), new_logs)
                out_ref[span, :] = result.astype(BF)
                one, two = rows_of(new_logs)
                new_log_ref[0, 0:1, span] = one
                new_log_ref[0, 1:2, span] = two

            by_rows(rows, PAIR, slowly)

    block = (rows, PAIR)
    first = pl.BlockSpec(block, lambda p, odd: (0, p))
    second = pl.BlockSpec(block, lambda p, odd: (0, pairs + p))
    log_block = pl.BlockSpec((1, 2, rows), lambda p, odd: (p, 0, 0))
    return pl.pallas_call(
        kernel,
        grid_spec=pltpu.PrefetchScalarGridSpec(
            num_scalar_prefetch=1,
            grid=(pairs,),
            in_specs=[
                first, first, second, whole(norms.shape), whole(norms_before.shape), first, log_block,
            ],
            out_specs=[first, log_block],
            scratch_shapes=[pltpu.SMEM((1,), jnp.int32)],
        ),
        out_shape=[shape_of((rows, D), BF), shape_of((pairs, 2, rows), F32)],
        compiler_params=params(),
        cost_estimate=cost(0, 0),
        name="earlier_forward",
    )(odd, qkv, pairs_before, pairs_before, norms, norms_before, own_out, own_log)


def text_project(scalars, image_text, image_segment, per_image, text, segments, weight):
    tokens = text.shape[1]
    bn = 512
    groups = lax.axis_size("dp")

    def kernel(sc_ref, text_of_ref, seg_of_ref, row_ref, mate_ref, seg_ref, w_ref, kv_ref, bias_ref, row_out, mate_out):
        kv_ref[...] = mm(row_ref[...], w_ref[...]).astype(BF)

        @pl.when(pl.program_id(0) == 0)
        def _():
            row_out[...] = row_ref[...]
            mate_out[...] = mate_ref[...]
            row = image_entry(sc_ref, text_of_ref, per_image, groups)
            caption = image_entry(sc_ref, seg_of_ref, per_image, groups)
            bias = jnp.where(seg_ref[pl.ds(row, 1), :] == caption, 0.0, NEGATIVE)
            bias_ref[...] = jnp.concatenate([bias, bias], axis=1).astype(F32)

    return pl.pallas_call(
        kernel,
        grid_spec=pltpu.PrefetchScalarGridSpec(
            num_scalar_prefetch=3,
            grid=(weight.shape[1] // bn,),
            in_specs=[
                pl.BlockSpec(
                    (None, tokens, D), lambda j, sc, of, _: (image_entry(sc, of, per_image, groups), 0, 0)
                ),
                pl.BlockSpec(
                    (None, tokens, D), lambda j, sc, of, _: (image_entry(sc, of, per_image, groups, 1), 0, 0)
                ),
                whole(segments.shape),
                pl.BlockSpec((D, bn), lambda j, *_: (0, j)),
            ],
            out_specs=[
                pl.BlockSpec((tokens, bn), lambda j, *_: (0, j)),
                whole((1, 2 * tokens)),
                whole((tokens, D)),
                whole((tokens, D)),
            ],
        ),
        out_shape=[
            shape_of((tokens, weight.shape[1]), BF),
            shape_of((1, 2 * tokens), F32),
            shape_of((tokens, D), BF),
            shape_of((tokens, D), BF),
        ],
        compiler_params=params(),
        cost_estimate=cost(0, 0),
        name="text_project",
    )(scalars, image_text, image_segment, text, text, segments, weight)


def cross_weights(scores, small):
    if small:
        return jnp.exp(scores)
    halves = []
    for h in (0, 1):
        s = scores[:, h * TEXT_LEN : (h + 1) * TEXT_LEN]
        halves.append(jnp.exp(s - jnp.max(s, axis=1, keepdims=True)))
    return jnp.concatenate(halves, axis=1)


def each_pair(pair, unrolled):
    def one(p, carry):
        pair(p)
        return carry

    lax.fori_loop(0, D // PAIR, one, 0, unroll=4 if unrolled else 1)


def both_heads(block):
    return jnp.concatenate([only_head(block, 0), only_head(block, 1)], axis=0)


def copies_of(hbm_refs, vmem_refs, sems):
    copies = [
        pltpu.make_async_copy(src, dst, sems.at[i])
        for i, (src, dst) in enumerate(zip(hbm_refs, vmem_refs))
    ]
    return copies


def start(*copies):
    for copy in copies:
        copy.start()


def wait(*copies):
    for copy in copies:
        copy.wait()


def middle_forward(attended, x, self_w, query_w, cross_w, gains, text_kv, bias):
    rows = x.shape[0]
    any_space = pl.BlockSpec(memory_space=pl.ANY)

    def kernel(
        at_ref, x_ref, sw_hbm, qw_hbm, cw_hbm, gains_ref, kv_ref, bias_ref,
        mid1_hbm, cq_hbm, mid2_hbm, acts_hbm,
        sw, qw, cw, mid1_ref, cq_ref, mid2_ref, acts_ref, sems, out_sems,
    ):
        loads = copies_of((sw_hbm, qw_hbm, cw_hbm), (sw, qw, cw), sems)
        outs = []

        def out(src, dst):
            copy = pltpu.make_async_copy(src, dst, out_sems.at[len(outs)])
            copy.start()
            outs.append(copy)

        start(loads[0])
        wait(loads[0])
        start(loads[1], loads[2])
        mid1_ref[...] = x_ref[...].astype(F32) + mm(at_ref[...], sw[...])
        out(mid1_ref, mid1_hbm)

        def norm2(span):
            normal, _ = normed(mid1_ref[span, :])
            acts_ref[0, span, :] = (normal * gains_ref[0:1, :] + gains_ref[1:2, :]).astype(BF)

        by_rows(rows, 128, norm2)
        out(acts_ref.at[0], acts_hbm.at[0])
        loads[1].wait()
        cq_ref[...] = mm(acts_ref[0], qw[...]).astype(BF)
        out(cq_ref, cq_hbm)
        small = small_scores(head_sums(cq_ref[...]), head_sums(kv_ref[:, :D]))
        bias_row = bias_ref[...]

        def attend(is_small):
            def pair(p):
                span = pl.ds(pl.multiple_of(p * PAIR, PAIR), PAIR)
                q = cq_ref[:, span] * SCALE
                v = kv_ref[:, pl.ds(pl.multiple_of(D + p * PAIR, PAIR), PAIR)]
                s = mm(q, both_heads(kv_ref[:, span]), NT) + bias_row
                w = cross_weights(s, is_small).astype(BF)
                both = mm(w, jnp.concatenate([with_ones(v, 0), with_ones(v, 1)], axis=0))
                acts_ref[1, :, span] = (both[:, :PAIR] / both[:, PAIR:]).astype(BF)

            each_pair(pair, is_small)

        @pl.when(small)
        def _():
            attend(True)

        @pl.when(jnp.logical_not(small))
        def _():
            attend(False)

        out(acts_ref.at[1], acts_hbm.at[1])
        loads[2].wait()
        mid2_ref[...] = mid1_ref[...] + mm(acts_ref[1], cw[...])
        out(mid2_ref, mid2_hbm)

        def norm3(span):
            normal, _ = normed(mid2_ref[span, :])
            acts_ref[2, span, :] = (normal * gains_ref[2:3, :] + gains_ref[3:4, :]).astype(BF)

        by_rows(rows, 128, norm3)
        out(acts_ref.at[2], acts_hbm.at[2])
        for copy in outs:
            copy.wait()

    token = (rows, D)
    return pl.pallas_call(
        kernel,
        grid=(1,),
        in_specs=[
            whole(token), whole(token), any_space, any_space, any_space,
            whole(gains.shape), whole(text_kv.shape), whole(bias.shape),
        ],
        out_specs=[any_space] * 4,
        out_shape=[shape_of(token, t) for t in (F32, BF, F32)] + [shape_of((3,) + token, BF)],
        scratch_shapes=[pltpu.VMEM((D, D), BF)] * 3
        + [pltpu.VMEM(token, t) for t in (F32, BF, F32)]
        + [pltpu.VMEM((3,) + token, BF), pltpu.SemaphoreType.DMA((3,)), pltpu.SemaphoreType.DMA((6,))],
        compiler_params=params(),
        cost_estimate=cost(0, 0),
        name="middle_forward",
    )(attended, x, self_w, query_w, cross_w, gains, text_kv, bias)


def feed_half(which, half, acts, grad3, up, down, shards, before):
    rows = acts.shape[1]
    bw = FF // (2 * shards)
    root = math.sqrt(2.0 / math.pi)
    each = 4
    steps = shards // each

    def kernel(which_ref, a_ref, g_ref, *rest):
        up_refs, down_refs = rest[:each], rest[each : 2 * each]
        hid_ref, da_ref = rest[-2:]
        parts = []
        for i in range(each):
            span = slice(i * bw, (i + 1) * bw)
            h = mm(a_ref[...], up_refs[i][...])
            dy = mm(g_ref[...], down_refs[i][...], NT)
            sq = h * h
            t = jnp.tanh(h * (root + (root * 0.044715) * sq))
            more = 0.5 + 0.5 * t
            hid_ref[0, :, span] = (h * more).astype(BF)
            slope = more + (h * (0.5 - 0.5 * (t * t))) * (root + (3 * root * 0.044715) * sq)
            dh = (dy * slope).astype(BF)
            hid_ref[1, :, span] = dh
            parts.append(dh)
        ups = jnp.concatenate([ref[...] for ref in up_refs], axis=1)
        part = mm(jnp.concatenate(parts, axis=1), ups, NT)

        @pl.when(pl.program_id(0) == 0)
        def _():
            if before is None:
                da_ref[...] = part
            else:
                da_ref[...] = rest[2 * each][...] + part

        @pl.when(pl.program_id(0) != 0)
        def _():
            da_ref[...] += part

    token = whole((rows, D))
    in_specs = [pl.BlockSpec((None, rows, D), lambda s, which: (2, 0, 0)), token]
    for i in range(each):
        in_specs.append(
            pl.BlockSpec((D, bw), lambda s, which, i=i: (0, 2 * (each * s + i) + number(which, half)))
        )
    for i in range(each):
        in_specs.append(
            pl.BlockSpec((bw, D), lambda s, which, i=i: (2 * (each * s + i) + number(which, half), 0))
        )
    operands = [which, acts, grad3] + [up] * each + [down] * each
    if before is not None:
        in_specs.append(token)
        operands.append(before)
    return pl.pallas_call(
        kernel,
        grid_spec=pltpu.PrefetchScalarGridSpec(
            num_scalar_prefetch=1,
            grid=(steps,),
            in_specs=in_specs,
            out_specs=[
                pl.BlockSpec((2, rows, each * bw), lambda s, which: (0, 0, s)),
                token,
            ],
        ),
        out_shape=[shape_of((2, rows, FF // 2), BF), shape_of((rows, D), F32)],
        compiler_params=params(),
        cost_estimate=cost(0, 0),
        name="feed_half",
    )(*operands)


def feed_output(own, mid2, hidden_own, hidden_other, down, shards):
    rows = mid2.shape[0]
    bw = FF // (2 * shards)
    each = 4
    steps = shards // each

    def kernel(own_ref, mid_ref, a_ref, b_ref, down_ref, out_ref, acc_ref):
        s = pl.program_id(0)
        first = number(own_ref, CORE) == 0
        pieces = []
        for i in range(each):
            span = slice(i * bw, (i + 1) * bw)
            a, b = a_ref[:, span], b_ref[:, span]
            pieces += [jnp.where(first, a, b), jnp.where(first, b, a)]
        part = mm(jnp.concatenate(pieces, axis=1), down_ref[...])

        @pl.when(s == 0)
        def _():
            acc_ref[...] = mid_ref[...] + part

        @pl.when(s != 0)
        def _():
            acc_ref[...] += part

        @pl.when(s == steps - 1)
        def _():
            out_ref[...] = acc_ref[...].astype(BF)

    token = whole((rows, D))
    hid = pl.BlockSpec((None, rows, each * bw), lambda s, own: (0, 0, s))
    return pl.pallas_call(
        kernel,
        grid_spec=pltpu.PrefetchScalarGridSpec(
            num_scalar_prefetch=1,
            grid=(steps,),
            in_specs=[token, hid, hid, pl.BlockSpec((2 * each * bw, D), lambda s, own: (s, 0))],
            out_specs=token,
            scratch_shapes=[pltpu.VMEM((rows, D), F32)],
        ),
        out_shape=shape_of((rows, D), BF),
        compiler_params=params(),
        cost_estimate=cost(0, 0),
        name="feed_output",
    )(own, mid2, hidden_own, hidden_other, down)


def middle_backward(
    own, d_act3, mid2, upstream, mid1, cq, text_kv, bias, cross_w, query_w, self_w, gains
):
    rows = mid2.shape[0]
    wide = D // 2
    any_space = pl.BlockSpec(memory_space=pl.ANY)
    chunk = 128

    def kernel(
        own_ref, da3_hbm, mid2_hbm, g_hbm, mid1_hbm, cq_hbm, kv_ref, bias_ref, cw_hbm, qw_hbm, sw_hbm, gains_ref,
        mine_hbm, sent_hbm, dmid1_hbm, dat_hbm, kv_ref_out, dgains_ref,
        da3, mid2_v, g_v, mid1_v, cq_v, cw, qw, sw, kv_acc, grads, dmid, dat, up2, sums, sems, out_sems,
    ):
        loads = copies_of(
            (da3_hbm, mid2_hbm, g_hbm, cw_hbm, cq_hbm, qw_hbm, mid1_hbm, sw_hbm),
            (da3, mid2_v, g_v, cw, cq_v, qw, mid1_v, sw),
            sems,
        )
        core_at = pl.multiple_of(number(own_ref, CORE) * wide, wide)
        mate_at = pl.multiple_of(number(own_ref, OTHER) * wide, wide)
        outs = []

        def out(src, dst):
            copy = pltpu.make_async_copy(src, dst, out_sems.at[len(outs)])
            copy.start()
            outs.append(copy)

        def out_grad(part):
            out(grads.at[part, :, pl.ds(core_at, wide)], mine_hbm.at[part])
            out(grads.at[part, :, pl.ds(mate_at, wide)], sent_hbm.at[part])

        def add_up(place, values):
            folded = values[:8]
            for i in range(8, rows, 8):
                folded = folded + values[i : i + 8]
            sums[place] += folded

        start(*loads[:3])
        sums[...] = jnp.zeros_like(sums)
        wait(*loads[:3])
        start(*loads[3:5])

        def back3(span):
            up = da3[span, :]
            normal, inverse = normed(mid2_v[span, :])
            add_up(2, up * normal)
            add_up(3, up)
            total = g_v[span, :].astype(F32) + norm_back(normal, inverse, gains_ref[2:3, :], up)
            dmid[span, :] = total
            grads[0, span, :] = total.astype(BF)

        back3(slice(0, rows))
        out_grad(0)
        wait(loads[3])
        start(*loads[5:7])
        dat[...] = mm(grads[0], cw[...], NT).astype(BF)
        loads[4].wait()
        small = small_scores(head_sums(cq_v[...]), head_sums(kv_ref[:, :D]))
        bias_row = bias_ref[...]
        side = lax.broadcasted_iota(jnp.int32, (2 * TEXT_LEN, 2 * TEXT_LEN), 0) // TEXT_LEN
        same = side == lax.broadcasted_iota(jnp.int32, side.shape, 1) // TEXT_LEN
        summing = jnp.where(same, 1.0, 0.0).astype(BF)

        def back_pairs(is_small):
            def pair(p):
                span = pl.ds(pl.multiple_of(p * PAIR, PAIR), PAIR)
                vspan = pl.ds(pl.multiple_of(D + p * PAIR, PAIR), PAIR)
                q = cq_v[:, span] * SCALE
                dc = dat[:, span]
                k = both_heads(kv_ref[:, span])
                v = both_heads(kv_ref[:, vspan])
                w = cross_weights(mm(q, k, NT) + bias_row, is_small)
                w = w / mm(w.astype(BF), summing)
                dw = mm(dc, v, NT)
                ds = (w * (dw - mm((w * dw).astype(BF), summing))).astype(BF)
                grads[1, :, span] = (mm(ds, k) * SCALE).astype(BF)
                dk = mm(ds, q, TN)
                dv = mm(w.astype(BF), dc, TN)
                kv_acc[:, span] = jnp.where(head_lanes(0), dk[:TEXT_LEN], dk[TEXT_LEN:]).astype(BF)
                kv_acc[:, vspan] = jnp.where(head_lanes(0), dv[:TEXT_LEN], dv[TEXT_LEN:]).astype(BF)

            each_pair(pair, is_small)

        @pl.when(small)
        def _():
            back_pairs(True)

        @pl.when(jnp.logical_not(small))
        def _():
            back_pairs(False)

        out_grad(1)
        kv_ref_out[0] = kv_acc[:, pl.ds(2 * core_at, D)]
        kv_ref_out[1] = kv_acc[:, pl.ds(2 * mate_at, D)]
        loads[5].wait()
        up2[...] = mm(grads[1], qw[...], NT)
        wait(loads[6])
        start(loads[7])

        def back2(span):
            up = up2[span, :]
            normal, inverse = normed(mid1_v[span, :])
            add_up(0, up * normal)
            add_up(1, up)
            total = dmid[span, :] + norm_back(normal, inverse, gains_ref[0:1, :], up)
            dmid[span, :] = total
            grads[2, span, :] = total.astype(BF)

        back2(slice(0, rows))
        out(dmid, dmid1_hbm)
        out_grad(2)
        loads[7].wait()
        dat[...] = mm(grads[2], sw[...], NT).astype(BF)
        out(dat, dat_hbm)
        dgains_ref[...] = jnp.zeros_like(dgains_ref)
        for i in range(4):
            dgains_ref[i : i + 1, :] = jnp.sum(sums[i], axis=0, keepdims=True)
        for copy in outs:
            copy.wait()

    token = (rows, D)
    halves = (3, rows, wide)
    text = (2, TEXT_LEN, D)
    return pl.pallas_call(
        kernel,
        grid_spec=pltpu.PrefetchScalarGridSpec(
            num_scalar_prefetch=1,
            grid=(1,),
            in_specs=[any_space] * 5
            + [whole(text_kv.shape), whole(bias.shape)]
            + [any_space] * 3
            + [whole(gains.shape)],
            out_specs=[any_space] * 4 + [whole(text), whole((8, D))],
            scratch_shapes=[pltpu.VMEM(token, t) for t in (F32, F32, BF, F32, BF)]
            + [pltpu.VMEM((D, D), BF)] * 3
            + [pltpu.VMEM(text_kv.shape, BF), pltpu.VMEM((3,) + token, BF)]
            + [pltpu.VMEM(token, F32), pltpu.VMEM(token, BF), pltpu.VMEM(token, F32)]
            + [pltpu.VMEM((4, 8, D), F32)]
            + [pltpu.SemaphoreType.DMA((8,)), pltpu.SemaphoreType.DMA((8,))],
        ),
        out_shape=[shape_of(halves, BF)] * 2
        + [shape_of(token, t) for t in (F32, BF)]
        + [shape_of(text, BF)]
        + [shape_of((8, D), F32)],
        compiler_params=params(),
        cost_estimate=cost(0, 0),
        name="middle_backward",
    )(own, d_act3, mid2, upstream, mid1, cq, text_kv, bias, cross_w, query_w, self_w, gains)


def deltas_of(d_out, out):
    prod = d_out.astype(F32) * out.astype(F32)
    high = prod.astype(BF)
    low = (prod - high.astype(F32)).astype(BF)
    row = lax.broadcasted_iota(jnp.int32, (8, PAIR), 0)
    lane = lax.broadcasted_iota(jnp.int32, (8, PAIR), 1)
    pick = jnp.where(lane // HEAD == row, 1.0, 0.0).astype(BF)
    return mm(pick, high, NT) + mm(pick, low, NT)


def key_block_back(k, v, q, d_out, logs, deltas, causal):
    keys = k.shape[0]
    k2, v2 = both_heads(k), both_heads(v)
    s = mm(k2, q, NT)
    dp = mm(v2, d_out, NT)
    weights, grads = [], []
    for h in (0, 1):
        span = slice(h * keys, (h + 1) * keys)
        p = jnp.exp(s[span] - logs[h : h + 1])
        if causal:
            at_k = lax.broadcasted_iota(jnp.int32, (keys, keys), 0)
            at_q = lax.broadcasted_iota(jnp.int32, (keys, keys), 1)
            first = jnp.where(at_q >= at_k, p[:, :keys], 0.0)
            p = first if p.shape[1] == keys else jnp.concatenate([first, p[:, keys:]], axis=1)
        weights.append(p.astype(BF))
        grads.append((p * (dp[span] - deltas[h : h + 1])).astype(BF))
    p2, ds2 = jnp.concatenate(weights, axis=0), jnp.concatenate(grads, axis=0)
    dv, dk = mm(p2, d_out), mm(ds2, q)
    lanes = head_lanes(0)
    dk = jnp.where(lanes, dk[:keys], dk[keys:]).astype(BF)
    dv = jnp.where(lanes, dv[:keys], dv[keys:]).astype(BF)
    return mm(ds2, k2, TN), dk, dv


def attention_backward(scalars, side, qkv, pairs_before, d_out, out, logs):
    rows = qkv.shape[0]
    half = rows // 2
    pairs = D // PAIR
    count = pairs // 2

    def kernel(
        sc_ref, q_ref, k_ref, v_ref, kb_ref, vb_ref, do_ref, out_ref, log_ref, grads_ref, before_ref, dq_ref
    ):
        q = q_ref[...] * SCALE
        d_o = do_ref[...]
        deltas = deltas_of(d_o, out_ref[...])
        log_rows = log_ref[0]

        @pl.when(number(sc_ref, ODD) == 0)
        def _():
            dq_ref[...] = jnp.zeros_like(dq_ref)
            before_ref[...] = jnp.zeros_like(before_ref)

        @pl.when(number(sc_ref, ODD) != 0)
        def _():
            for first in (0, half):
                span = slice(first, first + half)
                dq, dk, dv = key_block_back(
                    kb_ref[span, :], vb_ref[span, :], q, d_o, log_rows, deltas, False
                )
                if first == 0:
                    dq_ref[...] = dq
                else:
                    dq_ref[...] += dq
                before_ref[0, span, :] = dk
                before_ref[1, span, :] = dv

        for first in (0, half):
            span = slice(first, first + half)
            dq, dk, dv = key_block_back(
                k_ref[span, :], v_ref[span, :], q[first:], d_o[first:],
                log_rows[:, first:], deltas[:, first:], True,
            )
            dq_ref[first:, :] += dq
            grads_ref[1, span, :] = dk
            grads_ref[2, span, :] = dv
        grads_ref[0] = (dq_ref[...] * SCALE).astype(BF)

    block = (rows, PAIR)

    def at(offset):
        return pl.BlockSpec(block, lambda p, sc: (0, offset + number(sc, side) * count + p))

    return pl.pallas_call(
        kernel,
        grid_spec=pltpu.PrefetchScalarGridSpec(
            num_scalar_prefetch=1,
            grid=(count,),
            in_specs=[
                at(0), at(pairs), at(2 * pairs), at(0), at(pairs), at(0), at(0),
                pl.BlockSpec((1, 2, rows), lambda p, sc: (number(sc, side) * count + p, 0, 0)),
            ],
            out_specs=[
                pl.BlockSpec((3, rows, PAIR), lambda p, sc: (0, 0, p)),
                pl.BlockSpec((2, rows, PAIR), lambda p, sc: (0, 0, p)),
            ],
            scratch_shapes=[pltpu.VMEM(block, F32)],
        ),
        out_shape=[shape_of((3, rows, D // 2), BF), shape_of((2, rows, D // 2), BF)],
        compiler_params=params(),
        cost_estimate=cost(0, 0),
        name="attention_backward",
    )(scalars, qkv, qkv, qkv, pairs_before, pairs_before, d_out, out, logs)


def project_back(own, grads_own, grads_other, weight, x, name, before=None, others=None):
    rows = x.shape[0]
    count, _, width = grads_own.shape
    first = 3 - count
    chunk = 128

    def kernel(own_ref, ga_ref, gb_ref, wa_ref, wb_ref, x_ref, *refs):
        out_ref, sums_ref, acc_ref, part_sums = refs[-4:]
        j = pl.program_id(0)
        grad = jnp.concatenate([ga_ref[...], gb_ref[...]], axis=1)
        part = mm(grad, jnp.concatenate([wa_ref[...], wb_ref[...]], axis=1), NT)

        @pl.when(j == 0)
        def _():
            acc_ref[...] = part

        @pl.when(j != 0)
        def _():
            acc_ref[...] += part

        @pl.when(j == count - 1)
        def _():
            part_sums[...] = jnp.zeros_like(part_sums)

            def finish(span):
                total = acc_ref[span, :]
                normal, _ = normed(x_ref[span, :].astype(F32))
                for place, values in ((0, total * normal), (1, total)):
                    folded = values[:8]
                    for i in range(8, chunk, 8):
                        folded = folded + values[i : i + 8]
                    part_sums[place] += folded
                out_ref[span, :] = total.astype(BF)

            by_rows(rows, chunk, finish)
            rows_of_sums = [jnp.sum(part_sums[i], axis=0, keepdims=True) for i in (0, 1)]
            if before is None:
                sums_ref[...] = jnp.zeros_like(sums_ref)
                for i in (0, 1):
                    sums_ref[i : i + 1, :] = rows_of_sums[i]
            else:
                all_rows = [rows_of_sums[i] + refs[0][i : i + 1, :] for i in (0, 1)]
                all_rows += [refs[1][i : i + 1, :] for i in range(4)]
                strips = [
                    row[:, c * LANES : (c + 1) * LANES] for row in all_rows for c in range(D // LANES)
                ]
                sums_ref[...] = jnp.concatenate(strips, axis=0).astype(BF)

    grad = pl.BlockSpec((None, rows, width), lambda j, own: (j, 0, 0))
    more = [] if before is None else [before, others]
    sums_shape = shape_of((8, D), F32) if before is None else shape_of((6 * D // LANES, LANES), BF)
    return pl.pallas_call(
        kernel,
        grid_spec=pltpu.PrefetchScalarGridSpec(
            num_scalar_prefetch=1,
            grid=(count,),
            in_specs=[
                grad,
                grad,
                pl.BlockSpec((D, width), lambda j, own: (0, 2 * (first + j) + number(own, CORE))),
                pl.BlockSpec((D, width), lambda j, own: (0, 2 * (first + j) + 1 - number(own, CORE))),
                whole((rows, D)),
            ]
            + [whole(a.shape) for a in more],
            out_specs=[whole((rows, D)), whole(sums_shape.shape)],
            scratch_shapes=[pltpu.VMEM((rows, D), F32), pltpu.VMEM((2, 8, D), F32)],
        ),
        out_shape=[shape_of((rows, D), BF), sums_shape],
        compiler_params=params(),
        cost_estimate=cost(0, 0),
        name=name,
    )(own, grads_own, grads_other, weight, weight, x, *more)


def input_back(d_act, d_act_other, x, d_mid1, gain):
    rows = x.shape[0]
    tile = rows // 4

    def kernel(da_ref, db_ref, x_ref, dm_ref, gain_ref, out_ref):
        normal, inverse = normed(x_ref[...].astype(F32))
        up = da_ref[...].astype(F32) + db_ref[...].astype(F32)
        out_ref[...] = dm_ref[...] + norm_back(normal, inverse, gain_ref[...], up)

    row_block = pl.BlockSpec((tile, D), lambda i: (i, 0))
    return pl.pallas_call(
        kernel,
        grid=(rows // tile,),
        in_specs=[row_block] * 4 + [whole((1, D))],
        out_specs=row_block,
        out_shape=shape_of((rows, D), F32),
        compiler_params=params(),
        cost_estimate=cost(0, 0),
        name="input_back",
    )(d_act, d_act_other, x, d_mid1, gain)


def part_of(operand):
    if isinstance(operand, tuple):
        array, part = operand
        return array, array.shape[1:], lambda *at: (part,) + at
    return operand, operand.shape, None


def spec_of(operand, block, place):
    _, _, lead = part_of(operand)
    if lead is None:
        return pl.BlockSpec(block, place)
    return pl.BlockSpec((None,) + block, lambda *at: lead(*place(*at)))


def joined(refs):
    blocks = [ref[...] for ref in refs]
    return blocks[0] if len(blocks) == 1 else jnp.concatenate(blocks, axis=0)


def put_strips(ref, values, first=0):
    for c in range(values.shape[1] // LANES):
        ref[first + c] = values[:, c * LANES : (c + 1) * LANES]


def row_grad(scalars, lefts, rights, name):
    n = len(lefts)
    left_shapes = [part_of(a)[1] for a in lefts]
    right_shapes = [part_of(a)[1] for a in rights]
    rows = left_shapes[0][1]
    wide = right_shapes[0][1] // 2
    tile = 512
    strips = wide // LANES

    def kernel(sc_ref, *refs):
        left = joined(refs[:n])
        put_strips(refs[-2], mm(left, joined(refs[n : 2 * n]), TN).astype(BF))
        put_strips(refs[-1], mm(left, joined(refs[2 * n : 3 * n]), TN).astype(BF))

    operands = [part_of(a)[0] for a in lefts]
    in_specs = [
        spec_of(a, (shape[0], tile), lambda j, sc: (0, j)) for a, shape in zip(lefts, left_shapes)
    ]
    for place in (lambda j, sc: (0, number(sc, NOT_Y)), lambda j, sc: (0, number(sc, Y))):
        for a, shape in zip(rights, right_shapes):
            in_specs.append(spec_of(a, (shape[0], wide), place))
            operands.append(part_of(a)[0])
    return pl.pallas_call(
        kernel,
        grid_spec=pltpu.PrefetchScalarGridSpec(
            num_scalar_prefetch=1,
            grid=(rows // tile,),
            in_specs=in_specs,
            out_specs=[pl.BlockSpec((strips, tile, LANES), lambda j, sc: (0, j, 0))] * 2,
        ),
        out_shape=[shape_of((strips, rows, LANES), BF)] * 2,
        compiler_params=params(),
        cost_estimate=cost(0, 0),
        name=name,
    )(scalars, *operands)


def column_grad(scalars, lefts, rights, bw, name):
    n = len(lefts)
    left_shapes = [part_of(a)[1] for a in lefts]
    right_shapes = [part_of(a)[1] for a in rights]
    rows = left_shapes[0][1]
    cols = right_shapes[0][1]
    bn = 512
    blocks = rows // bw
    strips = bn // LANES

    def kernel(sc_ref, *refs):
        send_ref, keep_ref, product = refs[-3:]
        product[...] = mm(joined(refs[:n]), joined(refs[n : 2 * n]), TN).astype(BF)
        for i in range(blocks):
            block = product[pl.ds(pl.multiple_of(row_block(sc_ref, i, blocks) * bw, bw), bw), :]
            target = send_ref if i < blocks // 2 else keep_ref
            place = (i % (blocks // 2)) * bw
            for c in range(strips):
                target[c, place : place + bw, :] = block[:, c * LANES : (c + 1) * LANES]

    operands = [part_of(a)[0] for a in lefts] + [part_of(a)[0] for a in rights]
    in_specs = [spec_of(a, shape, lambda j, sc: (0, 0)) for a, shape in zip(lefts, left_shapes)]
    in_specs += [spec_of(a, (shape[0], bn), lambda j, sc: (0, j)) for a, shape in zip(rights, right_shapes)]
    return pl.pallas_call(
        kernel,
        grid_spec=pltpu.PrefetchScalarGridSpec(
            num_scalar_prefetch=1,
            grid=(cols // bn,),
            in_specs=in_specs,
            out_specs=[pl.BlockSpec((strips, rows // 2, LANES), lambda j, sc: (j, 0, 0))] * 2,
            scratch_shapes=[pltpu.VMEM((rows, bn), BF)],
        ),
        out_shape=[shape_of((cols // LANES, rows // 2, LANES), BF)] * 2,
        compiler_params=params(),
        cost_estimate=cost(0, 0),
        name=name,
    )(scalars, *operands)


def block_grads(scalars, bw, lefts, rights, blocks, name, text=None, captions=None, per_image=1):
    count = len(blocks)
    width = 512
    part = width // 2
    row_blocks = D // bw
    in_specs, operands = [], []
    for a, lead in lefts:
        if lead is None:
            in_specs.append(whole(a.shape))
        else:
            in_specs.append(pl.BlockSpec((None,) + a.shape[1:], lambda j, sc, *_, lead=lead: (lead, 0, 0)))
        operands.append(a)
    for a, place in rights:
        if isinstance(a, tuple):
            a, lead = a
            in_specs.append(
                pl.BlockSpec(
                    (None, a.shape[1], width), lambda j, sc, *_, place=place, lead=lead: (lead, 0, place(j))
                )
            )
        elif a.ndim == 3:
            in_specs.append(
                pl.BlockSpec((None, a.shape[1], width), lambda j, sc, *_, place=place: (place(j), 0, 0))
            )
        else:
            in_specs.append(pl.BlockSpec((a.shape[0], width), lambda j, sc, *_, place=place: (0, place(j))))
        operands.append(a)
    n, m = len(lefts), len(rights)
    if text is not None:
        for a, leads in ((text[0], (0, 1)), (text[1], (1, 0))):
            for lead in leads:
                in_specs.append(pl.BlockSpec((None,) + a.shape[1:], lambda j, sc, *_, lead=lead: (lead, 0, 0)))
                operands.append(a)
        wide = text[0].shape[2]
        for at in (0, 1):
            in_specs.append(
                pl.BlockSpec((D // 2, wide), lambda j, sc, *_, at=at: (number(sc, CORE), at))
            )
            operands.append(text[2])
        count += 1
    inputs_count = len(operands)

    prefetched = [scalars] if captions is None else [scalars, captions]
    groups = lax.axis_size("dp")

    def kernel(sc_ref, *refs):
        if captions is not None:
            captions_ref, refs = refs[0], refs[1:]
        left_refs, right_refs = refs[:n], refs[n : n + m]
        sent_a, kept_a, sent_b, kept_b, product = refs[inputs_count:]
        j = pl.program_id(0)

        if text is not None:
            text_refs = refs[n + m : inputs_count]

            @pl.when(j == count - 1)
            def _():
                product[...] = jnp.zeros_like(product)
                core = number(sc_ref, CORE)
                for i in (0, 1):
                    mine, others = text_refs[2 * i][...], text_refs[2 * i + 1][...]
                    low = jnp.where(core == 0, mine, others)
                    high = jnp.where(core == 0, others, mine)
                    term = mm(low, text_refs[4][...], NT) + mm(high, text_refs[5][...], NT)
                    at = pl.multiple_of(image_entry(sc_ref, captions_ref, per_image, groups, i) * TEXT_LEN, TEXT_LEN)
                    span = pl.ds(at, TEXT_LEN)
                    product[span, :] = add(product[span, :], term)

        for at, (left_places, right_places) in enumerate(blocks):

            @pl.when(j == at)
            def _(left_places=left_places, right_places=right_places):
                left = joined([left_refs[i] for i in left_places])
                right = joined([right_refs[i] for i in right_places])
                product[...] = mm(left, right, TN).astype(BF)

        eighth = part // 2
        sent_a[0] = product[:, pl.ds(pl.multiple_of(number(sc_ref, NOT_Y) * eighth, eighth), eighth)]
        kept_a[0] = product[:, pl.ds(pl.multiple_of(number(sc_ref, Y) * eighth, eighth), eighth)]
        for i in range(row_blocks):
            rows = product[pl.ds(pl.multiple_of(row_block(sc_ref, i, row_blocks) * bw, bw), bw), part:]
            target = sent_b if i < row_blocks // 2 else kept_b
            place = (i % (row_blocks // 2)) * bw
            for c in (0, 1):
                target[c, place : place + bw, :] = rows[:, c * LANES : (c + 1) * LANES]

    a_block, b_block = (1, D, LANES), (2, D // 2, LANES)
    return pl.pallas_call(
        kernel,
        grid_spec=pltpu.PrefetchScalarGridSpec(
            num_scalar_prefetch=len(prefetched),
            grid=(count,),
            in_specs=in_specs,
            out_specs=[
                pl.BlockSpec(a_block, lambda j, sc, *_: (j, 0, 0)),
                pl.BlockSpec(a_block, lambda j, sc, *_: (j, 0, 0)),
                pl.BlockSpec(b_block, lambda j, sc, *_: (j, 0, 0)),
                pl.BlockSpec(b_block, lambda j, sc, *_: (j, 0, 0)),
            ],
            scratch_shapes=[pltpu.VMEM((D, width), BF)],
        ),
        out_shape=[
            shape_of((count, D, LANES), BF),
            shape_of((count, D, LANES), BF),
            shape_of((2 * count, D // 2, LANES), BF),
            shape_of((2 * count, D // 2, LANES), BF),
        ],
        compiler_params=params(),
        cost_estimate=cost(0, 0),
        name=name,
    )(*prefetched, *operands)


def swap(block, axis, bit):
    route = [(i, i ^ (1 << bit)) for i in range(lax.axis_size(axis))]
    return lax.ppermute(block, axis, route)


def pick(block, place, dim):
    return lax.dynamic_index_in_dim(block, place, dim, keepdims=False)


def bit_of(index, bit):
    return (index >> bit) & 1


def add(a, b):
    return (a.astype(F32) + b.astype(F32)).astype(BF)


class Order:
    def __init__(self):
        self.token = None

    def then(self, *values):
        if self.token is not None:
            values = lax.optimization_barrier(values + (self.token,))[:-1]
        return values if len(values) > 1 else values[0]

    def mark(self, value):
        self.token = value
        return value


def exchange(block, axis, mask):
    route = [(i, i ^ mask) for i in range(lax.axis_size(axis))]
    return lax.ppermute(block, axis, route)


def flat(block):
    return block.reshape(-1, LANES)


def rows_at(first, count):
    return pl.ds(pl.multiple_of(first, 16) if not isinstance(first, int) else first, count)


def repeat(count, step):
    def one(i, carry):
        step(i)
        return carry

    lax.fori_loop(0, count, one, 0)


def sum_stage(order, name, scalars, inputs, outputs, work):
    n = len(inputs)

    def kernel(sc_ref, *refs):
        work(sc_ref, refs[:n], refs[n:])

    outs = pl.pallas_call(
        kernel,
        grid_spec=pltpu.PrefetchScalarGridSpec(
            num_scalar_prefetch=1,
            grid=(1,),
            in_specs=[whole(a.shape) for a in inputs],
            out_specs=[whole((rows, LANES)) for rows in outputs],
        ),
        out_shape=[shape_of((rows, LANES), BF) for rows in outputs],
        compiler_params=params(),
        cost_estimate=cost(0, 0),
        name=name,
    )(scalars, *inputs)
    order.mark(outs[0])
    return outs


class Streams:
    def __init__(self, a_strips, a_rows, b_strips, b_rows, left):
        self.a_strips, self.a_rows, self.b_strips, self.b_rows = a_strips, a_rows, b_strips, b_rows // 2
        self.left = left
        self.a_half = a_strips * left * a_rows
        self.b_half = b_strips * left * (b_rows // 2)
        self.a_first, self.b_first = 2 * self.a_half, 2 * self.b_half
        self.piece = (self.a_half + self.b_half) // left

    def by_place(self, kept, came, sent, sent_at, keep, mine, a):
        rows = 2 * (self.a_rows if a else self.b_rows)
        strips = self.a_strips if a else self.b_strips

        def step(i):
            for out, at, side in ((sent, sent_at, 1 - mine), (keep, 0, mine)):
                first = (2 * i + side) * rows
                out[rows_at(at + i * rows, rows), :] = (
                    kept[rows_at(first, rows), :] + came[rows_at(first, rows), :]
                )

        repeat(strips * self.left // 2, step)

    def second(self, kept, came, sent, keep, mine, a, came_at=0):
        rows = self.a_rows if a else self.b_rows
        strips = self.a_strips if a else self.b_strips

        def step(i):
            for out, side in ((sent, 1 - mine), (keep, mine)):
                first = i * 2 * rows + side * rows
                out[rows_at(i * rows, rows), :] = (
                    kept[rows_at(first, rows), :] + came[rows_at(came_at + first, rows), :]
                )

        repeat(strips * self.left, step)

    def third(self, kept_a, came_a, kept_b, came_b, sent, keep, place):
        a_rows, b_rows, left = self.a_rows, self.b_rows, self.left
        mine = place & 1
        for j in range(left // 2):
            for out, side in ((sent, 1 - mine), (keep, mine)):
                block = 2 * j + side
                base = j * self.piece

                def a_step(i, out=out, block=block, base=base):
                    first = (i * left + block) * a_rows
                    out[rows_at(base + i * a_rows, a_rows), :] = (
                        kept_a[rows_at(first, a_rows), :] + came_a[rows_at(first, a_rows), :]
                    )

                def b_step(i, out=out, block=block, base=base):
                    first = (i * left + block) * b_rows
                    at = base + self.a_strips * a_rows + i * b_rows
                    out[rows_at(at, b_rows), :] = (
                        kept_b[rows_at(first, b_rows), :] + came_b[rows_at(first, b_rows), :]
                    )

                repeat(self.a_strips, a_step)
                repeat(self.b_strips, b_step)


def add_rows(a, b, a_at, out, out_at, count):
    chunk = math.gcd(count, 256)

    def step(i):
        span = rows_at(a_at + i * chunk, chunk)
        out[rows_at(out_at + i * chunk, chunk), :] = a[span, :] + b[span, :]

    repeat(count // chunk, step)


def total_over_rest(pieces):
    for bit in range(2, lax.axis_size("dp").bit_length() - 1):
        pieces = [add(piece, swap(piece, "dp", bit)) for piece in pieces]
    return pieces


class Spread:
    def __init__(self, order, scalars, piece):
        self.order, self.scalars, self.piece = order, scalars, piece
        self.y = swap(order.then(piece), "dp", 1)

    def forward(self):
        self.piece, self.y = self.order.then(self.piece, self.y)
        self.core = swap(self.piece, "dp", 0)
        self.both = swap(self.y, "dp", 0)

    def finish(self, rows, shapes, write, name, rider=0):
        pieces = self.order.then(self.piece, self.core, self.y, self.both)
        out_shapes = list(shapes) + ([(rider, LANES)] if rider else [])

        def kernel(sc_ref, *refs):
            outs = refs[4:]
            for at in range(4):
                for k in range(4):

                    @pl.when(number(sc_ref, QUARTER) == at ^ k)
                    def _(at=at, k=k):
                        write(outs, refs[k], at & 1, at >> 1)

            if rider:
                total = refs[0][rows:, :].astype(F32)
                for ref in refs[1:4]:
                    total = total + ref[rows:, :].astype(F32)
                outs[-1][...] = total

        outs = pl.pallas_call(
            kernel,
            grid_spec=pltpu.PrefetchScalarGridSpec(
                num_scalar_prefetch=1,
                grid=(1,),
                in_specs=[whole(self.piece.shape)] * 4,
                out_specs=[whole(shape) for shape in out_shapes],
            ),
            out_shape=[shape_of(shape, F32) for shape in out_shapes],
            compiler_params=params(),
            cost_estimate=cost(0, 0),
            name=name,
        )(self.scalars, *pieces)
        self.order.mark(outs[0])
        return outs

    def finish_text(self, rows, bw):
        pieces = self.order.then(self.piece, self.core, self.y, self.both)
        shards = lax.axis_size("seq")
        half = bw // 2

        def kernel(sc_ref, *refs):
            out_ref = refs[4]

            def one(i, carry):
                place = i ^ number(sc_ref, ME)
                seq_at = (place & 1) * (shards // 2) + (place >> 1)
                at = pl.multiple_of(seq_at * rows, rows)
                first = pl.multiple_of(i * bw, bw)
                for core in (0, 1):
                    for y in (0, 1):
                        for k in range(4):

                            @pl.when(number(sc_ref, QUARTER) == (2 * y + core) ^ k)
                            def _(ref=refs[k], core=core, y=y):
                                col = core * (D // 2) + y * LANES
                                out_ref[pl.ds(first, bw), col : col + LANES] = ref[
                                    pl.ds(at, bw), :
                                ].astype(F32)
                                for c in (0, 1):
                                    col = core * (D // 2) + 256 + c * LANES
                                    out_ref[pl.ds(first + y * half, half), col : col + LANES] = ref[
                                        rows_at(at + bw + c * half, half), :
                                    ].astype(F32)

                return carry

            lax.fori_loop(0, shards, one, 0)

        return pl.pallas_call(
            kernel,
            grid_spec=pltpu.PrefetchScalarGridSpec(
                num_scalar_prefetch=1,
                grid=(1,),
                in_specs=[whole(self.piece.shape)] * 4,
                out_specs=whole((shards * bw, D)),
            ),
            out_shape=shape_of((shards * bw, D), F32),
            compiler_params=params(),
            cost_estimate=cost(0, 0),
            name="text_finish",
        )(self.scalars, *pieces)


def numbers_of(per_image):
    me, dp = lax.axis_index("seq"), lax.axis_index("dp")
    packed = (me % per_image) | ((dp & 3) << 1) | (me << 3) | ((dp >> 2) << 15)
    return packed.astype(jnp.int32).reshape(1)


def body(
    inputs,
    text_state,
    text_segment,
    image_text,
    image_segment,
    self_gain,
    self_shift,
    qkv_weight,
    self_weight,
    cross_gain,
    cross_shift,
    query_weight,
    text_weight,
    cross_weight,
    feed_gain,
    feed_shift,
    up_weight,
    down_weight,
    cotangent,
):
    rows = inputs.shape[0]
    shards = lax.axis_size("seq")
    groups = lax.axis_size("dp")
    me, dp = lax.axis_index("seq"), lax.axis_index("dp")
    per_image = IMG_TOK // rows
    order = Order()
    scalars = numbers_of(per_image)

    def over_core(block):
        return swap(block, "dp", 0)

    seq_bits = shards.bit_length() - 1
    dp_bits = groups.bit_length() - 1
    spread_steps = [("seq", b) for b in reversed(range(seq_bits))] + [("dp", 1), ("dp", 0)]
    bw = D // shards
    bw_ff = FF // (2 * shards)

    even_to_odd = [(i, i + 1) for i in range(0, shards, 2)]
    odd_to_even = [(i + 1, i) for i in range(0, shards, 2)]
    x_before = lax.ppermute(inputs, "seq", even_to_odd)
    cot_mate = over_core(cotangent)
    gain1, shift1 = self_gain.reshape(1, D), self_shift.reshape(1, D)
    act1, qkv, norms = norm_project(inputs, gain1, shift1, qkv_weight, 0, "norm_project")
    act1_mate = over_core(act1)
    own_out, own_log = causal_forward(qkv, norms)
    order.mark(own_out)
    text_state = order.then(text_state)
    text_kv, bias_row, text_row, text_row_mate = text_project(
        scalars, image_text, image_segment, per_image, text_state, text_segment, text_weight
    )
    order.mark(text_kv)
    x_before, act1_mate, cot_mate = order.then(x_before, act1_mate, cot_mate)
    act1_before, pairs_before, norms_before = norm_project(
        x_before, gain1, shift1, qkv_weight, D, "norm_project_before"
    )
    before_mate = over_core(act1_before)
    attended, log_rows = earlier_forward(
        scalars, qkv, pairs_before, norms, norms_before, own_out, own_log
    )
    order.mark(attended)
    before_mate, attended = order.then(before_mate, attended)
    attended_mate = over_core(attended)
    gains = jnp.stack([cross_gain, cross_shift, feed_gain, feed_shift] * 2)
    mid1, cq, mid2, acts = middle_forward(
        attended, inputs, self_weight, query_weight, cross_weight, gains, text_kv, bias_row
    )
    order.mark(mid1)
    attended_mate, acts = order.then(attended_mate, acts)
    acts_mate = over_core(acts)
    hid_other, d_act3 = feed_half(
        scalars, OTHER, acts, cotangent, up_weight, down_weight, shards, None
    )
    order.mark(d_act3)
    d_act3, acts_mate, hid_other = order.then(d_act3, acts_mate, hid_other)
    hid_mate = over_core(hid_other)
    hid_own, d_act3 = feed_half(
        scalars, CORE, acts, cotangent, up_weight, down_weight, shards, d_act3
    )
    order.mark(d_act3)
    hid_mate = order.then(hid_mate)

    left = shards // 2
    feed = Streams(D // 2 // LANES, bw_ff, FF // 2 // LANES, bw, left)
    feed_later = Streams(D // 2 // LANES, bw_ff, FF // 2 // LANES, bw, left // 2)
    mids = Streams(6, bw, 12, bw, left)
    qkvs = Streams(3, bw, 6, bw, left)
    others = range(1, left)

    sent, feed_a = row_grad(
        scalars, [(hid_own, 0), (hid_mate, 0)], [cotangent, cot_mate], "down_grad"
    )
    order.mark(sent)
    feed_a = flat(feed_a)
    came_fa = swap(flat(sent), "dp", 1)
    acts_late = order.then(acts)
    sent, feed_b = column_grad(
        scalars, [(acts_late, 2), (acts_mate, 2)], [(hid_own, 1), (hid_mate, 1)], bw, "up_grad"
    )
    order.mark(sent)
    feed_b = flat(feed_b)
    came_fb = swap(flat(sent), "seq", 0)

    d_act3 = order.then(d_act3)
    g_mine, g_sent, d_mid1, d_att, text_grads, d_gains = middle_backward(
        scalars, d_act3, mid2, cotangent, mid1, cq, text_kv, bias_row, cross_weight, query_weight,
        self_weight, gains,
    )
    order.mark(d_mid1)
    g_mate = over_core(g_sent)
    text_mate = over_core(text_grads)
    mid2_late = order.then(mid2)
    output = feed_output(scalars, mid2_late, hid_own, hid_other, down_weight, shards)
    order.mark(output)
    g_mine, g_mate, text_mate = order.then(g_mine, g_mate, text_mate)
    lefts = [(acts, 1), (acts_mate, 1), (acts, 0), (acts_mate, 0), (attended, None), (attended_mate, None)]
    lefts += [(text_row, None), (text_row_mate, None)]
    rights = [(g_mine, lambda j: jnp.minimum(j, 2)), (g_mate, lambda j: jnp.minimum(j, 2))]
    rights += [((text_grads, 0), lambda j: jnp.clip(j - 3, 0, 1))]
    rights += [((text_mate, 1), lambda j: jnp.clip(j - 3, 0, 1))]
    blocks = [((0, 1), (0, 1)), ((2, 3), (0, 1)), ((4, 5), (0, 1)), ((6, 7), (2, 3)), ((6, 7), (2, 3))]
    sent_a, mid_a, sent_b, mid_b = block_grads(
        scalars, bw, lefts, rights, blocks, "middle_grads",
        text=(text_grads, text_mate, text_weight), captions=image_text, per_image=per_image,
    )
    order.mark(mid_a)
    mid_sent_a, mid_sent_b = flat(sent_a), flat(sent_b)
    mid_a, mid_b = flat(mid_a), flat(mid_b)

    def second(streams, name, kept_a, came_a, kept_b, came_b=None):
        def work(sc, ins, outs):
            b_at = 0 if came_b is not None else 2 * streams.a_half
            streams.second(ins[0], ins[1], outs[0], outs[2], number(sc, X), True)
            streams.second(ins[2], ins[-1] if b_at == 0 else ins[1], outs[1], outs[3], number(sc, Y), False, b_at)

        inputs = order.then(kept_a, came_a, kept_b, *([] if came_b is None else [came_b]))
        sent_x, sent_y, kept_a, kept_b = sum_stage(
            order, name, scalars, inputs, [streams.a_half, streams.b_half] * 2, work
        )
        return kept_a, sent_x, kept_b, sent_y

    def third(streams, name, kept_a, came_a, kept_b, came_b, rider=0, skip=0, late=False):
        def work(sc, ins, outs):
            streams.third(ins[0], ins[1], ins[2], ins[3], outs[0], outs[1], number(sc, PLACE) >> skip)
            if rider:
                count = streams.left // 2 * streams.piece
                span = slice(streams.a_half, streams.a_half + rider)
                for out in outs:
                    out[count : count + rider, :] = ins[0][span, :] + ins[1][span, :]

        inputs = order.then(kept_a, came_a, kept_b, came_b)
        out_rows = streams.left // 2 * streams.piece + rider
        sent, kept = sum_stage(order, name, scalars, inputs, [out_rows] * 2, work)
        return kept, (lambda: swap(order.then(sent), "seq", 1 + skip)) if late else swap(sent, "seq", 1 + skip)

    def further(streams, name, kept, came, rider=0, skip=0):
        blocks = streams.left // 2
        for bit in range(1, streams.left.bit_length() - 1):
            half = blocks // 2 * streams.piece

            def work(sc, ins, outs, bit=bit, half=half):
                mine = (number(sc, PLACE) >> (bit + skip)) & 1
                for i in range(half // streams.piece):
                    for out, side in ((outs[0], 1 - mine), (outs[1], mine)):
                        add_rows(
                            ins[0], ins[1], (2 * i + side) * streams.piece, out, i * streams.piece, streams.piece
                        )
                if rider:
                    for out in outs:
                        out[half : half + rider, :] = ins[0][2 * half :, :] + ins[1][2 * half :, :]

            inputs = order.then(kept, came)
            sent, kept = sum_stage(order, name, scalars, inputs, [half + rider] * 2, work)
            came = swap(sent, "seq", bit + 1 + skip)
            blocks //= 2
        return kept, came

    def fourth(streams, name, kept, came, rider=0):
        def work(sc, ins, outs):
            add_rows(ins[0], ins[1], 0, outs[0], 0, streams.piece + rider)

        inputs = order.then(kept, came)
        (total,) = sum_stage(order, name, scalars, inputs, [streams.piece + rider], work)
        return total_over_rest([total])[0]


    mid_sent_a, mid_sent_b, came_fa, came_fb = order.then(mid_sent_a, mid_sent_b, came_fa, came_fb)
    came_ma, came_mb = swap(mid_sent_a, "dp", 1), swap(mid_sent_b, "seq", 0)
    inputs_f = order.then(feed_a, came_fa, feed_b, came_fb)

    def work_f(sc, ins, outs):
        mine = number(sc, PLACE) & 1
        feed.by_place(ins[0], ins[1], outs[0], 0, outs[1], mine, True)
        feed.by_place(ins[2], ins[3], outs[0], feed.a_half, outs[2], mine, False)

    feed_sent, feed_a, feed_b = sum_stage(
        order, "feed_second", scalars, inputs_f, [feed.a_half + feed.b_half, feed.a_half, feed.b_half], work_f
    )
    came_f = swap(feed_sent, "seq", 1)

    d_att = order.then(d_att)
    att_other, before_other = attention_backward(
        scalars, OTHER, qkv, pairs_before, d_att, attended, log_rows
    )
    order.mark(att_other)
    att_mate, before_mate_grads = over_core(att_other), over_core(before_other)
    d_att = order.then(d_att)
    att_own, before_own = attention_backward(scalars, CORE, qkv, pairs_before, d_att, attended, log_rows)
    order.mark(att_own)
    mid_a, mid_sent_x, mid_b, mid_sent_y = second(mids, "mid_second", mid_a, came_ma, mid_b, came_mb)
    came_ma, came_mb = swap(mid_sent_x, "seq", 0), swap(mid_sent_y, "dp", 1)

    act1_late, att_mate, before_mate_grads = order.then(act1, att_mate, before_mate_grads)
    lefts = [(act1_late, None), (act1_mate, None), (act1_before, None), (before_mate, None)]
    rights = [(att_own, lambda j: j), (att_mate, lambda j: j)]
    rights += [(before_own, lambda j: jnp.maximum(j - 1, 0))]
    rights += [(before_mate_grads, lambda j: jnp.maximum(j - 1, 0))]
    blocks = [((0, 1), (0, 1))] + [((0, 1, 2, 3), (0, 1, 2, 3))] * 2
    sent_a, qkv_a, sent_b, qkv_b = block_grads(scalars, bw, lefts, rights, blocks, "qkv_grads")
    order.mark(qkv_a)
    came_qa, came_qb = swap(flat(sent_a), "dp", 1), swap(flat(sent_b), "seq", 0)
    before_own, came_f = order.then(before_own, came_f)
    d_act_before, sums_before = project_back(
        scalars, before_own, before_other, qkv_weight, x_before, "project_back_before"
    )
    order.mark(d_act_before)
    mid_left = third(mids, "mid_third", mid_a, came_ma, mid_b, came_mb)
    feed_a, feed_sent_x, feed_b, feed_sent_y = second(feed_later, "feed_third", feed_a, came_f, feed_b)
    came_fa, came_fb = swap(feed_sent_x, "seq", 0), swap(feed_sent_y, "dp", 1)
    att_own = order.then(att_own)
    d_act, rider = project_back(
        scalars, att_own, att_other, qkv_weight, inputs, "project_back", sums_before, d_gains
    )
    order.mark(d_act)
    rides = rider.shape[0]

    inputs_q = order.then(flat(qkv_a), came_qa, flat(qkv_b), came_qb, rider)

    def work_q(sc, ins, outs):
        qkvs.second(ins[0], ins[1], outs[0], outs[2], number(sc, X), True)
        qkvs.second(ins[2], ins[3], outs[1], outs[3], number(sc, Y), False)
        for out in (outs[0], outs[2]):
            out[qkvs.a_half : qkvs.a_half + rides, :] = ins[4][...]

    sent_x, sent_y, qkv_a, qkv_b = sum_stage(
        order, "qkv_second", scalars, inputs_q,
        [qkvs.a_half + rides, qkvs.b_half] * 2, work_q,
    )
    came_qa, came_qb = swap(sent_x, "seq", 0), swap(sent_y, "dp", 1)
    mid_left = further(mids, "mid_further", *mid_left)
    feed_kept, feed_start = third(
        feed_later, "feed_join", feed_a, came_fa, feed_b, came_fb, skip=1, late=True
    )
    qkv_left = third(qkvs, "qkv_third", qkv_a, came_qa, qkv_b, came_qb, rides)
    d_act_before = order.then(d_act_before)
    d_act_late = lax.ppermute(d_act_before, "seq", odd_to_even)
    mid_piece = fourth(mids, "mid_fourth", *mid_left)

    text_rows = 2 * bw
    text_piece = jnp.concatenate(
        [mid_piece[5 * bw : 6 * bw], mid_piece[11 * bw : 12 * bw]], axis=0
    )
    order.mark(text_piece)
    text_pieces = [text_piece] + [exchange(text_piece, "seq", 2 * k) for k in others]

    def join(name, pieces):
        def work(sc, ins, outs):
            for i, ref in enumerate(ins):
                count = ref.shape[0]
                outs[0][i * count : (i + 1) * count, :] = ref[...]

        inputs = order.then(*pieces)
        return sum_stage(order, name, scalars, inputs, [len(pieces) * pieces[0].shape[0]], work)[0]

    qkv_left = further(qkvs, "qkv_further", *qkv_left, rides)
    text_block = join("text_join", text_pieces)
    came_text = swap(text_block, "seq", 0)
    mid_all = Spread(order, scalars, mid_piece)
    d_act, d_act_late = order.then(d_act, d_act_late)
    input_grad = input_back(d_act, d_act_late, inputs, d_mid1, gain1)
    order.mark(input_grad)
    qkv_piece = fourth(qkvs, "qkv_fourth", *qkv_left, rides)
    qkv_all = Spread(order, scalars, qkv_piece)
    feed_left = (feed_kept, feed_start())
    text_block = join("text_join", [text_block, came_text])
    text_all = Spread(order, scalars, text_block)
    mid_all.forward()

    b_rows = bw // 2

    def write_feed(outs, ref, at_core, y):
        at = 0
        strips = D // 2 // LANES
        for c in range(strips):
            col = y * (D // 2) + c * LANES
            outs[0][at_core * bw_ff : (at_core + 1) * bw_ff, col : col + LANES] = ref[
                at + c * bw_ff : at + (c + 1) * bw_ff, :
            ].astype(F32)
        at = at + strips * bw_ff
        per = bw_ff // LANES
        for c in range(FF // 2 // LANES):
            s, inside = divmod(c, per)
            col = (2 * s + at_core) * bw_ff + inside * LANES
            outs[1][y * b_rows : (y + 1) * b_rows, col : col + LANES] = ref[
                at + c * b_rows : at + (c + 1) * b_rows, :
            ].astype(F32)

    def writer(targets):
        count = len(targets)

        def write(outs, ref, at_core, y):
            for j, where in enumerate(targets):
                if where is None:
                    continue
                out, first = where
                col = first[at_core]
                outs[out][:, col + y * LANES : col + (y + 1) * LANES] = ref[
                    j * bw : (j + 1) * bw, :
                ].astype(F32)
                for half in (0, 1):
                    row_at = count * bw + (2 * j + half) * b_rows
                    to = col + 256 + half * LANES
                    outs[out][y * b_rows : (y + 1) * b_rows, to : to + LANES] = ref[
                        row_at : row_at + b_rows, :
                    ].astype(F32)

        return write

    targets = [(0, (0, 512)), (1, (0, 512)), (2, (0, 512)), (3, (0, 1024)), (3, (512, 1536)), None]
    cross_grad, query_grad, self_grad, text_weight_grad = mid_all.finish(
        mids.piece, [(bw, D), (bw, D), (bw, D), (bw, 2 * D)], writer(targets), "mids_finish"
    )
    qkv_all.forward()
    text_all.forward()
    targets = [(0, (0, 512)), (0, (1024, 1536)), (0, (2048, 2560))]
    qkv_grad, sums = qkv_all.finish(
        qkvs.piece, [(bw, 3 * D)], writer(targets), "qkv_finish", rider=rides
    )
    feed_left = further(feed_later, "feed_further", *feed_left, skip=1)
    feed_piece = fourth(feed_later, "feed_fourth", *feed_left)
    feed_all = Spread(order, scalars, feed_piece)
    text_grad = text_all.finish_text(text_rows, bw)
    order.mark(text_grad)
    feed_all.forward()
    down_grad, up_grad = feed_all.finish(
        feed.piece, [(2 * bw_ff, D), (bw, FF)], write_feed, "feed_finish"
    )
    sums = lax.dynamic_slice_in_dim(sums.reshape(6, D), me * bw, bw, 1)
    return (
        output,
        input_grad,
        text_grad.reshape(text_state.shape),
        sums[0],
        sums[1],
        qkv_grad,
        self_grad,
        sums[2],
        sums[3],
        query_grad,
        text_weight_grad,
        cross_grad,
        sums[4],
        sums[5],
        up_grad,
        down_grad,
    )


def solution(mesh):
    tokens = P(("dp", "seq"), None)
    return jax.shard_map(
        body,
        mesh=mesh,
        in_specs=(tokens,) + (P(),) * 17 + (tokens,),
        out_specs=(
            tokens,
            tokens,
            P(),
            P("seq"),
            P("seq"),
            P("seq", None),
            P("seq", None),
            P("seq"),
            P("seq"),
            P("seq", None),
            P("seq", None),
            P("seq", None),
            P("seq"),
            P("seq"),
            P("seq", None),
            P("seq", None),
        ),
        check_vma=False,
    )
```

```python
import functools
import math

import jax
import jax.numpy as jnp
from jax import lax
from jax.experimental import pallas as pl
from jax.experimental.pallas import tpu as pltpu
from jax.sharding import PartitionSpec as P

D = 1024
HEADS = 16
HEAD = 64
FF = 4096
TEXT_LEN = 128
IMG_TOK = 1024
PAIR = 2 * HEAD
LANES = 128
SCALE = 1.0 / math.sqrt(HEAD)

NEGATIVE = -1e30
EPSILON = 1e-05
BF = jnp.bfloat16
F32 = jnp.float32
NN = (((1,), (0,)), ((), ()))
NT = (((1,), (1,)), ((), ()))
TN = (((0,), (0,)), ((), ()))
VMEM_LIMIT = 65000 * 1024
ODD, CORE, OTHER, X, Y, NOT_Y, PLACE, QUARTER, ME, GROUP = range(10)


def mm(a, b, dims=NN):
    return lax.dot_general(a, b, dims, preferred_element_type=F32)


def normed(values):
    average = jnp.mean(values, axis=-1, keepdims=True)
    centered = values - average
    inverse = lax.rsqrt(jnp.mean(centered * centered, axis=-1, keepdims=True) + EPSILON)
    return centered * inverse, inverse


def norm_back(normal, inverse, gain, upstream):
    w = upstream * gain
    along = jnp.mean(w * normal, axis=-1, keepdims=True)
    return inverse * (w - jnp.mean(w, axis=-1, keepdims=True) - normal * along)


def head_lanes(h):
    lane = lax.broadcasted_iota(jnp.int32, (1, PAIR), 1)
    return (lane >= h * HEAD) & (lane < (h + 1) * HEAD)


def only_head(block, h):
    return jnp.where(head_lanes(h), block, jnp.zeros_like(block))


def by_rows(rows, size, step):
    def one(i, carry):
        step(pl.ds(pl.multiple_of(i * size, size), size))
        return carry

    if rows == size:
        step(slice(0, rows))
        return
    lax.fori_loop(0, rows // size, one, 0, unroll=2)


def params(grid_dims=1):
    return pltpu.CompilerParams(
        dimension_semantics=("arbitrary",) * grid_dims, vmem_limit_bytes=VMEM_LIMIT
    )


def cost(flops, moved):
    return pl.CostEstimate(flops=1, bytes_accessed=1, transcendentals=0)


def number(ref, which):
    packed = ref[0]
    if which == ODD:
        return packed & 1
    if which == CORE:
        return (packed >> 1) & 1
    if which == OTHER:
        return 1 - ((packed >> 1) & 1)
    if which == Y:
        return (packed >> 2) & 1
    if which == NOT_Y:
        return 1 - ((packed >> 2) & 1)
    if which == QUARTER:
        return (packed >> 1) & 3
    if which == ME:
        return (packed >> 3) & 4095
    if which == GROUP:
        return ((packed >> 1) & 3) | ((packed >> 15) << 2)
    if which == X:
        return (packed >> 3) & 1
    return (packed >> 4) & 2047


def image_entry(scalars_ref, table_ref, per_image, groups, other=0):
    group = number(scalars_ref, GROUP) ^ other
    return table_ref[table_ref.shape[0] // groups * group + number(scalars_ref, ME) // per_image]


def row_block(ref, i, blocks):
    x = number(ref, X)
    half = blocks // 2
    return 2 * i + 1 - x if i < half else 2 * (i - half) + x


def whole(shape):
    zeros = (0,) * len(shape)
    return pl.BlockSpec(shape, lambda *_: zeros)


def shape_of(shape, dtype):
    return jax.ShapeDtypeStruct(shape, dtype)


def head_sums(block):
    wide = block.astype(F32)
    lane = lax.broadcasted_iota(jnp.int32, (D, PAIR), 1)
    row = lax.broadcasted_iota(jnp.int32, (D, PAIR), 0)
    pick = jnp.where(row // HEAD == lane, 1.0, 0.0).astype(BF)
    return jnp.max(mm((wide * wide).astype(BF), pick), axis=0, keepdims=True)


def small_scores(q_sums, k_sums):
    return jnp.max(q_sums * k_sums) * (SCALE * SCALE) < 75.0 * 75.0


def norm_project(x, gain, shift, weight, first_col, name):
    rows, width = x.shape
    cols = weight.shape[1] - first_col
    bn = D

    def kernel(x_ref, gain_ref, shift_ref, w_ref, act_ref, out_ref, norm_ref):
        j = pl.program_id(0)

        @pl.when(j == 0)
        def _():
            norm_ref[...] = jnp.zeros_like(norm_ref)

            def norm_rows(span):
                normal, _ = normed(x_ref[span, :].astype(F32))
                act_ref[span, :] = (normal * gain_ref[...] + shift_ref[...]).astype(BF)

            by_rows(rows, 128, norm_rows)

        out = mm(act_ref[...], w_ref[...]).astype(BF)
        out_ref[...] = out
        for i in range(cols // bn - 1):

            @pl.when(j == i)
            def _(i=i):
                norm_ref[i : i + 1, :] = head_sums(out)

    return pl.pallas_call(
        kernel,
        grid=(cols // bn,),
        in_specs=[
            whole((rows, width)),
            whole((1, width)),
            whole((1, width)),
            pl.BlockSpec((width, bn), lambda j: (0, first_col // bn + j)),
        ],
        out_specs=[
            whole((rows, width)),
            pl.BlockSpec((rows, bn), lambda j: (0, j)),
            whole((8, PAIR)),
        ],
        out_shape=[
            shape_of((rows, width), BF),
            shape_of((rows, cols), BF),
            shape_of((8, PAIR), F32),
        ],
        compiler_params=params(),
        cost_estimate=cost(0, 0),
        name=name,
    )(x, gain, shift, weight)


def with_ones(v, h):
    ones = jnp.where(head_lanes(h), jnp.ones_like(v), jnp.zeros_like(v))
    return jnp.concatenate([only_head(v, h), ones], axis=1)


def rows_of(columns):
    turned = columns.T
    return turned[0:1], turned[HEAD : HEAD + 1]


def columns_of(log_rows):
    rows = log_rows.shape[1]
    turned = jnp.concatenate([log_rows, jnp.zeros((6, rows), F32)], axis=0).T
    return jnp.where(head_lanes(0), turned[:, 0:1], turned[:, 1:2])


def causal_forward(qkv, norms):
    rows = qkv.shape[0]
    half = rows // 2
    pairs = D // PAIR

    def kernel(q_ref, k_ref, v_ref, norm_ref, out_ref, log_ref, small_ref):
        @pl.when(pl.program_id(0) == 0)
        def _():
            small_ref[0] = small_scores(norm_ref[0:1, :], norm_ref[1:2, :]).astype(jnp.int32)

        below = lax.broadcasted_iota(jnp.int32, (half, half), 0) >= lax.broadcasted_iota(
            jnp.int32, (half, half), 1
        )

        @pl.when(small_ref[0] != 0)
        def _():
            early, late = slice(0, half), slice(half, rows)
            q_early, q_late = q_ref[early, :] * SCALE, q_ref[late, :] * SCALE
            k, v = k_ref[...], v_ref[...]
            values = [with_ones(v, h) for h in (0, 1)]
            p = jnp.exp(mm(q_early, both_heads(k[early]), NT))
            p = jnp.concatenate(
                [jnp.where(below, p[:, :half], 0.0).astype(BF), jnp.where(below, p[:, half:], 0.0).astype(BF)], axis=1
            )
            first = mm(p, jnp.concatenate([values[0][early], values[1][early]], axis=0))
            p = jnp.exp(mm(q_late, both_heads(k), NT))
            parts = [p[:, i * half : (i + 1) * half] for i in range(4)]
            parts = [parts[0], jnp.where(below, parts[1], 0.0), parts[2], jnp.where(below, parts[3], 0.0)]
            p = jnp.concatenate([part.astype(BF) for part in parts], axis=1)
            second = mm(p, jnp.concatenate(values, axis=0))
            for span, both in ((early, first), (late, second)):
                out_ref[span, :] = (both[:, :PAIR] / both[:, PAIR:]).astype(BF)
                one, two = rows_of(both[:, PAIR:])
                log_ref[0, 0:1, span] = jnp.log(one)
                log_ref[0, 1:2, span] = jnp.log(two)

        @pl.when(small_ref[0] == 0)
        def _():
            def slowly(span):
                q = q_ref[span, :] * SCALE
                k, v = k_ref[...], v_ref[...]
                at_q = span.start + lax.broadcasted_iota(jnp.int32, (PAIR, rows), 0)
                at_k = lax.broadcasted_iota(jnp.int32, (PAIR, rows), 1)
                total = jnp.zeros((PAIR, PAIR), F32)
                logs = jnp.zeros((PAIR, PAIR), F32)
                for h in (0, 1):
                    s = mm(q, only_head(k, h), NT)
                    s = jnp.where(at_q >= at_k, s, NEGATIVE)
                    top = jnp.max(s, axis=1, keepdims=True)
                    p = jnp.exp(s - top)
                    part = jnp.sum(p, axis=1, keepdims=True)
                    total = total + mm(p.astype(BF), only_head(v, h)) * (1.0 / part)
                    logs = jnp.where(head_lanes(h), top + jnp.log(part), logs)
                out_ref[span, :] = total.astype(BF)
                one, two = rows_of(logs)
                log_ref[0, 0:1, span] = one
                log_ref[0, 1:2, span] = two

            by_rows(rows, PAIR, slowly)

    block = (rows, PAIR)
    return pl.pallas_call(
        kernel,
        grid=(pairs,),
        in_specs=[
            pl.BlockSpec(block, lambda p: (0, p)),
            pl.BlockSpec(block, lambda p: (0, pairs + p)),
            pl.BlockSpec(block, lambda p: (0, 2 * pairs + p)),
            whole(norms.shape),
        ],
        out_specs=[
            pl.BlockSpec(block, lambda p: (0, p)),
            pl.BlockSpec((1, 2, rows), lambda p: (p, 0, 0)),
        ],
        out_shape=[shape_of((rows, D), BF), shape_of((pairs, 2, rows), F32)],
        scratch_shapes=[pltpu.SMEM((1,), jnp.int32)],
        compiler_params=params(),
        cost_estimate=cost(0, 0),
        name="causal_forward",
    )(qkv, qkv, qkv, norms)


def earlier_forward(odd, qkv, pairs_before, norms, norms_before, own_out, own_log):
    rows = qkv.shape[0]
    half = rows // 2
    pairs = D // PAIR

    def kernel(
        odd_ref, q_ref, k_ref, v_ref, norm_ref, before_ref, own_ref, log_ref, out_ref, new_log_ref, mode_ref
    ):
        @pl.when(pl.program_id(0) == 0)
        def _():
            small = small_scores(
                norm_ref[0:1, :], jnp.maximum(norm_ref[1:2, :], before_ref[0:1, :])
            )
            mode_ref[0] = number(odd_ref, ODD) * (2 - small.astype(jnp.int32))

        @pl.when(mode_ref[0] == 0)
        def _():
            out_ref[...] = own_ref[...]
            new_log_ref[...] = log_ref[...]

        @pl.when(mode_ref[0] == 1)
        def _():
            keys = both_heads(k_ref[...])
            values = jnp.concatenate([with_ones(v_ref[...], h) for h in (0, 1)], axis=0)
            old = jnp.exp(columns_of(log_ref[0]))
            for first in range(0, rows, 128):
                span = slice(first, first + 128)
                p = jnp.exp(mm(q_ref[span, :] * SCALE, keys, NT)).astype(BF)
                both = mm(p, values)
                total = old[span] + both[:, PAIR:]
                mixed = own_ref[span, :].astype(F32) * old[span] + both[:, :PAIR]
                out_ref[span, :] = (mixed / total).astype(BF)
                one, two = rows_of(total)
                new_log_ref[0, 0:1, span] = jnp.log(one)
                new_log_ref[0, 1:2, span] = jnp.log(two)

        @pl.when(mode_ref[0] == 2)
        def _():
            def slowly(span):
                q = q_ref[span, :] * SCALE
                total = own_ref[span, :].astype(F32)
                logs = columns_of(log_ref[0, :, span])
                result = jnp.zeros_like(total)
                new_logs = logs
                for h in (0, 1):
                    s = mm(q, only_head(k_ref[...], h), NT)
                    old = logs[:, h * HEAD : h * HEAD + 1]
                    top = jnp.maximum(old, jnp.max(s, axis=1, keepdims=True))
                    p = jnp.exp(s - top)
                    share = jnp.exp(old - top)
                    part = share + jnp.sum(p, axis=1, keepdims=True)
                    mixed = mm(p.astype(BF), only_head(v_ref[...], h))
                    mixed = mixed + only_head(total, h) * share
                    result = result + mixed * (1.0 / part)
                    new_logs = jnp.where(head_lanes(h), top + jnp.log(part), new_logs)
                out_ref[span, :] = result.astype(BF)
                one, two = rows_of(new_logs)
                new_log_ref[0, 0:1, span] = one
                new_log_ref[0, 1:2, span] = two

            by_rows(rows, PAIR, slowly)

    block = (rows, PAIR)
    first = pl.BlockSpec(block, lambda p, odd: (0, p))
    second = pl.BlockSpec(block, lambda p, odd: (0, pairs + p))
    log_block = pl.BlockSpec((1, 2, rows), lambda p, odd: (p, 0, 0))
    return pl.pallas_call(
        kernel,
        grid_spec=pltpu.PrefetchScalarGridSpec(
            num_scalar_prefetch=1,
            grid=(pairs,),
            in_specs=[
                first, first, second, whole(norms.shape), whole(norms_before.shape), first, log_block,
            ],
            out_specs=[first, log_block],
            scratch_shapes=[pltpu.SMEM((1,), jnp.int32)],
        ),
        out_shape=[shape_of((rows, D), BF), shape_of((pairs, 2, rows), F32)],
        compiler_params=params(),
        cost_estimate=cost(0, 0),
        name="earlier_forward",
    )(odd, qkv, pairs_before, pairs_before, norms, norms_before, own_out, own_log)


def text_project(scalars, image_text, image_segment, per_image, text, segments, weight):
    tokens = text.shape[1]
    bn = 1024
    groups = lax.axis_size("dp")

    def kernel(sc_ref, text_of_ref, seg_of_ref, row_ref, mate_ref, seg_ref, w_ref, kv_ref, bias_ref, row_out, mate_out):
        kv_ref[...] = mm(row_ref[...], w_ref[...]).astype(BF)

        @pl.when(pl.program_id(0) == 0)
        def _():
            row_out[...] = row_ref[...]
            mate_out[...] = mate_ref[...]
            row = image_entry(sc_ref, text_of_ref, per_image, groups)
            caption = image_entry(sc_ref, seg_of_ref, per_image, groups)
            bias = jnp.where(seg_ref[pl.ds(row, 1), :] == caption, 0.0, NEGATIVE)
            bias_ref[...] = jnp.concatenate([bias, bias], axis=1).astype(F32)

    return pl.pallas_call(
        kernel,
        grid_spec=pltpu.PrefetchScalarGridSpec(
            num_scalar_prefetch=3,
            grid=(weight.shape[1] // bn,),
            in_specs=[
                pl.BlockSpec(
                    (None, tokens, D), lambda j, sc, of, _: (image_entry(sc, of, per_image, groups), 0, 0)
                ),
                pl.BlockSpec(
                    (None, tokens, D), lambda j, sc, of, _: (image_entry(sc, of, per_image, groups, 1), 0, 0)
                ),
                whole(segments.shape),
                pl.BlockSpec((D, bn), lambda j, *_: (0, j)),
            ],
            out_specs=[
                pl.BlockSpec((tokens, bn), lambda j, *_: (0, j)),
                whole((1, 2 * tokens)),
                whole((tokens, D)),
                whole((tokens, D)),
            ],
        ),
        out_shape=[
            shape_of((tokens, weight.shape[1]), BF),
            shape_of((1, 2 * tokens), F32),
            shape_of((tokens, D), BF),
            shape_of((tokens, D), BF),
        ],
        compiler_params=params(),
        cost_estimate=cost(0, 0),
        name="text_project",
    )(scalars, image_text, image_segment, text, text, segments, weight)


def cross_weights(scores, small):
    if small:
        return jnp.exp(scores)
    halves = []
    for h in (0, 1):
        s = scores[:, h * TEXT_LEN : (h + 1) * TEXT_LEN]
        halves.append(jnp.exp(s - jnp.max(s, axis=1, keepdims=True)))
    return jnp.concatenate(halves, axis=1)


def each_pair(pair, unrolled):
    def one(p, carry):
        pair(p)
        return carry

    lax.fori_loop(0, D // PAIR, one, 0, unroll=4 if unrolled else 1)


def both_heads(block):
    return jnp.concatenate([only_head(block, 0), only_head(block, 1)], axis=0)


def copies_of(hbm_refs, vmem_refs, sems):
    copies = [
        pltpu.make_async_copy(src, dst, sems.at[i])
        for i, (src, dst) in enumerate(zip(hbm_refs, vmem_refs))
    ]
    return copies


def start(*copies):
    for copy in copies:
        copy.start()


def wait(*copies):
    for copy in copies:
        copy.wait()


def middle_forward(attended, x, self_w, query_w, cross_w, gains, text_kv, bias):
    rows = x.shape[0]
    any_space = pl.BlockSpec(memory_space=pl.ANY)

    def kernel(
        at_ref, x_ref, sw_hbm, qw_hbm, cw_hbm, gains_ref, kv_ref, bias_ref,
        mid1_hbm, cq_hbm, mid2_hbm, acts_hbm,
        sw, qw, cw, mid1_ref, cq_ref, mid2_ref, acts_ref, sems, out_sems,
    ):
        loads = copies_of((sw_hbm, qw_hbm, cw_hbm), (sw, qw, cw), sems)
        outs = []

        def out(src, dst):
            copy = pltpu.make_async_copy(src, dst, out_sems.at[len(outs)])
            copy.start()
            outs.append(copy)

        start(loads[0])
        wait(loads[0])
        start(loads[1], loads[2])
        mid1_ref[...] = x_ref[...].astype(F32) + mm(at_ref[...], sw[...])
        out(mid1_ref, mid1_hbm)

        def norm2(span):
            normal, _ = normed(mid1_ref[span, :])
            acts_ref[0, span, :] = (normal * gains_ref[0:1, :] + gains_ref[1:2, :]).astype(BF)

        by_rows(rows, 128, norm2)
        out(acts_ref.at[0], acts_hbm.at[0])
        loads[1].wait()
        cq_ref[...] = mm(acts_ref[0], qw[...]).astype(BF)
        out(cq_ref, cq_hbm)
        small = small_scores(head_sums(cq_ref[...]), head_sums(kv_ref[:, :D]))
        bias_row = bias_ref[...]

        def attend(is_small):
            def pair(p):
                span = pl.ds(pl.multiple_of(p * PAIR, PAIR), PAIR)
                q = cq_ref[:, span] * SCALE
                v = kv_ref[:, pl.ds(pl.multiple_of(D + p * PAIR, PAIR), PAIR)]
                s = mm(q, both_heads(kv_ref[:, span]), NT) + bias_row
                w = cross_weights(s, is_small).astype(BF)
                both = mm(w, jnp.concatenate([with_ones(v, 0), with_ones(v, 1)], axis=0))
                acts_ref[1, :, span] = (both[:, :PAIR] / both[:, PAIR:]).astype(BF)

            each_pair(pair, is_small)

        @pl.when(small)
        def _():
            attend(True)

        @pl.when(jnp.logical_not(small))
        def _():
            attend(False)

        out(acts_ref.at[1], acts_hbm.at[1])
        loads[2].wait()
        mid2_ref[...] = mid1_ref[...] + mm(acts_ref[1], cw[...])
        out(mid2_ref, mid2_hbm)

        def norm3(span):
            normal, _ = normed(mid2_ref[span, :])
            acts_ref[2, span, :] = (normal * gains_ref[2:3, :] + gains_ref[3:4, :]).astype(BF)

        by_rows(rows, 128, norm3)
        out(acts_ref.at[2], acts_hbm.at[2])
        for copy in outs:
            copy.wait()

    token = (rows, D)
    return pl.pallas_call(
        kernel,
        grid=(1,),
        in_specs=[
            whole(token), whole(token), any_space, any_space, any_space,
            whole(gains.shape), whole(text_kv.shape), whole(bias.shape),
        ],
        out_specs=[any_space] * 4,
        out_shape=[shape_of(token, t) for t in (F32, BF, F32)] + [shape_of((3,) + token, BF)],
        scratch_shapes=[pltpu.VMEM((D, D), BF)] * 3
        + [pltpu.VMEM(token, t) for t in (F32, BF, F32)]
        + [pltpu.VMEM((3,) + token, BF), pltpu.SemaphoreType.DMA((3,)), pltpu.SemaphoreType.DMA((6,))],
        compiler_params=params(),
        cost_estimate=cost(0, 0),
        name="middle_forward",
    )(attended, x, self_w, query_w, cross_w, gains, text_kv, bias)


def feed_half(which, half, acts, grad3, up, down, shards, before):
    rows = acts.shape[1]
    bw = FF // (2 * shards)
    root = math.sqrt(2.0 / math.pi)
    each = 4
    steps = shards // each

    def kernel(which_ref, a_ref, g_ref, *rest):
        up_refs, down_refs = rest[:each], rest[each : 2 * each]
        hid_ref, da_ref = rest[-2:]
        parts = []
        for i in range(each):
            span = slice(i * bw, (i + 1) * bw)
            h = mm(a_ref[...], up_refs[i][...])
            dy = mm(g_ref[...], down_refs[i][...], NT)
            sq = h * h
            t = jnp.tanh(h * (root + (root * 0.044715) * sq))
            more = 0.5 + 0.5 * t
            hid_ref[0, :, span] = (h * more).astype(BF)
            slope = more + (h * (0.5 - 0.5 * (t * t))) * (root + (3 * root * 0.044715) * sq)
            dh = (dy * slope).astype(BF)
            hid_ref[1, :, span] = dh
            parts.append(dh)
        ups = jnp.concatenate([ref[...] for ref in up_refs], axis=1)
        part = mm(jnp.concatenate(parts, axis=1), ups, NT)

        @pl.when(pl.program_id(0) == 0)
        def _():
            if before is None:
                da_ref[...] = part
            else:
                da_ref[...] = rest[2 * each][...] + part

        @pl.when(pl.program_id(0) != 0)
        def _():
            da_ref[...] += part

    token = whole((rows, D))
    in_specs = [pl.BlockSpec((None, rows, D), lambda s, which: (2, 0, 0)), token]
    for i in range(each):
        in_specs.append(
            pl.BlockSpec((D, bw), lambda s, which, i=i: (0, 2 * (each * s + i) + number(which, half)))
        )
    for i in range(each):
        in_specs.append(
            pl.BlockSpec((bw, D), lambda s, which, i=i: (2 * (each * s + i) + number(which, half), 0))
        )
    operands = [which, acts, grad3] + [up] * each + [down] * each
    if before is not None:
        in_specs.append(token)
        operands.append(before)
    return pl.pallas_call(
        kernel,
        grid_spec=pltpu.PrefetchScalarGridSpec(
            num_scalar_prefetch=1,
            grid=(steps,),
            in_specs=in_specs,
            out_specs=[
                pl.BlockSpec((2, rows, each * bw), lambda s, which: (0, 0, s)),
                token,
            ],
        ),
        out_shape=[shape_of((2, rows, FF // 2), BF), shape_of((rows, D), F32)],
        compiler_params=params(),
        cost_estimate=cost(0, 0),
        name="feed_half",
    )(*operands)


def feed_output(own, mid2, hidden_own, hidden_other, down, shards):
    rows = mid2.shape[0]
    bw = FF // (2 * shards)
    each = 4
    steps = shards // each

    def kernel(own_ref, mid_ref, a_ref, b_ref, down_ref, out_ref, acc_ref):
        s = pl.program_id(0)
        first = number(own_ref, CORE) == 0
        pieces = []
        for i in range(each):
            span = slice(i * bw, (i + 1) * bw)
            a, b = a_ref[:, span], b_ref[:, span]
            pieces += [jnp.where(first, a, b), jnp.where(first, b, a)]
        part = mm(jnp.concatenate(pieces, axis=1), down_ref[...])

        @pl.when(s == 0)
        def _():
            acc_ref[...] = mid_ref[...] + part

        @pl.when(s != 0)
        def _():
            acc_ref[...] += part

        @pl.when(s == steps - 1)
        def _():
            out_ref[...] = acc_ref[...].astype(BF)

    token = whole((rows, D))
    hid = pl.BlockSpec((None, rows, each * bw), lambda s, own: (0, 0, s))
    return pl.pallas_call(
        kernel,
        grid_spec=pltpu.PrefetchScalarGridSpec(
            num_scalar_prefetch=1,
            grid=(steps,),
            in_specs=[token, hid, hid, pl.BlockSpec((2 * each * bw, D), lambda s, own: (s, 0))],
            out_specs=token,
            scratch_shapes=[pltpu.VMEM((rows, D), F32)],
        ),
        out_shape=shape_of((rows, D), BF),
        compiler_params=params(),
        cost_estimate=cost(0, 0),
        name="feed_output",
    )(own, mid2, hidden_own, hidden_other, down)


def middle_backward(
    own, d_act3, mid2, upstream, mid1, cq, text_kv, bias, cross_w, query_w, self_w, gains
):
    rows = mid2.shape[0]
    wide = D // 2
    any_space = pl.BlockSpec(memory_space=pl.ANY)
    chunk = 128

    def kernel(
        own_ref, da3_hbm, mid2_hbm, g_hbm, mid1_hbm, cq_hbm, kv_ref, bias_ref, cw_hbm, qw_hbm, sw_hbm, gains_ref,
        mine_hbm, sent_hbm, dmid1_hbm, dat_hbm, kv_ref_out, dgains_ref,
        da3, mid2_v, g_v, mid1_v, cq_v, cw, qw, sw, kv_acc, grads, dmid, dat, up2, sums, sems, out_sems,
    ):
        loads = copies_of(
            (da3_hbm, mid2_hbm, g_hbm, cw_hbm, cq_hbm, qw_hbm, mid1_hbm, sw_hbm),
            (da3, mid2_v, g_v, cw, cq_v, qw, mid1_v, sw),
            sems,
        )
        core_at = pl.multiple_of(number(own_ref, CORE) * wide, wide)
        mate_at = pl.multiple_of(number(own_ref, OTHER) * wide, wide)
        outs = []

        def out(src, dst):
            copy = pltpu.make_async_copy(src, dst, out_sems.at[len(outs)])
            copy.start()
            outs.append(copy)

        def out_grad(part):
            out(grads.at[part, :, pl.ds(core_at, wide)], mine_hbm.at[part])
            out(grads.at[part, :, pl.ds(mate_at, wide)], sent_hbm.at[part])

        def add_up(place, values):
            folded = values[:8]
            for i in range(8, rows, 8):
                folded = folded + values[i : i + 8]
            sums[place] += folded

        start(*loads[:3])
        sums[...] = jnp.zeros_like(sums)
        wait(*loads[:3])
        start(*loads[3:5])

        def back3(span):
            up = da3[span, :]
            normal, inverse = normed(mid2_v[span, :])
            add_up(2, up * normal)
            add_up(3, up)
            total = g_v[span, :].astype(F32) + norm_back(normal, inverse, gains_ref[2:3, :], up)
            dmid[span, :] = total
            grads[0, span, :] = total.astype(BF)

        back3(slice(0, rows))
        out_grad(0)
        wait(loads[3])
        start(*loads[5:7])
        dat[...] = mm(grads[0], cw[...], NT).astype(BF)
        loads[4].wait()
        small = small_scores(head_sums(cq_v[...]), head_sums(kv_ref[:, :D]))
        bias_row = bias_ref[...]
        side = lax.broadcasted_iota(jnp.int32, (2 * TEXT_LEN, 2 * TEXT_LEN), 0) // TEXT_LEN
        same = side == lax.broadcasted_iota(jnp.int32, side.shape, 1) // TEXT_LEN
        summing = jnp.where(same, 1.0, 0.0).astype(BF)

        def back_pairs(is_small):
            def pair(p):
                span = pl.ds(pl.multiple_of(p * PAIR, PAIR), PAIR)
                vspan = pl.ds(pl.multiple_of(D + p * PAIR, PAIR), PAIR)
                q = cq_v[:, span] * SCALE
                dc = dat[:, span]
                k = both_heads(kv_ref[:, span])
                v = both_heads(kv_ref[:, vspan])
                w = cross_weights(mm(q, k, NT) + bias_row, is_small)
                w = w / mm(w.astype(BF), summing)
                dw = mm(dc, v, NT)
                ds = (w * (dw - mm((w * dw).astype(BF), summing))).astype(BF)
                grads[1, :, span] = (mm(ds, k) * SCALE).astype(BF)
                dk = mm(ds, q, TN)
                dv = mm(w.astype(BF), dc, TN)
                kv_acc[:, span] = jnp.where(head_lanes(0), dk[:TEXT_LEN], dk[TEXT_LEN:]).astype(BF)
                kv_acc[:, vspan] = jnp.where(head_lanes(0), dv[:TEXT_LEN], dv[TEXT_LEN:]).astype(BF)

            each_pair(pair, is_small)

        @pl.when(small)
        def _():
            back_pairs(True)

        @pl.when(jnp.logical_not(small))
        def _():
            back_pairs(False)

        out_grad(1)
        kv_ref_out[0] = kv_acc[:, pl.ds(2 * core_at, D)]
        kv_ref_out[1] = kv_acc[:, pl.ds(2 * mate_at, D)]
        loads[5].wait()
        up2[...] = mm(grads[1], qw[...], NT)
        wait(loads[6])
        start(loads[7])

        def back2(span):
            up = up2[span, :]
            normal, inverse = normed(mid1_v[span, :])
            add_up(0, up * normal)
            add_up(1, up)
            total = dmid[span, :] + norm_back(normal, inverse, gains_ref[0:1, :], up)
            dmid[span, :] = total
            grads[2, span, :] = total.astype(BF)

        back2(slice(0, rows))
        out(dmid, dmid1_hbm)
        out_grad(2)
        loads[7].wait()
        dat[...] = mm(grads[2], sw[...], NT).astype(BF)
        out(dat, dat_hbm)
        dgains_ref[...] = jnp.zeros_like(dgains_ref)
        for i in range(4):
            dgains_ref[i : i + 1, :] = jnp.sum(sums[i], axis=0, keepdims=True)
        for copy in outs:
            copy.wait()

    token = (rows, D)
    halves = (3, rows, wide)
    text = (2, TEXT_LEN, D)
    return pl.pallas_call(
        kernel,
        grid_spec=pltpu.PrefetchScalarGridSpec(
            num_scalar_prefetch=1,
            grid=(1,),
            in_specs=[any_space] * 5
            + [whole(text_kv.shape), whole(bias.shape)]
            + [any_space] * 3
            + [whole(gains.shape)],
            out_specs=[any_space] * 4 + [whole(text), whole((8, D))],
            scratch_shapes=[pltpu.VMEM(token, t) for t in (F32, F32, BF, F32, BF)]
            + [pltpu.VMEM((D, D), BF)] * 3
            + [pltpu.VMEM(text_kv.shape, BF), pltpu.VMEM((3,) + token, BF)]
            + [pltpu.VMEM(token, F32), pltpu.VMEM(token, BF), pltpu.VMEM(token, F32)]
            + [pltpu.VMEM((4, 8, D), F32)]
            + [pltpu.SemaphoreType.DMA((8,)), pltpu.SemaphoreType.DMA((8,))],
        ),
        out_shape=[shape_of(halves, BF)] * 2
        + [shape_of(token, t) for t in (F32, BF)]
        + [shape_of(text, BF)]
        + [shape_of((8, D), F32)],
        compiler_params=params(),
        cost_estimate=cost(0, 0),
        name="middle_backward",
    )(own, d_act3, mid2, upstream, mid1, cq, text_kv, bias, cross_w, query_w, self_w, gains)


def deltas_of(d_out, out):
    prod = d_out.astype(F32) * out.astype(F32)
    high = prod.astype(BF)
    low = (prod - high.astype(F32)).astype(BF)
    row = lax.broadcasted_iota(jnp.int32, (8, PAIR), 0)
    lane = lax.broadcasted_iota(jnp.int32, (8, PAIR), 1)
    pick = jnp.where(lane // HEAD == row, 1.0, 0.0).astype(BF)
    return mm(pick, high, NT) + mm(pick, low, NT)


def key_block_back(k, v, q, d_out, logs, deltas, causal):
    keys = k.shape[0]
    k2, v2 = both_heads(k), both_heads(v)
    s = mm(k2, q, NT)
    dp = mm(v2, d_out, NT)
    weights, grads = [], []
    for h in (0, 1):
        span = slice(h * keys, (h + 1) * keys)
        p = jnp.exp(s[span] - logs[h : h + 1])
        if causal:
            at_k = lax.broadcasted_iota(jnp.int32, (keys, keys), 0)
            at_q = lax.broadcasted_iota(jnp.int32, (keys, keys), 1)
            first = jnp.where(at_q >= at_k, p[:, :keys], 0.0)
            p = first if p.shape[1] == keys else jnp.concatenate([first, p[:, keys:]], axis=1)
        weights.append(p.astype(BF))
        grads.append((p * (dp[span] - deltas[h : h + 1])).astype(BF))
    p2, ds2 = jnp.concatenate(weights, axis=0), jnp.concatenate(grads, axis=0)
    dv, dk = mm(p2, d_out), mm(ds2, q)
    lanes = head_lanes(0)
    dk = jnp.where(lanes, dk[:keys], dk[keys:]).astype(BF)
    dv = jnp.where(lanes, dv[:keys], dv[keys:]).astype(BF)
    return mm(ds2, k2, TN), dk, dv


def attention_backward(scalars, side, qkv, pairs_before, d_out, out, logs):
    rows = qkv.shape[0]
    half = rows // 2
    pairs = D // PAIR
    count = pairs // 2

    def kernel(
        sc_ref, q_ref, k_ref, v_ref, kb_ref, vb_ref, do_ref, out_ref, log_ref, grads_ref, before_ref, dq_ref
    ):
        q = q_ref[...] * SCALE
        d_o = do_ref[...]
        deltas = deltas_of(d_o, out_ref[...])
        log_rows = log_ref[0]

        @pl.when(number(sc_ref, ODD) == 0)
        def _():
            dq_ref[...] = jnp.zeros_like(dq_ref)
            before_ref[...] = jnp.zeros_like(before_ref)

        @pl.when(number(sc_ref, ODD) != 0)
        def _():
            dq_ref[...], before_ref[0], before_ref[1] = key_block_back(
                kb_ref[...], vb_ref[...], q, d_o, log_rows, deltas, False
            )

        for first in (0, half):
            span = slice(first, first + half)
            dq, dk, dv = key_block_back(
                k_ref[span, :], v_ref[span, :], q[first:], d_o[first:],
                log_rows[:, first:], deltas[:, first:], True,
            )
            dq_ref[first:, :] += dq
            grads_ref[1, span, :] = dk
            grads_ref[2, span, :] = dv
        grads_ref[0] = (dq_ref[...] * SCALE).astype(BF)

    block = (rows, PAIR)

    def at(offset):
        return pl.BlockSpec(block, lambda p, sc: (0, offset + number(sc, side) * count + p))

    return pl.pallas_call(
        kernel,
        grid_spec=pltpu.PrefetchScalarGridSpec(
            num_scalar_prefetch=1,
            grid=(count,),
            in_specs=[
                at(0), at(pairs), at(2 * pairs), at(0), at(pairs), at(0), at(0),
                pl.BlockSpec((1, 2, rows), lambda p, sc: (number(sc, side) * count + p, 0, 0)),
            ],
            out_specs=[
                pl.BlockSpec((3, rows, PAIR), lambda p, sc: (0, 0, p)),
                pl.BlockSpec((2, rows, PAIR), lambda p, sc: (0, 0, p)),
            ],
            scratch_shapes=[pltpu.VMEM(block, F32)],
        ),
        out_shape=[shape_of((3, rows, D // 2), BF), shape_of((2, rows, D // 2), BF)],
        compiler_params=params(),
        cost_estimate=cost(0, 0),
        name="attention_backward",
    )(scalars, qkv, qkv, qkv, pairs_before, pairs_before, d_out, out, logs)


def project_back(own, grads_own, grads_other, weight, x, name, before=None, others=None):
    rows = x.shape[0]
    count, _, width = grads_own.shape
    first = 3 - count
    chunk = 128

    def kernel(own_ref, ga_ref, gb_ref, wa_ref, wb_ref, x_ref, *refs):
        out_ref, sums_ref, acc_ref, part_sums = refs[-4:]
        j = pl.program_id(0)
        grad = jnp.concatenate([ga_ref[...], gb_ref[...]], axis=1)
        part = mm(grad, jnp.concatenate([wa_ref[...], wb_ref[...]], axis=1), NT)

        @pl.when(j == 0)
        def _():
            acc_ref[...] = part

        @pl.when(j != 0)
        def _():
            acc_ref[...] += part

        @pl.when(j == count - 1)
        def _():
            part_sums[...] = jnp.zeros_like(part_sums)

            def finish(span):
                total = acc_ref[span, :]
                normal, _ = normed(x_ref[span, :].astype(F32))
                for place, values in ((0, total * normal), (1, total)):
                    folded = values[:8]
                    for i in range(8, chunk, 8):
                        folded = folded + values[i : i + 8]
                    part_sums[place] += folded
                out_ref[span, :] = total.astype(BF)

            by_rows(rows, chunk, finish)
            rows_of_sums = [jnp.sum(part_sums[i], axis=0, keepdims=True) for i in (0, 1)]
            if before is None:
                sums_ref[...] = jnp.zeros_like(sums_ref)
                for i in (0, 1):
                    sums_ref[i : i + 1, :] = rows_of_sums[i]
            else:
                all_rows = [rows_of_sums[i] + refs[0][i : i + 1, :] for i in (0, 1)]
                all_rows += [refs[1][i : i + 1, :] for i in range(4)]
                strips = [
                    row[:, c * LANES : (c + 1) * LANES] for row in all_rows for c in range(D // LANES)
                ]
                sums_ref[...] = jnp.concatenate(strips, axis=0).astype(BF)

    grad = pl.BlockSpec((None, rows, width), lambda j, own: (j, 0, 0))
    more = [] if before is None else [before, others]
    sums_shape = shape_of((8, D), F32) if before is None else shape_of((6 * D // LANES, LANES), BF)
    return pl.pallas_call(
        kernel,
        grid_spec=pltpu.PrefetchScalarGridSpec(
            num_scalar_prefetch=1,
            grid=(count,),
            in_specs=[
                grad,
                grad,
                pl.BlockSpec((D, width), lambda j, own: (0, 2 * (first + j) + number(own, CORE))),
                pl.BlockSpec((D, width), lambda j, own: (0, 2 * (first + j) + 1 - number(own, CORE))),
                whole((rows, D)),
            ]
            + [whole(a.shape) for a in more],
            out_specs=[whole((rows, D)), whole(sums_shape.shape)],
            scratch_shapes=[pltpu.VMEM((rows, D), F32), pltpu.VMEM((2, 8, D), F32)],
        ),
        out_shape=[shape_of((rows, D), BF), sums_shape],
        compiler_params=params(),
        cost_estimate=cost(0, 0),
        name=name,
    )(own, grads_own, grads_other, weight, weight, x, *more)


def input_back(d_act, d_act_other, x, d_mid1, gain):
    rows = x.shape[0]
    tile = rows // 4

    def kernel(da_ref, db_ref, x_ref, dm_ref, gain_ref, out_ref):
        normal, inverse = normed(x_ref[...].astype(F32))
        up = da_ref[...].astype(F32) + db_ref[...].astype(F32)
        out_ref[...] = dm_ref[...] + norm_back(normal, inverse, gain_ref[...], up)

    row_block = pl.BlockSpec((tile, D), lambda i: (i, 0))
    return pl.pallas_call(
        kernel,
        grid=(rows // tile,),
        in_specs=[row_block] * 4 + [whole((1, D))],
        out_specs=row_block,
        out_shape=shape_of((rows, D), F32),
        compiler_params=params(),
        cost_estimate=cost(0, 0),
        name="input_back",
    )(d_act, d_act_other, x, d_mid1, gain)


def part_of(operand):
    if isinstance(operand, tuple):
        array, part = operand
        return array, array.shape[1:], lambda *at: (part,) + at
    return operand, operand.shape, None


def spec_of(operand, block, place):
    _, _, lead = part_of(operand)
    if lead is None:
        return pl.BlockSpec(block, place)
    return pl.BlockSpec((None,) + block, lambda *at: lead(*place(*at)))


def joined(refs):
    blocks = [ref[...] for ref in refs]
    return blocks[0] if len(blocks) == 1 else jnp.concatenate(blocks, axis=0)


def put_strips(ref, values, first=0):
    for c in range(values.shape[1] // LANES):
        ref[first + c] = values[:, c * LANES : (c + 1) * LANES]


def row_grad(scalars, lefts, rights, name):
    n = len(lefts)
    left_shapes = [part_of(a)[1] for a in lefts]
    right_shapes = [part_of(a)[1] for a in rights]
    rows = left_shapes[0][1]
    wide = right_shapes[0][1] // 2
    tile = 512
    strips = wide // LANES

    def kernel(sc_ref, *refs):
        left = joined(refs[:n])
        put_strips(refs[-2], mm(left, joined(refs[n : 2 * n]), TN).astype(BF))
        put_strips(refs[-1], mm(left, joined(refs[2 * n : 3 * n]), TN).astype(BF))

    operands = [part_of(a)[0] for a in lefts]
    in_specs = [
        spec_of(a, (shape[0], tile), lambda j, sc: (0, j)) for a, shape in zip(lefts, left_shapes)
    ]
    for place in (lambda j, sc: (0, number(sc, NOT_Y)), lambda j, sc: (0, number(sc, Y))):
        for a, shape in zip(rights, right_shapes):
            in_specs.append(spec_of(a, (shape[0], wide), place))
            operands.append(part_of(a)[0])
    return pl.pallas_call(
        kernel,
        grid_spec=pltpu.PrefetchScalarGridSpec(
            num_scalar_prefetch=1,
            grid=(rows // tile,),
            in_specs=in_specs,
            out_specs=[pl.BlockSpec((strips, tile, LANES), lambda j, sc: (0, j, 0))] * 2,
        ),
        out_shape=[shape_of((strips, rows, LANES), BF)] * 2,
        compiler_params=params(),
        cost_estimate=cost(0, 0),
        name=name,
    )(scalars, *operands)


def column_grad(scalars, lefts, rights, bw, name):
    n = len(lefts)
    left_shapes = [part_of(a)[1] for a in lefts]
    right_shapes = [part_of(a)[1] for a in rights]
    rows = left_shapes[0][1]
    cols = right_shapes[0][1]
    bn = 1024
    blocks = rows // bw
    strips = bn // LANES

    def kernel(sc_ref, *refs):
        send_ref, keep_ref, product = refs[-3:]
        product[...] = mm(joined(refs[:n]), joined(refs[n : 2 * n]), TN).astype(BF)
        for i in range(blocks):
            block = product[pl.ds(pl.multiple_of(row_block(sc_ref, i, blocks) * bw, bw), bw), :]
            target = send_ref if i < blocks // 2 else keep_ref
            place = (i % (blocks // 2)) * bw
            for c in range(strips):
                target[c, place : place + bw, :] = block[:, c * LANES : (c + 1) * LANES]

    operands = [part_of(a)[0] for a in lefts] + [part_of(a)[0] for a in rights]
    in_specs = [spec_of(a, shape, lambda j, sc: (0, 0)) for a, shape in zip(lefts, left_shapes)]
    in_specs += [spec_of(a, (shape[0], bn), lambda j, sc: (0, j)) for a, shape in zip(rights, right_shapes)]
    return pl.pallas_call(
        kernel,
        grid_spec=pltpu.PrefetchScalarGridSpec(
            num_scalar_prefetch=1,
            grid=(cols // bn,),
            in_specs=in_specs,
            out_specs=[pl.BlockSpec((strips, rows // 2, LANES), lambda j, sc: (j, 0, 0))] * 2,
            scratch_shapes=[pltpu.VMEM((rows, bn), BF)],
        ),
        out_shape=[shape_of((cols // LANES, rows // 2, LANES), BF)] * 2,
        compiler_params=params(),
        cost_estimate=cost(0, 0),
        name=name,
    )(scalars, *operands)


def block_grads(scalars, bw, lefts, rights, blocks, name, text=None, captions=None, per_image=1):
    count = len(blocks)
    width = 512
    part = width // 2
    row_blocks = D // bw
    in_specs, operands = [], []
    for a, lead in lefts:
        if lead is None:
            in_specs.append(whole(a.shape))
        else:
            in_specs.append(pl.BlockSpec((None,) + a.shape[1:], lambda j, sc, *_, lead=lead: (lead, 0, 0)))
        operands.append(a)
    for a, place in rights:
        if isinstance(a, tuple):
            a, lead = a
            in_specs.append(
                pl.BlockSpec(
                    (None, a.shape[1], width), lambda j, sc, *_, place=place, lead=lead: (lead, 0, place(j))
                )
            )
        elif a.ndim == 3:
            in_specs.append(
                pl.BlockSpec((None, a.shape[1], width), lambda j, sc, *_, place=place: (place(j), 0, 0))
            )
        else:
            in_specs.append(pl.BlockSpec((a.shape[0], width), lambda j, sc, *_, place=place: (0, place(j))))
        operands.append(a)
    n, m = len(lefts), len(rights)
    if text is not None:
        for a, leads in ((text[0], (0, 1)), (text[1], (1, 0))):
            for lead in leads:
                in_specs.append(pl.BlockSpec((None,) + a.shape[1:], lambda j, sc, *_, lead=lead: (lead, 0, 0)))
                operands.append(a)
        wide = text[0].shape[2]
        for at in (0, 1):
            in_specs.append(
                pl.BlockSpec((D // 2, wide), lambda j, sc, *_, at=at: (number(sc, CORE), at))
            )
            operands.append(text[2])
        count += 1
    inputs_count = len(operands)

    prefetched = [scalars] if captions is None else [scalars, captions]
    groups = lax.axis_size("dp")

    def kernel(sc_ref, *refs):
        if captions is not None:
            captions_ref, refs = refs[0], refs[1:]
        left_refs, right_refs = refs[:n], refs[n : n + m]
        sent_a, kept_a, sent_b, kept_b, product = refs[inputs_count:]
        j = pl.program_id(0)

        if text is not None:
            text_refs = refs[n + m : inputs_count]

            @pl.when(j == count - 1)
            def _():
                product[...] = jnp.zeros_like(product)
                core = number(sc_ref, CORE)
                for i in (0, 1):
                    mine, others = text_refs[2 * i][...], text_refs[2 * i + 1][...]
                    low = jnp.where(core == 0, mine, others)
                    high = jnp.where(core == 0, others, mine)
                    term = mm(low, text_refs[4][...], NT) + mm(high, text_refs[5][...], NT)
                    at = pl.multiple_of(image_entry(sc_ref, captions_ref, per_image, groups, i) * TEXT_LEN, TEXT_LEN)
                    span = pl.ds(at, TEXT_LEN)
                    product[span, :] = add(product[span, :], term)

        for at, (left_places, right_places) in enumerate(blocks):

            @pl.when(j == at)
            def _(left_places=left_places, right_places=right_places):
                left = joined([left_refs[i] for i in left_places])
                right = joined([right_refs[i] for i in right_places])
                product[...] = mm(left, right, TN).astype(BF)

        eighth = part // 2
        sent_a[0] = product[:, pl.ds(pl.multiple_of(number(sc_ref, NOT_Y) * eighth, eighth), eighth)]
        kept_a[0] = product[:, pl.ds(pl.multiple_of(number(sc_ref, Y) * eighth, eighth), eighth)]
        for i in range(row_blocks):
            rows = product[pl.ds(pl.multiple_of(row_block(sc_ref, i, row_blocks) * bw, bw), bw), part:]
            target = sent_b if i < row_blocks // 2 else kept_b
            place = (i % (row_blocks // 2)) * bw
            for c in (0, 1):
                target[c, place : place + bw, :] = rows[:, c * LANES : (c + 1) * LANES]

    a_block, b_block = (1, D, LANES), (2, D // 2, LANES)
    return pl.pallas_call(
        kernel,
        grid_spec=pltpu.PrefetchScalarGridSpec(
            num_scalar_prefetch=len(prefetched),
            grid=(count,),
            in_specs=in_specs,
            out_specs=[
                pl.BlockSpec(a_block, lambda j, sc, *_: (j, 0, 0)),
                pl.BlockSpec(a_block, lambda j, sc, *_: (j, 0, 0)),
                pl.BlockSpec(b_block, lambda j, sc, *_: (j, 0, 0)),
                pl.BlockSpec(b_block, lambda j, sc, *_: (j, 0, 0)),
            ],
            scratch_shapes=[pltpu.VMEM((D, width), BF)],
        ),
        out_shape=[
            shape_of((count, D, LANES), BF),
            shape_of((count, D, LANES), BF),
            shape_of((2 * count, D // 2, LANES), BF),
            shape_of((2 * count, D // 2, LANES), BF),
        ],
        compiler_params=params(),
        cost_estimate=cost(0, 0),
        name=name,
    )(*prefetched, *operands)


def swap(block, axis, bit):
    route = [(i, i ^ (1 << bit)) for i in range(lax.axis_size(axis))]
    return lax.ppermute(block, axis, route)


def pick(block, place, dim):
    return lax.dynamic_index_in_dim(block, place, dim, keepdims=False)


def bit_of(index, bit):
    return (index >> bit) & 1


def add(a, b):
    return (a.astype(F32) + b.astype(F32)).astype(BF)


class Order:
    def __init__(self):
        self.token = None

    def then(self, *values):
        if self.token is not None:
            values = lax.optimization_barrier(values + (self.token,))[:-1]
        return values if len(values) > 1 else values[0]

    def mark(self, value):
        self.token = value
        return value


def exchange(block, axis, mask):
    route = [(i, i ^ mask) for i in range(lax.axis_size(axis))]
    return lax.ppermute(block, axis, route)


def flat(block):
    return block.reshape(-1, LANES)


def rows_at(first, count):
    return pl.ds(pl.multiple_of(first, 16) if not isinstance(first, int) else first, count)


def repeat(count, step):
    def one(i, carry):
        step(i)
        return carry

    lax.fori_loop(0, count, one, 0)


def sum_stage(order, name, scalars, inputs, outputs, work):
    n = len(inputs)

    def kernel(sc_ref, *refs):
        work(sc_ref, refs[:n], refs[n:])

    outs = pl.pallas_call(
        kernel,
        grid_spec=pltpu.PrefetchScalarGridSpec(
            num_scalar_prefetch=1,
            grid=(1,),
            in_specs=[whole(a.shape) for a in inputs],
            out_specs=[whole((rows, LANES)) for rows in outputs],
        ),
        out_shape=[shape_of((rows, LANES), BF) for rows in outputs],
        compiler_params=params(),
        cost_estimate=cost(0, 0),
        name=name,
    )(scalars, *inputs)
    order.mark(outs[0])
    return outs


class Streams:
    def __init__(self, a_strips, a_rows, b_strips, b_rows, left):
        self.a_strips, self.a_rows, self.b_strips, self.b_rows = a_strips, a_rows, b_strips, b_rows // 2
        self.left = left
        self.a_half = a_strips * left * a_rows
        self.b_half = b_strips * left * (b_rows // 2)
        self.a_first, self.b_first = 2 * self.a_half, 2 * self.b_half
        self.piece = (self.a_half + self.b_half) // left

    def by_place(self, kept, came, sent, sent_at, keep, mine, a):
        rows = 2 * (self.a_rows if a else self.b_rows)
        strips = self.a_strips if a else self.b_strips

        def step(i):
            for out, at, side in ((sent, sent_at, 1 - mine), (keep, 0, mine)):
                first = (2 * i + side) * rows
                out[rows_at(at + i * rows, rows), :] = (
                    kept[rows_at(first, rows), :] + came[rows_at(first, rows), :]
                )

        repeat(strips * self.left // 2, step)

    def second(self, kept, came, sent, keep, mine, a, came_at=0):
        rows = self.a_rows if a else self.b_rows
        strips = self.a_strips if a else self.b_strips

        def step(i):
            for out, side in ((sent, 1 - mine), (keep, mine)):
                first = i * 2 * rows + side * rows
                out[rows_at(i * rows, rows), :] = (
                    kept[rows_at(first, rows), :] + came[rows_at(came_at + first, rows), :]
                )

        repeat(strips * self.left, step)

    def third(self, kept_a, came_a, kept_b, came_b, sent, keep, place):
        a_rows, b_rows, left = self.a_rows, self.b_rows, self.left
        mine = place & 1
        for j in range(left // 2):
            for out, side in ((sent, 1 - mine), (keep, mine)):
                block = 2 * j + side
                base = j * self.piece

                def a_step(i, out=out, block=block, base=base):
                    first = (i * left + block) * a_rows
                    out[rows_at(base + i * a_rows, a_rows), :] = (
                        kept_a[rows_at(first, a_rows), :] + came_a[rows_at(first, a_rows), :]
                    )

                def b_step(i, out=out, block=block, base=base):
                    first = (i * left + block) * b_rows
                    at = base + self.a_strips * a_rows + i * b_rows
                    out[rows_at(at, b_rows), :] = (
                        kept_b[rows_at(first, b_rows), :] + came_b[rows_at(first, b_rows), :]
                    )

                repeat(self.a_strips, a_step)
                repeat(self.b_strips, b_step)


def add_rows(a, b, a_at, out, out_at, count):
    chunk = math.gcd(count, 256)

    def step(i):
        span = rows_at(a_at + i * chunk, chunk)
        out[rows_at(out_at + i * chunk, chunk), :] = a[span, :] + b[span, :]

    repeat(count // chunk, step)


def total_over_rest(pieces):
    for bit in range(2, lax.axis_size("dp").bit_length() - 1):
        pieces = [add(piece, swap(piece, "dp", bit)) for piece in pieces]
    return pieces


class Spread:
    def __init__(self, order, scalars, piece):
        self.order, self.scalars, self.piece = order, scalars, piece
        self.y = swap(order.then(piece), "dp", 1)

    def forward(self):
        self.piece, self.y = self.order.then(self.piece, self.y)
        self.core = swap(self.piece, "dp", 0)
        self.both = swap(self.y, "dp", 0)

    def finish(self, rows, shapes, write, name, rider=0):
        pieces = self.order.then(self.piece, self.core, self.y, self.both)
        out_shapes = list(shapes) + ([(rider, LANES)] if rider else [])

        def kernel(sc_ref, *refs):
            outs = refs[4:]
            for at in range(4):
                for k in range(4):

                    @pl.when(number(sc_ref, QUARTER) == at ^ k)
                    def _(at=at, k=k):
                        write(outs, refs[k], at & 1, at >> 1)

            if rider:
                total = refs[0][rows:, :].astype(F32)
                for ref in refs[1:4]:
                    total = total + ref[rows:, :].astype(F32)
                outs[-1][...] = total

        outs = pl.pallas_call(
            kernel,
            grid_spec=pltpu.PrefetchScalarGridSpec(
                num_scalar_prefetch=1,
                grid=(1,),
                in_specs=[whole(self.piece.shape)] * 4,
                out_specs=[whole(shape) for shape in out_shapes],
            ),
            out_shape=[shape_of(shape, F32) for shape in out_shapes],
            compiler_params=params(),
            cost_estimate=cost(0, 0),
            name=name,
        )(self.scalars, *pieces)
        self.order.mark(outs[0])
        return outs

    def finish_text(self, rows, bw):
        pieces = self.order.then(self.piece, self.core, self.y, self.both)
        shards = lax.axis_size("seq")
        half = bw // 2

        def kernel(sc_ref, *refs):
            out_ref = refs[4]

            def one(i, carry):
                place = i ^ number(sc_ref, ME)
                seq_at = (place & 1) * (shards // 2) + (place >> 1)
                at = pl.multiple_of(seq_at * rows, rows)
                first = pl.multiple_of(i * bw, bw)
                for core in (0, 1):
                    for y in (0, 1):
                        for k in range(4):

                            @pl.when(number(sc_ref, QUARTER) == (2 * y + core) ^ k)
                            def _(ref=refs[k], core=core, y=y):
                                col = core * (D // 2) + y * LANES
                                out_ref[pl.ds(first, bw), col : col + LANES] = ref[
                                    pl.ds(at, bw), :
                                ].astype(F32)
                                for c in (0, 1):
                                    col = core * (D // 2) + 256 + c * LANES
                                    out_ref[pl.ds(first + y * half, half), col : col + LANES] = ref[
                                        rows_at(at + bw + c * half, half), :
                                    ].astype(F32)

                return carry

            lax.fori_loop(0, shards, one, 0)

        return pl.pallas_call(
            kernel,
            grid_spec=pltpu.PrefetchScalarGridSpec(
                num_scalar_prefetch=1,
                grid=(1,),
                in_specs=[whole(self.piece.shape)] * 4,
                out_specs=whole((shards * bw, D)),
            ),
            out_shape=shape_of((shards * bw, D), F32),
            compiler_params=params(),
            cost_estimate=cost(0, 0),
            name="text_finish",
        )(self.scalars, *pieces)


def numbers_of(per_image):
    me, dp = lax.axis_index("seq"), lax.axis_index("dp")
    packed = (me % per_image) | ((dp & 3) << 1) | (me << 3) | ((dp >> 2) << 15)
    return packed.astype(jnp.int32).reshape(1)


def body(
    inputs,
    text_state,
    text_segment,
    image_text,
    image_segment,
    self_gain,
    self_shift,
    qkv_weight,
    self_weight,
    cross_gain,
    cross_shift,
    query_weight,
    text_weight,
    cross_weight,
    feed_gain,
    feed_shift,
    up_weight,
    down_weight,
    cotangent,
):
    rows = inputs.shape[0]
    shards = lax.axis_size("seq")
    groups = lax.axis_size("dp")
    me, dp = lax.axis_index("seq"), lax.axis_index("dp")
    per_image = IMG_TOK // rows
    order = Order()
    scalars = numbers_of(per_image)

    def over_core(block):
        return swap(block, "dp", 0)

    seq_bits = shards.bit_length() - 1
    dp_bits = groups.bit_length() - 1
    spread_steps = [("seq", b) for b in reversed(range(seq_bits))] + [("dp", 1), ("dp", 0)]
    bw = D // shards
    bw_ff = FF // (2 * shards)

    even_to_odd = [(i, i + 1) for i in range(0, shards, 2)]
    odd_to_even = [(i + 1, i) for i in range(0, shards, 2)]
    x_before = lax.ppermute(inputs, "seq", even_to_odd)
    cot_mate = over_core(cotangent)
    gain1, shift1 = self_gain.reshape(1, D), self_shift.reshape(1, D)
    act1, qkv, norms = norm_project(inputs, gain1, shift1, qkv_weight, 0, "norm_project")
    act1_mate = over_core(act1)
    own_out, own_log = causal_forward(qkv, norms)
    order.mark(own_out)
    text_state = order.then(text_state)
    text_kv, bias_row, text_row, text_row_mate = text_project(
        scalars, image_text, image_segment, per_image, text_state, text_segment, text_weight
    )
    order.mark(text_kv)
    x_before, act1_mate, cot_mate = order.then(x_before, act1_mate, cot_mate)
    act1_before, pairs_before, norms_before = norm_project(
        x_before, gain1, shift1, qkv_weight, D, "norm_project_before"
    )
    before_mate = over_core(act1_before)
    attended, log_rows = earlier_forward(
        scalars, qkv, pairs_before, norms, norms_before, own_out, own_log
    )
    order.mark(attended)
    before_mate, attended = order.then(before_mate, attended)
    attended_mate = over_core(attended)
    gains = jnp.stack([cross_gain, cross_shift, feed_gain, feed_shift] * 2)
    mid1, cq, mid2, acts = middle_forward(
        attended, inputs, self_weight, query_weight, cross_weight, gains, text_kv, bias_row
    )
    order.mark(mid1)
    attended_mate, acts = order.then(attended_mate, acts)
    acts_mate = over_core(acts)
    hid_other, d_act3 = feed_half(
        scalars, OTHER, acts, cotangent, up_weight, down_weight, shards, None
    )
    order.mark(d_act3)
    d_act3, acts_mate, hid_other = order.then(d_act3, acts_mate, hid_other)
    hid_mate = over_core(hid_other)
    hid_own, d_act3 = feed_half(
        scalars, CORE, acts, cotangent, up_weight, down_weight, shards, d_act3
    )
    order.mark(d_act3)
    hid_mate = order.then(hid_mate)

    left = shards // 2
    feed = Streams(D // 2 // LANES, bw_ff, FF // 2 // LANES, bw, left)
    feed_later = Streams(D // 2 // LANES, bw_ff, FF // 2 // LANES, bw, left // 2)
    mids = Streams(6, bw, 12, bw, left)
    qkvs = Streams(3, bw, 6, bw, left)
    others = range(1, left)

    sent, feed_a = row_grad(
        scalars, [(hid_own, 0), (hid_mate, 0)], [cotangent, cot_mate], "down_grad"
    )
    order.mark(sent)
    feed_a = flat(feed_a)
    came_fa = swap(flat(sent), "dp", 1)
    acts_late = order.then(acts)
    sent, feed_b = column_grad(
        scalars, [(acts_late, 2), (acts_mate, 2)], [(hid_own, 1), (hid_mate, 1)], bw, "up_grad"
    )
    order.mark(sent)
    feed_b = flat(feed_b)
    came_fb = swap(flat(sent), "seq", 0)

    d_act3 = order.then(d_act3)
    g_mine, g_sent, d_mid1, d_att, text_grads, d_gains = middle_backward(
        scalars, d_act3, mid2, cotangent, mid1, cq, text_kv, bias_row, cross_weight, query_weight,
        self_weight, gains,
    )
    order.mark(d_mid1)
    g_mate = over_core(g_sent)
    text_mate = over_core(text_grads)
    mid2_late = order.then(mid2)
    output = feed_output(scalars, mid2_late, hid_own, hid_other, down_weight, shards)
    order.mark(output)
    g_mine, g_mate, text_mate = order.then(g_mine, g_mate, text_mate)
    lefts = [(acts, 1), (acts_mate, 1), (acts, 0), (acts_mate, 0), (attended, None), (attended_mate, None)]
    lefts += [(text_row, None), (text_row_mate, None)]
    rights = [(g_mine, lambda j: jnp.minimum(j, 2)), (g_mate, lambda j: jnp.minimum(j, 2))]
    rights += [((text_grads, 0), lambda j: jnp.clip(j - 3, 0, 1))]
    rights += [((text_mate, 1), lambda j: jnp.clip(j - 3, 0, 1))]
    blocks = [((0, 1), (0, 1)), ((2, 3), (0, 1)), ((4, 5), (0, 1)), ((6, 7), (2, 3)), ((6, 7), (2, 3))]
    sent_a, mid_a, sent_b, mid_b = block_grads(
        scalars, bw, lefts, rights, blocks, "middle_grads",
        text=(text_grads, text_mate, text_weight), captions=image_text, per_image=per_image,
    )
    order.mark(mid_a)
    mid_sent_a, mid_sent_b = flat(sent_a), flat(sent_b)
    mid_a, mid_b = flat(mid_a), flat(mid_b)

    def second(streams, name, kept_a, came_a, kept_b, came_b=None):
        def work(sc, ins, outs):
            b_at = 0 if came_b is not None else 2 * streams.a_half
            streams.second(ins[0], ins[1], outs[0], outs[2], number(sc, X), True)
            streams.second(ins[2], ins[-1] if b_at == 0 else ins[1], outs[1], outs[3], number(sc, Y), False, b_at)

        inputs = order.then(kept_a, came_a, kept_b, *([] if came_b is None else [came_b]))
        sent_x, sent_y, kept_a, kept_b = sum_stage(
            order, name, scalars, inputs, [streams.a_half, streams.b_half] * 2, work
        )
        return kept_a, sent_x, kept_b, sent_y

    def third(streams, name, kept_a, came_a, kept_b, came_b, rider=0, skip=0, late=False):
        def work(sc, ins, outs):
            streams.third(ins[0], ins[1], ins[2], ins[3], outs[0], outs[1], number(sc, PLACE) >> skip)
            if rider:
                count = streams.left // 2 * streams.piece
                span = slice(streams.a_half, streams.a_half + rider)
                for out in outs:
                    out[count : count + rider, :] = ins[0][span, :] + ins[1][span, :]

        inputs = order.then(kept_a, came_a, kept_b, came_b)
        out_rows = streams.left // 2 * streams.piece + rider
        sent, kept = sum_stage(order, name, scalars, inputs, [out_rows] * 2, work)
        return kept, (lambda: swap(order.then(sent), "seq", 1 + skip)) if late else swap(sent, "seq", 1 + skip)

    def further(streams, name, kept, came, rider=0, skip=0):
        blocks = streams.left // 2
        for bit in range(1, streams.left.bit_length() - 1):
            half = blocks // 2 * streams.piece

            def work(sc, ins, outs, bit=bit, half=half):
                mine = (number(sc, PLACE) >> (bit + skip)) & 1
                for i in range(half // streams.piece):
                    for out, side in ((outs[0], 1 - mine), (outs[1], mine)):
                        add_rows(
                            ins[0], ins[1], (2 * i + side) * streams.piece, out, i * streams.piece, streams.piece
                        )
                if rider:
                    for out in outs:
                        out[half : half + rider, :] = ins[0][2 * half :, :] + ins[1][2 * half :, :]

            inputs = order.then(kept, came)
            sent, kept = sum_stage(order, name, scalars, inputs, [half + rider] * 2, work)
            came = swap(sent, "seq", bit + 1 + skip)
            blocks //= 2
        return kept, came

    def fourth(streams, name, kept, came, rider=0):
        def work(sc, ins, outs):
            add_rows(ins[0], ins[1], 0, outs[0], 0, streams.piece + rider)

        inputs = order.then(kept, came)
        (total,) = sum_stage(order, name, scalars, inputs, [streams.piece + rider], work)
        return total_over_rest([total])[0]


    mid_sent_a, mid_sent_b, came_fa, came_fb = order.then(mid_sent_a, mid_sent_b, came_fa, came_fb)
    came_ma, came_mb = swap(mid_sent_a, "dp", 1), swap(mid_sent_b, "seq", 0)
    inputs_f = order.then(feed_a, came_fa, feed_b, came_fb)

    def work_f(sc, ins, outs):
        mine = number(sc, PLACE) & 1
        feed.by_place(ins[0], ins[1], outs[0], 0, outs[1], mine, True)
        feed.by_place(ins[2], ins[3], outs[0], feed.a_half, outs[2], mine, False)

    feed_sent, feed_a, feed_b = sum_stage(
        order, "feed_second", scalars, inputs_f, [feed.a_half + feed.b_half, feed.a_half, feed.b_half], work_f
    )
    came_f = swap(feed_sent, "seq", 1)

    d_att = order.then(d_att)
    att_other, before_other = attention_backward(
        scalars, OTHER, qkv, pairs_before, d_att, attended, log_rows
    )
    order.mark(att_other)
    att_mate, before_mate_grads = over_core(att_other), over_core(before_other)
    d_att = order.then(d_att)
    att_own, before_own = attention_backward(scalars, CORE, qkv, pairs_before, d_att, attended, log_rows)
    order.mark(att_own)
    mid_a, mid_sent_x, mid_b, mid_sent_y = second(mids, "mid_second", mid_a, came_ma, mid_b, came_mb)
    came_ma, came_mb = swap(mid_sent_x, "seq", 0), swap(mid_sent_y, "dp", 1)

    act1_late, att_mate, before_mate_grads = order.then(act1, att_mate, before_mate_grads)
    lefts = [(act1_late, None), (act1_mate, None), (act1_before, None), (before_mate, None)]
    rights = [(att_own, lambda j: j), (att_mate, lambda j: j)]
    rights += [(before_own, lambda j: jnp.maximum(j - 1, 0))]
    rights += [(before_mate_grads, lambda j: jnp.maximum(j - 1, 0))]
    blocks = [((0, 1), (0, 1))] + [((0, 1, 2, 3), (0, 1, 2, 3))] * 2
    sent_a, qkv_a, sent_b, qkv_b = block_grads(scalars, bw, lefts, rights, blocks, "qkv_grads")
    order.mark(qkv_a)
    came_qa, came_qb = swap(flat(sent_a), "dp", 1), swap(flat(sent_b), "seq", 0)
    before_own, came_f = order.then(before_own, came_f)
    d_act_before, sums_before = project_back(
        scalars, before_own, before_other, qkv_weight, x_before, "project_back_before"
    )
    order.mark(d_act_before)
    mid_left = third(mids, "mid_third", mid_a, came_ma, mid_b, came_mb)
    feed_a, feed_sent_x, feed_b, feed_sent_y = second(feed_later, "feed_third", feed_a, came_f, feed_b)
    came_fa, came_fb = swap(feed_sent_x, "seq", 0), swap(feed_sent_y, "dp", 1)
    att_own = order.then(att_own)
    d_act, rider = project_back(
        scalars, att_own, att_other, qkv_weight, inputs, "project_back", sums_before, d_gains
    )
    order.mark(d_act)
    rides = rider.shape[0]

    inputs_q = order.then(flat(qkv_a), came_qa, flat(qkv_b), came_qb, rider)

    def work_q(sc, ins, outs):
        qkvs.second(ins[0], ins[1], outs[0], outs[2], number(sc, X), True)
        qkvs.second(ins[2], ins[3], outs[1], outs[3], number(sc, Y), False)
        for out in (outs[0], outs[2]):
            out[qkvs.a_half : qkvs.a_half + rides, :] = ins[4][...]

    sent_x, sent_y, qkv_a, qkv_b = sum_stage(
        order, "qkv_second", scalars, inputs_q,
        [qkvs.a_half + rides, qkvs.b_half] * 2, work_q,
    )
    came_qa, came_qb = swap(sent_x, "seq", 0), swap(sent_y, "dp", 1)
    mid_left = further(mids, "mid_further", *mid_left)
    feed_kept, feed_start = third(
        feed_later, "feed_join", feed_a, came_fa, feed_b, came_fb, skip=1, late=True
    )
    qkv_left = third(qkvs, "qkv_third", qkv_a, came_qa, qkv_b, came_qb, rides)
    d_act_before = order.then(d_act_before)
    d_act_late = lax.ppermute(d_act_before, "seq", odd_to_even)
    mid_piece = fourth(mids, "mid_fourth", *mid_left)

    text_rows = 2 * bw
    text_piece = jnp.concatenate(
        [mid_piece[5 * bw : 6 * bw], mid_piece[11 * bw : 12 * bw]], axis=0
    )
    order.mark(text_piece)
    text_pieces = [text_piece] + [exchange(text_piece, "seq", 2 * k) for k in others]

    def join(name, pieces):
        def work(sc, ins, outs):
            for i, ref in enumerate(ins):
                count = ref.shape[0]
                outs[0][i * count : (i + 1) * count, :] = ref[...]

        inputs = order.then(*pieces)
        return sum_stage(order, name, scalars, inputs, [len(pieces) * pieces[0].shape[0]], work)[0]

    qkv_left = further(qkvs, "qkv_further", *qkv_left, rides)
    text_block = join("text_join", text_pieces)
    came_text = swap(text_block, "seq", 0)
    mid_all = Spread(order, scalars, mid_piece)
    d_act, d_act_late = order.then(d_act, d_act_late)
    input_grad = input_back(d_act, d_act_late, inputs, d_mid1, gain1)
    order.mark(input_grad)
    qkv_piece = fourth(qkvs, "qkv_fourth", *qkv_left, rides)
    qkv_all = Spread(order, scalars, qkv_piece)
    feed_left = (feed_kept, feed_start())
    text_block = join("text_join", [text_block, came_text])
    text_all = Spread(order, scalars, text_block)
    mid_all.forward()

    b_rows = bw // 2

    def write_feed(outs, ref, at_core, y):
        at = 0
        strips = D // 2 // LANES
        for c in range(strips):
            col = y * (D // 2) + c * LANES
            outs[0][at_core * bw_ff : (at_core + 1) * bw_ff, col : col + LANES] = ref[
                at + c * bw_ff : at + (c + 1) * bw_ff, :
            ].astype(F32)
        at = at + strips * bw_ff
        per = bw_ff // LANES
        for c in range(FF // 2 // LANES):
            s, inside = divmod(c, per)
            col = (2 * s + at_core) * bw_ff + inside * LANES
            outs[1][y * b_rows : (y + 1) * b_rows, col : col + LANES] = ref[
                at + c * b_rows : at + (c + 1) * b_rows, :
            ].astype(F32)

    def writer(targets):
        count = len(targets)

        def write(outs, ref, at_core, y):
            for j, where in enumerate(targets):
                if where is None:
                    continue
                out, first = where
                col = first[at_core]
                outs[out][:, col + y * LANES : col + (y + 1) * LANES] = ref[
                    j * bw : (j + 1) * bw, :
                ].astype(F32)
                for half in (0, 1):
                    row_at = count * bw + (2 * j + half) * b_rows
                    to = col + 256 + half * LANES
                    outs[out][y * b_rows : (y + 1) * b_rows, to : to + LANES] = ref[
                        row_at : row_at + b_rows, :
                    ].astype(F32)

        return write

    targets = [(0, (0, 512)), (1, (0, 512)), (2, (0, 512)), (3, (0, 1024)), (3, (512, 1536)), None]
    cross_grad, query_grad, self_grad, text_weight_grad = mid_all.finish(
        mids.piece, [(bw, D), (bw, D), (bw, D), (bw, 2 * D)], writer(targets), "mids_finish"
    )
    qkv_all.forward()
    text_all.forward()
    targets = [(0, (0, 512)), (0, (1024, 1536)), (0, (2048, 2560))]
    qkv_grad, sums = qkv_all.finish(
        qkvs.piece, [(bw, 3 * D)], writer(targets), "qkv_finish", rider=rides
    )
    feed_left = further(feed_later, "feed_further", *feed_left, skip=1)
    feed_piece = fourth(feed_later, "feed_fourth", *feed_left)
    feed_all = Spread(order, scalars, feed_piece)
    text_grad = text_all.finish_text(text_rows, bw)
    order.mark(text_grad)
    feed_all.forward()
    down_grad, up_grad = feed_all.finish(
        feed.piece, [(2 * bw_ff, D), (bw, FF)], write_feed, "feed_finish"
    )
    sums = lax.dynamic_slice_in_dim(sums.reshape(6, D), me * bw, bw, 1)
    return (
        output,
        input_grad,
        text_grad.reshape(text_state.shape),
        sums[0],
        sums[1],
        qkv_grad,
        self_grad,
        sums[2],
        sums[3],
        query_grad,
        text_weight_grad,
        cross_grad,
        sums[4],
        sums[5],
        up_grad,
        down_grad,
    )


def solution(mesh):
    tokens = P(("dp", "seq"), None)
    return jax.shard_map(
        body,
        mesh=mesh,
        in_specs=(tokens,) + (P(),) * 17 + (tokens,),
        out_specs=(
            tokens,
            tokens,
            P(),
            P("seq"),
            P("seq"),
            P("seq", None),
            P("seq", None),
            P("seq"),
            P("seq"),
            P("seq", None),
            P("seq", None),
            P("seq", None),
            P("seq"),
            P("seq"),
            P("seq", None),
            P("seq", None),
        ),
        check_vma=False,
    )
```
